32 devices in a mesh: groups: 2 (over y), loc: 4 (over z), date: 2 (over x), mp: 2 (over core).
Axes of the slice: x: 2, y: 2, z: 4, core: 2. Of those that a mesh axis runs over, the one named last changes fastest.
Arguments:
- optical: bfloat16 [8, 48, 12, 1024], P(('groups', 'loc'), None, 'date'), parts along dimension 0, may hold values from -6 to 6
- radar: bfloat16 [8, 48, 12, 1024], P(('groups', 'loc'), None, 'date'), parts along dimension 0, may hold values from -6 to 6
- cloud: int32 [8, 12], P(('groups', 'loc')), parts along dimension 0, may hold values 0 or 1
- radar_drop: int32 [8, 12], P(('groups', 'loc')), parts along dimension 0, may hold values 0 or 1
- keep_index: int32 [8, 48], P(('groups', 'loc')), parts along dimension 0, may hold values from 0 to 195, as said below
- place_table: bfloat16 [196, 1024], replicated, may hold values from -3 to 3
- date_table: bfloat16 [12, 1024], replicated, may hold values from -3 to 3
- spatial_gain: float32 [1024], replicated, may hold values from 0.25 to 1.75
- spatial_weights: bfloat16 [1024, 4, 1024], P('date', None, 'mp')
- temporal_gain: float32 [1024], replicated, may hold values from 0.25 to 1.75
- temporal_weights: bfloat16 [1024, 4, 1024], P('date', None, 'mp')
- cotangent: bfloat16 [8, 48, 12, 1024], P(('groups', 'loc'), 'date'), parts along dimension 0, may hold values from -0.5 to 0.5
Outputs:
- encoded: bfloat16 [8, 48, 12, 1024], P(('groups', 'loc'), 'date'), parts along dimension 0
- spatial_grads: float32 [2048, 4, 1024], P(('groups', 'loc', 'date'), None, 'mp'), parts along dimension 0
- temporal_grads: float32 [2048, 4, 1024], P(('groups', 'loc', 'date'), None, 'mp'), parts along dimension 0
The draws below stay inside these ranges and needn't reach their ends.
There are 2 independent parts, one for each index of `groups`. The reference program is written for one: setup_inputs(seed, part) draws one part's arguments, and reference() takes and returns one part's arrays. A program takes and returns all parts, laid end to end along the dimension named above; an argument that names none is the same for every part. Nothing has to cross between parts.
Inputs may be any that keep to these rules, and one draw needn't show every extreme that they name: `keep_index`: the 48 patch numbers of one location are distinct.
All inputs are finite; a program needn't handle non-finite values. No bound on the sum of `cloud` or of `radar_drop` on one device may be relied on, other than what follows from the above.
Results may differ from the reference program's by a relative error of at most 0.02.
Values may be sent and summed in bfloat16 or wider, within the bound.
No kernel may reach another device: no remote copies, remote signals or barrier semaphores. Data moves between devices by JAX's collectives and lax.ppermute only.
A program may use at most 128 MiB of HBM per device.

```python
import math
import jax
import jax.numpy as jnp
from jax import lax

D = 1024
PATCHES = 196
DATES = 12
KEEP = 48
HEAD_DIM = 64
LOCS = 4
N_MP = 2


def weights_draw(key):
    base = jax.random.normal(key, (D, 4, D), jnp.float32) / math.sqrt(D)
    return base.astype(jnp.bfloat16)


def draw_spatial_weights(key, part):
    return weights_draw(jax.random.fold_in(key, 101))


def draw_temporal_weights(key, part):
    return weights_draw(jax.random.fold_in(key, 202))


def draw_keep_index(key, part):
    keys = jax.random.split(jax.random.fold_in(key, 303), LOCS)
    chosen = jax.vmap(lambda single: jax.random.permutation(single, PATCHES)[:KEEP])(keys)
    return chosen.astype(jnp.int32)


def plant(entries, rng, low, high):
    extent = entries.shape
    index_at = [jax.random.randint(jax.random.fold_in(rng, axis), (), 0, extent[axis]) for axis in range(len(extent))]
    entries = entries.at[tuple(index_at)].set(low)
    longest = extent.index(max(extent))
    index_at[longest] = (index_at[longest] + 1) % extent[longest]
    return entries.at[tuple(index_at)].set(high)


def with_spikes(result, key, source, target, parts, factor):
    def block_of(axis_at):
        return (jnp.arange(result.shape[axis_at]) // (result.shape[axis_at] // parts)).reshape((-1,) + (1,) * (result.ndim - 1 - axis_at))

    one_side = jax.random.permutation(key, parts)[block_of(target)]
    other_side = (block_of(target) + parts // 2) % parts
    return jnp.where((block_of(source) == one_side) | (block_of(source) == other_side), factor * result, result)


def levels(key, dims, cuts, least, high):
    level, own = 1.0, jax.random.fold_in(key, 6)
    for axis_at, shards_of in cuts:
        steps = jnp.exp(jax.random.uniform(jax.random.fold_in(own, axis_at), (shards_of,), jnp.float32, least / len(cuts), high / len(cuts)))
        level = level * jnp.repeat(steps, dims[axis_at] // shards_of).reshape([-1 if axis == axis_at else 1 for axis in range(len(dims))])
    return level


def normal_values(stream_key, shape, scale, bound, cuts=(), kind=jnp.bfloat16):
    level = levels(stream_key, shape, cuts, -0.22, 0.18) if cuts else 1.0
    drawn = jax.random.normal(stream_key, shape, jnp.float32) * scale * level
    return jnp.minimum(jnp.maximum(drawn, -bound), bound).astype(kind)


def heavy_noise(key, shape, scale, limit, cuts, heavy, dtype=jnp.bfloat16):
    drawn = scale * jax.random.normal(key, shape, jnp.float32)
    if cuts:
        drawn = drawn * levels(key, shape, cuts, -0.22, 0.18)
    return jnp.clip(with_spikes(drawn, jax.random.fold_in(key, 3), *heavy), -limit, limit).astype(dtype)


def setup_inputs(seed: int = 0, part: int = 0) -> dict:
    arg_keys = jax.random.split(jax.random.key(seed), 13)
    part_keys = jax.random.split(jax.random.fold_in(arg_keys[12], part), 13)
    optical = normal_values(part_keys[0], (LOCS, KEEP, DATES, D), 1.0, 6.0, ((0, 4), (2, 2)))
    radar = normal_values(part_keys[1], (LOCS, KEEP, DATES, D), 1.0, 6.0, ((0, 4), (2, 2)))
    cloud = plant((jax.random.randint(part_keys[2], (LOCS, DATES), 0, 2) < 1).astype(jnp.int32), jax.random.fold_in(part_keys[2], 1), 0, 1)
    radar_drop = plant((jax.random.randint(part_keys[3], (LOCS, DATES), 0, 4) < 1).astype(jnp.int32), jax.random.fold_in(part_keys[3], 1), 0, 1)
    keep_index = draw_keep_index(jax.random.fold_in(jax.random.fold_in(arg_keys[12], part), 71), part)
    place_table = normal_values(arg_keys[5], (PATCHES, D), 0.5, 3.0)
    date_table = normal_values(arg_keys[6], (DATES, D), 0.5, 3.0)
    spatial_gain = jnp.clip(1.0 + 0.15 * jax.random.normal(arg_keys[7], (D,), jnp.float32), 0.25, 1.75)
    spatial_weights = draw_spatial_weights(jax.random.fold_in(arg_keys[12], 71), part)
    temporal_gain = jnp.clip(1.0 + 0.15 * jax.random.normal(arg_keys[9], (D,), jnp.float32), 0.25, 1.75)
    temporal_weights = draw_temporal_weights(jax.random.fold_in(arg_keys[12], 71), part)
    cotangent = heavy_noise(part_keys[11], (LOCS, KEEP, DATES, D), (3 * (LOCS * DATES * KEEP) ** -0.5), 0.5, ((0, 4), (1, 2)), (0, 3, 4, 2.0))
    return dict(optical=optical, radar=radar, cloud=cloud, radar_drop=radar_drop, keep_index=keep_index, place_table=place_table, date_table=date_table, spatial_gain=spatial_gain, spatial_weights=spatial_weights, temporal_gain=temporal_gain, temporal_weights=temporal_weights, cotangent=cotangent)


EPSILON = 1e-05
SCORE_FORM = {True: 'lpthe,lqthe->lthpq', False: 'lpthe,lpshe->lphts'}
MIX_FORM = {True: 'lthpq,lqthe->lpthe', False: 'lphts,lpshe->lpthe'}
BACK_FORM = {True: 'lthpq,lpthe->lqthe', False: 'lphts,lpthe->lpshe'}

def product(form, left, right):
    return jnp.einsum(form, left.astype(jnp.float32), right.astype(jnp.float32))

def normalize(rows, gain):
    values = rows.astype(jnp.float32)
    centred = values - lax.optimization_barrier(jnp.mean(values, -1, keepdims=True))
    inv_scale = lax.rsqrt(lax.optimization_barrier(jnp.mean(centred * centred, -1, keepdims=True)) + EPSILON)
    normed = centred * inv_scale
    return (normed, inv_scale, (normed * gain).astype(jnp.bfloat16))

def forward_heads(hidden, intake, outlet, bias, spatial):
    triple = product('lptd,dce->lptce', hidden, intake).astype(jnp.bfloat16)
    heads = triple.reshape(triple.shape[:4] + (intake.shape[2] // HEAD_DIM, HEAD_DIM))
    queries = heads[:, :, :, 0]
    key_heads = heads[:, :, :, 1]
    value_heads = heads[:, :, :, 2]
    scores = product(SCORE_FORM[spatial], queries, key_heads) * HEAD_DIM ** (-0.5) + bias
    top = lax.optimization_barrier(jnp.max(scores, -1, keepdims=True))
    raised = jnp.exp(scores - top)
    attend = raised / lax.optimization_barrier(jnp.sum(raised, -1, keepdims=True))
    attend_low = attend.astype(jnp.bfloat16)
    mixed = product(MIX_FORM[spatial], attend_low, value_heads).astype(jnp.bfloat16)
    mixed = mixed.reshape(hidden.shape[:3] + (-1,))
    partial_out = product('lpte,de->lptd', mixed, outlet)
    return ((queries, key_heads, value_heads, attend, attend_low, mixed), partial_out)

def backward_heads(upstream, hidden, saved, intake, outlet, spatial, need_input):
    queries, key_heads, value_heads, attend, attend_low, mixed = saved
    back_mixed = product('lptd,de->lpte', upstream, outlet).astype(jnp.bfloat16)
    back_heads = back_mixed.reshape(queries.shape)
    back_attend = product(SCORE_FORM[spatial], back_heads, value_heads)
    back_values = product(BACK_FORM[spatial], attend_low, back_heads).astype(jnp.bfloat16)
    inner = back_attend - lax.optimization_barrier(jnp.sum(back_attend * attend, -1, keepdims=True))
    back_scores = (attend * inner * HEAD_DIM ** (-0.5)).astype(jnp.bfloat16)
    back_queries = product(MIX_FORM[spatial], back_scores, key_heads).astype(jnp.bfloat16)
    back_keys = product(BACK_FORM[spatial], back_scores, queries).astype(jnp.bfloat16)
    back_triple = jnp.stack([back_queries, back_keys, back_values], axis=3).reshape(hidden.shape[:3] + (3, -1))
    grad_intake = product('lptd,lptce->dce', hidden, back_triple)
    grad_outlet = product('lptd,lpte->de', upstream, mixed)
    grads = jnp.concatenate([grad_intake, grad_outlet[:, None, :]], axis=1)
    if need_input:
        return (grads, product('lptce,dce->lptd', back_triple, intake))
    return (grads, None)

def run_layer(rows, gain, weights, bias, spatial):
    normed, inv_scale, hidden = normalize(rows, gain)
    width = weights.shape[2] // N_MP
    saves = []
    total = jnp.zeros(rows.shape, jnp.float32)
    for group in range(N_MP):
        block = weights[:, :, group * width:(group + 1) * width]
        saved, partial_out = forward_heads(hidden, block[:, 0:3], block[:, 3], bias, spatial)
        saves.append(saved)
        rounded = lax.optimization_barrier(partial_out.astype(jnp.bfloat16))
        total = total + rounded.astype(jnp.float32)
    output = (rows.astype(jnp.float32) + total).astype(jnp.bfloat16)
    return ((normed, inv_scale, hidden, saves), output)

def back_layer(upstream, record, gain, weights, spatial, need_input):
    normed, inv_scale, hidden, saves = record
    width = weights.shape[2] // N_MP
    pieces = []
    back_sum = jnp.zeros(upstream.shape, jnp.float32)
    for group in range(N_MP):
        block = weights[:, :, group * width:(group + 1) * width]
        grads, back_part = backward_heads(upstream, hidden, saves[group], block[:, 0:3], block[:, 3], spatial, need_input)
        pieces.append(grads)
        if need_input:
            rounded = lax.optimization_barrier(back_part.astype(jnp.bfloat16))
            back_sum = back_sum + rounded.astype(jnp.float32)
    grads_all = jnp.concatenate(pieces, axis=2)
    if not need_input:
        return (grads_all, None)
    scaled = back_sum * gain
    inner = scaled - lax.optimization_barrier(jnp.mean(scaled, -1, keepdims=True)) - normed * lax.optimization_barrier(jnp.mean(scaled * normed, -1, keepdims=True))
    back_rows = (upstream.astype(jnp.float32) + inv_scale * inner).astype(jnp.bfloat16)
    return (grads_all, back_rows)

def reference(optical, radar, cloud, radar_drop, keep_index, place_table, date_table, spatial_gain, spatial_weights, temporal_gain, temporal_weights, cotangent):
    optical_keep = (1 - cloud).astype(jnp.float32)[:, None, :, None]
    radar_keep = (1 - radar_drop).astype(jnp.float32)[:, None, :, None]
    places = jnp.take(place_table, keep_index, axis=0).astype(jnp.float32)[:, :, None, :]
    start = (optical.astype(jnp.float32) * optical_keep + radar.astype(jnp.float32) * radar_keep + places).astype(jnp.bfloat16)
    spatial_record, spatial_out = run_layer(start, spatial_gain, spatial_weights, 0.0, True)
    joined = (spatial_out.astype(jnp.float32) + date_table.astype(jnp.float32)[None, None]).astype(jnp.bfloat16)
    survive = 1 - cloud * radar_drop
    dates = cloud.shape[1]
    same = jnp.arange(dates)[:, None] == jnp.arange(dates)[None, :]
    allowed = (survive[:, None, :] == 1) | same[None]
    bias = jnp.where(allowed, 0.0, -1000000000.0).astype(jnp.float32)[:, None, None]
    temporal_record, encoded = run_layer(joined, temporal_gain, temporal_weights, bias, False)
    temporal_grads, back_joined = back_layer(cotangent, temporal_record, temporal_gain, temporal_weights, False, True)
    spatial_grads, unused = back_layer(back_joined, spatial_record, spatial_gain, spatial_weights, True, False)
    return (encoded, spatial_grads, temporal_grads)
```

```python
import functools

import jax
import jax.numpy as jnp
from jax import lax
from jax.experimental import pallas as pl
from jax.experimental.pallas import tpu as pltpu
from jax.sharding import PartitionSpec as P

HEAD_DIM = 64
EPSILON = 1e-05
CROSS = -1e30
BF = jnp.bfloat16
F32 = jnp.float32
NN = (((1,), (0,)), ((), ()))
NT = (((1,), (1,)), ((), ()))
TN = (((0,), (0,)), ((), ()))
VMEM_LIMIT = 56 * 1024 * 1024


def dot(left, right, dims):
    return lax.dot_general(left, right, dims, preferred_element_type=F32)


def statistics(rows):
    values = rows.astype(F32)
    centred = values - jnp.mean(values, -1, keepdims=True)
    inv_scale = lax.rsqrt(jnp.mean(centred * centred, -1, keepdims=True) + EPSILON)
    return centred * inv_scale, inv_scale


class Heads:
    def __init__(self, width):
        self.lanes = min(width, 256)
        self.count = self.lanes // HEAD_DIM
        owner = lax.broadcasted_iota(jnp.int32, (1, self.lanes), 1) // HEAD_DIM
        self.masks = [(owner == head).astype(F32) for head in range(self.count)]

    def stack(self, block):
        return jnp.concatenate([block * mask.astype(BF) for mask in self.masks], axis=0)

    def unstack(self, tall):
        rows = tall.shape[0] // self.count
        total = tall[0:rows] * self.masks[0]
        for head in range(1, self.count):
            total = total + tall[head * rows : (head + 1) * rows] * self.masks[head]
        return total


def span(part, offsets, number):
    rows = part.shape[1]
    return pl.ds(pl.multiple_of(offsets[number], 128), rows)


def rows_times(rows_ref, parts, offsets, kind, out_ref, column):
    width = parts[0].shape[2]
    step = min(width, 256)
    for at in range(0, width, step):
        total = None
        for number, part in enumerate(parts):
            term = dot(rows_ref[:, span(part, offsets, number)], part[kind, :, at : at + step], NN)
            total = term if total is None else total + term
        out_ref[:, column + at : column + at + step] = total.astype(out_ref.dtype)


def attention(triple_ref, bias_ref, attend_ref, mixed_ref, blocks):
    width = triple_ref.shape[1] // 3
    heads = Heads(width)
    rows = triple_ref.shape[0] // blocks
    groups = width // heads.lanes
    bias = jnp.concatenate([bias_ref[...]] * heads.count, axis=0)
    for block in range(blocks):
        at = slice(block * rows, (block + 1) * rows)
        for group in range(groups):
            lane = group * heads.lanes
            queries = heads.stack(triple_ref[at, lane : lane + heads.lanes])
            keys = triple_ref[at, width + lane : width + lane + heads.lanes]
            values = triple_ref[at, 2 * width + lane : 2 * width + lane + heads.lanes]
            scores = dot(queries, keys, NT) * HEAD_DIM ** (-0.5) + bias
            raised = jnp.exp(scores - jnp.max(scores, -1, keepdims=True))
            attend = raised * (1.0 / jnp.sum(raised, -1, keepdims=True))
            attend_ref[block * groups + group] = attend
            mixed = heads.unstack(dot(attend.astype(BF), values, NN))
            mixed_ref[at, lane : lane + heads.lanes] = mixed.astype(BF)


def attention_back(triple_ref, attend_ref, back_mixed_ref, back_triple_ref, blocks):
    width = triple_ref.shape[1] // 3
    heads = Heads(width)
    rows = triple_ref.shape[0] // blocks
    groups = width // heads.lanes
    for block in range(blocks):
        at = slice(block * rows, (block + 1) * rows)
        for group in range(groups):
            lane = group * heads.lanes
            queries = heads.stack(triple_ref[at, lane : lane + heads.lanes])
            keys = triple_ref[at, width + lane : width + lane + heads.lanes]
            values = triple_ref[at, 2 * width + lane : 2 * width + lane + heads.lanes]
            back = heads.stack(back_mixed_ref[at, lane : lane + heads.lanes])
            attend = attend_ref[block * groups + group]
            back_attend = dot(back, values, NT)
            back_values = dot(attend.astype(BF), back, TN)
            inner = back_attend - jnp.sum(back_attend * attend, -1, keepdims=True)
            back_scores = (attend * inner * HEAD_DIM ** (-0.5)).astype(BF)
            back_queries = heads.unstack(dot(back_scores, keys, NN))
            back_keys = dot(back_scores, queries, TN)
            for number, term in enumerate((back_queries, back_keys, back_values)):
                first = number * width + lane
                back_triple_ref[at, first : first + heads.lanes] = term.astype(BF)


def normalize_into(rows_ref, gain_ref, hidden_ref, blocks):
    rows = rows_ref.shape[0] // blocks
    for block in range(blocks):
        at = slice(block * rows, (block + 1) * rows)
        normed, _ = statistics(rows_ref[at, :])
        hidden_ref[at, :] = (normed * gain_ref[...]).astype(BF)


def times_outlet(mixed_ref, parts, offsets, out_ref):
    for number, part in enumerate(parts):
        out_ref[:, span(part, offsets, number)] = dot(mixed_ref[...], part[3], NT).astype(BF)


def spatial_forward_kernel(count, blocks, offsets, start, gain, bias, *refs):
    parts, (hidden, triple, attend, mixed, partial) = refs[:count], refs[count:]
    normalize_into(start, gain, hidden, blocks)
    for kind in range(3):
        rows_times(hidden, parts, offsets, kind, triple, kind * mixed.shape[1])
    attention(triple, bias, attend, mixed, blocks)
    times_outlet(mixed, parts, offsets, partial)


def temporal_kernel(count, sources, moves, blocks, offsets, gain, bias, date_rows, cotangent, *refs):
    origins, refs = refs[:sources], refs[sources:]
    parts, refs = refs[:count], refs[count:]
    joined, hidden, mixed, partial, back_triple, back_part, triple, attend, back_mixed = refs
    rows = date_rows.shape[0]
    for source, at, to, size in moves:
        dated = origins[source][at : at + size, :].astype(F32)
        dated = dated + date_rows[to % rows : to % rows + size, :].astype(F32)
        joined[to : to + size, :] = dated.astype(BF)
    normalize_into(joined, gain, hidden, blocks)
    for kind in range(3):
        rows_times(hidden, parts, offsets, kind, triple, kind * mixed.shape[1])
    rows_times(cotangent, parts, offsets, 3, back_mixed, 0)
    attention(triple, bias, attend, mixed, blocks)
    times_outlet(mixed, parts, offsets, partial)
    attention_back(triple, attend, back_mixed, back_triple, blocks)
    width = mixed.shape[1]
    for number, part in enumerate(parts):
        total = None
        for kind in range(3):
            term = dot(back_triple[:, kind * width : (kind + 1) * width], part[kind], NT)
            total = term if total is None else total + term
        back_part[:, span(part, offsets, number)] = total.astype(BF)


def norm_back_kernel(moves, step, gain, here, there, joined, cotangent, *outs):
    for at in range(0, joined.shape[0], step):
        span_here = slice(at, at + step)
        normed, inv_scale = statistics(joined[span_here, :])
        total = here[span_here, :].astype(F32) + there[span_here, :].astype(F32)
        scaled = total * gain[...]
        inner = (
            scaled
            - jnp.mean(scaled, -1, keepdims=True)
            - normed * jnp.mean(scaled * normed, -1, keepdims=True)
        )
        back = (cotangent[span_here, :].astype(F32) + inv_scale * inner).astype(BF)
        for target, first, to, size in moves:
            if at <= first < at + step:
                outs[target][to : to + size, :] = back[first - at : first - at + size]


def spatial_backward_kernel(count, sources, moves, blocks, offsets, triple, attend, *refs):
    origins, refs = refs[:sources], refs[sources:]
    parts, (upstream, back_triple, back_mixed) = refs[:count], refs[count:]
    for source, at, to, size in moves:
        upstream[to : to + size, :] = origins[source][at : at + size, :]
    rows_times(upstream, parts, offsets, 3, back_mixed, 0)
    attention_back(triple, attend, back_mixed, back_triple, blocks)


def call(body, outs, args, scratch=(), flops=0):
    smem = pl.BlockSpec(memory_space=pltpu.SMEM)
    vmem = pl.BlockSpec(memory_space=pltpu.VMEM)
    specs = [smem if arg.dtype == jnp.int32 else vmem for arg in args]
    moved = sum(arg.size * arg.dtype.itemsize for arg in args)
    moved = moved + sum(out.size * out.dtype.itemsize for out in outs)
    return pl.pallas_call(
        body,
        out_shape=list(outs),
        in_specs=specs,
        out_specs=[vmem] * len(outs),
        scratch_shapes=list(scratch),
        compiler_params=pltpu.CompilerParams(vmem_limit_bytes=VMEM_LIMIT),
        cost_estimate=pl.CostEstimate(flops=flops, bytes_accessed=moved, transcendentals=0),
    )(*args)


def swap(array, axis):
    return lax.ppermute(array, axis, [(0, 1), (1, 0)])


def gather_weights(weights, sizes):
    own = weights.transpose(1, 0, 2)
    rows = own.shape[1]
    if sizes["date"] != 2 or sizes["groups"] != 2 or rows % 256:
        return [lax.all_gather(own, "date", axis=1, tiled=True)], jnp.zeros((1,), jnp.int32)
    side = lax.axis_index("groups")
    here = lax.axis_index("date")
    half = rows // 2
    sent = lax.dynamic_slice_in_dim(own, side * half, half, 1)
    first = swap(sent, "date")
    second = swap(first, "groups")
    other = (1 - here) * rows
    offsets = jnp.stack([here * rows, other + side * half, other + (1 - side) * half])
    return [own, first, second], offsets.astype(jnp.int32)


def add_over_heads(partial, sizes):
    if sizes["mp"] == 2:
        return partial.astype(F32) + swap(partial, "mp").astype(F32)
    return lax.psum(partial.astype(F32), "mp")


def ring_sum(term_of, sizes):
    count = sizes["loc"]
    here = lax.axis_index("loc")
    total = term_of((here + count - 1) % count)
    ring = [(at, (at + 1) % count) for at in range(count)]
    for step in range(1, count):
        arrived = lax.ppermute(total.astype(BF), "loc", ring)
        total = arrived.astype(F32) + term_of((here + 2 * count - 1 - step) % count)
    return total


def weight_grads(hidden, back_triple, upstream, mixed, sizes):
    width = mixed.shape[1]
    model = hidden.shape[1]
    count = sizes["loc"] * sizes["date"]
    if sizes["date"] != 2:
        intake = dot(hidden, back_triple, TN)
        outlet = dot(upstream, mixed, TN)
        whole = jnp.concatenate([intake, outlet], axis=1).reshape(model, 4, width)
        part = lax.psum_scatter(
            whole.astype(BF), ("loc", "date"), scatter_dimension=0, tiled=True
        )
        return part.astype(F32)
    here = lax.axis_index("date")
    block = model // count

    def columns(rows, of):
        parts = rows.reshape(rows.shape[0], sizes["loc"], 2, block)
        picked = lax.dynamic_slice_in_dim(parts, of, 1, 2)
        return picked.reshape(rows.shape[0], -1)

    def both(rows):
        return jnp.concatenate([columns(rows, here), swap(columns(rows, 1 - here), "date")], axis=0)

    def whole(rows):
        return jnp.concatenate([rows, swap(rows, "date")], axis=0)

    outlet = dot(both(upstream), whole(mixed), TN)
    intake = dot(both(hidden), whole(back_triple), TN)

    def term_of(array):
        return lambda place: lax.dynamic_slice_in_dim(array, place * block, block, 0)

    outlet = ring_sum(term_of(outlet), sizes)
    intake = ring_sum(term_of(intake), sizes)
    return jnp.concatenate([intake, outlet], axis=1).reshape(block, 4, width)


def per_device(
    sizes,
    optical,
    radar,
    cloud,
    radar_drop,
    keep_index,
    place_table,
    date_table,
    spatial_gain,
    spatial_weights,
    temporal_gain,
    temporal_weights,
    cotangent,
):
    spatial_parts, spatial_offsets = gather_weights(spatial_weights, sizes)
    temporal_parts, temporal_offsets = gather_weights(temporal_weights, sizes)
    _, patches, dates_here, model = optical.shape
    patches_here, dates = cotangent.shape[1:3]
    width = spatial_weights.shape[2]
    rows = patches * dates_here
    here = lax.axis_index("date")
    first = here * dates_here
    paired = sizes["date"] == 2 and dates_here % 2 == 0 and patches_here % 8 == 0

    if paired:
        pairs, eights = dates_here // 2, patches_here // 8
        spatial_blocks, temporal_blocks = pairs, eights
        half_rows = eights * 16

        def own_first(array, axis):
            return jnp.where(here == 0, array, jnp.flip(array, axis))

        def spatial_rows(array):
            array = array.reshape(pairs, 2, 2, eights, 8, -1)
            return own_first(array, 2).transpose(0, 2, 3, 1, 4, 5).reshape(rows, -1)

        def temporal_rows(array):
            array = array.reshape(2, pairs, 2, eights, 8, -1)
            return own_first(array, 0).transpose(3, 0, 1, 2, 4, 5).reshape(rows, -1)

        def temporal_whole(array):
            array = array.reshape(eights, 2, pairs, 2, 8, -1).transpose(1, 2, 3, 0, 4, 5)
            return own_first(array, 0).reshape(dates, patches_here, -1)

    else:
        spatial_blocks = 1 if rows <= 192 else dates_here
        temporal_blocks = patches_here // 8 if patches_here % 8 == 0 else 1

        def spatial_rows(array):
            return array.reshape(rows, -1)

        def temporal_rows(array):
            array = array.reshape(dates, temporal_blocks, patches_here // temporal_blocks, -1)
            return array.transpose(1, 0, 2, 3).reshape(rows, -1)

        def temporal_whole(array):
            array = array.reshape(temporal_blocks, dates, patches_here // temporal_blocks, -1)
            return array.transpose(1, 0, 2, 3).reshape(dates, patches_here, -1)

    cloud_here = lax.dynamic_slice_in_dim(cloud, first, dates_here, 1)[0]
    drop_here = lax.dynamic_slice_in_dim(radar_drop, first, dates_here, 1)[0]
    optical_keep = (1 - cloud_here).astype(F32)[:, None, None]
    radar_keep = (1 - drop_here).astype(F32)[:, None, None]
    places = jnp.take(place_table, keep_index[0], axis=0).astype(F32)[None]
    start = (
        optical[0].transpose(1, 0, 2).astype(F32) * optical_keep
        + radar[0].transpose(1, 0, 2).astype(F32) * radar_keep
        + places
    ).astype(BF)
    start = spatial_rows(start)

    dates_at = jnp.arange(dates, dtype=jnp.int32)
    patches_at = jnp.arange(patches_here, dtype=jnp.int32)
    ones_here = jnp.ones((dates, patches_here, 1), jnp.int32)
    temporal_size = rows // temporal_blocks
    date_at = temporal_rows(ones_here * dates_at[:, None, None])[:temporal_size, 0]
    patch_at = temporal_rows(ones_here * patches_at[None, :, None])[:temporal_size, 0]
    spatial_size = rows // spatial_blocks
    spatial_date = jnp.ones((dates_here, patches, 1), jnp.int32) * dates_at[:dates_here, None, None]
    spatial_date = spatial_rows(spatial_date)[:spatial_size, 0]
    spatial_bias = jnp.where(spatial_date[:, None] == spatial_date[None, :], 0.0, CROSS).astype(F32)
    survive = 1 - cloud[0] * radar_drop[0]
    same_date = date_at[:, None] == date_at[None, :]
    allowed = (jnp.take(survive, date_at)[None, :] == 1) | same_date
    temporal_bias = jnp.where(
        patch_at[:, None] == patch_at[None, :], jnp.where(allowed, 0.0, -1000000000.0), CROSS
    ).astype(F32)
    date_rows = jnp.take(date_table, date_at, axis=0)
    cotangent_rows = temporal_rows(cotangent[0].transpose(1, 0, 2))

    spatial_gain = spatial_gain[None]
    temporal_gain = temporal_gain[None]
    lanes = min(width, 256)

    def shape(*dims, dtype=BF):
        return jax.ShapeDtypeStruct(dims, dtype)

    def attend_dims(blocks):
        return (blocks * (width // lanes), lanes // HEAD_DIM * (rows // blocks), rows // blocks)

    layer_flops = 2 * rows * model * width * 4
    hidden, triple, attend, mixed, partial = call(
        functools.partial(spatial_forward_kernel, len(spatial_parts), spatial_blocks),
        (
            shape(rows, model),
            shape(rows, 3 * width),
            shape(*attend_dims(spatial_blocks), dtype=F32),
            shape(rows, width),
            shape(rows, model),
        ),
        (spatial_offsets, start, spatial_gain, spatial_bias, *spatial_parts),
        flops=layer_flops,
    )
    spatial_out = (start.astype(F32) + add_over_heads(partial, sizes)).astype(BF)
    if paired:
        blocked = spatial_out.reshape(pairs, 2, half_rows, model)
        origins = (
            blocked[:, 0].reshape(-1, model),
            swap(blocked[:, 1].reshape(-1, model), "date"),
        )
        moves = [
            (half, pair * half_rows + eight * 16, (eight * 2 + half) * pairs * 16 + pair * 16, 16)
            for half in range(2)
            for pair in range(pairs)
            for eight in range(eights)
        ]
    else:
        moved = lax.all_to_all(
            spatial_out.reshape(dates_here, patches, model),
            "date",
            split_axis=1,
            concat_axis=0,
            tiled=True,
        )
        origins = (temporal_rows(moved),)
        moves = [(0, at * temporal_size, at * temporal_size, temporal_size) for at in range(temporal_blocks)]
    joined, temporal_hidden, temporal_mixed, temporal_partial, temporal_triple, back_part = call(
        functools.partial(
            temporal_kernel, len(temporal_parts), len(origins), moves, temporal_blocks
        ),
        (
            shape(rows, model),
            shape(rows, model),
            shape(rows, width),
            shape(rows, model),
            shape(rows, 3 * width),
            shape(rows, model),
        ),
        (
            temporal_offsets,
            temporal_gain,
            temporal_bias,
            date_rows,
            cotangent_rows,
            *origins,
            *temporal_parts,
        ),
        scratch=(
            pltpu.VMEM((rows, 3 * width), BF),
            pltpu.VMEM(attend_dims(temporal_blocks), F32),
            pltpu.VMEM((rows, width), BF),
        ),
        flops=2 * layer_flops,
    )
    if sizes["mp"] == 2:
        others = swap(back_part, "mp")
    else:
        others = (lax.psum(back_part.astype(F32), "mp") - back_part.astype(F32)).astype(BF)
    if paired:
        turned = [(source, to, at, size) for source, at, to, size in moves]
        turned_shapes = (shape(rows // 2, model), shape(rows // 2, model))
    else:
        turned = moves
        turned_shapes = (shape(rows, model),)
    backs = call(
        functools.partial(norm_back_kernel, turned, temporal_size),
        turned_shapes,
        (temporal_gain, back_part, others, joined, cotangent_rows),
    )
    if paired:
        back_origins = (backs[0], swap(backs[1], "date"))
        back_moves = [
            (half, pair * half_rows, (pair * 2 + half) * half_rows, half_rows)
            for half in range(2)
            for pair in range(pairs)
        ]
        back_moves = [
            (half, at + eight * 16, to + eight * 16, 16)
            for half, at, to, _ in back_moves
            for eight in range(eights)
        ]
    else:
        back = lax.all_to_all(
            temporal_whole(backs[0]), "date", split_axis=0, concat_axis=1, tiled=True
        )
        back_origins = (back.reshape(rows, model),)
        back_moves = [(0, at * spatial_size, at * spatial_size, spatial_size) for at in range(spatial_blocks)]
    upstream, back_triple = call(
        functools.partial(
            spatial_backward_kernel, len(spatial_parts), len(back_origins), back_moves, spatial_blocks
        ),
        (shape(rows, model), shape(rows, 3 * width)),
        (spatial_offsets, triple, attend, *back_origins, *spatial_parts),
        scratch=(pltpu.VMEM((rows, width), BF),),
        flops=layer_flops,
    )
    encoded = (joined.astype(F32) + add_over_heads(temporal_partial, sizes)).astype(BF)
    encoded = temporal_whole(encoded).transpose(1, 0, 2)[None]
    temporal_grads = weight_grads(
        temporal_hidden, temporal_triple, cotangent_rows, temporal_mixed, sizes
    )
    spatial_grads = weight_grads(hidden, back_triple, upstream, mixed, sizes)
    return (encoded, spatial_grads, temporal_grads)


def solution(mesh):
    in_specs = (
        P(("groups", "loc"), None, "date", None),
        P(("groups", "loc"), None, "date", None),
        P(("groups", "loc"), None),
        P(("groups", "loc"), None),
        P(("groups", "loc"), None),
        P(),
        P(),
        P(),
        P("date", None, "mp"),
        P(),
        P("date", None, "mp"),
        P(("groups", "loc"), "date", None, None),
    )
    out_specs = (
        P(("groups", "loc"), "date", None, None),
        P(("groups", "loc", "date"), None, "mp"),
        P(("groups", "loc", "date"), None, "mp"),
    )
    return jax.shard_map(
        functools.partial(per_device, dict(mesh.shape)),
        mesh=mesh,
        in_specs=in_specs,
        out_specs=out_specs,
        check_vma=False,
    )
```

```python
import functools

import jax
import jax.numpy as jnp
from jax import lax
from jax.experimental import pallas as pl
from jax.experimental.pallas import tpu as pltpu
from jax.sharding import PartitionSpec as P

HEAD_DIM = 64
EPSILON = 1e-05
CROSS = -1e30
BF = jnp.bfloat16
F32 = jnp.float32
NN = (((1,), (0,)), ((), ()))
NT = (((1,), (1,)), ((), ()))
TN = (((0,), (0,)), ((), ()))
VMEM_LIMIT = 56 * 1024 * 1024


def dot(left, right, dims):
    return lax.dot_general(left, right, dims, preferred_element_type=F32)


def statistics(rows):
    values = rows.astype(F32)
    centred = values - jnp.mean(values, -1, keepdims=True)
    inv_scale = lax.rsqrt(jnp.mean(centred * centred, -1, keepdims=True) + EPSILON)
    return centred * inv_scale, inv_scale


class Heads:
    def __init__(self, width):
        self.lanes = min(width, 256)
        self.count = self.lanes // HEAD_DIM
        owner = lax.broadcasted_iota(jnp.int32, (1, self.lanes), 1) // HEAD_DIM
        self.masks = [(owner == head).astype(F32) for head in range(self.count)]

    def stack(self, block):
        return jnp.concatenate([block * mask.astype(BF) for mask in self.masks], axis=0)

    def unstack(self, tall):
        rows = tall.shape[0] // self.count
        total = tall[0:rows] * self.masks[0]
        for head in range(1, self.count):
            total = total + tall[head * rows : (head + 1) * rows] * self.masks[head]
        return total


class Weights:
    def __init__(self, arrays, table, offsets):
        self.arrays, self.table, self.offsets = list(arrays), table, offsets

    def only(self, kinds):
        used = sorted({entry[0] for kind in kinds for entry in self.table[kind]})
        table = {
            kind: [(used.index(array), at, place) for array, at, place in self.table[kind]]
            for kind in kinds
        }
        return Weights([self.arrays[number] for number in used], table, self.offsets)


def views(table, refs, offsets, kind):
    found = []
    for array, at, place in table[kind]:
        part = refs[array].at[at]
        found.append((part, pl.ds(pl.multiple_of(offsets[place], 128), part.shape[0])))
    return found


def rows_times(rows_ref, parts, out_ref, column):
    width = parts[0][0].shape[1]
    step = min(width, 256)
    for at in range(0, width, step):
        total = None
        for part, columns in parts:
            term = dot(rows_ref[:, columns], part[:, at : at + step], NN)
            total = term if total is None else total + term
        out_ref[:, column + at : column + at + step] = total.astype(out_ref.dtype)


def emit_columns(rows_ref, outs, place, date_count, loc_count):
    block = rows_ref.shape[1] // (date_count * loc_count)
    for number, out in enumerate(outs):
        date = place if number == 0 else 1 - place
        for loc in range(loc_count):
            at = pl.multiple_of((loc * date_count + date) * block, block)
            out[:, loc * block : (loc + 1) * block] = rows_ref[:, pl.ds(at, block)]


def attention(triple_ref, bias_ref, attend_ref, mixed_ref, blocks):
    width = triple_ref.shape[1] // 3
    heads = Heads(width)
    rows = triple_ref.shape[0] // blocks
    groups = width // heads.lanes
    bias = jnp.concatenate([bias_ref[...]] * heads.count, axis=0)
    for block in range(blocks):
        at = slice(block * rows, (block + 1) * rows)
        for group in range(groups):
            lane = group * heads.lanes
            queries = heads.stack(triple_ref[at, lane : lane + heads.lanes])
            keys = triple_ref[at, width + lane : width + lane + heads.lanes]
            values = triple_ref[at, 2 * width + lane : 2 * width + lane + heads.lanes]
            scores = dot(queries, keys, NT) * HEAD_DIM ** (-0.5) + bias
            raised = jnp.exp(scores - jnp.max(scores, -1, keepdims=True))
            attend = raised * (1.0 / jnp.sum(raised, -1, keepdims=True))
            attend_ref[block * groups + group] = attend
            mixed = heads.unstack(dot(attend.astype(BF), values, NN))
            mixed_ref[at, lane : lane + heads.lanes] = mixed.astype(BF)


def attention_back(triple_ref, attend_ref, back_mixed_ref, back_triple_ref, blocks):
    width = triple_ref.shape[1] // 3
    heads = Heads(width)
    rows = triple_ref.shape[0] // blocks
    groups = width // heads.lanes
    for block in range(blocks):
        at = slice(block * rows, (block + 1) * rows)
        for group in range(groups):
            lane = group * heads.lanes
            queries = heads.stack(triple_ref[at, lane : lane + heads.lanes])
            keys = triple_ref[at, width + lane : width + lane + heads.lanes]
            values = triple_ref[at, 2 * width + lane : 2 * width + lane + heads.lanes]
            back = heads.stack(back_mixed_ref[at, lane : lane + heads.lanes])
            attend = attend_ref[block * groups + group]
            back_attend = dot(back, values, NT)
            back_values = dot(attend.astype(BF), back, TN)
            inner = back_attend - jnp.sum(back_attend * attend, -1, keepdims=True)
            back_scores = (attend * inner * HEAD_DIM ** (-0.5)).astype(BF)
            back_queries = heads.unstack(dot(back_scores, keys, NN))
            back_keys = dot(back_scores, queries, TN)
            for number, term in enumerate((back_queries, back_keys, back_values)):
                first = number * width + lane
                back_triple_ref[at, first : first + heads.lanes] = term.astype(BF)


def normalize_into(rows_ref, gain_ref, hidden_ref, blocks):
    rows = rows_ref.shape[0] // blocks
    for block in range(blocks):
        at = slice(block * rows, (block + 1) * rows)
        normed, _ = statistics(rows_ref[at, :])
        hidden_ref[at, :] = (normed * gain_ref[...]).astype(BF)


def spatial_forward_kernel(plan, place, offsets, gain, bias, *refs):
    sources, refs = refs[: plan.origins], refs[plan.origins :]
    arrays, refs = refs[: plan.arrays], refs[plan.arrays :]
    partials, refs = refs[: plan.origins], refs[plan.origins :]
    columns, refs = refs[: plan.columns], refs[plan.columns :]
    triple, attend, mixed, start, hidden, whole = refs
    for source, at, to, size in plan.moves:
        start[to : to + size, :] = sources[source][at : at + size, :]
    normalize_into(start, gain, hidden, plan.blocks)
    plan.emit(hidden, columns, place[0])
    for kind in range(3):
        rows_times(hidden, views(plan.table, arrays, offsets, kind), triple, kind * mixed.shape[1])
    attention(triple, bias, attend, mixed, plan.blocks)
    for part, features in views(plan.table, arrays, offsets, 3):
        whole[:, features] = dot(mixed[...], part[...], NT).astype(BF)
    for source, at, to, size in plan.moves:
        partials[source][at : at + size, :] = whole[to : to + size, :]


def temporal_kernel(plan, place, offsets, gain, bias, date_rows, cotangent, *refs):
    sources, refs = refs[: plan.sources], refs[plan.sources :]
    arrays, refs = refs[: plan.arrays], refs[plan.arrays :]
    hidden_columns, refs = refs[: plan.columns], refs[plan.columns :]
    upstream_columns, refs = refs[: plan.columns], refs[plan.columns :]
    joined, mixed, partial, back_triple, back_part, hidden, triple, attend, back_mixed = refs
    rows = date_rows.shape[0]
    for source, at, to, size in plan.moves:
        if source == 0 and plan.sources > 1:
            total = sources[1][at : at + size, :].astype(F32) + sources[2][at : at + size, :].astype(F32)
            out = (sources[0][at : at + size, :].astype(F32) + total).astype(BF)
        else:
            out = sources[-1][at : at + size, :]
        dated = out.astype(F32) + date_rows[to % rows : to % rows + size, :].astype(F32)
        joined[to : to + size, :] = dated.astype(BF)
    normalize_into(joined, gain, hidden, plan.blocks)
    plan.emit(hidden, hidden_columns, place[0])
    plan.emit(cotangent, upstream_columns, place[0])
    width = mixed.shape[1]
    for kind in range(3):
        rows_times(hidden, views(plan.table, arrays, offsets, kind), triple, kind * width)
    outlet = views(plan.table, arrays, offsets, 3)
    rows_times(cotangent, outlet, back_mixed, 0)
    attention(triple, bias, attend, mixed, plan.blocks)
    for part, features in outlet:
        partial[:, features] = dot(mixed[...], part[...], NT).astype(BF)
    attention_back(triple, attend, back_mixed, back_triple, plan.blocks)
    intakes = [views(plan.table, arrays, offsets, kind) for kind in range(3)]
    for entries in zip(*intakes):
        total = None
        for kind, (part, features) in enumerate(entries):
            term = dot(back_triple[:, kind * width : (kind + 1) * width], part[...], NT)
            total = term if total is None else total + term
        back_part[:, features] = total.astype(BF)


def norm_back_kernel(moves, step, gain, here, there, joined, cotangent, *outs):
    for at in range(0, joined.shape[0], step):
        span_here = slice(at, at + step)
        normed, inv_scale = statistics(joined[span_here, :])
        total = here[span_here, :].astype(F32) + there[span_here, :].astype(F32)
        scaled = total * gain[...]
        inner = (
            scaled
            - jnp.mean(scaled, -1, keepdims=True)
            - normed * jnp.mean(scaled * normed, -1, keepdims=True)
        )
        back = (cotangent[span_here, :].astype(F32) + inv_scale * inner).astype(BF)
        for target, to, first, size in moves:
            if at <= first < at + step:
                outs[target][to : to + size, :] = back[first - at : first - at + size]


def spatial_backward_kernel(plan, place, offsets, triple, attend, *refs):
    sources, refs = refs[: plan.origins], refs[plan.origins :]
    arrays, refs = refs[: plan.arrays], refs[plan.arrays :]
    columns, refs = refs[: plan.columns], refs[plan.columns :]
    back_triple, upstream, back_mixed = refs
    for source, at, to, size in plan.moves:
        upstream[to : to + size, :] = sources[source][at : at + size, :]
    plan.emit(upstream, columns, place[0])
    rows_times(upstream, views(plan.table, arrays, offsets, 3), back_mixed, 0)
    attention_back(triple, attend, back_mixed, back_triple, plan.blocks)


def grad_kernel(loc_count, loc, left_own, left_other, right_own, right_other, first, rest):
    block = first.shape[0]
    for step in range(loc_count):
        at = lax.rem(loc[0] + (2 * loc_count - 1 - step), loc_count) * block
        columns = pl.ds(pl.multiple_of(at, block), block)
        total = dot(left_own[:, columns], right_own[...], TN)
        total = total + dot(left_other[:, columns], right_other[...], TN)
        if step == 0:
            first[...] = total.astype(BF)
        else:
            rest[step - 1] = total


def finish_kernel(*refs):
    out = refs[-1]
    column = 0
    for arrived, rest in zip(refs[0:-1:2], refs[1:-1:2]):
        for at in range(0, rest.shape[1], 256):
            total = arrived[:, at : at + 256].astype(F32) + rest[:, at : at + 256]
            kind, lane = (column + at) // out.shape[2], (column + at) % out.shape[2]
            out[:, kind, lane : lane + 256] = total
        column += rest.shape[1]


class Plan:
    def __init__(self, blocks, moves, origins, weights, emit, columns, sources=0):
        self.blocks, self.moves, self.origins = blocks, moves, origins
        self.arrays, self.table = len(weights.arrays), weights.table
        self.emit, self.columns, self.sources = emit, columns, sources


def call(body, outs, args, scratch=(), flops=0):
    smem = pl.BlockSpec(memory_space=pltpu.SMEM)
    vmem = pl.BlockSpec(memory_space=pltpu.VMEM)
    specs = [smem if arg.dtype == jnp.int32 else vmem for arg in args]
    moved = sum(arg.size * arg.dtype.itemsize for arg in args)
    moved = moved + sum(out.size * out.dtype.itemsize for out in outs)
    return pl.pallas_call(
        body,
        out_shape=list(outs),
        in_specs=specs,
        out_specs=[vmem] * len(outs),
        scratch_shapes=list(scratch),
        compiler_params=pltpu.CompilerParams(vmem_limit_bytes=VMEM_LIMIT),
        cost_estimate=pl.CostEstimate(flops=flops, bytes_accessed=moved, transcendentals=0),
    )(*args)


def swap(array, axis):
    return lax.ppermute(array, axis, [(0, 1), (1, 0)])


def gather_weights(weights, sizes):
    rows = weights.shape[0]
    own = weights.transpose(1, 0, 2)
    if sizes["date"] != 2 or sizes["groups"] != 2 or sizes["loc"] % 2 or rows % 512:
        whole = lax.all_gather(own, "date", axis=1, tiled=True)
        table = {kind: [(0, kind, 0)] for kind in range(4)}
        return Weights([whole], table, jnp.zeros((1,), jnp.int32))
    side, here = lax.axis_index("groups"), lax.axis_index("date")
    even = lax.axis_index("loc") % 2
    quarter = rows // 4
    pairs = [(at, at ^ 1) for at in range(sizes["loc"])]

    def place(group, loc):
        return (1 - here) * rows + (group * 2 + loc) * quarter

    offsets = [here * rows, place(side, even), place(1 - side, even), place(side, 1 - even)]
    offsets = jnp.stack(offsets + [place(1 - side, 1 - even)]).astype(jnp.int32)
    sent = lax.dynamic_slice_in_dim(weights, (side * 2 + even) * quarter, quarter, 0)
    sent = sent.transpose(1, 0, 2)
    arrays, table = [own], {}
    for kinds in ((0, 1), (2, 3)):
        across = swap(sent[kinds[0] : kinds[1] + 1], "date")
        group = swap(across, "groups")
        loc = lax.ppermute(across, "loc", pairs)
        far = (swap(loc[0:1], "groups"), lax.ppermute(group[1:2], "loc", pairs))
        first = len(arrays)
        arrays += [across, group, loc, *far]
        for number, kind in enumerate(kinds):
            table[kind] = [
                (0, kind, 0),
                (first, number, 1),
                (first + 1, number, 2),
                (first + 2, number, 3),
                (first + 3 + number, 0, 4),
            ]
    return Weights(arrays, table, offsets)


def add_over_heads(partial, sizes):
    if sizes["mp"] == 2:
        return partial.astype(F32) + swap(partial, "mp").astype(F32)
    return lax.psum(partial.astype(F32), "mp")


def whole_grads(hidden, back_triple, upstream, mixed):
    width = mixed.shape[1]
    intake = dot(hidden, back_triple, TN)
    outlet = dot(upstream, mixed, TN)
    whole = jnp.concatenate([intake, outlet], axis=1).reshape(-1, 4, width)
    part = lax.psum_scatter(whole.astype(BF), ("loc", "date"), scatter_dimension=0, tiled=True)
    return part.astype(F32)


def ring_terms(left, right, other_left, other_right, sizes):
    count = sizes["loc"]
    loc = lax.axis_index("loc").astype(jnp.int32)[None]
    block, width = left.shape[1] // count, right.shape[1]
    return call(
        functools.partial(grad_kernel, count),
        (
            jax.ShapeDtypeStruct((block, width), BF),
            jax.ShapeDtypeStruct((count - 1, block, width), F32),
        ),
        (loc, left, other_left, right, other_right),
        flops=4 * left.shape[0] * left.shape[1] * width,
    )


def ring_sum(terms, sizes):
    count = sizes["loc"]
    ring = [(at, (at + 1) % count) for at in range(count)]
    total, rest = terms
    for step in range(count - 1):
        arrived = lax.ppermute(total, "loc", ring)
        if step < count - 2:
            total = (arrived.astype(F32) + rest[step]).astype(BF)
    return arrived, rest[count - 2]


def weight_grads(hidden, back_triple, upstream, mixed, sizes):
    width = mixed.shape[1]
    block = hidden[0].shape[1] // sizes["loc"]
    half = back_triple.shape[1] // 2
    other_hidden, other_upstream = swap(hidden[1], "date"), swap(upstream[1], "date")
    outlet = ring_terms(upstream[0], mixed, other_upstream, swap(mixed, "date"), sizes)
    outlet = ring_sum(outlet, sizes)
    intakes = []
    for at in (0, half):
        right = back_triple[:, at : at + half]
        terms = ring_terms(hidden[0], right, other_hidden, swap(right, "date"), sizes)
        intakes += ring_sum(terms, sizes)
    return call(
        finish_kernel,
        (jax.ShapeDtypeStruct((block, 4, width), F32),),
        (*intakes, *outlet),
    )[0]


def per_device(
    sizes,
    optical,
    radar,
    cloud,
    radar_drop,
    keep_index,
    place_table,
    date_table,
    spatial_gain,
    spatial_weights,
    temporal_gain,
    temporal_weights,
    cotangent,
):
    spatial = gather_weights(spatial_weights, sizes)
    temporal = gather_weights(temporal_weights, sizes)
    _, patches, dates_here, model = optical.shape
    patches_here, dates = cotangent.shape[1:3]
    width = spatial_weights.shape[2]
    rows = patches * dates_here
    here = lax.axis_index("date")
    first = here * dates_here
    paired = sizes["date"] == 2 and dates_here % 2 == 0 and patches_here % 8 == 0

    if paired:
        pairs, eights = dates_here // 2, patches_here // 8
        spatial_blocks, temporal_blocks = pairs, eights
        half_rows = eights * 16

        def own_first(array, axis):
            return jnp.where(here == 0, array, jnp.flip(array, axis))

        def spatial_rows(array):
            array = array.reshape(pairs, 2, 2, eights, 8, -1)
            return own_first(array, 2).transpose(0, 2, 3, 1, 4, 5).reshape(rows, -1)

        def temporal_rows(array):
            array = array.reshape(2, pairs, 2, eights, 8, -1)
            return own_first(array, 0).transpose(3, 0, 1, 2, 4, 5).reshape(rows, -1)

        def temporal_whole(array):
            array = array.reshape(eights, 2, pairs, 2, 8, -1).transpose(1, 2, 3, 0, 4, 5)
            return own_first(array, 0).reshape(dates, patches_here, -1)

    else:
        spatial_blocks = 1 if rows <= 192 else dates_here
        temporal_blocks = patches_here // 8 if patches_here % 8 == 0 else 1

        def spatial_rows(array):
            return array.reshape(rows, -1)

        def temporal_rows(array):
            array = array.reshape(dates, temporal_blocks, patches_here // temporal_blocks, -1)
            return array.transpose(1, 0, 2, 3).reshape(rows, -1)

        def temporal_whole(array):
            array = array.reshape(temporal_blocks, dates, patches_here // temporal_blocks, -1)
            return array.transpose(1, 0, 2, 3).reshape(dates, patches_here, -1)

    cloud_here = lax.dynamic_slice_in_dim(cloud, first, dates_here, 1)[0]
    drop_here = lax.dynamic_slice_in_dim(radar_drop, first, dates_here, 1)[0]
    optical_keep = (1 - cloud_here).astype(F32)[:, None, None]
    radar_keep = (1 - drop_here).astype(F32)[:, None, None]
    places = jnp.take(place_table, keep_index[0], axis=0).astype(F32)[None]
    start = (
        optical[0].transpose(1, 0, 2).astype(F32) * optical_keep
        + radar[0].transpose(1, 0, 2).astype(F32) * radar_keep
        + places
    ).astype(BF)
    start = spatial_rows(start)

    dates_at = jnp.arange(dates, dtype=jnp.int32)
    patches_at = jnp.arange(patches_here, dtype=jnp.int32)
    ones_here = jnp.ones((dates, patches_here, 1), jnp.int32)
    temporal_size = rows // temporal_blocks
    date_at = temporal_rows(ones_here * dates_at[:, None, None])[:temporal_size, 0]
    patch_at = temporal_rows(ones_here * patches_at[None, :, None])[:temporal_size, 0]
    spatial_size = rows // spatial_blocks
    spatial_date = jnp.ones((dates_here, patches, 1), jnp.int32) * dates_at[:dates_here, None, None]
    spatial_date = spatial_rows(spatial_date)[:spatial_size, 0]
    spatial_bias = jnp.where(spatial_date[:, None] == spatial_date[None, :], 0.0, CROSS).astype(F32)
    survive = 1 - cloud[0] * radar_drop[0]
    same_date = date_at[:, None] == date_at[None, :]
    survive_at = temporal_rows(ones_here * survive[:, None, None])[:temporal_size, 0]
    allowed = (survive_at[None, :] == 1) | same_date
    temporal_bias = jnp.where(
        patch_at[:, None] == patch_at[None, :], jnp.where(allowed, 0.0, -1000000000.0), CROSS
    ).astype(F32)
    date_rows = jnp.broadcast_to(date_table[:, None], (dates, patches_here, model))
    date_rows = temporal_rows(date_rows)[:temporal_size]
    cotangent_rows = temporal_rows(cotangent[0].transpose(1, 0, 2))

    spatial_gain = spatial_gain[None]
    temporal_gain = temporal_gain[None]
    lanes = min(width, 256)

    def shape(*dims, dtype=BF):
        return jax.ShapeDtypeStruct(dims, dtype)

    def attend_dims(blocks):
        return (blocks * (width // lanes), lanes // HEAD_DIM * (rows // blocks), rows // blocks)

    layer_flops = 2 * rows * model * width * 4
    place = here.astype(jnp.int32)[None]
    if paired:
        half = rows // 2

        def emit(rows_ref, outs, at):
            emit_columns(rows_ref, outs, at, 2, sizes["loc"])

        column_shapes = (shape(rows, model // 2), shape(rows, model // 2))
        blocked = start.reshape(pairs, 2, half_rows, model)
        origins = (blocked[:, 0].reshape(half, model), blocked[:, 1].reshape(half, model))
        spatial_moves = [
            (side, pair * half_rows, (pair * 2 + side) * half_rows, half_rows)
            for side in range(2)
            for pair in range(pairs)
        ]
        temporal_moves = [
            (side, pair * half_rows + eight * 16, (eight * 2 + side) * pairs * 16 + pair * 16, 16)
            for side in range(2)
            for pair in range(pairs)
            for eight in range(eights)
        ]
        half_shapes = (shape(half, model), shape(half, model))
    else:

        def emit(rows_ref, outs, at):
            outs[0][...] = rows_ref[...]

        column_shapes = (shape(rows, model),)
        origins = (start,)
        spatial_moves = [(0, at * spatial_size, at * spatial_size, spatial_size) for at in range(spatial_blocks)]
        temporal_moves = [(0, at * temporal_size, at * temporal_size, temporal_size) for at in range(temporal_blocks)]
        half_shapes = (shape(rows, model),)
    columns = len(column_shapes)
    origins, spatial_bias, temporal_bias, date_rows, cotangent_rows = lax.optimization_barrier(
        (origins, spatial_bias, temporal_bias, date_rows, cotangent_rows)
    )

    plan = Plan(spatial_blocks, spatial_moves, len(origins), spatial, emit, columns)
    outs = call(
        functools.partial(spatial_forward_kernel, plan),
        (
            *half_shapes,
            *column_shapes,
            shape(rows, 3 * width),
            shape(*attend_dims(spatial_blocks), dtype=F32),
            shape(rows, width),
        ),
        (place, spatial.offsets, spatial_gain, spatial_bias, *origins, *spatial.arrays),
        scratch=(
            pltpu.VMEM((rows, model), BF),
            pltpu.VMEM((rows, model), BF),
            pltpu.VMEM((rows, model), BF),
        ),
        flops=layer_flops,
    )
    partials, outs = outs[: len(origins)], outs[len(origins) :]
    hidden, (triple, attend, mixed) = outs[:columns], outs[columns:]
    if paired:
        there = (origins[1].astype(F32) + add_over_heads(partials[1], sizes)).astype(BF)
        sources = (origins[0], partials[0], swap(partials[0], "mp"), swap(there, "date"))
    else:
        spatial_out = (start.astype(F32) + add_over_heads(partials[0], sizes)).astype(BF)
        moved = lax.all_to_all(
            spatial_out.reshape(dates_here, patches, model),
            "date",
            split_axis=1,
            concat_axis=0,
            tiled=True,
        )
        sources = (temporal_rows(moved),)
    plan = Plan(
        temporal_blocks, temporal_moves, len(origins), temporal, emit, columns, len(sources)
    )
    outs = call(
        functools.partial(temporal_kernel, plan),
        (
            *column_shapes,
            *column_shapes,
            shape(rows, model),
            shape(rows, width),
            shape(rows, model),
            shape(rows, 3 * width),
            shape(rows, model),
        ),
        (
            place,
            temporal.offsets,
            temporal_gain,
            temporal_bias,
            date_rows,
            cotangent_rows,
            *sources,
            *temporal.arrays,
        ),
        scratch=(
            pltpu.VMEM((rows, model), BF),
            pltpu.VMEM((rows, 3 * width), BF),
            pltpu.VMEM(attend_dims(temporal_blocks), F32),
            pltpu.VMEM((rows, width), BF),
        ),
        flops=2 * layer_flops,
    )
    temporal_hidden, temporal_upstream = outs[:columns], outs[columns : 2 * columns]
    joined, temporal_mixed, temporal_partial, temporal_triple, back_part = outs[2 * columns :]

    if sizes["mp"] == 2:
        others = swap(back_part, "mp")
    else:
        others = (lax.psum(back_part.astype(F32), "mp") - back_part.astype(F32)).astype(BF)
    backs = call(
        functools.partial(norm_back_kernel, temporal_moves, temporal_size),
        half_shapes,
        (temporal_gain, back_part, others, joined, cotangent_rows),
    )
    if paired:
        back_origins = (backs[0], swap(backs[1], "date"))
    else:
        back = lax.all_to_all(
            temporal_whole(backs[0]), "date", split_axis=0, concat_axis=1, tiled=True
        )
        back_origins = (back.reshape(rows, model),)
    outlet = spatial.only((3,))
    plan = Plan(spatial_blocks, spatial_moves, len(origins), outlet, emit, columns)
    outs = call(
        functools.partial(spatial_backward_kernel, plan),
        (*column_shapes, shape(rows, 3 * width)),
        (place, outlet.offsets, triple, attend, *back_origins, *outlet.arrays),
        scratch=(pltpu.VMEM((rows, model), BF), pltpu.VMEM((rows, width), BF)),
        flops=layer_flops,
    )
    upstream, back_triple = outs[:columns], outs[columns]
    encoded = (joined.astype(F32) + add_over_heads(temporal_partial, sizes)).astype(BF)
    encoded = temporal_whole(encoded).transpose(1, 0, 2)[None]
    if paired:
        temporal_grads = weight_grads(
            temporal_hidden, temporal_triple, temporal_upstream, temporal_mixed, sizes
        )
        spatial_grads = weight_grads(hidden, back_triple, upstream, mixed, sizes)
    else:
        temporal_grads = whole_grads(
            temporal_hidden[0], temporal_triple, temporal_upstream[0], temporal_mixed
        )
        spatial_grads = whole_grads(hidden[0], back_triple, upstream[0], mixed)
    return (encoded, spatial_grads, temporal_grads)


def solution(mesh):
    in_specs = (
        P(("groups", "loc"), None, "date", None),
        P(("groups", "loc"), None, "date", None),
        P(("groups", "loc"), None),
        P(("groups", "loc"), None),
        P(("groups", "loc"), None),
        P(),
        P(),
        P(),
        P("date", None, "mp"),
        P(),
        P("date", None, "mp"),
        P(("groups", "loc"), "date", None, None),
    )
    out_specs = (
        P(("groups", "loc"), "date", None, None),
        P(("groups", "loc", "date"), None, "mp"),
        P(("groups", "loc", "date"), None, "mp"),
    )
    return jax.shard_map(
        functools.partial(per_device, dict(mesh.shape)),
        mesh=mesh,
        in_specs=in_specs,
        out_specs=out_specs,
        check_vma=False,
    )
```

```python
import functools

import jax
import jax.numpy as jnp
from jax import lax
from jax.experimental import pallas as pl
from jax.experimental.pallas import tpu as pltpu
from jax.sharding import PartitionSpec as P

HEAD_DIM = 64
EPSILON = 1e-05
CROSS = -1e30
BF = jnp.bfloat16
F32 = jnp.float32
NN = (((1,), (0,)), ((), ()))
NT = (((1,), (1,)), ((), ()))
TN = (((0,), (0,)), ((), ()))
VMEM_LIMIT = 56 * 1024 * 1024


def dot(left, right, dims):
    return lax.dot_general(left, right, dims, preferred_element_type=F32)


def statistics(rows):
    values = rows.astype(F32)
    centred = values - jnp.mean(values, -1, keepdims=True)
    inv_scale = lax.rsqrt(jnp.mean(centred * centred, -1, keepdims=True) + EPSILON)
    return centred * inv_scale, inv_scale


class Heads:
    def __init__(self, width):
        self.lanes = min(width, 256)
        self.count = self.lanes // HEAD_DIM
        owner = lax.broadcasted_iota(jnp.int32, (1, self.lanes), 1) // HEAD_DIM
        self.masks = [(owner == head).astype(F32) for head in range(self.count)]

    def stack(self, block):
        return jnp.concatenate([block * mask.astype(BF) for mask in self.masks], axis=0)

    def unstack(self, tall):
        rows = tall.shape[0] // self.count
        total = tall[0:rows] * self.masks[0]
        for head in range(1, self.count):
            total = total + tall[head * rows : (head + 1) * rows] * self.masks[head]
        return total


class Weights:
    def __init__(self, arrays, table, offsets):
        self.arrays, self.table, self.offsets = list(arrays), table, offsets

    def only(self, kinds):
        used = sorted({entry[0] for kind in kinds for entry in self.table[kind]})
        table = {
            kind: [(used.index(array), at, place) for array, at, place in self.table[kind]]
            for kind in kinds
        }
        return Weights([self.arrays[number] for number in used], table, self.offsets)


def views(table, refs, offsets, kind):
    found = []
    for array, at, place in table[kind]:
        part = refs[array].at[at]
        found.append((part, pl.ds(pl.multiple_of(offsets[place], 128), part.shape[0])))
    return found


def rows_times(rows_ref, parts, out_ref, column):
    width = parts[0][0].shape[1]
    step = min(width, 256)
    for at in range(0, width, step):
        total = None
        for part, columns in parts:
            term = dot(rows_ref[:, columns], part[:, at : at + step], NN)
            total = term if total is None else total + term
        out_ref[:, column + at : column + at + step] = total.astype(out_ref.dtype)


def emit_own(rows_ref, out, at, date, loc_count):
    block = rows_ref.shape[1] // (2 * loc_count)
    for loc in range(loc_count):
        first = pl.multiple_of((loc * 2 + date) * block, block)
        out[:, at + loc * block : at + (loc + 1) * block] = rows_ref[:, pl.ds(first, block)]


def emit_half(rows_ref, out, at, date, core, loc_count):
    block = rows_ref.shape[1] // (2 * loc_count)
    for number in range(loc_count // 2):
        loc = core * (loc_count // 2) + number
        first = pl.multiple_of((loc * 2 + date) * block, block)
        out[:, at + number * block : at + (number + 1) * block] = rows_ref[:, pl.ds(first, block)]


def attention(triple_ref, bias_ref, attend_ref, mixed_ref, blocks):
    width = triple_ref.shape[1] // 3
    heads = Heads(width)
    rows = triple_ref.shape[0] // blocks
    groups = width // heads.lanes
    bias = jnp.concatenate([bias_ref[...]] * heads.count, axis=0)
    for block in range(blocks):
        at = slice(block * rows, (block + 1) * rows)
        for group in range(groups):
            lane = group * heads.lanes
            queries = heads.stack(triple_ref[at, lane : lane + heads.lanes])
            keys = triple_ref[at, width + lane : width + lane + heads.lanes]
            values = triple_ref[at, 2 * width + lane : 2 * width + lane + heads.lanes]
            scores = dot(queries, keys, NT) * HEAD_DIM ** (-0.5) + bias
            raised = jnp.exp(scores - jnp.max(scores, -1, keepdims=True))
            attend = raised * (1.0 / jnp.sum(raised, -1, keepdims=True))
            attend_ref[block * groups + group] = attend
            mixed = heads.unstack(dot(attend.astype(BF), values, NN))
            mixed_ref[at, lane : lane + heads.lanes] = mixed.astype(BF)


def attention_back(triple_ref, attend_ref, back_mixed_ref, back_triple_ref, blocks):
    width = triple_ref.shape[1] // 3
    heads = Heads(width)
    rows = triple_ref.shape[0] // blocks
    groups = width // heads.lanes
    for block in range(blocks):
        at = slice(block * rows, (block + 1) * rows)
        for group in range(groups):
            lane = group * heads.lanes
            queries = heads.stack(triple_ref[at, lane : lane + heads.lanes])
            keys = triple_ref[at, width + lane : width + lane + heads.lanes]
            values = triple_ref[at, 2 * width + lane : 2 * width + lane + heads.lanes]
            back = heads.stack(back_mixed_ref[at, lane : lane + heads.lanes])
            attend = attend_ref[block * groups + group]
            back_attend = dot(back, values, NT)
            back_values = dot(attend.astype(BF), back, TN)
            inner = back_attend - jnp.sum(back_attend * attend, -1, keepdims=True)
            back_scores = (attend * inner * HEAD_DIM ** (-0.5)).astype(BF)
            back_queries = heads.unstack(dot(back_scores, keys, NN))
            back_keys = dot(back_scores, queries, TN)
            for number, term in enumerate((back_queries, back_keys, back_values)):
                first = number * width + lane
                back_triple_ref[at, first : first + heads.lanes] = term.astype(BF)


def normalize_into(rows_ref, gain_ref, hidden_ref, blocks):
    rows = rows_ref.shape[0] // blocks
    for block in range(blocks):
        at = slice(block * rows, (block + 1) * rows)
        normed, _ = statistics(rows_ref[at, :])
        hidden_ref[at, :] = (normed * gain_ref[...]).astype(BF)


def spatial_forward_kernel(plan, where, offsets, gain, bias, cotangent, *refs):
    sources, refs = refs[: plan.origins], refs[plan.origins :]
    arrays, refs = refs[: plan.arrays], refs[plan.arrays :]
    partials, refs = refs[: plan.origins], refs[plan.origins :]
    grads, refs = refs[: plan.grads], refs[plan.grads :]
    triple, attend, mixed, start, hidden, whole = refs
    for source, at, to, size in plan.moves:
        start[to : to + size, :] = sources[source][at : at + size, :]
    normalize_into(start, gain, hidden, plan.blocks)
    width = mixed.shape[1]
    for kind in range(3):
        rows_times(hidden, views(plan.table, arrays, offsets, kind), triple, kind * width)
    attention(triple, bias, attend, mixed, plan.blocks)
    for part, features in views(plan.table, arrays, offsets, 3):
        whole[:, features] = dot(mixed[...], part[...], NT).astype(BF)
    for source, at, to, size in plan.moves:
        partials[source][at : at + size, :] = whole[to : to + size, :]
    if plan.paired:
        own_hidden, own_cotangent, sent = grads
        half = hidden.shape[1] // 4
        here, core = where[0], where[1]
        emit_own(hidden, own_hidden, 0, here, plan.locs)
        emit_own(cotangent, own_cotangent, 0, here, plan.locs)
        emit_half(hidden, sent, 0, 1 - here, core, plan.locs)
        emit_half(cotangent, sent, half, 1 - here, core, plan.locs)
        sent[:, 2 * half :] = mixed[...]
    else:
        grads[0][...] = hidden[...]


def between_kernel(start, here, there, kept, out, passed):
    total = here[...].astype(F32) + there[...].astype(F32)
    out[...] = (start[...].astype(F32) + total).astype(BF)


def temporal_kernel(plan, where, offsets, gain, bias, date_rows, cotangent, *refs):
    sources, refs = refs[: plan.sources], refs[plan.sources :]
    arrays, refs = refs[: plan.arrays], refs[plan.arrays :]
    grads, refs = refs[: plan.grads], refs[plan.grads :]
    joined, mixed, partial, back_triple, back_part, hidden, triple, attend, back_mixed = refs
    rows = date_rows.shape[0]
    for source, at, to, size in plan.moves:
        if source == 0 and plan.sources > 1:
            total = sources[1][at : at + size, :].astype(F32) + sources[2][at : at + size, :].astype(F32)
            out = (sources[0][at : at + size, :].astype(F32) + total).astype(BF)
        else:
            out = sources[-1][at : at + size, :]
        dated = out.astype(F32) + date_rows[to % rows : to % rows + size, :].astype(F32)
        joined[to : to + size, :] = dated.astype(BF)
    normalize_into(joined, gain, hidden, plan.blocks)
    width = mixed.shape[1]
    for kind in range(3):
        rows_times(hidden, views(plan.table, arrays, offsets, kind), triple, kind * width)
    outlet = views(plan.table, arrays, offsets, 3)
    rows_times(cotangent, outlet, back_mixed, 0)
    attention(triple, bias, attend, mixed, plan.blocks)
    for part, features in outlet:
        partial[:, features] = dot(mixed[...], part[...], NT).astype(BF)
    if plan.paired:
        own_hidden, sent = grads
        half = hidden.shape[1] // 4
        emit_own(hidden, own_hidden, 0, where[0], plan.locs)
        emit_half(hidden, sent, 0, 1 - where[0], where[1], plan.locs)
        sent[:, half:] = mixed[...]
    else:
        grads[0][...] = hidden[...]
    attention_back(triple, attend, back_mixed, back_triple, plan.blocks)
    intakes = [views(plan.table, arrays, offsets, kind) for kind in range(3)]
    for entries in zip(*intakes):
        total = None
        for kind, (part, features) in enumerate(entries):
            term = dot(back_triple[:, kind * width : (kind + 1) * width], part[...], NT)
            total = term if total is None else total + term
        back_part[:, features] = total.astype(BF)


def norm_back_kernel(moves, step, gain, here, there, joined, cotangent, kept, *outs):
    for at in range(0, joined.shape[0], step):
        span_here = slice(at, at + step)
        normed, inv_scale = statistics(joined[span_here, :])
        total = here[span_here, :].astype(F32) + there[span_here, :].astype(F32)
        scaled = total * gain[...]
        inner = (
            scaled
            - jnp.mean(scaled, -1, keepdims=True)
            - normed * jnp.mean(scaled * normed, -1, keepdims=True)
        )
        back = (cotangent[span_here, :].astype(F32) + inv_scale * inner).astype(BF)
        for target, to, first, size in moves:
            if at <= first < at + step:
                outs[target][to : to + size, :] = back[first - at : first - at + size]


def spatial_backward_kernel(plan, where, offsets, triple, attend, *refs):
    sources, refs = refs[: plan.origins], refs[plan.origins :]
    arrays, refs = refs[: plan.arrays], refs[plan.arrays :]
    grads, refs = refs[: plan.grads], refs[plan.grads :]
    back_triples, (upstream, back_mixed, back_triple) = refs[:-3], refs[-3:]
    for source, at, to, size in plan.moves:
        upstream[to : to + size, :] = sources[source][at : at + size, :]
    if plan.paired:
        emit_own(upstream, grads[0], 0, where[0], plan.locs)
        emit_half(upstream, grads[1], 0, 1 - where[0], where[1], plan.locs)
    else:
        grads[0][...] = upstream[...]
    rows_times(upstream, views(plan.table, arrays, offsets, 3), back_mixed, 0)
    attention_back(triple, attend, back_mixed, back_triple, plan.blocks)
    at = 0
    for out in back_triples:
        out[...] = back_triple[:, at : at + out.shape[1]]
        at += out.shape[1]


def grad_kernel(ats, width, where, left, half_here, half_there, right, right_other, sent, far, near, other):
    half_at, there_at, right_at, other_at = ats
    lanes = other.shape[1] // 2
    core, loc = where[1], where[2]
    at = pl.multiple_of(core * lanes, lanes)
    other[:, pl.ds(at, lanes)] = half_here[:, half_at : half_at + lanes]
    at = pl.multiple_of((1 - core) * lanes, lanes)
    other[:, pl.ds(at, lanes)] = half_there[:, there_at : there_at + lanes]
    block = near.shape[0]
    parity = lax.rem(loc, 2)
    beside = loc + 1 - 2 * parity
    for number, place in enumerate((lax.rem(beside + 2, 4), beside, lax.rem(loc + 2, 4), loc)):
        columns = pl.ds(pl.multiple_of(place * block, block), block)
        for first in range(0, width, 256):
            lane = slice(first, first + 256)
            total = dot(left[:, columns], right[:, right_at + first : right_at + first + 256], TN)
            total = total + dot(
                other[:, columns], right_other[:, other_at + first : other_at + first + 256], TN
            )
            if number < 2:
                sent[number * block : (number + 1) * block, lane] = total.astype(BF)
            elif number == 2:
                far[:, lane] = total
            else:
                near[:, lane] = total


def finish_kernel(*refs):
    out = refs[-1]
    block = out.shape[0]
    column = 0
    for near, beside, far in zip(refs[0:-1:3], refs[1:-1:3], refs[2:-1:3]):
        for at in range(0, near.shape[1], 256):
            lane = slice(at, at + 256)
            total = near[:, lane] + beside[block:, lane].astype(F32) + far[:, lane].astype(F32)
            kind, first = (column + at) // out.shape[2], (column + at) % out.shape[2]
            out[:, kind, first : first + 256] = total
        column += near.shape[1]


def slice_kernel(number, weights, out):
    for kind in range(out.shape[0]):
        out[kind] = weights[:, kind, :]


class Plan:
    def __init__(self, blocks, moves, origins, weights, paired, locs, grads, sources=0):
        self.blocks, self.moves, self.origins = blocks, moves, origins
        self.arrays, self.table = len(weights.arrays), weights.table
        self.paired, self.locs, self.grads, self.sources = paired, locs, grads, sources


def call(body, outs, args, scratch=(), flops=0, kept=None):
    smem = pl.BlockSpec(memory_space=pltpu.SMEM)
    vmem = pl.BlockSpec(memory_space=pltpu.VMEM)
    specs = [smem if arg.dtype == jnp.int32 else vmem for arg in args]
    out_specs = [vmem] * len(outs)
    aliases = {}
    outs = list(outs)
    moved = sum(arg.size * arg.dtype.itemsize for arg in args)
    moved = moved + sum(out.size * out.dtype.itemsize for out in outs)
    if kept is not None:
        specs[kept] = pl.BlockSpec(memory_space=pl.ANY)
        out_specs.append(pl.BlockSpec(memory_space=pl.ANY))
        outs.append(jax.ShapeDtypeStruct(args[kept].shape, args[kept].dtype))
        aliases = {kept: len(outs) - 1}
    return pl.pallas_call(
        body,
        out_shape=outs,
        in_specs=specs,
        out_specs=out_specs,
        scratch_shapes=list(scratch),
        input_output_aliases=aliases,
        compiler_params=pltpu.CompilerParams(vmem_limit_bytes=VMEM_LIMIT),
        cost_estimate=pl.CostEstimate(flops=flops, bytes_accessed=moved, transcendentals=0),
    )(*args)


def swap(array, axis):
    return lax.ppermute(array, axis, [(0, 1), (1, 0)])


PAIRS = [(0, 1), (1, 0), (2, 3), (3, 2)]
APART = [(0, 2), (1, 3), (2, 0), (3, 1)]


def quarter_of(weights, number):
    rows, kinds, width = weights.shape
    return pl.pallas_call(
        slice_kernel,
        out_shape=jax.ShapeDtypeStruct((kinds, rows // 4, width), weights.dtype),
        grid_spec=pltpu.PrefetchScalarGridSpec(
            num_scalar_prefetch=1,
            grid=(1,),
            in_specs=[pl.BlockSpec((rows // 4, kinds, width), lambda at, number: (number[0], 0, 0))],
            out_specs=pl.BlockSpec((kinds, rows // 4, width), lambda at, number: (0, 0, 0)),
        ),
    )(number.astype(jnp.int32)[None], weights)


def gather_weights(spatial, temporal, paired):
    if not paired:
        found = []
        for weights in (spatial, temporal):
            whole = lax.all_gather(weights.transpose(1, 0, 2), "date", axis=1, tiled=True)
            table = {kind: [(0, kind, 0)] for kind in range(4)}
            found.append(Weights([whole], table, jnp.zeros((1,), jnp.int32)))
        return found
    rows = spatial.shape[0]
    side, here = lax.axis_index("groups"), lax.axis_index("date")
    even = lax.axis_index("loc") % 2
    numbers = [side * 2 + even, (1 - side) * 2 + even, side * 2 + 1 - even, (1 - side) * 2 + 1 - even]
    offsets = [here * rows] + [(1 - here) * rows + number * (rows // 4) for number in numbers]
    offsets = jnp.stack(offsets).astype(jnp.int32)
    own = quarter_of(spatial, numbers[0])
    first = swap(own, "date")
    last = swap(quarter_of(spatial, numbers[3]), "date")
    arrays = [spatial.transpose(1, 0, 2), first, swap(first, "groups")]
    arrays += [lax.ppermute(first, "loc", PAIRS), last]
    table = {kind: [(number, kind, number) for number in range(5)] for kind in range(4)}
    spatial = Weights(arrays, table, offsets)
    first = swap(quarter_of(temporal, numbers[0]), "date")
    group, loc = swap(first, "groups"), lax.ppermute(first, "loc", PAIRS)
    far = (swap(loc[0:2], "groups"), lax.ppermute(group[2:4], "loc", PAIRS))
    arrays = [temporal.transpose(1, 0, 2), first, group, loc, *far]
    table = {
        kind: [(number, kind, number) for number in range(4)] + [(4 + kind // 2, kind % 2, 4)]
        for kind in range(4)
    }
    return [spatial, Weights(arrays, table, offsets)]


def add_over_heads(partial, sizes):
    if sizes["mp"] == 2:
        return partial.astype(F32) + swap(partial, "mp").astype(F32)
    return lax.psum(partial.astype(F32), "mp")


def whole_grads(hidden, back_triple, upstream, mixed):
    width = mixed.shape[1]
    intake = dot(hidden, back_triple, TN)
    outlet = dot(upstream, mixed, TN)
    whole = jnp.concatenate([intake, outlet], axis=1).reshape(-1, 4, width)
    part = lax.psum_scatter(whole.astype(BF), ("loc", "date"), scatter_dimension=0, tiled=True)
    return part.astype(F32)


def summed(where, left, halves, right, other_right, width):
    (half_here, half_at), (half_there, there_at) = halves
    (right, right_at), (other_right, other_at) = right, other_right
    rows, columns = left.shape
    block = columns // 4
    sent, far, near = call(
        functools.partial(grad_kernel, (half_at, there_at, right_at, other_at), width),
        (
            jax.ShapeDtypeStruct((2 * block, width), BF),
            jax.ShapeDtypeStruct((block, width), F32),
            jax.ShapeDtypeStruct((block, width), F32),
        ),
        (where, left, half_here, half_there, right, other_right),
        scratch=(pltpu.VMEM((rows, columns), BF),),
        flops=4 * rows * columns * width,
    )
    beside = lax.ppermute(sent, "loc", PAIRS)
    far = (far + beside[:block].astype(F32)).astype(BF)
    return near, beside, lax.ppermute(far, "loc", APART)


def finish(terms, width):
    block = terms[0].shape[0]
    return call(finish_kernel, (jax.ShapeDtypeStruct((block, 4, width), F32),), terms)[0]


def per_device(
    sizes,
    optical,
    radar,
    cloud,
    radar_drop,
    keep_index,
    place_table,
    date_table,
    spatial_gain,
    spatial_weights,
    temporal_gain,
    temporal_weights,
    cotangent,
):
    _, patches, dates_here, model = optical.shape
    patches_here, dates = cotangent.shape[1:3]
    width = spatial_weights.shape[2]
    rows = patches * dates_here
    here = lax.axis_index("date")
    first = here * dates_here
    paired = sizes["groups"] == 2 and sizes["loc"] == 4 and sizes["date"] == 2 and sizes["mp"] == 2
    paired = paired and dates_here % 2 == 0 and patches_here % 8 == 0 and model % 1024 == 0
    spatial, temporal = gather_weights(spatial_weights, temporal_weights, paired)

    if paired:
        pairs, eights = dates_here // 2, patches_here // 8
        spatial_blocks, temporal_blocks = pairs, eights
        half_rows = eights * 16

        def own_first(array, axis):
            return jnp.where(here == 0, array, jnp.flip(array, axis))

        def spatial_rows(array):
            array = array.reshape(pairs, 2, 2, eights, 8, -1)
            return own_first(array, 2).transpose(0, 2, 3, 1, 4, 5).reshape(rows, -1)

        def temporal_rows(array):
            array = array.reshape(2, pairs, 2, eights, 8, -1)
            return own_first(array, 0).transpose(3, 0, 1, 2, 4, 5).reshape(rows, -1)

        def temporal_whole(array):
            array = array.reshape(eights, 2, pairs, 2, 8, -1).transpose(1, 2, 3, 0, 4, 5)
            return own_first(array, 0).reshape(dates, patches_here, -1)

    else:
        spatial_blocks = 1 if rows <= 192 else dates_here
        temporal_blocks = patches_here // 8 if patches_here % 8 == 0 else 1

        def spatial_rows(array):
            return array.reshape(rows, -1)

        def temporal_rows(array):
            array = array.reshape(dates, temporal_blocks, patches_here // temporal_blocks, -1)
            return array.transpose(1, 0, 2, 3).reshape(rows, -1)

        def temporal_whole(array):
            array = array.reshape(temporal_blocks, dates, patches_here // temporal_blocks, -1)
            return array.transpose(1, 0, 2, 3).reshape(dates, patches_here, -1)

    cloud_here = lax.dynamic_slice_in_dim(cloud, first, dates_here, 1)[0]
    drop_here = lax.dynamic_slice_in_dim(radar_drop, first, dates_here, 1)[0]
    optical_keep = (1 - cloud_here).astype(F32)[:, None, None]
    radar_keep = (1 - drop_here).astype(F32)[:, None, None]
    places = jnp.take(place_table, keep_index[0], axis=0).astype(F32)[None]
    start = (
        optical[0].transpose(1, 0, 2).astype(F32) * optical_keep
        + radar[0].transpose(1, 0, 2).astype(F32) * radar_keep
        + places
    ).astype(BF)
    start = spatial_rows(start)

    dates_at = jnp.arange(dates, dtype=jnp.int32)
    patches_at = jnp.arange(patches_here, dtype=jnp.int32)
    ones_here = jnp.ones((dates, patches_here, 1), jnp.int32)
    temporal_size = rows // temporal_blocks
    date_at = temporal_rows(ones_here * dates_at[:, None, None])[:temporal_size, 0]
    patch_at = temporal_rows(ones_here * patches_at[None, :, None])[:temporal_size, 0]
    spatial_size = rows // spatial_blocks
    spatial_date = jnp.ones((dates_here, patches, 1), jnp.int32) * dates_at[:dates_here, None, None]
    spatial_date = spatial_rows(spatial_date)[:spatial_size, 0]
    spatial_bias = jnp.where(spatial_date[:, None] == spatial_date[None, :], 0.0, CROSS).astype(F32)
    survive = 1 - cloud[0] * radar_drop[0]
    same_date = date_at[:, None] == date_at[None, :]
    survive_at = temporal_rows(ones_here * survive[:, None, None])[:temporal_size, 0]
    allowed = (survive_at[None, :] == 1) | same_date
    temporal_bias = jnp.where(
        patch_at[:, None] == patch_at[None, :], jnp.where(allowed, 0.0, -1000000000.0), CROSS
    ).astype(F32)
    date_rows = jnp.broadcast_to(date_table[:, None], (dates, patches_here, model))
    date_rows = temporal_rows(date_rows)[:temporal_size]
    cotangent_rows = temporal_rows(cotangent[0].transpose(1, 0, 2))

    spatial_gain = spatial_gain[None]
    temporal_gain = temporal_gain[None]
    lanes = min(width, 256)

    def shape(*dims, dtype=BF):
        return jax.ShapeDtypeStruct(dims, dtype)

    def attend_dims(blocks):
        return (blocks * (width // lanes), lanes // HEAD_DIM * (rows // blocks), rows // blocks)

    layer_flops = 2 * rows * model * width * 4
    where = jnp.stack([here, lax.axis_index("mp"), lax.axis_index("loc")]).astype(jnp.int32)
    if paired:
        half = rows // 2
        blocked = start.reshape(pairs, 2, half_rows, model)
        origins = (blocked[:, 0].reshape(half, model), blocked[:, 1].reshape(half, model))
        spatial_moves = [
            (side, pair * half_rows, (pair * 2 + side) * half_rows, half_rows)
            for side in range(2)
            for pair in range(pairs)
        ]
        temporal_moves = [
            (side, pair * half_rows + eight * 16, (eight * 2 + side) * pairs * 16 + pair * 16, 16)
            for side in range(2)
            for pair in range(pairs)
            for eight in range(eights)
        ]
        half_shapes = (shape(half, model), shape(half, model))
        own, quarter = shape(rows, model // 2), model // 4
        forward_grads = (own, own, shape(rows, 2 * quarter + width))
        temporal_grads = (own, shape(rows, quarter + width))
        backward_grads = (own, shape(rows, quarter))
        back_shapes = (shape(rows, 3 * width // 2), shape(rows, 3 * width // 2))
    else:
        origins = (start,)
        spatial_moves = [(0, at * spatial_size, at * spatial_size, spatial_size) for at in range(spatial_blocks)]
        temporal_moves = [(0, at * temporal_size, at * temporal_size, temporal_size) for at in range(temporal_blocks)]
        half_shapes = (shape(rows, model),)
        forward_grads = temporal_grads = backward_grads = (shape(rows, model),)
        back_shapes = (shape(rows, 3 * width),)
    origins, spatial_bias, temporal_bias, date_rows, cotangent_rows = lax.optimization_barrier(
        (origins, spatial_bias, temporal_bias, date_rows, cotangent_rows)
    )

    def plan_of(blocks, moves, weights, grads, sources=0):
        return Plan(blocks, moves, len(origins), weights, paired, sizes["loc"], len(grads), sources)

    plan = plan_of(spatial_blocks, spatial_moves, spatial, forward_grads)
    outs = call(
        functools.partial(spatial_forward_kernel, plan),
        (
            *half_shapes,
            *forward_grads,
            shape(rows, 3 * width),
            shape(*attend_dims(spatial_blocks), dtype=F32),
            shape(rows, width),
        ),
        (where, spatial.offsets, spatial_gain, spatial_bias, cotangent_rows, *origins, *spatial.arrays),
        scratch=(
            pltpu.VMEM((rows, model), BF),
            pltpu.VMEM((rows, model), BF),
            pltpu.VMEM((rows, model), BF),
        ),
        flops=layer_flops,
    )
    partials, outs = outs[: len(origins)], outs[len(origins) :]
    forward, (triple, attend, mixed) = outs[: len(forward_grads)], outs[len(forward_grads) :]
    if paired:
        there, early = call(
            between_kernel,
            (shape(half, model),),
            (origins[1], partials[1], swap(partials[1], "mp"), forward[2]),
            kept=3,
        )
        sources = (origins[0], partials[0], swap(partials[0], "mp"), swap(there, "date"))
        early_other = swap(early, "date")
    else:
        spatial_out = (start.astype(F32) + add_over_heads(partials[0], sizes)).astype(BF)
        moved = lax.all_to_all(
            spatial_out.reshape(dates_here, patches, model),
            "date",
            split_axis=1,
            concat_axis=0,
            tiled=True,
        )
        sources = (temporal_rows(moved),)
    plan = plan_of(temporal_blocks, temporal_moves, temporal, temporal_grads, len(sources))
    outs = call(
        functools.partial(temporal_kernel, plan),
        (
            *temporal_grads,
            shape(rows, model),
            shape(rows, width),
            shape(rows, model),
            shape(rows, 3 * width),
            shape(rows, model),
        ),
        (
            where,
            temporal.offsets,
            temporal_gain,
            temporal_bias,
            date_rows,
            cotangent_rows,
            *sources,
            *temporal.arrays,
        ),
        scratch=(
            pltpu.VMEM((rows, model), BF),
            pltpu.VMEM((rows, 3 * width), BF),
            pltpu.VMEM(attend_dims(temporal_blocks), F32),
            pltpu.VMEM((rows, width), BF),
        ),
        flops=2 * layer_flops,
    )
    middle, outs = outs[: len(temporal_grads)], outs[len(temporal_grads) :]
    joined, temporal_mixed, temporal_partial, temporal_triple, back_part = outs

    if sizes["mp"] == 2:
        others = swap(back_part, "mp")
    else:
        others = (lax.psum(back_part.astype(F32), "mp") - back_part.astype(F32)).astype(BF)
    *backs, temporal_triple = call(
        functools.partial(norm_back_kernel, temporal_moves, temporal_size),
        half_shapes,
        (temporal_gain, back_part, others, joined, cotangent_rows, temporal_triple),
        kept=5,
    )
    if paired:
        back_origins = (backs[0], swap(backs[1], "date"))
    else:
        back = lax.all_to_all(
            temporal_whole(backs[0]), "date", split_axis=0, concat_axis=1, tiled=True
        )
        back_origins = (back.reshape(rows, model),)
    outlet = spatial.only((3,))
    plan = plan_of(spatial_blocks, spatial_moves, outlet, backward_grads)
    outs = call(
        functools.partial(spatial_backward_kernel, plan),
        (*backward_grads, *back_shapes),
        (where, outlet.offsets, triple, attend, *back_origins, *outlet.arrays),
        scratch=(
            pltpu.VMEM((rows, model), BF),
            pltpu.VMEM((rows, width), BF),
            pltpu.VMEM((rows, 3 * width), BF),
        ),
        flops=layer_flops,
    )
    backward, back_triples = outs[: len(backward_grads)], outs[len(backward_grads) :]
    encoded = (joined.astype(F32) + add_over_heads(temporal_partial, sizes)).astype(BF)
    encoded = temporal_whole(encoded).transpose(1, 0, 2)[None]
    if not paired:
        return (
            encoded,
            whole_grads(forward[0], back_triples[0], backward[0], mixed),
            whole_grads(middle[0], temporal_triple, cotangent_rows, temporal_mixed),
        )
    early_there = swap(early_other[:, : 2 * quarter], "mp")
    middle_other = swap(middle[1], "date")
    middle_there = swap(middle_other[:, :quarter], "mp")
    triple_other = swap(temporal_triple, "date")
    temporal_outlet = summed(
        where,
        forward[1],
        ((early_other, quarter), (early_there, quarter)),
        (temporal_mixed, 0),
        (middle_other, quarter),
        width,
    )
    temporal_intake = summed(
        where,
        middle[0],
        ((middle_other, 0), (middle_there, 0)),
        (temporal_triple, 0),
        (triple_other, 0),
        3 * width,
    )
    backward_other = swap(backward[1], "date")
    backward_there = swap(backward_other, "mp")
    back_others = [swap(array, "date") for array in back_triples]
    spatial_outlet = summed(
        where,
        backward[0],
        ((backward_other, 0), (backward_there, 0)),
        (mixed, 0),
        (early_other, 2 * quarter),
        width,
    )
    terms = []
    for right, other in zip(back_triples, back_others):
        terms += summed(
            where,
            forward[0],
            ((early_other, 0), (early_there, 0)),
            (right, 0),
            (other, 0),
            right.shape[1],
        )
    temporal_grads = finish((*temporal_intake, *temporal_outlet), width)
    spatial_grads = finish((*terms, *spatial_outlet), width)
    return (encoded, spatial_grads, temporal_grads)


def solution(mesh):
    in_specs = (
        P(("groups", "loc"), None, "date", None),
        P(("groups", "loc"), None, "date", None),
        P(("groups", "loc"), None),
        P(("groups", "loc"), None),
        P(("groups", "loc"), None),
        P(),
        P(),
        P(),
        P("date", None, "mp"),
        P(),
        P("date", None, "mp"),
        P(("groups", "loc"), "date", None, None),
    )
    out_specs = (
        P(("groups", "loc"), "date", None, None),
        P(("groups", "loc", "date"), None, "mp"),
        P(("groups", "loc", "date"), None, "mp"),
    )
    return jax.shard_map(
        functools.partial(per_device, dict(mesh.shape)),
        mesh=mesh,
        in_specs=in_specs,
        out_specs=out_specs,
        check_vma=False,
    )
```

```python
import functools

import jax
import jax.numpy as jnp
from jax import lax
from jax.experimental import pallas as pl
from jax.experimental.pallas import tpu as pltpu
from jax.sharding import PartitionSpec as P

HEAD_DIM = 64
EPSILON = 1e-05
CROSS = -1e30
BF = jnp.bfloat16
F32 = jnp.float32
NN = (((1,), (0,)), ((), ()))
NT = (((1,), (1,)), ((), ()))
TN = (((0,), (0,)), ((), ()))
VMEM_LIMIT = 56 * 1024 * 1024


def dot(left, right, dims):
    return lax.dot_general(left, right, dims, preferred_element_type=F32)


def statistics(rows):
    values = rows.astype(F32)
    centred = values - jnp.mean(values, -1, keepdims=True)
    inv_scale = lax.rsqrt(jnp.mean(centred * centred, -1, keepdims=True) + EPSILON)
    return centred * inv_scale, inv_scale


class Heads:
    def __init__(self, width):
        self.lanes = min(width, 256)
        self.count = self.lanes // HEAD_DIM
        owner = lax.broadcasted_iota(jnp.int32, (1, self.lanes), 1) // HEAD_DIM
        self.masks = [(owner == head).astype(F32) for head in range(self.count)]

    def stack(self, block):
        return jnp.concatenate([block * mask.astype(BF) for mask in self.masks], axis=0)

    def unstack(self, tall):
        rows = tall.shape[0] // self.count
        total = tall[0:rows] * self.masks[0]
        for head in range(1, self.count):
            total = total + tall[head * rows : (head + 1) * rows] * self.masks[head]
        return total


class Weights:
    def __init__(self, arrays, table, offsets):
        self.arrays, self.table, self.offsets = list(arrays), table, offsets

    def only(self, kinds):
        used = sorted({entry[0] for kind in kinds for entry in self.table[kind]})
        table = {
            kind: [(used.index(array), at, place) for array, at, place in self.table[kind]]
            for kind in kinds
        }
        return Weights([self.arrays[number] for number in used], table, self.offsets)


def views(table, refs, offsets, kind):
    found = []
    for array, at, place in table[kind]:
        part = refs[array].at[at]
        found.append((part, pl.ds(pl.multiple_of(offsets[place], 128), part.shape[0])))
    return found


def rows_times(rows_ref, parts, out_ref, column):
    width = parts[0][0].shape[1]
    step = min(width, 256)
    for at in range(0, width, step):
        total = None
        for part, columns in parts:
            term = dot(rows_ref[:, columns], part[:, at : at + step], NN)
            total = term if total is None else total + term
        out_ref[:, column + at : column + at + step] = total.astype(out_ref.dtype)


def emit_own(rows_ref, out, at, date, loc_count):
    block = rows_ref.shape[1] // (2 * loc_count)
    for loc in range(loc_count):
        first = pl.multiple_of((loc * 2 + date) * block, block)
        out[:, at + loc * block : at + (loc + 1) * block] = rows_ref[:, pl.ds(first, block)]


def emit_half(rows_ref, out, at, date, core, loc_count):
    block = rows_ref.shape[1] // (2 * loc_count)
    for number in range(loc_count // 2):
        loc = core * (loc_count // 2) + number
        first = pl.multiple_of((loc * 2 + date) * block, block)
        out[:, at + number * block : at + (number + 1) * block] = rows_ref[:, pl.ds(first, block)]


def attention(triple_ref, bias_ref, attend_ref, mixed_ref, blocks):
    width = triple_ref.shape[1] // 3
    heads = Heads(width)
    rows = triple_ref.shape[0] // blocks
    groups = width // heads.lanes
    bias = jnp.concatenate([bias_ref[...]] * heads.count, axis=0)
    for block in range(blocks):
        at = slice(block * rows, (block + 1) * rows)
        for group in range(groups):
            lane = group * heads.lanes
            queries = heads.stack(triple_ref[at, lane : lane + heads.lanes])
            keys = triple_ref[at, width + lane : width + lane + heads.lanes]
            values = triple_ref[at, 2 * width + lane : 2 * width + lane + heads.lanes]
            scores = dot(queries, keys, NT) * HEAD_DIM ** (-0.5) + bias
            raised = jnp.exp(scores - jnp.max(scores, -1, keepdims=True))
            attend = raised * (1.0 / jnp.sum(raised, -1, keepdims=True))
            attend_ref[block * groups + group] = attend
            mixed = heads.unstack(dot(attend.astype(BF), values, NN))
            mixed_ref[at, lane : lane + heads.lanes] = mixed.astype(BF)


def attention_back(triple_ref, attend_ref, back_mixed_ref, back_triple_ref, blocks):
    width = triple_ref.shape[1] // 3
    heads = Heads(width)
    rows = triple_ref.shape[0] // blocks
    groups = width // heads.lanes
    for block in range(blocks):
        at = slice(block * rows, (block + 1) * rows)
        for group in range(groups):
            lane = group * heads.lanes
            queries = heads.stack(triple_ref[at, lane : lane + heads.lanes])
            keys = triple_ref[at, width + lane : width + lane + heads.lanes]
            values = triple_ref[at, 2 * width + lane : 2 * width + lane + heads.lanes]
            back = heads.stack(back_mixed_ref[at, lane : lane + heads.lanes])
            attend = attend_ref[block * groups + group]
            back_attend = dot(back, values, NT)
            back_values = dot(attend.astype(BF), back, TN)
            inner = back_attend - jnp.sum(back_attend * attend, -1, keepdims=True)
            back_scores = (attend * inner * HEAD_DIM ** (-0.5)).astype(BF)
            back_queries = heads.unstack(dot(back_scores, keys, NN))
            back_keys = dot(back_scores, queries, TN)
            for number, term in enumerate((back_queries, back_keys, back_values)):
                first = number * width + lane
                back_triple_ref[at, first : first + heads.lanes] = term.astype(BF)


def normalize_into(rows_ref, gain_ref, hidden_ref, blocks):
    rows = rows_ref.shape[0] // blocks
    for block in range(blocks):
        at = slice(block * rows, (block + 1) * rows)
        normed, _ = statistics(rows_ref[at, :])
        hidden_ref[at, :] = (normed * gain_ref[...]).astype(BF)


def spatial_forward_kernel(plan, where, offsets, gain, bias, cotangent, *refs):
    sources, refs = refs[: plan.origins], refs[plan.origins :]
    arrays, refs = refs[: plan.arrays], refs[plan.arrays :]
    partials, refs = refs[: plan.origins], refs[plan.origins :]
    grads, refs = refs[: plan.grads], refs[plan.grads :]
    triple, attend, mixed, start, hidden, whole = refs
    for source, at, to, size in plan.moves:
        start[to : to + size, :] = sources[source][at : at + size, :]
    normalize_into(start, gain, hidden, plan.blocks)
    width = mixed.shape[1]
    for kind in range(3):
        rows_times(hidden, views(plan.table, arrays, offsets, kind), triple, kind * width)
    attention(triple, bias, attend, mixed, plan.blocks)
    for part, features in views(plan.table, arrays, offsets, 3):
        whole[:, features] = dot(mixed[...], part[...], NT).astype(BF)
    for source, at, to, size in plan.moves:
        partials[source][at : at + size, :] = whole[to : to + size, :]
    if plan.paired:
        own_hidden, own_cotangent, sent = grads
        half = hidden.shape[1] // 4
        here, core = where[0], where[1]
        emit_own(hidden, own_hidden, 0, here, plan.locs)
        emit_own(cotangent, own_cotangent, 0, here, plan.locs)
        emit_half(hidden, sent, 0, 1 - here, core, plan.locs)
        emit_half(cotangent, sent, half, 1 - here, core, plan.locs)
        sent[:, 2 * half :] = mixed[...]
    else:
        grads[0][...] = hidden[...]


def between_kernel(start, here, there, kept, out, passed):
    total = here[...].astype(F32) + there[...].astype(F32)
    out[...] = (start[...].astype(F32) + total).astype(BF)


def temporal_kernel(plan, where, offsets, gain, bias, date_rows, cotangent, *refs):
    sources, refs = refs[: plan.sources], refs[plan.sources :]
    arrays, refs = refs[: plan.arrays], refs[plan.arrays :]
    grads, refs = refs[: plan.grads], refs[plan.grads :]
    joined, mixed, partial, back_part = refs[:4]
    back_triples, (hidden, triple, attend, back_mixed, back_triple) = refs[4:-5], refs[-5:]
    rows = date_rows.shape[0]
    for source, at, to, size in plan.moves:
        if source == 0 and plan.sources > 1:
            total = sources[1][at : at + size, :].astype(F32) + sources[2][at : at + size, :].astype(F32)
            out = (sources[0][at : at + size, :].astype(F32) + total).astype(BF)
        else:
            out = sources[-1][at : at + size, :]
        dated = out.astype(F32) + date_rows[to % rows : to % rows + size, :].astype(F32)
        joined[to : to + size, :] = dated.astype(BF)
    normalize_into(joined, gain, hidden, plan.blocks)
    width = mixed.shape[1]
    for kind in range(3):
        rows_times(hidden, views(plan.table, arrays, offsets, kind), triple, kind * width)
    outlet = views(plan.table, arrays, offsets, 3)
    rows_times(cotangent, outlet, back_mixed, 0)
    attention(triple, bias, attend, mixed, plan.blocks)
    for part, features in outlet:
        partial[:, features] = dot(mixed[...], part[...], NT).astype(BF)
    if plan.paired:
        own_hidden, sent = grads
        half = hidden.shape[1] // 4
        emit_own(hidden, own_hidden, 0, where[0], plan.locs)
        emit_half(hidden, sent, 0, 1 - where[0], where[1], plan.locs)
        sent[:, half:] = mixed[...]
    else:
        grads[0][...] = hidden[...]
    attention_back(triple, attend, back_mixed, back_triple, plan.blocks)
    intakes = [views(plan.table, arrays, offsets, kind) for kind in range(3)]
    for entries in zip(*intakes):
        total = None
        for kind, (part, features) in enumerate(entries):
            term = dot(back_triple[:, kind * width : (kind + 1) * width], part[...], NT)
            total = term if total is None else total + term
        back_part[:, features] = total.astype(BF)
    split_columns(back_triple, back_triples)


def split_columns(whole, outs):
    at = 0
    for out in outs:
        out[...] = whole[:, at : at + out.shape[1]]
        at += out.shape[1]


def norm_back_kernel(moves, step, gain, here, there, joined, cotangent, kept, *outs):
    for at in range(0, joined.shape[0], step):
        span_here = slice(at, at + step)
        normed, inv_scale = statistics(joined[span_here, :])
        total = here[span_here, :].astype(F32) + there[span_here, :].astype(F32)
        scaled = total * gain[...]
        inner = (
            scaled
            - jnp.mean(scaled, -1, keepdims=True)
            - normed * jnp.mean(scaled * normed, -1, keepdims=True)
        )
        back = (cotangent[span_here, :].astype(F32) + inv_scale * inner).astype(BF)
        for target, to, first, size in moves:
            if at <= first < at + step:
                outs[target][to : to + size, :] = back[first - at : first - at + size]


def spatial_backward_kernel(plan, where, offsets, triple, attend, kept, *refs):
    sources, refs = refs[: plan.origins], refs[plan.origins :]
    arrays, refs = refs[: plan.arrays], refs[plan.arrays :]
    grads, refs = refs[: plan.grads], refs[plan.grads :]
    back_triples, (upstream, back_mixed, back_triple) = refs[:-4], refs[-3:]
    for source, at, to, size in plan.moves:
        upstream[to : to + size, :] = sources[source][at : at + size, :]
    if plan.paired:
        emit_own(upstream, grads[0], 0, where[0], plan.locs)
        emit_own(upstream, grads[1], 0, 1 - where[0], plan.locs)
    else:
        grads[0][...] = upstream[...]
    rows_times(upstream, views(plan.table, arrays, offsets, 3), back_mixed, 0)
    attention_back(triple, attend, back_mixed, back_triple, plan.blocks)
    split_columns(back_triple, back_triples)
    if plan.paired:
        half = upstream.shape[1] // 2
        grads[1][:, half:] = back_triple[:, : grads[1].shape[1] - half]


def grad_kernel(products, count, where, *refs):
    sent, far, near, other = refs[-4:]
    core, loc = where[1], where[2]
    block = near.shape[0]
    beside = loc + 1 - 2 * lax.rem(loc, 2)
    places = (lax.rem(beside + 2, 4), beside, lax.rem(loc + 2, 4), loc)
    column = 0
    for left, others, (right, right_at), (right_other, other_at), width in products:
        left, right, right_other = refs[left], refs[right], refs[right_other]
        lanes = other.shape[1] // len(others)
        for number, (source, at) in enumerate(others):
            to = 0
            if len(others) > 1:
                to = pl.multiple_of((core if number == 0 else 1 - core) * lanes, lanes)
            other[:, pl.ds(to, lanes)] = refs[source][:, at : at + lanes]
        for number, place in enumerate(places):
            columns = pl.ds(pl.multiple_of(place * block, block), block)
            for first in range(0, width, 256):
                lane = slice(column + first, column + first + 256)
                here = right[:, right_at + first : right_at + first + 256]
                there = right_other[:, other_at + first : other_at + first + 256]
                total = dot(left[:, columns], here, TN) + dot(other[:, columns], there, TN)
                if number < 2:
                    sent[number * block : (number + 1) * block, lane] = total.astype(BF)
                elif number == 2:
                    far[:, lane] = total
                else:
                    near[:, lane] = total
        column += width


def finish_kernel(*refs):
    out = refs[-1]
    block = out.shape[0]
    column = 0
    for near, beside, far in zip(refs[0:-1:3], refs[1:-1:3], refs[2:-1:3]):
        for at in range(0, near.shape[1], 256):
            lane = slice(at, at + 256)
            total = near[:, lane] + beside[block:, lane].astype(F32) + far[:, lane].astype(F32)
            kind, first = (3 * out.shape[2] + column + at) // out.shape[2] % 4, (column + at) % out.shape[2]
            out[:, kind, first : first + 256] = total
        column += near.shape[1]


def finish_last_kernel(kept, *refs):
    finish_kernel(*refs[:-1])


def fence_kernel(*refs):
    pass


def grad_after_kernel(products, count, where, *refs):
    args, rest = refs[:count], refs[count + 1 :]
    grad_kernel(products, count, where, *args, *rest[:3], *rest[4:])


class Plan:
    def __init__(self, blocks, moves, origins, weights, paired, locs, grads, sources=0):
        self.blocks, self.moves, self.origins = blocks, moves, origins
        self.arrays, self.table = len(weights.arrays), weights.table
        self.paired, self.locs, self.grads, self.sources = paired, locs, grads, sources


def call(body, outs, args, scratch=(), flops=0, kept=None):
    smem = pl.BlockSpec(memory_space=pltpu.SMEM)
    vmem = pl.BlockSpec(memory_space=pltpu.VMEM)
    specs = [smem if arg.dtype == jnp.int32 else vmem for arg in args]
    out_specs = [vmem] * len(outs)
    aliases = {}
    outs = list(outs)
    moved = sum(arg.size * arg.dtype.itemsize for arg in args)
    moved = moved + sum(out.size * out.dtype.itemsize for out in outs)
    if kept is not None:
        specs[kept] = pl.BlockSpec(memory_space=pl.ANY)
        out_specs.append(pl.BlockSpec(memory_space=pl.ANY))
        outs.append(jax.ShapeDtypeStruct(args[kept].shape, args[kept].dtype))
        aliases = {kept: len(outs) - 1}
    return pl.pallas_call(
        body,
        out_shape=outs,
        in_specs=specs,
        out_specs=out_specs,
        scratch_shapes=list(scratch),
        input_output_aliases=aliases,
        compiler_params=pltpu.CompilerParams(vmem_limit_bytes=VMEM_LIMIT),
        cost_estimate=pl.CostEstimate(flops=flops, bytes_accessed=moved, transcendentals=0),
    )(*args)


def fence(*arrays):
    anywhere = [pl.BlockSpec(memory_space=pl.ANY)] * len(arrays)
    return pl.pallas_call(
        fence_kernel,
        out_shape=[jax.ShapeDtypeStruct(array.shape, array.dtype) for array in arrays],
        in_specs=anywhere,
        out_specs=anywhere,
        input_output_aliases={number: number for number in range(len(arrays))},
    )(*arrays)


def swap(array, axis):
    return lax.ppermute(array, axis, [(0, 1), (1, 0)])


PAIRS = [(0, 1), (1, 0), (2, 3), (3, 2)]
APART = [(0, 2), (1, 3), (2, 0), (3, 1)]


def quarter_of(weights, number):
    rows = weights.shape[0]
    return lax.dynamic_slice_in_dim(weights, number * (rows // 4), rows // 4, 0)


def by_kind(weights):
    return weights.transpose(1, 0, 2)


def gather_weights(spatial, temporal, paired):
    if not paired:
        found = []
        for weights in (spatial, temporal):
            whole = lax.all_gather(weights.transpose(1, 0, 2), "date", axis=1, tiled=True)
            table = {kind: [(0, kind, 0)] for kind in range(4)}
            found.append(Weights([whole], table, jnp.zeros((1,), jnp.int32)))
        return found
    rows = spatial.shape[0]
    side, here = lax.axis_index("groups"), lax.axis_index("date")
    even = lax.axis_index("loc") % 2
    numbers = [side * 2 + even, (1 - side) * 2 + even, side * 2 + 1 - even, (1 - side) * 2 + 1 - even]
    offsets = [here * rows] + [(1 - here) * rows + number * (rows // 4) for number in numbers]
    offsets = jnp.stack(offsets).astype(jnp.int32)
    first = swap(quarter_of(spatial, numbers[0]), "date")
    last = swap(quarter_of(spatial, numbers[3]), "date")
    temporal_sent, first = fence(quarter_of(temporal, numbers[0]), first)
    arrays = [spatial, first, swap(first, "groups"), lax.ppermute(first, "loc", PAIRS), last]
    table = {kind: [(number, kind, number) for number in range(5)] for kind in range(4)}
    spatial_parts = Weights([by_kind(array) for array in arrays], table, offsets)
    first = swap(temporal_sent, "date")
    group, loc = swap(first, "groups"), lax.ppermute(first, "loc", PAIRS)
    middle = rows // 8
    far = (swap(loc[:middle], "groups"), lax.ppermute(group[middle:], "loc", PAIRS))
    arrays = [temporal, first, group, loc, jnp.concatenate(far, axis=0)]
    return [spatial_parts, Weights([by_kind(array) for array in arrays], table, offsets)]


def add_over_heads(partial, sizes):
    if sizes["mp"] == 2:
        return partial.astype(F32) + swap(partial, "mp").astype(F32)
    return lax.psum(partial.astype(F32), "mp")


def whole_grads(hidden, back_triple, upstream, mixed):
    width = mixed.shape[1]
    intake = dot(hidden, back_triple, TN)
    outlet = dot(upstream, mixed, TN)
    whole = jnp.concatenate([intake, outlet], axis=1).reshape(-1, 4, width)
    part = lax.psum_scatter(whole.astype(BF), ("loc", "date"), scatter_dimension=0, tiled=True)
    return part.astype(F32)


def summed(where, args, products, kept=None):
    rows, columns = args[products[0][0]].shape
    block, width = columns // 4, sum(product[-1] for product in products)
    passed = () if kept is None else (kept,)
    outs = call(
        functools.partial(grad_kernel if kept is None else grad_after_kernel, products, len(args)),
        (
            jax.ShapeDtypeStruct((2 * block, width), BF),
            jax.ShapeDtypeStruct((block, width), F32),
            jax.ShapeDtypeStruct((block, width), F32),
        ),
        (where, *args, *passed),
        scratch=(pltpu.VMEM((rows, columns), BF),),
        flops=4 * rows * columns * width,
        kept=None if kept is None else 1 + len(args),
    )
    return outs


def summed_over_loc(outs):
    sent, far, near = outs[:3]
    beside = lax.ppermute(sent, "loc", PAIRS)
    far = (far + beside[: far.shape[0]].astype(F32)).astype(BF)
    return near, beside, lax.ppermute(far, "loc", APART)


def finish(terms, width, kept=None):
    out = jax.ShapeDtypeStruct((terms[0].shape[0], 4, width), F32)
    if kept is None:
        return call(finish_kernel, (out,), terms)
    return call(finish_last_kernel, (out,), (kept, *terms), kept=0)


def per_device(
    sizes,
    optical,
    radar,
    cloud,
    radar_drop,
    keep_index,
    place_table,
    date_table,
    spatial_gain,
    spatial_weights,
    temporal_gain,
    temporal_weights,
    cotangent,
):
    _, patches, dates_here, model = optical.shape
    patches_here, dates = cotangent.shape[1:3]
    width = spatial_weights.shape[2]
    rows = patches * dates_here
    here = lax.axis_index("date")
    first = here * dates_here
    paired = sizes["groups"] == 2 and sizes["loc"] == 4 and sizes["date"] == 2 and sizes["mp"] == 2
    paired = paired and dates_here % 2 == 0 and patches_here % 8 == 0 and model % 1024 == 0
    spatial, temporal = gather_weights(spatial_weights, temporal_weights, paired)

    if paired:
        pairs, eights = dates_here // 2, patches_here // 8
        spatial_blocks, temporal_blocks = pairs, eights
        half_rows = eights * 16

        def own_first(array, axis):
            return jnp.where(here == 0, array, jnp.flip(array, axis))

        def spatial_rows(array):
            array = array.reshape(pairs, 2, 2, eights, 8, -1)
            return own_first(array, 2).transpose(0, 2, 3, 1, 4, 5).reshape(rows, -1)

        def temporal_rows(array):
            array = array.reshape(2, pairs, 2, eights, 8, -1)
            return own_first(array, 0).transpose(3, 0, 1, 2, 4, 5).reshape(rows, -1)

        def temporal_whole(array):
            array = array.reshape(eights, 2, pairs, 2, 8, -1).transpose(1, 2, 3, 0, 4, 5)
            return own_first(array, 0).reshape(dates, patches_here, -1)

    else:
        spatial_blocks = 1 if rows <= 192 else dates_here
        temporal_blocks = patches_here // 8 if patches_here % 8 == 0 else 1

        def spatial_rows(array):
            return array.reshape(rows, -1)

        def temporal_rows(array):
            array = array.reshape(dates, temporal_blocks, patches_here // temporal_blocks, -1)
            return array.transpose(1, 0, 2, 3).reshape(rows, -1)

        def temporal_whole(array):
            array = array.reshape(temporal_blocks, dates, patches_here // temporal_blocks, -1)
            return array.transpose(1, 0, 2, 3).reshape(dates, patches_here, -1)

    cloud_here = lax.dynamic_slice_in_dim(cloud, first, dates_here, 1)[0]
    drop_here = lax.dynamic_slice_in_dim(radar_drop, first, dates_here, 1)[0]
    optical_keep = (1 - cloud_here).astype(F32)[:, None, None]
    radar_keep = (1 - drop_here).astype(F32)[:, None, None]
    places = jnp.take(place_table, keep_index[0], axis=0).astype(F32)[None]
    start = (
        optical[0].transpose(1, 0, 2).astype(F32) * optical_keep
        + radar[0].transpose(1, 0, 2).astype(F32) * radar_keep
        + places
    ).astype(BF)
    start = spatial_rows(start)

    dates_at = jnp.arange(dates, dtype=jnp.int32)
    patches_at = jnp.arange(patches_here, dtype=jnp.int32)
    ones_here = jnp.ones((dates, patches_here, 1), jnp.int32)
    temporal_size = rows // temporal_blocks
    date_at = temporal_rows(ones_here * dates_at[:, None, None])[:temporal_size, 0]
    patch_at = temporal_rows(ones_here * patches_at[None, :, None])[:temporal_size, 0]
    spatial_size = rows // spatial_blocks
    spatial_date = jnp.ones((dates_here, patches, 1), jnp.int32) * dates_at[:dates_here, None, None]
    spatial_date = spatial_rows(spatial_date)[:spatial_size, 0]
    spatial_bias = jnp.where(spatial_date[:, None] == spatial_date[None, :], 0.0, CROSS).astype(F32)
    survive = 1 - cloud[0] * radar_drop[0]
    same_date = date_at[:, None] == date_at[None, :]
    survive_at = temporal_rows(ones_here * survive[:, None, None])[:temporal_size, 0]
    allowed = (survive_at[None, :] == 1) | same_date
    temporal_bias = jnp.where(
        patch_at[:, None] == patch_at[None, :], jnp.where(allowed, 0.0, -1000000000.0), CROSS
    ).astype(F32)
    date_rows = jnp.broadcast_to(date_table[:, None], (dates, patches_here, model))
    date_rows = temporal_rows(date_rows)[:temporal_size]
    cotangent_rows = temporal_rows(cotangent[0].transpose(1, 0, 2))

    spatial_gain = spatial_gain[None]
    temporal_gain = temporal_gain[None]
    lanes = min(width, 256)

    def shape(*dims, dtype=BF):
        return jax.ShapeDtypeStruct(dims, dtype)

    def attend_dims(blocks):
        return (blocks * (width // lanes), lanes // HEAD_DIM * (rows // blocks), rows // blocks)

    layer_flops = 2 * rows * model * width * 4
    where = jnp.stack([here, lax.axis_index("mp"), lax.axis_index("loc")]).astype(jnp.int32)
    if paired:
        half = rows // 2
        blocked = start.reshape(pairs, 2, half_rows, model)
        origins = (blocked[:, 0].reshape(half, model), blocked[:, 1].reshape(half, model))
        spatial_moves = [
            (side, pair * half_rows, (pair * 2 + side) * half_rows, half_rows)
            for side in range(2)
            for pair in range(pairs)
        ]
        temporal_moves = [
            (side, pair * half_rows + eight * 16, (eight * 2 + side) * pairs * 16 + pair * 16, 16)
            for side in range(2)
            for pair in range(pairs)
            for eight in range(eights)
        ]
        half_shapes = (shape(half, model), shape(half, model))
        own, quarter = shape(rows, model // 2), model // 4
        forward_grads = (own, own, shape(rows, 2 * quarter + width))
        temporal_grads = (own, shape(rows, quarter + width))
        back_shapes = (shape(rows, 3 * width // 2), shape(rows, 3 * width // 2))
        backward_grads = (own, shape(rows, model // 2 + 3 * width // 2))
    else:
        origins = (start,)
        spatial_moves = [(0, at * spatial_size, at * spatial_size, spatial_size) for at in range(spatial_blocks)]
        temporal_moves = [(0, at * temporal_size, at * temporal_size, temporal_size) for at in range(temporal_blocks)]
        half_shapes = (shape(rows, model),)
        forward_grads = temporal_grads = backward_grads = (shape(rows, model),)
        back_shapes = (shape(rows, 3 * width),)
    origins, spatial_bias, temporal_bias, date_rows, cotangent_rows = lax.optimization_barrier(
        (origins, spatial_bias, temporal_bias, date_rows, cotangent_rows)
    )

    def plan_of(blocks, moves, weights, grads, sources=0):
        return Plan(blocks, moves, len(origins), weights, paired, sizes["loc"], len(grads), sources)

    plan = plan_of(spatial_blocks, spatial_moves, spatial, forward_grads)
    outs = call(
        functools.partial(spatial_forward_kernel, plan),
        (
            *half_shapes,
            *forward_grads,
            shape(rows, 3 * width),
            shape(*attend_dims(spatial_blocks), dtype=F32),
            shape(rows, width),
        ),
        (where, spatial.offsets, spatial_gain, spatial_bias, cotangent_rows, *origins, *spatial.arrays),
        scratch=(
            pltpu.VMEM((rows, model), BF),
            pltpu.VMEM((rows, model), BF),
            pltpu.VMEM((rows, model), BF),
        ),
        flops=layer_flops,
    )
    partials, outs = outs[: len(origins)], outs[len(origins) :]
    forward, (triple, attend, mixed) = outs[: len(forward_grads)], outs[len(forward_grads) :]
    if paired:
        there, early = call(
            between_kernel,
            (shape(half, model),),
            (origins[1], partials[1], swap(partials[1], "mp"), forward[2]),
            kept=3,
        )
        sources = (origins[0], partials[0], swap(partials[0], "mp"), swap(there, "date"))
        early, temporal.arrays[-1] = fence(early, temporal.arrays[-1])
        early_other = swap(early, "date")
    else:
        spatial_out = (start.astype(F32) + add_over_heads(partials[0], sizes)).astype(BF)
        moved = lax.all_to_all(
            spatial_out.reshape(dates_here, patches, model),
            "date",
            split_axis=1,
            concat_axis=0,
            tiled=True,
        )
        sources = (temporal_rows(moved),)
    plan = plan_of(temporal_blocks, temporal_moves, temporal, temporal_grads, len(sources))
    outs = call(
        functools.partial(temporal_kernel, plan),
        (
            *temporal_grads,
            shape(rows, model),
            shape(rows, width),
            shape(rows, model),
            shape(rows, model),
            *back_shapes,
        ),
        (
            where,
            temporal.offsets,
            temporal_gain,
            temporal_bias,
            date_rows,
            cotangent_rows,
            *sources,
            *temporal.arrays,
        ),
        scratch=(
            pltpu.VMEM((rows, model), BF),
            pltpu.VMEM((rows, 3 * width), BF),
            pltpu.VMEM(attend_dims(temporal_blocks), F32),
            pltpu.VMEM((rows, width), BF),
            pltpu.VMEM((rows, 3 * width), BF),
        ),
        flops=2 * layer_flops,
    )
    middle, outs = outs[: len(temporal_grads)], outs[len(temporal_grads) :]
    (joined, temporal_mixed, temporal_partial, back_part), temporal_triples = outs[:4], outs[4:]
    if paired:
        back_part, early_other = fence(back_part, early_other)

    if sizes["mp"] == 2:
        others = swap(back_part, "mp")
    else:
        others = (lax.psum(back_part.astype(F32), "mp") - back_part.astype(F32)).astype(BF)
    *backs, temporal_last = call(
        functools.partial(norm_back_kernel, temporal_moves, temporal_size),
        half_shapes,
        (temporal_gain, back_part, others, joined, cotangent_rows, temporal_triples[-1]),
        kept=5,
    )
    temporal_triples = (*temporal_triples[:-1], temporal_last)
    if paired:
        back_origins = (backs[0], swap(backs[1], "date"))
        early_there = swap(early_other[:, : 2 * quarter], "mp")
        middle_other = swap(middle[1], "date")
        sums = summed(
            where,
            (forward[1], early_other, early_there, temporal_mixed, middle_other),
            ((0, ((1, quarter), (2, quarter)), (3, 0), (4, quarter), width),),
        )
        temporal_sums = [(sums[0], sums[1])]
        kept = sums[2]
    else:
        back = lax.all_to_all(
            temporal_whole(backs[0]), "date", split_axis=0, concat_axis=1, tiled=True
        )
        back_origins = (back.reshape(rows, model),)
        kept = temporal_last
    outlet = spatial.only((3,))
    plan = plan_of(spatial_blocks, spatial_moves, outlet, backward_grads)
    *outs, kept = call(
        functools.partial(spatial_backward_kernel, plan),
        (*backward_grads, *back_shapes),
        (where, outlet.offsets, triple, attend, kept, *back_origins, *outlet.arrays),
        scratch=(
            pltpu.VMEM((rows, model), BF),
            pltpu.VMEM((rows, width), BF),
            pltpu.VMEM((rows, 3 * width), BF),
        ),
        flops=layer_flops,
        kept=4,
    )
    backward, back_triples = outs[: len(backward_grads)], outs[len(backward_grads) :]
    encoded = (joined.astype(F32) + add_over_heads(temporal_partial, sizes)).astype(BF)
    encoded = temporal_whole(encoded).transpose(1, 0, 2)[None]
    if not paired:
        return (
            encoded,
            whole_grads(forward[0], back_triples[0], backward[0], mixed),
            whole_grads(middle[0], kept, cotangent_rows, temporal_mixed),
        )
    temporal_terms = [*summed_over_loc((*temporal_sums[0], kept))]
    middle_there = swap(middle_other[:, :quarter], "mp")
    kept = backward[0]
    for number, right in enumerate(temporal_triples):
        *sums, kept = summed(
            where,
            (middle[0], middle_other, middle_there, right, swap(right, "date")),
            ((0, ((1, 0), (2, 0)), (3, 0), (4, 0), right.shape[1]),),
            kept=kept,
        )
        if number == 0:
            upstream_own, kept = kept, sums[2]
            first_sums = sums
        else:
            temporal_terms += summed_over_loc((*first_sums[:2], kept))
            temporal_terms += summed_over_loc(sums)
            kept = None
    half = model // 2
    backward_other = swap(backward[1], "date")
    *sums, kept = summed(
        where,
        (
            upstream_own,
            backward_other,
            mixed,
            early_other,
            forward[0],
            early_there,
            back_triples[0],
        ),
        (
            (0, ((1, 0),), (2, 0), (3, 2 * quarter), width),
            (4, ((3, 0), (5, 0)), (6, 0), (1, half), back_triples[0].shape[1]),
        ),
        kept=temporal_terms[6],
    )
    temporal_terms[6] = kept
    spatial_terms = [*summed_over_loc(sums)]
    sums = summed(
        where,
        (forward[0], early_other, early_there, back_triples[1], swap(back_triples[1], "date")),
        ((0, ((1, 0), (2, 0)), (3, 0), (4, 0), back_triples[1].shape[1]),),
    )
    spatial_terms += summed_over_loc(sums)
    (temporal_grads,) = finish(temporal_terms, width)
    spatial_grads, temporal_grads = finish(spatial_terms, width, kept=temporal_grads)
    return (encoded, spatial_grads, temporal_grads)


def solution(mesh):
    in_specs = (
        P(("groups", "loc"), None, "date", None),
        P(("groups", "loc"), None, "date", None),
        P(("groups", "loc"), None),
        P(("groups", "loc"), None),
        P(("groups", "loc"), None),
        P(),
        P(),
        P(),
        P("date", None, "mp"),
        P(),
        P("date", None, "mp"),
        P(("groups", "loc"), "date", None, None),
    )
    out_specs = (
        P(("groups", "loc"), "date", None, None),
        P(("groups", "loc", "date"), None, "mp"),
        P(("groups", "loc", "date"), None, "mp"),
    )
    return jax.shard_map(
        functools.partial(per_device, dict(mesh.shape)),
        mesh=mesh,
        in_specs=in_specs,
        out_specs=out_specs,
        check_vma=False,
    )
```

```python
import functools

import jax
import jax.numpy as jnp
from jax import lax
from jax.experimental import pallas as pl
from jax.experimental.pallas import tpu as pltpu
from jax.sharding import PartitionSpec as P

HEAD_DIM = 64
EPSILON = 1e-05
CROSS = -1e30
BF = jnp.bfloat16
F32 = jnp.float32
NN = (((1,), (0,)), ((), ()))
NT = (((1,), (1,)), ((), ()))
TN = (((0,), (0,)), ((), ()))
VMEM_LIMIT = 56 * 1024 * 1024


def dot(left, right, dims):
    return lax.dot_general(left, right, dims, preferred_element_type=F32)


def statistics(rows):
    values = rows.astype(F32)
    centred = values - jnp.mean(values, -1, keepdims=True)
    inv_scale = lax.rsqrt(jnp.mean(centred * centred, -1, keepdims=True) + EPSILON)
    return centred * inv_scale, inv_scale


class Heads:
    def __init__(self, width):
        self.lanes = min(width, 256)
        self.count = self.lanes // HEAD_DIM
        owner = lax.broadcasted_iota(jnp.int32, (1, self.lanes), 1) // HEAD_DIM
        self.masks = [(owner == head).astype(F32) for head in range(self.count)]

    def stack(self, block):
        return jnp.concatenate([block * mask.astype(BF) for mask in self.masks], axis=0)

    def unstack(self, tall):
        rows = tall.shape[0] // self.count
        total = tall[0:rows] * self.masks[0]
        for head in range(1, self.count):
            total = total + tall[head * rows : (head + 1) * rows] * self.masks[head]
        return total


class Weights:
    def __init__(self, arrays, table, offsets):
        self.arrays, self.table, self.offsets = list(arrays), table, offsets

    def only(self, kinds):
        used = sorted({entry[0] for kind in kinds for entry in self.table[kind]})
        table = {
            kind: [(used.index(array), at, place) for array, at, place in self.table[kind]]
            for kind in kinds
        }
        return Weights([self.arrays[number] for number in used], table, self.offsets)


def views(table, refs, offsets, kind):
    found = []
    for array, at, place in table[kind]:
        part = refs[array].at[at]
        found.append((part, pl.ds(pl.multiple_of(offsets[place], 128), part.shape[0])))
    return found


def rows_times(rows_ref, parts, out_ref, column):
    width = parts[0][0].shape[1]
    step = min(width, 256)
    for at in range(0, width, step):
        total = None
        for part, columns in parts:
            term = dot(rows_ref[:, columns], part[:, at : at + step], NN)
            total = term if total is None else total + term
        out_ref[:, column + at : column + at + step] = total.astype(out_ref.dtype)


def emit_own(rows_ref, out, at, date, loc_count):
    block = rows_ref.shape[1] // (2 * loc_count)
    for loc in range(loc_count):
        first = pl.multiple_of((loc * 2 + date) * block, block)
        out[:, at + loc * block : at + (loc + 1) * block] = rows_ref[:, pl.ds(first, block)]


def emit_half(rows_ref, out, at, date, core, loc_count):
    block = rows_ref.shape[1] // (2 * loc_count)
    for number in range(loc_count // 2):
        loc = core * (loc_count // 2) + number
        first = pl.multiple_of((loc * 2 + date) * block, block)
        out[:, at + number * block : at + (number + 1) * block] = rows_ref[:, pl.ds(first, block)]


def attention(triple_ref, bias_ref, attend_ref, mixed_ref, blocks):
    width = triple_ref.shape[1] // 3
    heads = Heads(width)
    rows = triple_ref.shape[0] // blocks
    groups = width // heads.lanes
    bias = jnp.concatenate([bias_ref[...]] * heads.count, axis=0)
    for block in range(blocks):
        at = slice(block * rows, (block + 1) * rows)
        for group in range(groups):
            lane = group * heads.lanes
            queries = heads.stack(triple_ref[at, lane : lane + heads.lanes])
            keys = triple_ref[at, width + lane : width + lane + heads.lanes]
            values = triple_ref[at, 2 * width + lane : 2 * width + lane + heads.lanes]
            scores = dot(queries, keys, NT) * HEAD_DIM ** (-0.5) + bias
            raised = jnp.exp(scores - jnp.max(scores, -1, keepdims=True))
            attend = raised * (1.0 / jnp.sum(raised, -1, keepdims=True))
            attend_ref[block * groups + group] = attend
            mixed = heads.unstack(dot(attend.astype(BF), values, NN))
            mixed_ref[at, lane : lane + heads.lanes] = mixed.astype(BF)


def attention_back(triple_ref, attend_ref, back_mixed_ref, back_triple_ref, blocks):
    width = triple_ref.shape[1] // 3
    heads = Heads(width)
    rows = triple_ref.shape[0] // blocks
    groups = width // heads.lanes
    for block in range(blocks):
        at = slice(block * rows, (block + 1) * rows)
        for group in range(groups):
            lane = group * heads.lanes
            queries = heads.stack(triple_ref[at, lane : lane + heads.lanes])
            keys = triple_ref[at, width + lane : width + lane + heads.lanes]
            values = triple_ref[at, 2 * width + lane : 2 * width + lane + heads.lanes]
            back = heads.stack(back_mixed_ref[at, lane : lane + heads.lanes])
            attend = attend_ref[block * groups + group]
            back_attend = dot(back, values, NT)
            back_values = dot(attend.astype(BF), back, TN)
            inner = back_attend - jnp.sum(back_attend * attend, -1, keepdims=True)
            back_scores = (attend * inner * HEAD_DIM ** (-0.5)).astype(BF)
            back_queries = heads.unstack(dot(back_scores, keys, NN))
            back_keys = dot(back_scores, queries, TN)
            for number, term in enumerate((back_queries, back_keys, back_values)):
                first = number * width + lane
                back_triple_ref[at, first : first + heads.lanes] = term.astype(BF)


def normalize_into(rows_ref, gain_ref, hidden_ref, blocks):
    rows = rows_ref.shape[0] // blocks
    for block in range(blocks):
        at = slice(block * rows, (block + 1) * rows)
        normed, _ = statistics(rows_ref[at, :])
        hidden_ref[at, :] = (normed * gain_ref[...]).astype(BF)


def spatial_forward_kernel(plan, where, offsets, gain, bias, cotangent, *refs):
    sources, refs = refs[: plan.origins], refs[plan.origins :]
    arrays, refs = refs[: plan.arrays], refs[plan.arrays :]
    partials, refs = refs[: plan.origins], refs[plan.origins :]
    grads, refs = refs[: plan.grads], refs[plan.grads :]
    triple, attend, mixed, start, hidden, whole = refs
    for source, at, to, size in plan.moves:
        start[to : to + size, :] = sources[source][at : at + size, :]
    normalize_into(start, gain, hidden, plan.blocks)
    width = mixed.shape[1]
    for kind in range(3):
        rows_times(hidden, views(plan.table, arrays, offsets, kind), triple, kind * width)
    attention(triple, bias, attend, mixed, plan.blocks)
    for part, features in views(plan.table, arrays, offsets, 3):
        whole[:, features] = dot(mixed[...], part[...], NT).astype(BF)
    for source, at, to, size in plan.moves:
        partials[source][at : at + size, :] = whole[to : to + size, :]
    if plan.paired:
        own_hidden, own_cotangent, sent = grads
        half = hidden.shape[1] // 4
        here, core = where[0], where[1]
        emit_own(hidden, own_hidden, 0, here, plan.locs)
        emit_own(cotangent, own_cotangent, 0, here, plan.locs)
        emit_half(hidden, sent, 0, 1 - here, core, plan.locs)
        emit_half(cotangent, sent, half, 1 - here, core, plan.locs)
        sent[:, 2 * half :] = mixed[...]
    else:
        grads[0][...] = hidden[...]


def between_kernel(start, here, there, kept, out, passed):
    total = here[...].astype(F32) + there[...].astype(F32)
    out[...] = (start[...].astype(F32) + total).astype(BF)


def temporal_kernel(plan, where, offsets, gain, bias, date_rows, cotangent, *refs):
    sources, refs = refs[: plan.sources], refs[plan.sources :]
    arrays, refs = refs[: plan.arrays], refs[plan.arrays :]
    grads, refs = refs[: plan.grads], refs[plan.grads :]
    joined, mixed, partial, back_part = refs[:4]
    back_triples, (hidden, triple, attend, back_mixed, back_triple) = refs[4:-5], refs[-5:]
    rows = date_rows.shape[0]
    for source, at, to, size in plan.moves:
        if source == 0 and plan.sources > 1:
            total = sources[1][at : at + size, :].astype(F32) + sources[2][at : at + size, :].astype(F32)
            out = (sources[0][at : at + size, :].astype(F32) + total).astype(BF)
        else:
            out = sources[-1][at : at + size, :]
        dated = out.astype(F32) + date_rows[to % rows : to % rows + size, :].astype(F32)
        joined[to : to + size, :] = dated.astype(BF)
    normalize_into(joined, gain, hidden, plan.blocks)
    width = mixed.shape[1]
    for kind in range(3):
        rows_times(hidden, views(plan.table, arrays, offsets, kind), triple, kind * width)
    outlet = views(plan.table, arrays, offsets, 3)
    rows_times(cotangent, outlet, back_mixed, 0)
    attention(triple, bias, attend, mixed, plan.blocks)
    for part, features in outlet:
        partial[:, features] = dot(mixed[...], part[...], NT).astype(BF)
    if plan.paired:
        own_hidden, sent = grads
        half = hidden.shape[1] // 4
        emit_own(hidden, own_hidden, 0, where[0], plan.locs)
        emit_half(hidden, sent, 0, 1 - where[0], where[1], plan.locs)
        sent[:, half:] = mixed[...]
    else:
        grads[0][...] = hidden[...]
    attention_back(triple, attend, back_mixed, back_triple, plan.blocks)
    intakes = [views(plan.table, arrays, offsets, kind) for kind in range(3)]
    for entries in zip(*intakes):
        total = None
        for kind, (part, features) in enumerate(entries):
            term = dot(back_triple[:, kind * width : (kind + 1) * width], part[...], NT)
            total = term if total is None else total + term
        back_part[:, features] = total.astype(BF)
    split_columns(back_triple, back_triples)


def split_columns(whole, outs):
    at = 0
    for out in outs:
        out[...] = whole[:, at : at + out.shape[1]]
        at += out.shape[1]


def norm_back_kernel(moves, step, gain, here, there, joined, cotangent, kept, *outs):
    for at in range(0, joined.shape[0], step):
        span_here = slice(at, at + step)
        normed, inv_scale = statistics(joined[span_here, :])
        total = here[span_here, :].astype(F32) + there[span_here, :].astype(F32)
        scaled = total * gain[...]
        inner = (
            scaled
            - jnp.mean(scaled, -1, keepdims=True)
            - normed * jnp.mean(scaled * normed, -1, keepdims=True)
        )
        back = (cotangent[span_here, :].astype(F32) + inv_scale * inner).astype(BF)
        for target, to, first, size in moves:
            if at <= first < at + step:
                outs[target][to : to + size, :] = back[first - at : first - at + size]


def spatial_backward_kernel(plan, where, offsets, triple, attend, kept, *refs):
    sources, refs = refs[: plan.origins], refs[plan.origins :]
    arrays, refs = refs[: plan.arrays], refs[plan.arrays :]
    grads, refs = refs[: plan.grads], refs[plan.grads :]
    back_triples, (upstream, back_mixed, back_triple) = refs[:-4], refs[-3:]
    for source, at, to, size in plan.moves:
        upstream[to : to + size, :] = sources[source][at : at + size, :]
    if plan.paired:
        emit_own(upstream, grads[0], 0, where[0], plan.locs)
        emit_own(upstream, grads[1], 0, 1 - where[0], plan.locs)
    else:
        grads[0][...] = upstream[...]
    rows_times(upstream, views(plan.table, arrays, offsets, 3), back_mixed, 0)
    attention_back(triple, attend, back_mixed, back_triple, plan.blocks)
    split_columns(back_triple, back_triples)
    if plan.paired:
        half = upstream.shape[1] // 2
        grads[1][:, half:] = back_triple[:, : grads[1].shape[1] - half]


def grad_kernel(products, count, where, *refs):
    sent, far, near, other = refs[-4:]
    core, loc = where[1], where[2]
    block = near.shape[0]
    beside = loc + 1 - 2 * lax.rem(loc, 2)
    places = (lax.rem(beside + 2, 4), beside, lax.rem(loc + 2, 4), loc)
    column = 0
    for left, others, (right, right_at), (right_other, other_at), width in products:
        left, right, right_other = refs[left], refs[right], refs[right_other]
        lanes = other.shape[1] // len(others)
        for number, (source, at) in enumerate(others):
            to = 0
            if len(others) > 1:
                to = pl.multiple_of((core if number == 0 else 1 - core) * lanes, lanes)
            other[:, pl.ds(to, lanes)] = refs[source][:, at : at + lanes]
        for number, place in enumerate(places):
            columns = pl.ds(pl.multiple_of(place * block, block), block)
            for first in range(0, width, 256):
                lane = slice(column + first, column + first + 256)
                here = right[:, right_at + first : right_at + first + 256]
                there = right_other[:, other_at + first : other_at + first + 256]
                total = dot(left[:, columns], here, TN) + dot(other[:, columns], there, TN)
                if number < 2:
                    sent[number * block : (number + 1) * block, lane] = total.astype(BF)
                elif number == 2:
                    far[:, lane] = total
                else:
                    near[:, lane] = total
        column += width


def finish_kernel(*refs):
    out = refs[-1]
    block = out.shape[0]
    column = 0
    for near, beside, far in zip(refs[0:-1:3], refs[1:-1:3], refs[2:-1:3]):
        for at in range(0, near.shape[1], 256):
            lane = slice(at, at + 256)
            total = near[:, lane] + beside[block:, lane].astype(F32) + far[:, lane].astype(F32)
            kind, first = (3 * out.shape[2] + column + at) // out.shape[2] % 4, (column + at) % out.shape[2]
            out[:, kind, first : first + 256] = total
        column += near.shape[1]


def finish_last_kernel(kept, *refs):
    finish_kernel(*refs[:-1])


def fence_kernel(*refs):
    pass


def grad_after_kernel(products, count, passed, where, *refs):
    args, rest = refs[:count], refs[count + passed :]
    grad_kernel(products, count, where, *args, *rest[:3], rest[-1])


class Plan:
    def __init__(self, blocks, moves, origins, weights, paired, locs, grads, sources=0):
        self.blocks, self.moves, self.origins = blocks, moves, origins
        self.arrays, self.table = len(weights.arrays), weights.table
        self.paired, self.locs, self.grads, self.sources = paired, locs, grads, sources


def call(body, outs, args, scratch=(), flops=0, kept=()):
    smem = pl.BlockSpec(memory_space=pltpu.SMEM)
    vmem = pl.BlockSpec(memory_space=pltpu.VMEM)
    specs = [smem if arg.dtype == jnp.int32 else vmem for arg in args]
    out_specs = [vmem] * len(outs)
    aliases = {}
    outs = list(outs)
    moved = sum(arg.size * arg.dtype.itemsize for arg in args)
    moved = moved + sum(out.size * out.dtype.itemsize for out in outs)
    for number in kept:
        specs[number] = pl.BlockSpec(memory_space=pl.ANY)
        out_specs.append(pl.BlockSpec(memory_space=pl.ANY))
        outs.append(jax.ShapeDtypeStruct(args[number].shape, args[number].dtype))
        aliases[number] = len(outs) - 1
    return pl.pallas_call(
        body,
        out_shape=outs,
        in_specs=specs,
        out_specs=out_specs,
        scratch_shapes=list(scratch),
        input_output_aliases=aliases,
        compiler_params=pltpu.CompilerParams(vmem_limit_bytes=VMEM_LIMIT),
        cost_estimate=pl.CostEstimate(flops=flops, bytes_accessed=moved, transcendentals=0),
    )(*args)


def fence(*arrays):
    anywhere = [pl.BlockSpec(memory_space=pl.ANY)] * len(arrays)
    return pl.pallas_call(
        fence_kernel,
        out_shape=[jax.ShapeDtypeStruct(array.shape, array.dtype) for array in arrays],
        in_specs=anywhere,
        out_specs=anywhere,
        input_output_aliases={number: number for number in range(len(arrays))},
    )(*arrays)


def swap(array, axis):
    return lax.ppermute(array, axis, [(0, 1), (1, 0)])


PAIRS = [(0, 1), (1, 0), (2, 3), (3, 2)]
APART = [(0, 2), (1, 3), (2, 0), (3, 1)]


def quarter_of(weights, number):
    rows = weights.shape[0]
    return lax.dynamic_slice_in_dim(weights, number * (rows // 4), rows // 4, 0)


def by_kind(weights):
    return weights.transpose(1, 0, 2)


def whole_weights(weights):
    whole = lax.all_gather(weights.transpose(1, 0, 2), "date", axis=1, tiled=True)
    return Weights([whole], {kind: [(0, kind, 0)] for kind in range(4)}, jnp.zeros((1,), jnp.int32))


def quarters(rows):
    side, here = lax.axis_index("groups"), lax.axis_index("date")
    even = lax.axis_index("loc") % 2
    numbers = [side * 2 + even, (1 - side) * 2 + even, side * 2 + 1 - even, (1 - side) * 2 + 1 - even]
    offsets = [here * rows] + [(1 - here) * rows + number * (rows // 4) for number in numbers]
    return numbers, jnp.stack(offsets).astype(jnp.int32)


def weights_of(arrays, offsets):
    table = {kind: [(number, kind, number) for number in range(5)] for kind in range(4)}
    return Weights([by_kind(array) for array in arrays], table, offsets)


def gather_first(weights, last, numbers, offsets):
    first = swap(quarter_of(weights, numbers[0]), "date")
    last = swap(last, "date")
    arrays = [weights, first, swap(first, "groups"), lax.ppermute(first, "loc", PAIRS), last]
    return weights_of(arrays, offsets)


def gather_second(weights, first, offsets):
    group, loc = swap(first, "groups"), lax.ppermute(first, "loc", PAIRS)
    middle = first.shape[0] // 2
    far = (swap(loc[:middle], "groups"), lax.ppermute(group[middle:], "loc", PAIRS))
    return weights_of([weights, first, group, loc, jnp.concatenate(far, axis=0)], offsets)


def add_over_heads(partial, sizes):
    if sizes["mp"] == 2:
        return partial.astype(F32) + swap(partial, "mp").astype(F32)
    return lax.psum(partial.astype(F32), "mp")


def whole_grads(hidden, back_triple, upstream, mixed):
    width = mixed.shape[1]
    intake = dot(hidden, back_triple, TN)
    outlet = dot(upstream, mixed, TN)
    whole = jnp.concatenate([intake, outlet], axis=1).reshape(-1, 4, width)
    part = lax.psum_scatter(whole.astype(BF), ("loc", "date"), scatter_dimension=0, tiled=True)
    return part.astype(F32)


def summed(where, args, products, kept=()):
    rows, columns = args[products[0][0]].shape
    block, width = columns // 4, sum(product[-1] for product in products)
    return call(
        functools.partial(grad_after_kernel, products, len(args), len(kept)),
        (
            jax.ShapeDtypeStruct((2 * block, width), BF),
            jax.ShapeDtypeStruct((block, width), F32),
            jax.ShapeDtypeStruct((block, width), F32),
        ),
        (where, *args, *kept),
        scratch=(pltpu.VMEM((rows, columns), BF),),
        flops=4 * rows * columns * width,
        kept=tuple(range(1 + len(args), 1 + len(args) + len(kept))),
    )


def summed_over_loc(outs):
    sent, far, near = outs[:3]
    beside = lax.ppermute(sent, "loc", PAIRS)
    far = (far + beside[: far.shape[0]].astype(F32)).astype(BF)
    return near, beside, lax.ppermute(far, "loc", APART)


def finish(terms, width, kept=None):
    out = jax.ShapeDtypeStruct((terms[0].shape[0], 4, width), F32)
    if kept is None:
        return call(finish_kernel, (out,), terms)
    return call(finish_last_kernel, (out,), (kept, *terms), kept=(0,))


def per_device(
    sizes,
    optical,
    radar,
    cloud,
    radar_drop,
    keep_index,
    place_table,
    date_table,
    spatial_gain,
    spatial_weights,
    temporal_gain,
    temporal_weights,
    cotangent,
):
    _, patches, dates_here, model = optical.shape
    patches_here, dates = cotangent.shape[1:3]
    width = spatial_weights.shape[2]
    rows = patches * dates_here
    here = lax.axis_index("date")
    first = here * dates_here
    paired = sizes["groups"] == 2 and sizes["loc"] == 4 and sizes["date"] == 2 and sizes["mp"] == 2
    paired = paired and dates_here % 2 == 0 and patches_here % 8 == 0 and model % 1024 == 0
    if paired:
        numbers, offsets = quarters(spatial_weights.shape[0])
        last_sent = quarter_of(spatial_weights, numbers[3])
    else:
        spatial, temporal = whole_weights(spatial_weights), whole_weights(temporal_weights)

    if paired:
        pairs, eights = dates_here // 2, patches_here // 8
        spatial_blocks, temporal_blocks = pairs, eights
        half_rows = eights * 16

        def own_first(array, axis):
            return jnp.where(here == 0, array, jnp.flip(array, axis))

        def spatial_rows(array):
            array = array.reshape(pairs, 2, 2, eights, 8, -1)
            return own_first(array, 2).transpose(0, 2, 3, 1, 4, 5).reshape(rows, -1)

        def temporal_rows(array):
            array = array.reshape(2, pairs, 2, eights, 8, -1)
            return own_first(array, 0).transpose(3, 0, 1, 2, 4, 5).reshape(rows, -1)

        def temporal_whole(array):
            array = array.reshape(eights, 2, pairs, 2, 8, -1).transpose(1, 2, 3, 0, 4, 5)
            return own_first(array, 0).reshape(dates, patches_here, -1)

    else:
        spatial_blocks = 1 if rows <= 192 else dates_here
        temporal_blocks = patches_here // 8 if patches_here % 8 == 0 else 1

        def spatial_rows(array):
            return array.reshape(rows, -1)

        def temporal_rows(array):
            array = array.reshape(dates, temporal_blocks, patches_here // temporal_blocks, -1)
            return array.transpose(1, 0, 2, 3).reshape(rows, -1)

        def temporal_whole(array):
            array = array.reshape(temporal_blocks, dates, patches_here // temporal_blocks, -1)
            return array.transpose(1, 0, 2, 3).reshape(dates, patches_here, -1)

    cloud_here = lax.dynamic_slice_in_dim(cloud, first, dates_here, 1)[0]
    drop_here = lax.dynamic_slice_in_dim(radar_drop, first, dates_here, 1)[0]
    optical_keep = (1 - cloud_here).astype(F32)[:, None, None]
    radar_keep = (1 - drop_here).astype(F32)[:, None, None]
    places = jnp.take(place_table, keep_index[0], axis=0).astype(F32)[None]
    start = (
        optical[0].transpose(1, 0, 2).astype(F32) * optical_keep
        + radar[0].transpose(1, 0, 2).astype(F32) * radar_keep
        + places
    ).astype(BF)
    start = spatial_rows(start)

    dates_at = jnp.arange(dates, dtype=jnp.int32)
    patches_at = jnp.arange(patches_here, dtype=jnp.int32)
    ones_here = jnp.ones((dates, patches_here, 1), jnp.int32)
    temporal_size = rows // temporal_blocks
    date_at = temporal_rows(ones_here * dates_at[:, None, None])[:temporal_size, 0]
    patch_at = temporal_rows(ones_here * patches_at[None, :, None])[:temporal_size, 0]
    spatial_size = rows // spatial_blocks
    spatial_date = jnp.ones((dates_here, patches, 1), jnp.int32) * dates_at[:dates_here, None, None]
    spatial_date = spatial_rows(spatial_date)[:spatial_size, 0]
    spatial_bias = jnp.where(spatial_date[:, None] == spatial_date[None, :], 0.0, CROSS).astype(F32)
    survive = 1 - cloud[0] * radar_drop[0]
    same_date = date_at[:, None] == date_at[None, :]
    survive_at = temporal_rows(ones_here * survive[:, None, None])[:temporal_size, 0]
    allowed = (survive_at[None, :] == 1) | same_date
    temporal_bias = jnp.where(
        patch_at[:, None] == patch_at[None, :], jnp.where(allowed, 0.0, -1000000000.0), CROSS
    ).astype(F32)
    date_rows = jnp.broadcast_to(date_table[:, None], (dates, patches_here, model))
    date_rows = temporal_rows(date_rows)[:temporal_size]
    cotangent_rows = temporal_rows(cotangent[0].transpose(1, 0, 2))

    spatial_gain = spatial_gain[None]
    temporal_gain = temporal_gain[None]
    lanes = min(width, 256)

    def shape(*dims, dtype=BF):
        return jax.ShapeDtypeStruct(dims, dtype)

    def attend_dims(blocks):
        return (blocks * (width // lanes), lanes // HEAD_DIM * (rows // blocks), rows // blocks)

    layer_flops = 2 * rows * model * width * 4
    where = jnp.stack([here, lax.axis_index("mp"), lax.axis_index("loc")]).astype(jnp.int32)
    if paired:
        half = rows // 2
        blocked = start.reshape(pairs, 2, half_rows, model)
        origins = (blocked[:, 0].reshape(half, model), blocked[:, 1].reshape(half, model))
        spatial_moves = [
            (side, pair * half_rows, (pair * 2 + side) * half_rows, half_rows)
            for side in range(2)
            for pair in range(pairs)
        ]
        temporal_moves = [
            (side, pair * half_rows + eight * 16, (eight * 2 + side) * pairs * 16 + pair * 16, 16)
            for side in range(2)
            for pair in range(pairs)
            for eight in range(eights)
        ]
        half_shapes = (shape(half, model), shape(half, model))
        own, quarter = shape(rows, model // 2), model // 4
        forward_grads = (own, own, shape(rows, 2 * quarter + width))
        temporal_grads = (own, shape(rows, quarter + width))
        back_shapes = (shape(rows, 3 * width // 2), shape(rows, 3 * width // 2))
        backward_grads = (own, shape(rows, model // 2 + 3 * width // 2))
    else:
        origins = (start,)
        spatial_moves = [(0, at * spatial_size, at * spatial_size, spatial_size) for at in range(spatial_blocks)]
        temporal_moves = [(0, at * temporal_size, at * temporal_size, temporal_size) for at in range(temporal_blocks)]
        half_shapes = (shape(rows, model),)
        forward_grads = temporal_grads = backward_grads = (shape(rows, model),)
        back_shapes = (shape(rows, 3 * width),)
    origins, spatial_bias, temporal_bias, date_rows, cotangent_rows = lax.optimization_barrier(
        (origins, spatial_bias, temporal_bias, date_rows, cotangent_rows)
    )

    if paired:
        sent = quarter_of(temporal_weights, numbers[0])
        last_sent, sent, far_origin = fence(last_sent, sent, origins[1])
        origins = (origins[0], far_origin)
        spatial = gather_first(spatial_weights, last_sent, numbers, offsets)
        temporal_first = swap(sent, "date")

    def plan_of(blocks, moves, weights, grads, sources=0):
        return Plan(blocks, moves, len(origins), weights, paired, sizes["loc"], len(grads), sources)

    plan = plan_of(spatial_blocks, spatial_moves, spatial, forward_grads)
    outs = call(
        functools.partial(spatial_forward_kernel, plan),
        (
            *half_shapes,
            *forward_grads,
            shape(rows, 3 * width),
            shape(*attend_dims(spatial_blocks), dtype=F32),
            shape(rows, width),
        ),
        (where, spatial.offsets, spatial_gain, spatial_bias, cotangent_rows, *origins, *spatial.arrays),
        scratch=(
            pltpu.VMEM((rows, model), BF),
            pltpu.VMEM((rows, model), BF),
            pltpu.VMEM((rows, model), BF),
        ),
        flops=layer_flops,
    )
    partials, outs = outs[: len(origins)], outs[len(origins) :]
    forward, (triple, attend, mixed) = outs[: len(forward_grads)], outs[len(forward_grads) :]
    if paired:
        temporal_first, kept = fence(temporal_first, partials[1])
        partials = (partials[0], kept)
        temporal = gather_second(temporal_weights, temporal_first, offsets)
        there, early = call(
            between_kernel,
            (shape(half, model),),
            (origins[1], partials[1], swap(partials[1], "mp"), forward[2]),
            kept=(3,),
        )
        early, there = fence(early, swap(there, "date"))
        sources = (origins[0], partials[0], swap(partials[0], "mp"), there)
        early_other = swap(early, "date")
    else:
        spatial_out = (start.astype(F32) + add_over_heads(partials[0], sizes)).astype(BF)
        moved = lax.all_to_all(
            spatial_out.reshape(dates_here, patches, model),
            "date",
            split_axis=1,
            concat_axis=0,
            tiled=True,
        )
        sources = (temporal_rows(moved),)
    plan = plan_of(temporal_blocks, temporal_moves, temporal, temporal_grads, len(sources))
    outs = call(
        functools.partial(temporal_kernel, plan),
        (
            *temporal_grads,
            shape(rows, model),
            shape(rows, width),
            shape(rows, model),
            shape(rows, model),
            *back_shapes,
        ),
        (
            where,
            temporal.offsets,
            temporal_gain,
            temporal_bias,
            date_rows,
            cotangent_rows,
            *sources,
            *temporal.arrays,
        ),
        scratch=(
            pltpu.VMEM((rows, model), BF),
            pltpu.VMEM((rows, 3 * width), BF),
            pltpu.VMEM(attend_dims(temporal_blocks), F32),
            pltpu.VMEM((rows, width), BF),
            pltpu.VMEM((rows, 3 * width), BF),
        ),
        flops=2 * layer_flops,
    )
    middle, outs = outs[: len(temporal_grads)], outs[len(temporal_grads) :]
    (joined, temporal_mixed, temporal_partial, back_part), temporal_triples = outs[:4], outs[4:]
    if paired:
        back_part, early_other = fence(back_part, early_other)

    if sizes["mp"] == 2:
        others = swap(back_part, "mp")
    else:
        others = (lax.psum(back_part.astype(F32), "mp") - back_part.astype(F32)).astype(BF)
    *backs, temporal_last = call(
        functools.partial(norm_back_kernel, temporal_moves, temporal_size),
        half_shapes,
        (temporal_gain, back_part, others, joined, cotangent_rows, temporal_triples[-1]),
        kept=(5,),
    )
    temporal_triples = (*temporal_triples[:-1], temporal_last)
    if paired:
        back_origins = (backs[0], swap(backs[1], "date"))
        early_there = swap(early_other[:, : 2 * quarter], "mp")
        middle_other = swap(middle[1], "date")
        sums = summed(
            where,
            (forward[1], early_other, early_there, temporal_mixed, middle_other),
            ((0, ((1, quarter), (2, quarter)), (3, 0), (4, quarter), width),),
        )
        temporal_sums = [(sums[0], sums[1])]
        kept = sums[2]
    else:
        back = lax.all_to_all(
            temporal_whole(backs[0]), "date", split_axis=0, concat_axis=1, tiled=True
        )
        back_origins = (back.reshape(rows, model),)
        kept = temporal_last
    outlet = spatial.only((3,))
    plan = plan_of(spatial_blocks, spatial_moves, outlet, backward_grads)
    *outs, kept = call(
        functools.partial(spatial_backward_kernel, plan),
        (*backward_grads, *back_shapes),
        (where, outlet.offsets, triple, attend, kept, *back_origins, *outlet.arrays),
        scratch=(
            pltpu.VMEM((rows, model), BF),
            pltpu.VMEM((rows, width), BF),
            pltpu.VMEM((rows, 3 * width), BF),
        ),
        flops=layer_flops,
        kept=(4,),
    )
    backward, back_triples = outs[: len(backward_grads)], outs[len(backward_grads) :]
    encoded = (joined.astype(F32) + add_over_heads(temporal_partial, sizes)).astype(BF)
    encoded = temporal_whole(encoded).transpose(1, 0, 2)[None]
    if not paired:
        return (
            encoded,
            whole_grads(forward[0], back_triples[0], backward[0], mixed),
            whole_grads(middle[0], kept, cotangent_rows, temporal_mixed),
        )
    temporal_terms = [*summed_over_loc((*temporal_sums[0], kept))]
    middle_there = swap(middle_other[:, :quarter], "mp")
    others = [swap(array, "date") for array in temporal_triples]
    *sums, upstream_own, temporal_terms[1] = summed(
        where,
        (middle[0], middle_other, middle_there, *temporal_triples, *others),
        tuple(
            (0, ((1, 0), (2, 0)), (3 + number, 0), (5 + number, 0), temporal_triples[number].shape[1])
            for number in range(2)
        ),
        kept=(backward[0], temporal_terms[1]),
    )
    temporal_terms += summed_over_loc(sums)
    half = model // 2
    backward_other = swap(backward[1], "date")
    *sums, kept = summed(
        where,
        (
            upstream_own,
            backward_other,
            mixed,
            early_other,
            forward[0],
            early_there,
            back_triples[0],
        ),
        (
            (0, ((1, 0),), (2, 0), (3, 2 * quarter), width),
            (4, ((3, 0), (5, 0)), (6, 0), (1, half), back_triples[0].shape[1]),
        ),
        kept=(temporal_terms[3],),
    )
    temporal_terms[3] = kept
    spatial_terms = [*summed_over_loc(sums)]
    sums = summed(
        where,
        (forward[0], early_other, early_there, back_triples[1], swap(back_triples[1], "date")),
        ((0, ((1, 0), (2, 0)), (3, 0), (4, 0), back_triples[1].shape[1]),),
    )
    spatial_terms += summed_over_loc(sums)
    (temporal_grads,) = finish(temporal_terms, width)
    spatial_grads, temporal_grads = finish(spatial_terms, width, kept=temporal_grads)
    return (encoded, spatial_grads, temporal_grads)


def solution(mesh):
    in_specs = (
        P(("groups", "loc"), None, "date", None),
        P(("groups", "loc"), None, "date", None),
        P(("groups", "loc"), None),
        P(("groups", "loc"), None),
        P(("groups", "loc"), None),
        P(),
        P(),
        P(),
        P("date", None, "mp"),
        P(),
        P("date", None, "mp"),
        P(("groups", "loc"), "date", None, None),
    )
    out_specs = (
        P(("groups", "loc"), "date", None, None),
        P(("groups", "loc", "date"), None, "mp"),
        P(("groups", "loc", "date"), None, "mp"),
    )
    return jax.shard_map(
        functools.partial(per_device, dict(mesh.shape)),
        mesh=mesh,
        in_specs=in_specs,
        out_specs=out_specs,
        check_vma=False,
    )
```

```python
import functools

import jax
import jax.numpy as jnp
from jax import lax
from jax.experimental import pallas as pl
from jax.experimental.pallas import tpu as pltpu
from jax.sharding import PartitionSpec as P

HEAD_DIM = 64
EPSILON = 1e-05
CROSS = -1e30
BF = jnp.bfloat16
F32 = jnp.float32
NN = (((1,), (0,)), ((), ()))
NT = (((1,), (1,)), ((), ()))
TN = (((0,), (0,)), ((), ()))
VMEM_LIMIT = 56 * 1024 * 1024


def dot(left, right, dims):
    return lax.dot_general(left, right, dims, preferred_element_type=F32)


def statistics(rows):
    values = rows.astype(F32)
    centred = values - jnp.mean(values, -1, keepdims=True)
    inv_scale = lax.rsqrt(jnp.mean(centred * centred, -1, keepdims=True) + EPSILON)
    return centred * inv_scale, inv_scale


class Heads:
    def __init__(self, width):
        self.lanes = min(width, 256)
        self.count = self.lanes // HEAD_DIM
        owner = lax.broadcasted_iota(jnp.int32, (1, self.lanes), 1) // HEAD_DIM
        self.masks = [(owner == head).astype(F32) for head in range(self.count)]

    def stack(self, block):
        return jnp.concatenate([block * mask.astype(BF) for mask in self.masks], axis=0)

    def unstack(self, tall):
        rows = tall.shape[0] // self.count
        total = tall[0:rows] * self.masks[0]
        for head in range(1, self.count):
            total = total + tall[head * rows : (head + 1) * rows] * self.masks[head]
        return total


class Weights:
    def __init__(self, arrays, table):
        self.arrays, self.table = list(arrays), table

    def only(self, kinds):
        used = sorted({entry[0] for kind in kinds for entry in self.table[kind]})
        table = {
            kind: [(used.index(array), at, place) for array, at, place in self.table[kind]]
            for kind in kinds
        }
        return Weights([self.arrays[number] for number in used], table)


def first_row(number, rows, where):
    if number == 0:
        return where[0] * rows
    side, even = where[3], lax.rem(where[2], 2)
    side = side if number in (1, 3) else 1 - side
    even = even if number in (1, 2) else 1 - even
    return (1 - where[0]) * rows + (side * 2 + even) * (rows // 4)


def views(plan, refs, where, kind):
    found = []
    for array, at, place in plan.table[kind]:
        part = refs[array].at[at]
        if plan.paired:
            first = pl.multiple_of(first_row(place, refs[plan.table[kind][0][0]].shape[1], where), 128)
            found.append((part, pl.ds(first, part.shape[0])))
        else:
            found.append((part, slice(None)))
    return found


def rows_times(rows_ref, parts, out_ref, column):
    width = parts[0][0].shape[1]
    step = min(width, 256)
    for at in range(0, width, step):
        total = None
        for part, columns in parts:
            term = dot(rows_ref[:, columns], part[:, at : at + step], NN)
            total = term if total is None else total + term
        out_ref[:, column + at : column + at + step] = total.astype(out_ref.dtype)


def emit_own(rows_ref, out, at, date, loc_count):
    block = rows_ref.shape[1] // (2 * loc_count)
    for loc in range(loc_count):
        first = pl.multiple_of((loc * 2 + date) * block, block)
        out[:, at + loc * block : at + (loc + 1) * block] = rows_ref[:, pl.ds(first, block)]


def emit_half(rows_ref, out, at, date, core, loc_count):
    block = rows_ref.shape[1] // (2 * loc_count)
    for number in range(loc_count // 2):
        loc = core * (loc_count // 2) + number
        first = pl.multiple_of((loc * 2 + date) * block, block)
        out[:, at + number * block : at + (number + 1) * block] = rows_ref[:, pl.ds(first, block)]


def groups_of(size, spans, modulus, axis):
    shape = (size, 1) if axis == 0 else (1, size)
    return lax.rem(lax.broadcasted_iota(jnp.int32, shape, axis) // spans, modulus)


def spatial_bias(plan, size):
    query, key = (groups_of(size, *plan.date_of, axis) for axis in range(2))
    return jnp.where(query == key, 0.0, CROSS).astype(F32)


def temporal_bias(plan, size, survive):
    query, key = (groups_of(size, *plan.patch_of, axis) for axis in range(2))
    query_date, key_date = (groups_of(size, *plan.date_of, axis) for axis in range(2))
    allowed = (survive[...] == 1.0) | (query_date == key_date)
    return jnp.where(query == key, jnp.where(allowed, 0.0, -1000000000.0), CROSS).astype(F32)


def attention(triple_ref, bias, attend_ref, mixed_ref, blocks):
    width = triple_ref.shape[1] // 3
    heads = Heads(width)
    rows = triple_ref.shape[0] // blocks
    groups = width // heads.lanes
    bias = jnp.concatenate([bias] * heads.count, axis=0)
    for block in range(blocks):
        at = slice(block * rows, (block + 1) * rows)
        for group in range(groups):
            lane = group * heads.lanes
            queries = heads.stack(triple_ref[at, lane : lane + heads.lanes])
            keys = triple_ref[at, width + lane : width + lane + heads.lanes]
            values = triple_ref[at, 2 * width + lane : 2 * width + lane + heads.lanes]
            scores = dot(queries, keys, NT) * HEAD_DIM ** (-0.5) + bias
            raised = jnp.exp(scores - jnp.max(scores, -1, keepdims=True))
            attend = raised * (1.0 / jnp.sum(raised, -1, keepdims=True))
            attend_ref[block * groups + group] = attend
            mixed = heads.unstack(dot(attend.astype(BF), values, NN))
            mixed_ref[at, lane : lane + heads.lanes] = mixed.astype(BF)


def attention_back(triple_ref, attend_ref, back_mixed_ref, back_triple_ref, blocks):
    width = triple_ref.shape[1] // 3
    heads = Heads(width)
    rows = triple_ref.shape[0] // blocks
    groups = width // heads.lanes
    for block in range(blocks):
        at = slice(block * rows, (block + 1) * rows)
        for group in range(groups):
            lane = group * heads.lanes
            queries = heads.stack(triple_ref[at, lane : lane + heads.lanes])
            keys = triple_ref[at, width + lane : width + lane + heads.lanes]
            values = triple_ref[at, 2 * width + lane : 2 * width + lane + heads.lanes]
            back = heads.stack(back_mixed_ref[at, lane : lane + heads.lanes])
            attend = attend_ref[block * groups + group]
            back_attend = dot(back, values, NT)
            back_values = dot(attend.astype(BF), back, TN)
            inner = back_attend - jnp.sum(back_attend * attend, -1, keepdims=True)
            back_scores = (attend * inner * HEAD_DIM ** (-0.5)).astype(BF)
            back_queries = heads.unstack(dot(back_scores, keys, NN))
            back_keys = dot(back_scores, queries, TN)
            for number, term in enumerate((back_queries, back_keys, back_values)):
                first = number * width + lane
                back_triple_ref[at, first : first + heads.lanes] = term.astype(BF)


def normalize_into(rows_ref, gain_ref, hidden_ref, blocks):
    rows = rows_ref.shape[0] // blocks
    for block in range(blocks):
        at = slice(block * rows, (block + 1) * rows)
        normed, _ = statistics(rows_ref[at, :])
        hidden_ref[at, :] = (normed * gain_ref[...]).astype(BF)


def spatial_forward_kernel(plan, where, gain, cotangent, *refs):
    sources, refs = refs[: plan.origins], refs[plan.origins :]
    arrays, refs = refs[: plan.arrays], refs[plan.arrays :]
    partials, refs = refs[: plan.origins], refs[plan.origins :]
    grads, refs = refs[: plan.grads], refs[plan.grads :]
    triple, attend, mixed, start, hidden, whole = refs
    for source, at, to, size in plan.moves:
        start[to : to + size, :] = sources[source][at : at + size, :]
    normalize_into(start, gain, hidden, plan.blocks)
    width = mixed.shape[1]
    for kind in range(3):
        rows_times(hidden, views(plan, arrays, where, kind), triple, kind * width)
    bias = spatial_bias(plan, start.shape[0] // plan.blocks)
    attention(triple, bias, attend, mixed, plan.blocks)
    for part, features in views(plan, arrays, where, 3):
        whole[:, features] = dot(mixed[...], part[...], NT).astype(BF)
    for source, at, to, size in plan.moves:
        partials[source][at : at + size, :] = whole[to : to + size, :]
    if plan.paired:
        own_hidden, own_cotangent, sent = grads
        half = hidden.shape[1] // 4
        here, core = where[0], where[1]
        emit_own(hidden, own_hidden, 0, here, plan.locs)
        emit_own(cotangent, own_cotangent, 0, here, plan.locs)
        emit_half(hidden, sent, 0, 1 - here, core, plan.locs)
        emit_half(cotangent, sent, half, 1 - here, core, plan.locs)
        sent[:, 2 * half :] = mixed[...]
    else:
        grads[0][...] = hidden[...]


def between_kernel(start, here, there, kept, out, passed):
    total = here[...].astype(F32) + there[...].astype(F32)
    out[...] = (start[...].astype(F32) + total).astype(BF)


def temporal_kernel(plan, where, gain, survive, date_rows, cotangent, *refs):
    sources, refs = refs[: plan.sources], refs[plan.sources :]
    arrays, refs = refs[: plan.arrays], refs[plan.arrays :]
    grads, refs = refs[: plan.grads], refs[plan.grads :]
    joined, mixed, partial, back_part = refs[:4]
    back_triples, (hidden, triple, attend, back_mixed, back_triple) = refs[4:-5], refs[-5:]
    rows = joined.shape[0] // plan.blocks
    patches = rows // date_rows.shape[0]
    for source, at, to, size in plan.moves:
        if source == 0 and plan.sources > 1:
            total = sources[1][at : at + size, :].astype(F32) + sources[2][at : at + size, :].astype(F32)
            out = (sources[0][at : at + size, :].astype(F32) + total).astype(BF)
        else:
            out = sources[-1][at : at + size, :]
        out = out.astype(F32)
        dated = [
            out[at : at + patches] + date_rows[(to % rows + at) // patches : (to % rows + at) // patches + 1, :]
            for at in range(0, size, patches)
        ]
        joined[to : to + size, :] = jnp.concatenate(dated, axis=0).astype(BF)
    normalize_into(joined, gain, hidden, plan.blocks)
    width = mixed.shape[1]
    for kind in range(3):
        rows_times(hidden, views(plan, arrays, where, kind), triple, kind * width)
    outlet = views(plan, arrays, where, 3)
    rows_times(cotangent, outlet, back_mixed, 0)
    bias = temporal_bias(plan, joined.shape[0] // plan.blocks, survive)
    attention(triple, bias, attend, mixed, plan.blocks)
    for part, features in outlet:
        partial[:, features] = dot(mixed[...], part[...], NT).astype(BF)
    if plan.paired:
        own_hidden, sent = grads
        half = hidden.shape[1] // 4
        emit_own(hidden, own_hidden, 0, where[0], plan.locs)
        emit_half(hidden, sent, 0, 1 - where[0], where[1], plan.locs)
    else:
        grads[0][...] = hidden[...]
    attention_back(triple, attend, back_mixed, back_triple, plan.blocks)
    intakes = [views(plan, arrays, where, kind) for kind in range(3)]
    for entries in zip(*intakes):
        total = None
        for kind, (part, features) in enumerate(entries):
            term = dot(back_triple[:, kind * width : (kind + 1) * width], part[...], NT)
            total = term if total is None else total + term
        back_part[:, features] = total.astype(BF)
    split_columns(back_triple, back_triples)
    if plan.paired:
        sent[:, half:] = back_triple[:, : sent.shape[1] - half]


def split_columns(whole, outs):
    at = 0
    for out in outs:
        out[...] = whole[:, at : at + out.shape[1]]
        at += out.shape[1]


def norm_back_kernel(moves, step, gain, here, there, joined, cotangent, *outs):
    for at in range(0, joined.shape[0], step):
        span_here = slice(at, at + step)
        normed, inv_scale = statistics(joined[span_here, :])
        total = here[span_here, :].astype(F32) + there[span_here, :].astype(F32)
        scaled = total * gain[...]
        inner = (
            scaled
            - jnp.mean(scaled, -1, keepdims=True)
            - normed * jnp.mean(scaled * normed, -1, keepdims=True)
        )
        back = (cotangent[span_here, :].astype(F32) + inv_scale * inner).astype(BF)
        for target, to, first, size in moves:
            if at <= first < at + step:
                outs[target][to : to + size, :] = back[first - at : first - at + size]


def spatial_backward_kernel(plan, where, triple, attend, kept, *refs):
    sources, refs = refs[: plan.origins], refs[plan.origins :]
    arrays, refs = refs[: plan.arrays], refs[plan.arrays :]
    grads, refs = refs[: plan.grads], refs[plan.grads :]
    back_triples, (upstream, back_mixed, back_triple) = refs[:-4], refs[-3:]
    for source, at, to, size in plan.moves:
        upstream[to : to + size, :] = sources[source][at : at + size, :]
    if plan.paired:
        emit_own(upstream, grads[0], 0, where[0], plan.locs)
        emit_own(upstream, grads[1], 0, 1 - where[0], plan.locs)
    else:
        grads[0][...] = upstream[...]
    rows_times(upstream, views(plan, arrays, where, 3), back_mixed, 0)
    attention_back(triple, attend, back_mixed, back_triple, plan.blocks)
    split_columns(back_triple, back_triples)
    if plan.paired:
        half = upstream.shape[1] // 2
        grads[1][:, half:] = back_triple[:, : grads[1].shape[1] - half]


def grad_kernel(products, count, where, *refs):
    sent, far, near, other = refs[-4:]
    core, loc = where[1], where[2]
    block = near.shape[0]
    beside = loc + 1 - 2 * lax.rem(loc, 2)
    places = (lax.rem(beside + 2, 4), beside, lax.rem(loc + 2, 4), loc)
    column = 0
    for left, others, (right, right_at), (right_other, other_at), width in products:
        left, right, right_other = refs[left], refs[right], refs[right_other]
        lanes = other.shape[1] // len(others)
        for number, (source, at) in enumerate(others):
            to = 0
            if len(others) > 1:
                to = pl.multiple_of((core if number == 0 else 1 - core) * lanes, lanes)
            other[:, pl.ds(to, lanes)] = refs[source][:, at : at + lanes]
        for number, place in enumerate(places):
            columns = pl.ds(pl.multiple_of(place * block, block), block)
            for first in range(0, width, 256):
                lane = slice(column + first, column + first + 256)
                here = right[:, right_at + first : right_at + first + 256]
                there = right_other[:, other_at + first : other_at + first + 256]
                total = dot(left[:, columns], here, TN) + dot(other[:, columns], there, TN)
                if number < 2:
                    sent[number * block : (number + 1) * block, lane] = total.astype(BF)
                elif number == 2:
                    far[:, lane] = total
                else:
                    near[:, lane] = total
        column += width


def finish_kernel(*refs):
    out = refs[-1]
    block = out.shape[0]
    column = 0
    for near, beside, far in zip(refs[0:-1:3], refs[1:-1:3], refs[2:-1:3]):
        for at in range(0, near.shape[1], 256):
            lane = slice(at, at + 256)
            total = near[:, lane] + beside[block:, lane].astype(F32) + far[:, lane].astype(F32)
            kind, first = (3 * out.shape[2] + column + at) // out.shape[2] % 4, (column + at) % out.shape[2]
            out[:, kind, first : first + 256] = total
        column += near.shape[1]


def finish_last_kernel(kept, *refs):
    finish_kernel(*refs[:-1])


def fence_kernel(*refs):
    pass


def grad_after_kernel(products, count, passed, where, *refs):
    args, rest = refs[:count], refs[count + passed :]
    grad_kernel(products, count, where, *args, *rest[:3], rest[-1])


def rows_kernel(cloud, drop, keep, where, optical, radar, table, date_table, cotangent, *refs):
    own, other, upstream, dates_out, wide_table, places = refs
    here = where[0]
    dates, patches, _ = optical.shape
    pairs, half = dates // 2, patches // 2
    wide_table[...] = table[...].astype(F32)
    for patch in range(patches):
        places[patch : patch + 1, :] = wide_table[pl.ds(keep[0, patch], 1), :]
    for pair in range(pairs):
        found = []
        for number in range(2):
            date = pair * 2 + number
            at = here * dates + date
            seen = (1 - cloud[0, at]).astype(F32)
            kept = (1 - drop[0, at]).astype(F32)
            found.append(optical[date].astype(F32) * seen + radar[date].astype(F32) * kept + places[...])
        halves = [(rows[:half], rows[half:]) for rows in found]
        for out, swapped in ((own, 0), (other, 1)):
            picked = [jnp.where(here == swapped, first, second) for first, second in halves]
            for eight in range(0, half, 8):
                rows = jnp.concatenate([rows[eight : eight + 8] for rows in picked], axis=0)
                at = pair * half * 2 + eight * 2
                out[at : at + 16, :] = rows.astype(BF)
    block = 4 * pairs * 8
    for side in range(2):
        owner = here if side == 0 else 1 - here
        for pair in range(pairs):
            found = [cotangent[owner * dates + pair * 2 + number].astype(F32) for number in range(2)]
            for eight in range(half // 8):
                rows = jnp.concatenate([rows[eight * 8 : eight * 8 + 8] for rows in found], axis=0)
                at = eight * block + side * pairs * 16 + pair * 16
                upstream[at : at + 16, :] = rows.astype(BF)
    whole = date_table[...].astype(F32)
    flipped = jnp.concatenate([whole[dates:], whole[:dates]], axis=0)
    dates_out[...] = jnp.where(here == 0, whole, flipped)


class Plan:
    def __init__(self, blocks, moves, origins, weights, paired, locs, grads, sources=0, date_of=None, patch_of=None):
        self.date_of, self.patch_of = date_of, patch_of
        self.blocks, self.moves, self.origins = blocks, moves, origins
        self.arrays, self.table = len(weights.arrays), weights.table
        self.paired, self.locs, self.grads, self.sources = paired, locs, grads, sources


def call(body, outs, args, scratch=(), flops=0, kept=()):
    smem = pl.BlockSpec(memory_space=pltpu.SMEM)
    vmem = pl.BlockSpec(memory_space=pltpu.VMEM)
    specs = [smem if arg.dtype == jnp.int32 else vmem for arg in args]
    out_specs = [vmem] * len(outs)
    aliases = {}
    outs = list(outs)
    moved = sum(arg.size * arg.dtype.itemsize for arg in args)
    moved = moved + sum(out.size * out.dtype.itemsize for out in outs)
    for number in kept:
        specs[number] = pl.BlockSpec(memory_space=pl.ANY)
        out_specs.append(pl.BlockSpec(memory_space=pl.ANY))
        outs.append(jax.ShapeDtypeStruct(args[number].shape, args[number].dtype))
        aliases[number] = len(outs) - 1
    return pl.pallas_call(
        body,
        out_shape=outs,
        in_specs=specs,
        out_specs=out_specs,
        scratch_shapes=list(scratch),
        input_output_aliases=aliases,
        compiler_params=pltpu.CompilerParams(vmem_limit_bytes=VMEM_LIMIT),
        cost_estimate=pl.CostEstimate(flops=flops, bytes_accessed=moved, transcendentals=0),
    )(*args)


def fence(*arrays):
    anywhere = [pl.BlockSpec(memory_space=pl.ANY)] * len(arrays)
    return pl.pallas_call(
        fence_kernel,
        out_shape=[jax.ShapeDtypeStruct(array.shape, array.dtype) for array in arrays],
        in_specs=anywhere,
        out_specs=anywhere,
        input_output_aliases={number: number for number in range(len(arrays))},
    )(*arrays)


def swap(array, axis):
    return lax.ppermute(array, axis, [(0, 1), (1, 0)])


PAIRS = [(0, 1), (1, 0), (2, 3), (3, 2)]
APART = [(0, 2), (1, 3), (2, 0), (3, 1)]


def quarter_of(weights, number):
    rows = weights.shape[0]
    return lax.dynamic_slice_in_dim(weights, number * (rows // 4), rows // 4, 0)


def by_kind(weights):
    return weights.transpose(1, 0, 2)


def whole_weights(weights):
    whole = lax.all_gather(weights.transpose(1, 0, 2), "date", axis=1, tiled=True)
    return Weights([whole], {kind: [(0, kind, 0)] for kind in range(4)})


def quarters():
    side, even = lax.axis_index("groups"), lax.axis_index("loc") % 2
    return side * 2 + even, (1 - side) * 2 + 1 - even


def gather_weights(weights, first, last):
    arrays = [weights, first, swap(first, "groups"), lax.ppermute(first, "loc", PAIRS), swap(last, "date")]
    table = {kind: [(number, kind, number) for number in range(5)] for kind in range(4)}
    return Weights([by_kind(array) for array in arrays], table)


def add_over_heads(partial, sizes):
    if sizes["mp"] == 2:
        return partial.astype(F32) + swap(partial, "mp").astype(F32)
    return lax.psum(partial.astype(F32), "mp")


def whole_grads(hidden, back_triple, upstream, mixed):
    width = mixed.shape[1]
    intake = dot(hidden, back_triple, TN)
    outlet = dot(upstream, mixed, TN)
    whole = jnp.concatenate([intake, outlet], axis=1).reshape(-1, 4, width)
    part = lax.psum_scatter(whole.astype(BF), ("loc", "date"), scatter_dimension=0, tiled=True)
    return part.astype(F32)


def summed(where, args, products, kept=()):
    rows, columns = args[products[0][0]].shape
    block, width = columns // 4, sum(product[-1] for product in products)
    return call(
        functools.partial(grad_after_kernel, products, len(args), len(kept)),
        (
            jax.ShapeDtypeStruct((2 * block, width), BF),
            jax.ShapeDtypeStruct((block, width), F32),
            jax.ShapeDtypeStruct((block, width), F32),
        ),
        (where, *args, *kept),
        scratch=(pltpu.VMEM((rows, columns), BF),),
        flops=4 * rows * columns * width,
        kept=tuple(range(1 + len(args), 1 + len(args) + len(kept))),
    )


def summed_over_loc(outs):
    sent, far, near = outs[:3]
    beside = lax.ppermute(sent, "loc", PAIRS)
    far = (far + beside[: far.shape[0]].astype(F32)).astype(BF)
    return near, beside, lax.ppermute(far, "loc", APART)


def finish(terms, width, kept=None):
    out = jax.ShapeDtypeStruct((terms[0].shape[0], 4, width), F32)
    if kept is None:
        return call(finish_kernel, (out,), terms)
    return call(finish_last_kernel, (out,), (kept, *terms), kept=(0,))


def per_device(
    sizes,
    optical,
    radar,
    cloud,
    radar_drop,
    keep_index,
    place_table,
    date_table,
    spatial_gain,
    spatial_weights,
    temporal_gain,
    temporal_weights,
    cotangent,
):
    _, patches, dates_here, model = optical.shape
    patches_here, dates = cotangent.shape[1:3]
    width = spatial_weights.shape[2]
    rows = patches * dates_here
    here = lax.axis_index("date")
    first = here * dates_here
    paired = sizes["groups"] == 2 and sizes["loc"] == 4 and sizes["date"] == 2 and sizes["mp"] == 2
    paired = paired and dates_here % 2 == 0 and patches_here % 8 == 0 and model % 1024 == 0
    if paired:
        first_quarter, last_quarter = quarters()
        first_sent = quarter_of(spatial_weights, first_quarter)
    else:
        spatial, temporal = whole_weights(spatial_weights), whole_weights(temporal_weights)

    if paired:
        pairs, eights = dates_here // 2, patches_here // 8
        spatial_blocks, temporal_blocks = pairs, eights
        half_rows = eights * 16

        def temporal_whole(array):
            array = array.reshape(eights, 2, pairs, 2, 8, -1).transpose(1, 2, 3, 0, 4, 5)
            return jnp.where(here == 0, array, jnp.flip(array, 0)).reshape(dates, patches_here, -1)

        spatial_date, temporal_date, temporal_patch = (8, 2), (8, rows), (1, 8)
    else:
        spatial_blocks = 1 if rows <= 192 else dates_here
        temporal_blocks = patches_here // 8 if patches_here % 8 == 0 else 1

        def temporal_rows(array):
            array = array.reshape(dates, temporal_blocks, patches_here // temporal_blocks, -1)
            return array.transpose(1, 0, 2, 3).reshape(rows, -1)

        def temporal_whole(array):
            array = array.reshape(temporal_blocks, dates, patches_here // temporal_blocks, -1)
            return array.transpose(1, 0, 2, 3).reshape(dates, patches_here, -1)

        in_block = patches_here // temporal_blocks
        spatial_date, temporal_date, temporal_patch = (patches, rows), (in_block, rows), (1, in_block)
    spatial_size, temporal_size = rows // spatial_blocks, rows // temporal_blocks

    survive = (1 - cloud[0] * radar_drop[0]).astype(F32)
    side = lax.axis_index("groups") if paired else here
    where = jnp.stack([here, lax.axis_index("mp"), lax.axis_index("loc"), side]).astype(jnp.int32)
    optical_rows, radar_rows = optical[0].transpose(1, 0, 2), radar[0].transpose(1, 0, 2)
    cotangent_rows = cotangent[0].transpose(1, 0, 2)
    if paired:
        survive = jnp.where(here == 0, survive, jnp.roll(survive, dates_here))
    else:
        cloud_here = lax.dynamic_slice_in_dim(cloud, first, dates_here, 1)[0]
        drop_here = lax.dynamic_slice_in_dim(radar_drop, first, dates_here, 1)[0]
        places = jnp.take(place_table, keep_index[0], axis=0).astype(F32)[None]
        start = (
            optical_rows.astype(F32) * (1 - cloud_here).astype(F32)[:, None, None]
            + radar_rows.astype(F32) * (1 - drop_here).astype(F32)[:, None, None]
            + places
        ).astype(BF)
        start = start.reshape(rows, model)
        cotangent_rows = temporal_rows(cotangent_rows)
        date_rows = date_table.astype(F32)
    survive = jnp.repeat(survive, temporal_size // dates)[None]

    spatial_gain = spatial_gain[None]
    temporal_gain = temporal_gain[None]
    lanes = min(width, 256)

    def shape(*dims, dtype=BF):
        return jax.ShapeDtypeStruct(dims, dtype)

    def attend_dims(blocks):
        return (blocks * (width // lanes), lanes // HEAD_DIM * (rows // blocks), rows // blocks)

    layer_flops = 2 * rows * model * width * 4
    if paired:
        half = rows // 2
        own_start, other_start, cotangent_rows, date_rows = call(
            rows_kernel,
            (
                shape(half, model),
                shape(half, model),
                shape(rows, model),
                shape(dates, model, dtype=F32),
            ),
            (
                cloud,
                radar_drop,
                keep_index,
                where,
                optical_rows,
                radar_rows,
                place_table,
                date_table,
                cotangent_rows,
            ),
            scratch=(pltpu.VMEM(place_table.shape, F32), pltpu.VMEM((patches, model), F32)),
        )
        last_sent = quarter_of(spatial_weights, last_quarter)
        last_sent, own_start = fence(last_sent, own_start)
        origins = (own_start, other_start)
        spatial = gather_weights(spatial_weights, swap(first_sent, "date"), last_sent)
        sent = [quarter_of(temporal_weights, number) for number in (first_quarter, last_quarter)]
        *sent, cotangent_rows = fence(*sent, cotangent_rows)
        temporal_first = swap(sent[0], "date")
        spatial_moves = [
            (side, pair * half_rows, (pair * 2 + side) * half_rows, half_rows)
            for side in range(2)
            for pair in range(pairs)
        ]
        temporal_moves = [
            (side, pair * half_rows + eight * 16, (eight * 2 + side) * pairs * 16 + pair * 16, 16)
            for side in range(2)
            for pair in range(pairs)
            for eight in range(eights)
        ]
        half_shapes = (shape(half, model), shape(half, model))
        own, quarter = shape(rows, model // 2), model // 4
        forward_grads = (own, own, shape(rows, 2 * quarter + width))
        temporal_grads = (own, shape(rows, quarter + 3 * width // 2))
        back_shapes = (shape(rows, 3 * width // 2), shape(rows, 3 * width // 2))
        backward_grads = (own, shape(rows, model // 2 + 3 * width // 2))
    else:
        origins = (start,)
        spatial_moves = [(0, at * spatial_size, at * spatial_size, spatial_size) for at in range(spatial_blocks)]
        temporal_moves = [(0, at * temporal_size, at * temporal_size, temporal_size) for at in range(temporal_blocks)]
        half_shapes = (shape(rows, model),)
        forward_grads = temporal_grads = backward_grads = (shape(rows, model),)
        back_shapes = (shape(rows, 3 * width),)

    def plan_of(blocks, moves, weights, grads, sources=0, date_of=spatial_date, patch_of=None):
        return Plan(
            blocks, moves, len(origins), weights, paired, sizes["loc"], len(grads), sources, date_of, patch_of
        )

    plan = plan_of(spatial_blocks, spatial_moves, spatial, forward_grads)
    outs = call(
        functools.partial(spatial_forward_kernel, plan),
        (
            *half_shapes,
            *forward_grads,
            shape(rows, 3 * width),
            shape(*attend_dims(spatial_blocks), dtype=F32),
            shape(rows, width),
        ),
        (where, spatial_gain, cotangent_rows, *origins, *spatial.arrays),
        scratch=(
            pltpu.VMEM((rows, model), BF),
            pltpu.VMEM((rows, model), BF),
            pltpu.VMEM((rows, model), BF),
        ),
        flops=layer_flops,
    )
    partials, outs = outs[: len(origins)], outs[len(origins) :]
    forward, (triple, attend, mixed) = outs[: len(forward_grads)], outs[len(forward_grads) :]
    if paired:
        temporal_first, kept = fence(temporal_first, partials[1])
        partials = (partials[0], kept)
        temporal = gather_weights(temporal_weights, temporal_first, sent[1])
        there, early = call(
            between_kernel,
            (shape(half, model),),
            (origins[1], partials[1], swap(partials[1], "mp"), forward[2]),
            kept=(3,),
        )
        early, there = fence(early, swap(there, "date"))
        sources = (origins[0], partials[0], swap(partials[0], "mp"), there)
        early_other = swap(early, "date")
    else:
        spatial_out = (start.astype(F32) + add_over_heads(partials[0], sizes)).astype(BF)
        moved = lax.all_to_all(
            spatial_out.reshape(dates_here, patches, model),
            "date",
            split_axis=1,
            concat_axis=0,
            tiled=True,
        )
        sources = (temporal_rows(moved),)
    plan = plan_of(
        temporal_blocks,
        temporal_moves,
        temporal,
        temporal_grads,
        len(sources),
        temporal_date,
        temporal_patch,
    )
    outs = call(
        functools.partial(temporal_kernel, plan),
        (
            *temporal_grads,
            shape(rows, model),
            shape(rows, width),
            shape(rows, model),
            shape(rows, model),
            *back_shapes,
        ),
        (
            where,
            temporal_gain,
            survive,
            date_rows,
            cotangent_rows,
            *sources,
            *temporal.arrays,
        ),
        scratch=(
            pltpu.VMEM((rows, model), BF),
            pltpu.VMEM((rows, 3 * width), BF),
            pltpu.VMEM(attend_dims(temporal_blocks), F32),
            pltpu.VMEM((rows, width), BF),
            pltpu.VMEM((rows, 3 * width), BF),
        ),
        flops=2 * layer_flops,
    )
    middle, outs = outs[: len(temporal_grads)], outs[len(temporal_grads) :]
    (joined, temporal_mixed, temporal_partial, back_part), temporal_triples = outs[:4], outs[4:]
    if paired:
        back_part, early_other = fence(back_part, early_other)

    if sizes["mp"] == 2:
        others = swap(back_part, "mp")
    else:
        others = (lax.psum(back_part.astype(F32), "mp") - back_part.astype(F32)).astype(BF)
    backs = call(
        functools.partial(norm_back_kernel, temporal_moves, temporal_size),
        half_shapes,
        (temporal_gain, back_part, others, joined, cotangent_rows),
    )
    if paired:
        mixed_sent, back_sent = fence(temporal_mixed, swap(backs[1], "date"))
        early_there = swap(early_other[:, : 2 * quarter], "mp")
        middle_other = swap(middle[1], "date")
        middle_there = swap(middle_other[:, :quarter], "mp")
        last_half = swap(temporal_triples[1], "date")
        part = temporal_triples[0].shape[1]
        others = ((1, 0), (2, 0))
        *intake, kept, back_sent = summed(
            where,
            (middle[0], middle_other, middle_there, *temporal_triples, last_half),
            ((0, others, (3, 0), (1, quarter), part), (0, others, (4, 0), (5, 0), part)),
            kept=(back_sent,),
        )
        back_origins = (backs[0], back_sent)
    else:
        back = lax.all_to_all(
            temporal_whole(backs[0]), "date", split_axis=0, concat_axis=1, tiled=True
        )
        back_origins = (back.reshape(rows, model),)
        kept = temporal_triples[0]
    outlet = spatial.only((3,))
    plan = plan_of(spatial_blocks, spatial_moves, outlet, backward_grads)
    *outs, kept = call(
        functools.partial(spatial_backward_kernel, plan),
        (*backward_grads, *back_shapes),
        (where, triple, attend, kept, *back_origins, *outlet.arrays),
        scratch=(
            pltpu.VMEM((rows, model), BF),
            pltpu.VMEM((rows, width), BF),
            pltpu.VMEM((rows, 3 * width), BF),
        ),
        flops=layer_flops,
        kept=(3,),
    )
    backward, back_triples = outs[: len(backward_grads)], outs[len(backward_grads) :]
    encoded = (joined.astype(F32) + add_over_heads(temporal_partial, sizes)).astype(BF)
    encoded = temporal_whole(encoded).transpose(1, 0, 2)[None]
    if not paired:
        return (
            encoded,
            whole_grads(forward[0], back_triples[0], backward[0], mixed),
            whole_grads(middle[0], kept, cotangent_rows, temporal_mixed),
        )
    intake = summed_over_loc((*intake, kept))
    *outlet, upstream_own = summed(
        where,
        (forward[1], early_other, early_there, mixed_sent, swap(mixed_sent, "date")),
        ((0, ((1, quarter), (2, quarter)), (3, 0), (4, 0), width),),
        kept=(backward[0],),
    )
    temporal_terms = [*summed_over_loc(outlet), *intake]
    half = model // 2
    backward_other = swap(backward[1], "date")
    *sums, kept = summed(
        where,
        (
            upstream_own,
            backward_other,
            mixed,
            early_other,
            forward[0],
            early_there,
            back_triples[0],
        ),
        (
            (0, ((1, 0),), (2, 0), (3, 2 * quarter), width),
            (4, ((3, 0), (5, 0)), (6, 0), (1, half), back_triples[0].shape[1]),
        ),
        kept=(temporal_terms[4],),
    )
    temporal_terms[4] = kept
    spatial_terms = [*summed_over_loc(sums)]
    sums = summed(
        where,
        (forward[0], early_other, early_there, back_triples[1], swap(back_triples[1], "date")),
        ((0, ((1, 0), (2, 0)), (3, 0), (4, 0), back_triples[1].shape[1]),),
    )
    spatial_terms += summed_over_loc(sums)
    (temporal_grads,) = finish(temporal_terms, width)
    spatial_grads, temporal_grads = finish(spatial_terms, width, kept=temporal_grads)
    return (encoded, spatial_grads, temporal_grads)


def solution(mesh):
    in_specs = (
        P(("groups", "loc"), None, "date", None),
        P(("groups", "loc"), None, "date", None),
        P(("groups", "loc"), None),
        P(("groups", "loc"), None),
        P(("groups", "loc"), None),
        P(),
        P(),
        P(),
        P("date", None, "mp"),
        P(),
        P("date", None, "mp"),
        P(("groups", "loc"), "date", None, None),
    )
    out_specs = (
        P(("groups", "loc"), "date", None, None),
        P(("groups", "loc", "date"), None, "mp"),
        P(("groups", "loc", "date"), None, "mp"),
    )
    return jax.shard_map(
        functools.partial(per_device, dict(mesh.shape)),
        mesh=mesh,
        in_specs=in_specs,
        out_specs=out_specs,
        check_vma=False,
    )
```

```python
import functools

import jax
import jax.numpy as jnp
from jax import lax
from jax.experimental import pallas as pl
from jax.experimental.pallas import tpu as pltpu
from jax.sharding import PartitionSpec as P

HEAD_DIM = 64
EPSILON = 1e-05
CROSS = -1e30
BF = jnp.bfloat16
F32 = jnp.float32
NN = (((1,), (0,)), ((), ()))
NT = (((1,), (1,)), ((), ()))
TN = (((0,), (0,)), ((), ()))
VMEM_LIMIT = 56 * 1024 * 1024


def dot(left, right, dims):
    return lax.dot_general(left, right, dims, preferred_element_type=F32)


def statistics(rows):
    values = rows.astype(F32)
    centred = values - jnp.mean(values, -1, keepdims=True)
    inv_scale = lax.rsqrt(jnp.mean(centred * centred, -1, keepdims=True) + EPSILON)
    return centred * inv_scale, inv_scale


class Heads:
    def __init__(self, width):
        self.lanes = min(width, 256)
        self.count = self.lanes // HEAD_DIM
        owner = lax.broadcasted_iota(jnp.int32, (1, self.lanes), 1) // HEAD_DIM
        self.masks = [(owner == head).astype(F32) for head in range(self.count)]

    def stack(self, block):
        return jnp.concatenate([block * mask.astype(BF) for mask in self.masks], axis=0)

    def unstack(self, tall):
        rows = tall.shape[0] // self.count
        total = tall[0:rows] * self.masks[0]
        for head in range(1, self.count):
            total = total + tall[head * rows : (head + 1) * rows] * self.masks[head]
        return total


class Weights:
    def __init__(self, arrays, table):
        self.arrays, self.table = list(arrays), table

    def only(self, kinds):
        used = sorted({entry[0] for kind in kinds for entry in self.table[kind]})
        table = {
            kind: [(used.index(array), at, place) for array, at, place in self.table[kind]]
            for kind in kinds
        }
        return Weights([self.arrays[number] for number in used], table)


def first_row(number, rows, where):
    if number == 0:
        return where[0] * rows
    side, even = where[3], lax.rem(where[2], 2)
    side = side if number in (1, 3) else 1 - side
    even = even if number in (1, 2) else 1 - even
    return (1 - where[0]) * rows + (side * 2 + even) * (rows // 4)


def views(plan, refs, where, kind):
    found = []
    for array, at, place in plan.table[kind]:
        part = refs[array].at[at]
        if plan.paired:
            first = pl.multiple_of(first_row(place, refs[plan.table[kind][0][0]].shape[1], where), 128)
            found.append((part, pl.ds(first, part.shape[0])))
        else:
            found.append((part, slice(None)))
    return found


def rows_times(rows_ref, parts, out_ref, column):
    width = parts[0][0].shape[1]
    step = min(width, 256)
    for at in range(0, width, step):
        total = None
        for part, columns in parts:
            term = dot(rows_ref[:, columns], part[:, at : at + step], NN)
            total = term if total is None else total + term
        out_ref[:, column + at : column + at + step] = total.astype(out_ref.dtype)


def emit_own(rows_ref, out, at, date, loc_count):
    block = rows_ref.shape[1] // (2 * loc_count)
    for loc in range(loc_count):
        first = pl.multiple_of((loc * 2 + date) * block, block)
        out[:, at + loc * block : at + (loc + 1) * block] = rows_ref[:, pl.ds(first, block)]


def emit_half(rows_ref, out, at, date, core, loc_count):
    block = rows_ref.shape[1] // (2 * loc_count)
    for number in range(loc_count // 2):
        loc = core * (loc_count // 2) + number
        first = pl.multiple_of((loc * 2 + date) * block, block)
        out[:, at + number * block : at + (number + 1) * block] = rows_ref[:, pl.ds(first, block)]


def groups_of(size, spans, modulus, axis):
    shape = (size, 1) if axis == 0 else (1, size)
    return lax.rem(lax.broadcasted_iota(jnp.int32, shape, axis) // spans, modulus)


def spatial_bias(plan, size):
    query, key = (groups_of(size, *plan.date_of, axis) for axis in range(2))
    return jnp.where(query == key, 0.0, CROSS).astype(F32)


def temporal_bias(plan, size, survive):
    query, key = (groups_of(size, *plan.patch_of, axis) for axis in range(2))
    query_date, key_date = (groups_of(size, *plan.date_of, axis) for axis in range(2))
    allowed = (survive[...] == 1.0) | (query_date == key_date)
    return jnp.where(query == key, jnp.where(allowed, 0.0, -1000000000.0), CROSS).astype(F32)


def attention(triple_ref, bias, attend_ref, mixed_ref, blocks):
    width = triple_ref.shape[1] // 3
    heads = Heads(width)
    rows = triple_ref.shape[0] // blocks
    groups = width // heads.lanes
    bias = jnp.concatenate([bias] * heads.count, axis=0)
    for block in range(blocks):
        at = slice(block * rows, (block + 1) * rows)
        for group in range(groups):
            lane = group * heads.lanes
            queries = heads.stack(triple_ref[at, lane : lane + heads.lanes])
            keys = triple_ref[at, width + lane : width + lane + heads.lanes]
            values = triple_ref[at, 2 * width + lane : 2 * width + lane + heads.lanes]
            scores = dot(queries, keys, NT) * HEAD_DIM ** (-0.5) + bias
            raised = jnp.exp(scores - jnp.max(scores, -1, keepdims=True))
            attend = raised * (1.0 / jnp.sum(raised, -1, keepdims=True))
            attend_ref[block * groups + group] = attend
            mixed = heads.unstack(dot(attend.astype(BF), values, NN))
            mixed_ref[at, lane : lane + heads.lanes] = mixed.astype(BF)


def attention_back(triple_ref, attend_ref, back_mixed_ref, back_triple_ref, blocks):
    width = triple_ref.shape[1] // 3
    heads = Heads(width)
    rows = triple_ref.shape[0] // blocks
    groups = width // heads.lanes
    for block in range(blocks):
        at = slice(block * rows, (block + 1) * rows)
        for group in range(groups):
            lane = group * heads.lanes
            queries = heads.stack(triple_ref[at, lane : lane + heads.lanes])
            keys = triple_ref[at, width + lane : width + lane + heads.lanes]
            values = triple_ref[at, 2 * width + lane : 2 * width + lane + heads.lanes]
            back = heads.stack(back_mixed_ref[at, lane : lane + heads.lanes])
            attend = attend_ref[block * groups + group]
            back_attend = dot(back, values, NT)
            back_values = dot(attend.astype(BF), back, TN)
            inner = back_attend - jnp.sum(back_attend * attend, -1, keepdims=True)
            back_scores = (attend * inner * HEAD_DIM ** (-0.5)).astype(BF)
            back_queries = heads.unstack(dot(back_scores, keys, NN))
            back_keys = dot(back_scores, queries, TN)
            for number, term in enumerate((back_queries, back_keys, back_values)):
                first = number * width + lane
                back_triple_ref[at, first : first + heads.lanes] = term.astype(BF)


def normalize_into(rows_ref, gain_ref, hidden_ref, blocks):
    rows = rows_ref.shape[0] // blocks
    for block in range(blocks):
        at = slice(block * rows, (block + 1) * rows)
        normed, _ = statistics(rows_ref[at, :])
        hidden_ref[at, :] = (normed * gain_ref[...]).astype(BF)


def spatial_forward_kernel(plan, where, gain, cotangent, *refs):
    sources, refs = refs[: plan.origins], refs[plan.origins :]
    arrays, refs = refs[: plan.arrays], refs[plan.arrays :]
    partials, refs = refs[: plan.origins], refs[plan.origins :]
    grads, refs = refs[: plan.grads], refs[plan.grads :]
    triple, attend, mixed, start, hidden, whole = refs
    for source, at, to, size in plan.moves:
        start[to : to + size, :] = sources[source][at : at + size, :]
    normalize_into(start, gain, hidden, plan.blocks)
    width = mixed.shape[1]
    for kind in range(3):
        rows_times(hidden, views(plan, arrays, where, kind), triple, kind * width)
    bias = spatial_bias(plan, start.shape[0] // plan.blocks)
    attention(triple, bias, attend, mixed, plan.blocks)
    for part, features in views(plan, arrays, where, 3):
        whole[:, features] = dot(mixed[...], part[...], NT).astype(BF)
    for source, at, to, size in plan.moves:
        partials[source][at : at + size, :] = whole[to : to + size, :]
    if plan.paired:
        own_hidden, own_cotangent, sent = grads
        half = hidden.shape[1] // 4
        here, core = where[0], where[1]
        emit_own(hidden, own_hidden, 0, here, plan.locs)
        emit_own(cotangent, own_cotangent, 0, here, plan.locs)
        emit_half(hidden, sent, 0, 1 - here, core, plan.locs)
        emit_half(cotangent, sent, half, 1 - here, core, plan.locs)
        sent[:, 2 * half :] = mixed[...]
    else:
        grads[0][...] = hidden[...]


def between_kernel(start, here, there, kept, out, passed):
    total = here[...].astype(F32) + there[...].astype(F32)
    out[...] = (start[...].astype(F32) + total).astype(BF)


def temporal_kernel(plan, where, gain, survive, date_rows, cotangent, *refs):
    sources, refs = refs[: plan.sources], refs[plan.sources :]
    arrays, refs = refs[: plan.arrays], refs[plan.arrays :]
    grads, refs = refs[: plan.grads], refs[plan.grads :]
    joined, mixed, partial, back_part = refs[:4]
    back_triples, (hidden, triple, attend, back_mixed, back_triple) = refs[4:-5], refs[-5:]
    rows = joined.shape[0] // plan.blocks
    patches = rows // date_rows.shape[0]
    for source, at, to, size in plan.moves:
        if source == 0 and plan.sources > 1:
            total = sources[1][at : at + size, :].astype(F32) + sources[2][at : at + size, :].astype(F32)
            out = (sources[0][at : at + size, :].astype(F32) + total).astype(BF)
        else:
            out = sources[-1][at : at + size, :]
        out = out.astype(F32)
        dated = [
            out[at : at + patches] + date_rows[(to % rows + at) // patches : (to % rows + at) // patches + 1, :]
            for at in range(0, size, patches)
        ]
        joined[to : to + size, :] = jnp.concatenate(dated, axis=0).astype(BF)
    normalize_into(joined, gain, hidden, plan.blocks)
    width = mixed.shape[1]
    for kind in range(3):
        rows_times(hidden, views(plan, arrays, where, kind), triple, kind * width)
    outlet = views(plan, arrays, where, 3)
    rows_times(cotangent, outlet, back_mixed, 0)
    bias = temporal_bias(plan, joined.shape[0] // plan.blocks, survive)
    attention(triple, bias, attend, mixed, plan.blocks)
    for part, features in outlet:
        partial[:, features] = dot(mixed[...], part[...], NT).astype(BF)
    if plan.paired:
        own_hidden, sent, last = grads
        half = hidden.shape[1] // 4
        emit_own(hidden, own_hidden, 0, where[0], plan.locs)
        emit_half(hidden, sent, 0, 1 - where[0], where[1], plan.locs)
    else:
        grads[0][...] = hidden[...]
    attention_back(triple, attend, back_mixed, back_triple, plan.blocks)
    intakes = [views(plan, arrays, where, kind) for kind in range(3)]
    for entries in zip(*intakes):
        total = None
        for kind, (part, features) in enumerate(entries):
            term = dot(back_triple[:, kind * width : (kind + 1) * width], part[...], NT)
            total = term if total is None else total + term
        back_part[:, features] = total.astype(BF)
    split_columns(back_triple, back_triples)
    if plan.paired:
        split = sent.shape[1] - half
        sent[:, half:] = back_triple[:, :split]
        last[:, :split] = back_triple[:, split:]
        last[:, split:] = mixed[...]


def split_columns(whole, outs):
    at = 0
    for out in outs:
        out[...] = whole[:, at : at + out.shape[1]]
        at += out.shape[1]


def norm_back_kernel(moves, step, gain, here, there, joined, cotangent, kept, *outs):
    for at in range(0, joined.shape[0], step):
        span_here = slice(at, at + step)
        normed, inv_scale = statistics(joined[span_here, :])
        total = here[span_here, :].astype(F32) + there[span_here, :].astype(F32)
        scaled = total * gain[...]
        inner = (
            scaled
            - jnp.mean(scaled, -1, keepdims=True)
            - normed * jnp.mean(scaled * normed, -1, keepdims=True)
        )
        back = (cotangent[span_here, :].astype(F32) + inv_scale * inner).astype(BF)
        for target, to, first, size in moves:
            if at <= first < at + step:
                outs[target][to : to + size, :] = back[first - at : first - at + size]


def spatial_backward_kernel(plan, where, triple, attend, kept, *refs):
    sources, refs = refs[: plan.origins], refs[plan.origins :]
    arrays, refs = refs[: plan.arrays], refs[plan.arrays :]
    grads, refs = refs[: plan.grads], refs[plan.grads :]
    back_triples, (upstream, back_mixed, back_triple) = refs[:-4], refs[-3:]
    for source, at, to, size in plan.moves:
        upstream[to : to + size, :] = sources[source][at : at + size, :]
    if plan.paired:
        emit_own(upstream, grads[0], 0, where[0], plan.locs)
        emit_own(upstream, grads[1], 0, 1 - where[0], plan.locs)
    else:
        grads[0][...] = upstream[...]
    rows_times(upstream, views(plan, arrays, where, 3), back_mixed, 0)
    attention_back(triple, attend, back_mixed, back_triple, plan.blocks)
    split_columns(back_triple, back_triples)
    if plan.paired:
        half = upstream.shape[1] // 2
        grads[1][:, half:] = back_triple[:, : grads[1].shape[1] - half]


def grad_kernel(products, count, where, *refs):
    sent, far, near, other = refs[-4:]
    core, loc = where[1], where[2]
    block = near.shape[0]
    beside = loc + 1 - 2 * lax.rem(loc, 2)
    places = (lax.rem(beside + 2, 4), beside, lax.rem(loc + 2, 4), loc)
    column = 0
    for left, others, (right, right_at), (right_other, other_at), width in products:
        left, right, right_other = refs[left], refs[right], refs[right_other]
        lanes = other.shape[1] // len(others)
        for number, (source, at) in enumerate(others):
            to = 0
            if len(others) > 1:
                to = pl.multiple_of((core if number == 0 else 1 - core) * lanes, lanes)
            other[:, pl.ds(to, lanes)] = refs[source][:, at : at + lanes]
        for number, place in enumerate(places):
            columns = pl.ds(pl.multiple_of(place * block, block), block)
            for first in range(0, width, 256):
                lane = slice(column + first, column + first + 256)
                here = right[:, right_at + first : right_at + first + 256]
                there = right_other[:, other_at + first : other_at + first + 256]
                total = dot(left[:, columns], here, TN) + dot(other[:, columns], there, TN)
                if number < 2:
                    sent[number * block : (number + 1) * block, lane] = total.astype(BF)
                elif number == 2:
                    far[:, lane] = total
                else:
                    near[:, lane] = total
        column += width


def finish_kernel(kind_first, *refs):
    out = refs[-1]
    block = out.shape[0]
    column = 0
    for near, beside, far in zip(refs[0:-1:3], refs[1:-1:3], refs[2:-1:3]):
        for at in range(0, near.shape[1], 256):
            lane = slice(at, at + 256)
            total = near[:, lane] + beside[block:, lane].astype(F32) + far[:, lane].astype(F32)
            kind, first = (kind_first * out.shape[2] + column + at) // out.shape[2] % 4, (column + at) % out.shape[2]
            out[:, kind, first : first + 256] = total
        column += near.shape[1]


def finish_last_kernel(kind_first, kept, *refs):
    finish_kernel(kind_first, *refs[:-1])


def fence_kernel(*refs):
    pass


def grad_after_kernel(products, count, passed, where, *refs):
    args, rest = refs[:count], refs[count + passed :]
    grad_kernel(products, count, where, *args, *rest[:3], rest[-1])


def rows_kernel(cloud, drop, keep, where, optical, radar, table, date_table, cotangent, *refs):
    own, other, upstream, dates_out, wide_table, places = refs
    here = where[0]
    dates, patches, _ = optical.shape
    pairs, half = dates // 2, patches // 2
    wide_table[...] = table[...].astype(F32)
    for patch in range(patches):
        places[patch : patch + 1, :] = wide_table[pl.ds(keep[0, patch], 1), :]
    for pair in range(pairs):
        found = []
        for number in range(2):
            date = pair * 2 + number
            at = here * dates + date
            seen = (1 - cloud[0, at]).astype(F32)
            kept = (1 - drop[0, at]).astype(F32)
            found.append(optical[date].astype(F32) * seen + radar[date].astype(F32) * kept + places[...])
        halves = [(rows[:half], rows[half:]) for rows in found]
        for out, swapped in ((own, 0), (other, 1)):
            picked = [jnp.where(here == swapped, first, second) for first, second in halves]
            for eight in range(0, half, 8):
                rows = jnp.concatenate([rows[eight : eight + 8] for rows in picked], axis=0)
                at = pair * half * 2 + eight * 2
                out[at : at + 16, :] = rows.astype(BF)
    block = 4 * pairs * 8
    for side in range(2):
        owner = here if side == 0 else 1 - here
        for pair in range(pairs):
            found = [cotangent[owner * dates + pair * 2 + number].astype(F32) for number in range(2)]
            for eight in range(half // 8):
                rows = jnp.concatenate([rows[eight * 8 : eight * 8 + 8] for rows in found], axis=0)
                at = eight * block + side * pairs * 16 + pair * 16
                upstream[at : at + 16, :] = rows.astype(BF)
    whole = date_table[...].astype(F32)
    flipped = jnp.concatenate([whole[dates:], whole[:dates]], axis=0)
    dates_out[...] = jnp.where(here == 0, whole, flipped)


class Plan:
    def __init__(self, blocks, moves, origins, weights, paired, locs, grads, sources=0, date_of=None, patch_of=None):
        self.date_of, self.patch_of = date_of, patch_of
        self.blocks, self.moves, self.origins = blocks, moves, origins
        self.arrays, self.table = len(weights.arrays), weights.table
        self.paired, self.locs, self.grads, self.sources = paired, locs, grads, sources


def call(body, outs, args, scratch=(), flops=0, kept=()):
    smem = pl.BlockSpec(memory_space=pltpu.SMEM)
    vmem = pl.BlockSpec(memory_space=pltpu.VMEM)
    specs = [smem if arg.dtype == jnp.int32 else vmem for arg in args]
    out_specs = [vmem] * len(outs)
    aliases = {}
    outs = list(outs)
    moved = sum(arg.size * arg.dtype.itemsize for arg in args)
    moved = moved + sum(out.size * out.dtype.itemsize for out in outs)
    for number in kept:
        specs[number] = pl.BlockSpec(memory_space=pl.ANY)
        out_specs.append(pl.BlockSpec(memory_space=pl.ANY))
        outs.append(jax.ShapeDtypeStruct(args[number].shape, args[number].dtype))
        aliases[number] = len(outs) - 1
    return pl.pallas_call(
        body,
        out_shape=outs,
        in_specs=specs,
        out_specs=out_specs,
        scratch_shapes=list(scratch),
        input_output_aliases=aliases,
        compiler_params=pltpu.CompilerParams(vmem_limit_bytes=VMEM_LIMIT),
        cost_estimate=pl.CostEstimate(flops=flops, bytes_accessed=moved, transcendentals=0),
    )(*args)


def fence(*arrays):
    anywhere = [pl.BlockSpec(memory_space=pl.ANY)] * len(arrays)
    return pl.pallas_call(
        fence_kernel,
        out_shape=[jax.ShapeDtypeStruct(array.shape, array.dtype) for array in arrays],
        in_specs=anywhere,
        out_specs=anywhere,
        input_output_aliases={number: number for number in range(len(arrays))},
    )(*arrays)


def swap(array, axis):
    return lax.ppermute(array, axis, [(0, 1), (1, 0)])


PAIRS = [(0, 1), (1, 0), (2, 3), (3, 2)]
APART = [(0, 2), (1, 3), (2, 0), (3, 1)]


def quarter_of(weights, number):
    rows = weights.shape[0]
    return lax.dynamic_slice_in_dim(weights, number * (rows // 4), rows // 4, 0)


def by_kind(weights):
    return weights.transpose(1, 0, 2)


def whole_weights(weights):
    whole = lax.all_gather(weights.transpose(1, 0, 2), "date", axis=1, tiled=True)
    return Weights([whole], {kind: [(0, kind, 0)] for kind in range(4)})


def quarters():
    side, even = lax.axis_index("groups"), lax.axis_index("loc") % 2
    return side * 2 + even, (1 - side) * 2 + 1 - even


def gather_weights(weights, first, last):
    arrays = [weights, first, swap(first, "groups"), lax.ppermute(first, "loc", PAIRS), swap(last, "date")]
    table = {kind: [(number, kind, number) for number in range(5)] for kind in range(4)}
    return Weights([by_kind(array) for array in arrays], table)


def add_over_heads(partial, sizes):
    if sizes["mp"] == 2:
        return partial.astype(F32) + swap(partial, "mp").astype(F32)
    return lax.psum(partial.astype(F32), "mp")


def whole_grads(hidden, back_triple, upstream, mixed):
    width = mixed.shape[1]
    intake = dot(hidden, back_triple, TN)
    outlet = dot(upstream, mixed, TN)
    whole = jnp.concatenate([intake, outlet], axis=1).reshape(-1, 4, width)
    part = lax.psum_scatter(whole.astype(BF), ("loc", "date"), scatter_dimension=0, tiled=True)
    return part.astype(F32)


def summed(where, args, products, kept=()):
    rows, columns = args[products[0][0]].shape
    block, width = columns // 4, sum(product[-1] for product in products)
    return call(
        functools.partial(grad_after_kernel, products, len(args), len(kept)),
        (
            jax.ShapeDtypeStruct((2 * block, width), BF),
            jax.ShapeDtypeStruct((block, width), F32),
            jax.ShapeDtypeStruct((block, width), F32),
        ),
        (where, *args, *kept),
        scratch=(pltpu.VMEM((rows, columns), BF),),
        flops=4 * rows * columns * width,
        kept=tuple(range(1 + len(args), 1 + len(args) + len(kept))),
    )


def summed_over_loc(outs):
    sent, far, near = outs[:3]
    beside = lax.ppermute(sent, "loc", PAIRS)
    far = (far + beside[: far.shape[0]].astype(F32)).astype(BF)
    return near, beside, lax.ppermute(far, "loc", APART)


def finish(terms, width, kind_first, kept=None):
    out = jax.ShapeDtypeStruct((terms[0].shape[0], 4, width), F32)
    if kept is None:
        return call(functools.partial(finish_kernel, kind_first), (out,), terms)
    return call(functools.partial(finish_last_kernel, kind_first), (out,), (kept, *terms), kept=(0,))


def per_device(
    sizes,
    optical,
    radar,
    cloud,
    radar_drop,
    keep_index,
    place_table,
    date_table,
    spatial_gain,
    spatial_weights,
    temporal_gain,
    temporal_weights,
    cotangent,
):
    _, patches, dates_here, model = optical.shape
    patches_here, dates = cotangent.shape[1:3]
    width = spatial_weights.shape[2]
    rows = patches * dates_here
    here = lax.axis_index("date")
    first = here * dates_here
    paired = sizes["groups"] == 2 and sizes["loc"] == 4 and sizes["date"] == 2 and sizes["mp"] == 2
    paired = paired and dates_here % 2 == 0 and patches_here % 8 == 0 and model % 1024 == 0
    if paired:
        first_quarter, last_quarter = quarters()
        first_sent = quarter_of(spatial_weights, first_quarter)
    else:
        spatial, temporal = whole_weights(spatial_weights), whole_weights(temporal_weights)

    if paired:
        pairs, eights = dates_here // 2, patches_here // 8
        spatial_blocks, temporal_blocks = pairs, eights
        half_rows = eights * 16

        def temporal_whole(array):
            array = array.reshape(eights, 2, pairs, 2, 8, -1).transpose(1, 2, 3, 0, 4, 5)
            return jnp.where(here == 0, array, jnp.flip(array, 0)).reshape(dates, patches_here, -1)

        spatial_date, temporal_date, temporal_patch = (8, 2), (8, rows), (1, 8)
    else:
        spatial_blocks = 1 if rows <= 192 else dates_here
        temporal_blocks = patches_here // 8 if patches_here % 8 == 0 else 1

        def temporal_rows(array):
            array = array.reshape(dates, temporal_blocks, patches_here // temporal_blocks, -1)
            return array.transpose(1, 0, 2, 3).reshape(rows, -1)

        def temporal_whole(array):
            array = array.reshape(temporal_blocks, dates, patches_here // temporal_blocks, -1)
            return array.transpose(1, 0, 2, 3).reshape(dates, patches_here, -1)

        in_block = patches_here // temporal_blocks
        spatial_date, temporal_date, temporal_patch = (patches, rows), (in_block, rows), (1, in_block)
    spatial_size, temporal_size = rows // spatial_blocks, rows // temporal_blocks

    survive = (1 - cloud[0] * radar_drop[0]).astype(F32)
    side = lax.axis_index("groups") if paired else here
    where = jnp.stack([here, lax.axis_index("mp"), lax.axis_index("loc"), side]).astype(jnp.int32)
    optical_rows, radar_rows = optical[0].transpose(1, 0, 2), radar[0].transpose(1, 0, 2)
    cotangent_rows = cotangent[0].transpose(1, 0, 2)
    if paired:
        survive = jnp.where(here == 0, survive, jnp.roll(survive, dates_here))
    else:
        cloud_here = lax.dynamic_slice_in_dim(cloud, first, dates_here, 1)[0]
        drop_here = lax.dynamic_slice_in_dim(radar_drop, first, dates_here, 1)[0]
        places = jnp.take(place_table, keep_index[0], axis=0).astype(F32)[None]
        start = (
            optical_rows.astype(F32) * (1 - cloud_here).astype(F32)[:, None, None]
            + radar_rows.astype(F32) * (1 - drop_here).astype(F32)[:, None, None]
            + places
        ).astype(BF)
        start = start.reshape(rows, model)
        cotangent_rows = temporal_rows(cotangent_rows)
        date_rows = date_table.astype(F32)
    survive = jnp.repeat(survive, temporal_size // dates)[None]

    spatial_gain = spatial_gain[None]
    temporal_gain = temporal_gain[None]
    lanes = min(width, 256)

    def shape(*dims, dtype=BF):
        return jax.ShapeDtypeStruct(dims, dtype)

    def attend_dims(blocks):
        return (blocks * (width // lanes), lanes // HEAD_DIM * (rows // blocks), rows // blocks)

    layer_flops = 2 * rows * model * width * 4
    if paired:
        half = rows // 2
        own_start, other_start, cotangent_rows, date_rows = call(
            rows_kernel,
            (
                shape(half, model),
                shape(half, model),
                shape(rows, model),
                shape(dates, model, dtype=F32),
            ),
            (
                cloud,
                radar_drop,
                keep_index,
                where,
                optical_rows,
                radar_rows,
                place_table,
                date_table,
                cotangent_rows,
            ),
            scratch=(pltpu.VMEM(place_table.shape, F32), pltpu.VMEM((patches, model), F32)),
        )
        last_sent = quarter_of(spatial_weights, last_quarter)
        last_sent, own_start = fence(last_sent, own_start)
        origins = (own_start, other_start)
        spatial = gather_weights(spatial_weights, swap(first_sent, "date"), last_sent)
        sent = [quarter_of(temporal_weights, number) for number in (first_quarter, last_quarter)]
        *sent, cotangent_rows = fence(*sent, cotangent_rows)
        temporal_first = swap(sent[0], "date")
        spatial_moves = [
            (side, pair * half_rows, (pair * 2 + side) * half_rows, half_rows)
            for side in range(2)
            for pair in range(pairs)
        ]
        temporal_moves = [
            (side, pair * half_rows + eight * 16, (eight * 2 + side) * pairs * 16 + pair * 16, 16)
            for side in range(2)
            for pair in range(pairs)
            for eight in range(eights)
        ]
        half_shapes = (shape(half, model), shape(half, model))
        own, quarter = shape(rows, model // 2), model // 4
        forward_grads = (own, own, shape(rows, 2 * quarter + width))
        temporal_grads = (
            own,
            shape(rows, quarter + 3 * width // 2),
            shape(rows, 3 * width // 2 + width),
        )
        back_shapes = (shape(rows, 3 * width // 2), shape(rows, 3 * width // 2))
        backward_grads = (own, shape(rows, model // 2 + 3 * width // 2))
    else:
        origins = (start,)
        spatial_moves = [(0, at * spatial_size, at * spatial_size, spatial_size) for at in range(spatial_blocks)]
        temporal_moves = [(0, at * temporal_size, at * temporal_size, temporal_size) for at in range(temporal_blocks)]
        half_shapes = (shape(rows, model),)
        forward_grads = temporal_grads = backward_grads = (shape(rows, model),)
        back_shapes = (shape(rows, 3 * width),)

    def plan_of(blocks, moves, weights, grads, sources=0, date_of=spatial_date, patch_of=None):
        return Plan(
            blocks, moves, len(origins), weights, paired, sizes["loc"], len(grads), sources, date_of, patch_of
        )

    plan = plan_of(spatial_blocks, spatial_moves, spatial, forward_grads)
    outs = call(
        functools.partial(spatial_forward_kernel, plan),
        (
            *half_shapes,
            *forward_grads,
            shape(rows, 3 * width),
            shape(*attend_dims(spatial_blocks), dtype=F32),
            shape(rows, width),
        ),
        (where, spatial_gain, cotangent_rows, *origins, *spatial.arrays),
        scratch=(
            pltpu.VMEM((rows, model), BF),
            pltpu.VMEM((rows, model), BF),
            pltpu.VMEM((rows, model), BF),
        ),
        flops=layer_flops,
    )
    partials, outs = outs[: len(origins)], outs[len(origins) :]
    forward, (triple, attend, mixed) = outs[: len(forward_grads)], outs[len(forward_grads) :]
    if paired:
        temporal_first, kept = fence(temporal_first, partials[1])
        partials = (partials[0], kept)
        temporal = gather_weights(temporal_weights, temporal_first, sent[1])
        there, early = call(
            between_kernel,
            (shape(half, model),),
            (origins[1], partials[1], swap(partials[1], "mp"), forward[2]),
            kept=(3,),
        )
        early, there = fence(early, swap(there, "date"))
        sources = (origins[0], partials[0], swap(partials[0], "mp"), there)
        early_other = swap(early, "date")
    else:
        spatial_out = (start.astype(F32) + add_over_heads(partials[0], sizes)).astype(BF)
        moved = lax.all_to_all(
            spatial_out.reshape(dates_here, patches, model),
            "date",
            split_axis=1,
            concat_axis=0,
            tiled=True,
        )
        sources = (temporal_rows(moved),)
    plan = plan_of(
        temporal_blocks,
        temporal_moves,
        temporal,
        temporal_grads,
        len(sources),
        temporal_date,
        temporal_patch,
    )
    outs = call(
        functools.partial(temporal_kernel, plan),
        (
            *temporal_grads,
            shape(rows, model),
            shape(rows, width),
            shape(rows, model),
            shape(rows, model),
            *(() if paired else back_shapes),
        ),
        (
            where,
            temporal_gain,
            survive,
            date_rows,
            cotangent_rows,
            *sources,
            *temporal.arrays,
        ),
        scratch=(
            pltpu.VMEM((rows, model), BF),
            pltpu.VMEM((rows, 3 * width), BF),
            pltpu.VMEM(attend_dims(temporal_blocks), F32),
            pltpu.VMEM((rows, width), BF),
            pltpu.VMEM((rows, 3 * width), BF),
        ),
        flops=2 * layer_flops,
    )
    middle, outs = outs[: len(temporal_grads)], outs[len(temporal_grads) :]
    (joined, temporal_mixed, temporal_partial, back_part), temporal_triples = outs[:4], outs[4:]
    if paired:
        back_part, early_other = fence(back_part, early_other)

    if sizes["mp"] == 2:
        others = swap(back_part, "mp")
    else:
        others = (lax.psum(back_part.astype(F32), "mp") - back_part.astype(F32)).astype(BF)
    *backs, last_sent = call(
        functools.partial(norm_back_kernel, temporal_moves, temporal_size),
        half_shapes,
        (temporal_gain, back_part, others, joined, cotangent_rows, middle[-1]),
        kept=(5,),
    )
    if paired:
        back_origins = (backs[0], swap(backs[1], "date"))
        early_there = swap(early_other[:, : 2 * quarter], "mp")
        middle_other, back_own = fence(swap(middle[1], "date"), backs[0])
        back_origins = (back_own, back_origins[1])
        middle_there = swap(middle_other[:, :quarter], "mp")
        part = 3 * width // 2
        others = ((1, 0), (2, 0))
        *intake, kept = summed(
            where,
            (middle[0], middle_other, middle_there, middle[1]),
            ((0, others, (3, quarter), (1, quarter), part),),
        )
    else:
        back = lax.all_to_all(
            temporal_whole(backs[0]), "date", split_axis=0, concat_axis=1, tiled=True
        )
        back_origins = (back.reshape(rows, model),)
        kept = temporal_triples[0]
    outlet = spatial.only((3,))
    plan = plan_of(spatial_blocks, spatial_moves, outlet, backward_grads)
    *outs, kept = call(
        functools.partial(spatial_backward_kernel, plan),
        (*backward_grads, *back_shapes),
        (where, triple, attend, kept, *back_origins, *outlet.arrays),
        scratch=(
            pltpu.VMEM((rows, model), BF),
            pltpu.VMEM((rows, width), BF),
            pltpu.VMEM((rows, 3 * width), BF),
        ),
        flops=layer_flops,
        kept=(3,),
    )
    backward, back_triples = outs[: len(backward_grads)], outs[len(backward_grads) :]
    encoded = (joined.astype(F32) + add_over_heads(temporal_partial, sizes)).astype(BF)
    encoded = temporal_whole(encoded).transpose(1, 0, 2)[None]
    if not paired:
        return (
            encoded,
            whole_grads(forward[0], back_triples[0], backward[0], mixed),
            whole_grads(middle[0], kept, cotangent_rows, temporal_mixed),
        )
    intake = [*summed_over_loc((*intake, kept))]
    last_other = swap(last_sent, "date")
    *sums, upstream_own, intake[1] = summed(
        where,
        (middle[0], middle_other, middle_there, last_sent, last_other, forward[1], early_other, early_there),
        (
            (0, others, (3, 0), (4, 0), part),
            (5, ((6, quarter), (7, quarter)), (3, part), (4, part), width),
        ),
        kept=(backward[0], intake[1]),
    )
    outlet = [*summed_over_loc(sums)]
    half = model // 2
    backward_other = swap(backward[1], "date")
    *sums, intake[2], outlet[0] = summed(
        where,
        (
            upstream_own,
            backward_other,
            mixed,
            early_other,
            forward[0],
            early_there,
            back_triples[0],
        ),
        (
            (0, ((1, 0),), (2, 0), (3, 2 * quarter), width),
            (4, ((3, 0), (5, 0)), (6, 0), (1, half), back_triples[0].shape[1]),
        ),
        kept=(intake[2], outlet[0]),
    )
    spatial_terms = [*summed_over_loc(sums)]
    sums = summed(
        where,
        (forward[0], early_other, early_there, back_triples[1], swap(back_triples[1], "date")),
        ((0, ((1, 0), (2, 0)), (3, 0), (4, 0), back_triples[1].shape[1]),),
        kept=(spatial_terms[0],),
    )
    *sums, spatial_terms[0] = sums
    spatial_terms += summed_over_loc(sums)
    (temporal_grads,) = finish((*intake, *outlet), width, 0)
    spatial_grads, temporal_grads = finish(spatial_terms, width, 3, kept=temporal_grads)
    return (encoded, spatial_grads, temporal_grads)


def solution(mesh):
    in_specs = (
        P(("groups", "loc"), None, "date", None),
        P(("groups", "loc"), None, "date", None),
        P(("groups", "loc"), None),
        P(("groups", "loc"), None),
        P(("groups", "loc"), None),
        P(),
        P(),
        P(),
        P("date", None, "mp"),
        P(),
        P("date", None, "mp"),
        P(("groups", "loc"), "date", None, None),
    )
    out_specs = (
        P(("groups", "loc"), "date", None, None),
        P(("groups", "loc", "date"), None, "mp"),
        P(("groups", "loc", "date"), None, "mp"),
    )
    return jax.shard_map(
        functools.partial(per_device, dict(mesh.shape)),
        mesh=mesh,
        in_specs=in_specs,
        out_specs=out_specs,
        check_vma=False,
    )
```

```python
import functools

import jax
import jax.numpy as jnp
from jax import lax
from jax.experimental import pallas as pl
from jax.experimental.pallas import tpu as pltpu
from jax.sharding import PartitionSpec as P

HEAD_DIM = 64
EPSILON = 1e-05
CROSS = -1e30
BF = jnp.bfloat16
F32 = jnp.float32
NN = (((1,), (0,)), ((), ()))
NT = (((1,), (1,)), ((), ()))
TN = (((0,), (0,)), ((), ()))
VMEM_LIMIT = 56 * 1024 * 1024


def dot(left, right, dims):
    return lax.dot_general(left, right, dims, preferred_element_type=F32)


def statistics(rows):
    values = rows.astype(F32)
    centred = values - jnp.mean(values, -1, keepdims=True)
    inv_scale = lax.rsqrt(jnp.mean(centred * centred, -1, keepdims=True) + EPSILON)
    return centred * inv_scale, inv_scale


class Heads:
    def __init__(self, width):
        self.lanes = min(width, 256)
        self.count = self.lanes // HEAD_DIM
        owner = lax.broadcasted_iota(jnp.int32, (1, self.lanes), 1) // HEAD_DIM
        self.masks = [(owner == head).astype(F32) for head in range(self.count)]

    def stack(self, block):
        return jnp.concatenate([block * mask.astype(BF) for mask in self.masks], axis=0)

    def unstack(self, tall):
        rows = tall.shape[0] // self.count
        total = tall[0:rows] * self.masks[0]
        for head in range(1, self.count):
            total = total + tall[head * rows : (head + 1) * rows] * self.masks[head]
        return total


class Weights:
    def __init__(self, arrays, table):
        self.arrays, self.table = list(arrays), table

    def only(self, kinds):
        used = sorted({entry[0] for kind in kinds for entry in self.table[kind]})
        table = {
            kind: [(used.index(array), at, place) for array, at, place in self.table[kind]]
            for kind in kinds
        }
        return Weights([self.arrays[number] for number in used], table)


def first_row(number, rows, where):
    if number == 0:
        return where[0] * rows
    side, even = where[3], lax.rem(where[2], 2)
    side = side if number in (1, 3) else 1 - side
    even = even if number in (1, 2) else 1 - even
    return (1 - where[0]) * rows + (side * 2 + even) * (rows // 4)


def views(plan, refs, where, kind):
    found = []
    for array, at, place in plan.table[kind]:
        part = refs[array].at[at]
        if plan.paired:
            first = pl.multiple_of(first_row(place, refs[plan.table[kind][0][0]].shape[1], where), 128)
            found.append((part, pl.ds(first, part.shape[0])))
        else:
            found.append((part, slice(None)))
    return found


def rows_times(rows_ref, parts, out_ref, column):
    width = parts[0][0].shape[1]
    step = min(width, 256)
    for at in range(0, width, step):
        total = None
        for part, columns in parts:
            term = dot(rows_ref[:, columns], part[:, at : at + step], NN)
            total = term if total is None else total + term
        out_ref[:, column + at : column + at + step] = total.astype(out_ref.dtype)


def emit_own(rows_ref, out, at, date, loc_count):
    block = rows_ref.shape[1] // (2 * loc_count)
    for loc in range(loc_count):
        first = pl.multiple_of((loc * 2 + date) * block, block)
        out[:, at + loc * block : at + (loc + 1) * block] = rows_ref[:, pl.ds(first, block)]


def emit_half(rows_ref, out, at, date, core, loc_count):
    block = rows_ref.shape[1] // (2 * loc_count)
    for number in range(loc_count // 2):
        loc = core * (loc_count // 2) + number
        first = pl.multiple_of((loc * 2 + date) * block, block)
        out[:, at + number * block : at + (number + 1) * block] = rows_ref[:, pl.ds(first, block)]


def groups_of(size, spans, modulus, axis):
    shape = (size, 1) if axis == 0 else (1, size)
    return lax.rem(lax.broadcasted_iota(jnp.int32, shape, axis) // spans, modulus)


def spatial_bias(plan, size):
    query, key = (groups_of(size, *plan.date_of, axis) for axis in range(2))
    return jnp.where(query == key, 0.0, CROSS).astype(F32)


def temporal_bias(plan, size, survive):
    query, key = (groups_of(size, *plan.patch_of, axis) for axis in range(2))
    query_date, key_date = (groups_of(size, *plan.date_of, axis) for axis in range(2))
    allowed = (survive[...] == 1.0) | (query_date == key_date)
    return jnp.where(query == key, jnp.where(allowed, 0.0, -1000000000.0), CROSS).astype(F32)


def attention(triple_ref, bias, attend_ref, mixed_ref, blocks):
    width = triple_ref.shape[1] // 3
    heads = Heads(width)
    rows = triple_ref.shape[0] // blocks
    groups = width // heads.lanes
    bias = jnp.concatenate([bias] * heads.count, axis=0)
    for block in range(blocks):
        at = slice(block * rows, (block + 1) * rows)
        for group in range(groups):
            lane = group * heads.lanes
            queries = heads.stack(triple_ref[at, lane : lane + heads.lanes])
            keys = triple_ref[at, width + lane : width + lane + heads.lanes]
            values = triple_ref[at, 2 * width + lane : 2 * width + lane + heads.lanes]
            scores = dot(queries, keys, NT) * HEAD_DIM ** (-0.5) + bias
            raised = jnp.exp(scores - jnp.max(scores, -1, keepdims=True))
            attend = raised * (1.0 / jnp.sum(raised, -1, keepdims=True))
            attend_ref[block * groups + group] = attend
            mixed = heads.unstack(dot(attend.astype(BF), values, NN))
            mixed_ref[at, lane : lane + heads.lanes] = mixed.astype(BF)


def attention_back(triple_ref, attend_ref, back_mixed_ref, back_triple_ref, blocks):
    width = triple_ref.shape[1] // 3
    heads = Heads(width)
    rows = triple_ref.shape[0] // blocks
    groups = width // heads.lanes
    for block in range(blocks):
        at = slice(block * rows, (block + 1) * rows)
        for group in range(groups):
            lane = group * heads.lanes
            queries = heads.stack(triple_ref[at, lane : lane + heads.lanes])
            keys = triple_ref[at, width + lane : width + lane + heads.lanes]
            values = triple_ref[at, 2 * width + lane : 2 * width + lane + heads.lanes]
            back = heads.stack(back_mixed_ref[at, lane : lane + heads.lanes])
            attend = attend_ref[block * groups + group]
            back_attend = dot(back, values, NT)
            back_values = dot(attend.astype(BF), back, TN)
            inner = back_attend - jnp.sum(back_attend * attend, -1, keepdims=True)
            back_scores = (attend * inner * HEAD_DIM ** (-0.5)).astype(BF)
            back_queries = heads.unstack(dot(back_scores, keys, NN))
            back_keys = dot(back_scores, queries, TN)
            for number, term in enumerate((back_queries, back_keys, back_values)):
                first = number * width + lane
                back_triple_ref[at, first : first + heads.lanes] = term.astype(BF)


def normalize_into(rows_ref, gain_ref, hidden_ref, blocks):
    rows = rows_ref.shape[0] // blocks
    for block in range(blocks):
        at = slice(block * rows, (block + 1) * rows)
        normed, _ = statistics(rows_ref[at, :])
        hidden_ref[at, :] = (normed * gain_ref[...]).astype(BF)


def spatial_forward_kernel(plan, where, gain, cotangent, *refs):
    sources, refs = refs[: plan.origins], refs[plan.origins :]
    arrays, refs = refs[: plan.arrays], refs[plan.arrays :]
    partials, refs = refs[: plan.origins], refs[plan.origins :]
    grads, refs = refs[: plan.grads], refs[plan.grads :]
    triple, attend, mixed, start, hidden, whole = refs
    for source, at, to, size in plan.moves:
        start[to : to + size, :] = sources[source][at : at + size, :]
    normalize_into(start, gain, hidden, plan.blocks)
    width = mixed.shape[1]
    for kind in range(3):
        rows_times(hidden, views(plan, arrays, where, kind), triple, kind * width)
    bias = spatial_bias(plan, start.shape[0] // plan.blocks)
    attention(triple, bias, attend, mixed, plan.blocks)
    for part, features in views(plan, arrays, where, 3):
        whole[:, features] = dot(mixed[...], part[...], NT).astype(BF)
    for source, at, to, size in plan.moves:
        partials[source][at : at + size, :] = whole[to : to + size, :]
    if plan.paired:
        own_hidden, own_cotangent, sent = grads
        half = hidden.shape[1] // 4
        here, core = where[0], where[1]
        emit_own(hidden, own_hidden, 0, here, plan.locs)
        emit_own(cotangent, own_cotangent, 0, here, plan.locs)
        emit_half(hidden, sent, 0, 1 - here, core, plan.locs)
        emit_half(cotangent, sent, half, 1 - here, core, plan.locs)
        sent[:, 2 * half :] = mixed[...]
    else:
        grads[0][...] = hidden[...]


def between_kernel(start, here, there, kept, out, passed):
    total = here[...].astype(F32) + there[...].astype(F32)
    out[...] = (start[...].astype(F32) + total).astype(BF)


def temporal_kernel(plan, where, gain, survive, date_rows, cotangent, *refs):
    sources, refs = refs[: plan.sources], refs[plan.sources :]
    arrays, refs = refs[: plan.arrays], refs[plan.arrays :]
    grads, refs = refs[: plan.grads], refs[plan.grads :]
    joined, mixed, partial, back_part = refs[:4]
    back_triples, (hidden, triple, attend, back_mixed, back_triple) = refs[4:-5], refs[-5:]
    rows = joined.shape[0] // plan.blocks
    patches = rows // date_rows.shape[0]
    for source, at, to, size in plan.moves:
        if source == 0 and plan.sources > 1:
            total = sources[1][at : at + size, :].astype(F32) + sources[2][at : at + size, :].astype(F32)
            out = (sources[0][at : at + size, :].astype(F32) + total).astype(BF)
        else:
            out = sources[-1][at : at + size, :]
        out = out.astype(F32)
        dated = [
            out[at : at + patches] + date_rows[(to % rows + at) // patches : (to % rows + at) // patches + 1, :]
            for at in range(0, size, patches)
        ]
        joined[to : to + size, :] = jnp.concatenate(dated, axis=0).astype(BF)
    normalize_into(joined, gain, hidden, plan.blocks)
    width = mixed.shape[1]
    for kind in range(3):
        rows_times(hidden, views(plan, arrays, where, kind), triple, kind * width)
    outlet = views(plan, arrays, where, 3)
    rows_times(cotangent, outlet, back_mixed, 0)
    bias = temporal_bias(plan, joined.shape[0] // plan.blocks, survive)
    attention(triple, bias, attend, mixed, plan.blocks)
    for part, features in outlet:
        partial[:, features] = dot(mixed[...], part[...], NT).astype(BF)
    if plan.paired:
        own_hidden, sent, last = grads
        half = hidden.shape[1] // 2
        emit_own(hidden, own_hidden, 0, where[0], plan.locs)
        emit_own(hidden, sent, 0, 1 - where[0], plan.locs)
    else:
        grads[0][...] = hidden[...]
    attention_back(triple, attend, back_mixed, back_triple, plan.blocks)
    intakes = [views(plan, arrays, where, kind) for kind in range(3)]
    for entries in zip(*intakes):
        total = None
        for kind, (part, features) in enumerate(entries):
            term = dot(back_triple[:, kind * width : (kind + 1) * width], part[...], NT)
            total = term if total is None else total + term
        back_part[:, features] = total.astype(BF)
    split_columns(back_triple, back_triples)
    if plan.paired:
        split = sent.shape[1] - half
        sent[:, half:] = back_triple[:, :split]
        last[:, :split] = back_triple[:, split:]
        last[:, split:] = mixed[...]


def split_columns(whole, outs):
    at = 0
    for out in outs:
        out[...] = whole[:, at : at + out.shape[1]]
        at += out.shape[1]


def norm_back_kernel(moves, step, gain, here, there, joined, cotangent, kept, *outs):
    for at in range(0, joined.shape[0], step):
        span_here = slice(at, at + step)
        normed, inv_scale = statistics(joined[span_here, :])
        total = here[span_here, :].astype(F32) + there[span_here, :].astype(F32)
        scaled = total * gain[...]
        inner = (
            scaled
            - jnp.mean(scaled, -1, keepdims=True)
            - normed * jnp.mean(scaled * normed, -1, keepdims=True)
        )
        back = (cotangent[span_here, :].astype(F32) + inv_scale * inner).astype(BF)
        for target, to, first, size in moves:
            if at <= first < at + step:
                outs[target][to : to + size, :] = back[first - at : first - at + size]


def spatial_backward_kernel(plan, where, triple, attend, kept, *refs):
    sources, refs = refs[: plan.origins], refs[plan.origins :]
    arrays, refs = refs[: plan.arrays], refs[plan.arrays :]
    grads, refs = refs[: plan.grads], refs[plan.grads :]
    back_triples, (upstream, back_mixed, back_triple) = refs[:-4], refs[-3:]
    for source, at, to, size in plan.moves:
        upstream[to : to + size, :] = sources[source][at : at + size, :]
    if plan.paired:
        emit_own(upstream, grads[0], 0, where[0], plan.locs)
        emit_own(upstream, grads[1], 0, 1 - where[0], plan.locs)
    else:
        grads[0][...] = upstream[...]
    rows_times(upstream, views(plan, arrays, where, 3), back_mixed, 0)
    attention_back(triple, attend, back_mixed, back_triple, plan.blocks)
    split_columns(back_triple, back_triples)
    if plan.paired:
        half = upstream.shape[1] // 2
        grads[1][:, half:] = back_triple[:, : grads[1].shape[1] - half]


def grad_kernel(products, count, where, *refs):
    sent, far, near, other = refs[-4:]
    core, loc = where[1], where[2]
    block = near.shape[0]
    beside = loc + 1 - 2 * lax.rem(loc, 2)
    places = (lax.rem(beside + 2, 4), beside, lax.rem(loc + 2, 4), loc)
    column = 0
    for left, others, (right, right_at), (right_other, other_at), width in products:
        left, right, right_other = refs[left], refs[right], refs[right_other]
        lanes = other.shape[1] // len(others)
        for number, (source, at) in enumerate(others):
            to = 0
            if len(others) > 1:
                to = pl.multiple_of((core if number == 0 else 1 - core) * lanes, lanes)
            other[:, pl.ds(to, lanes)] = refs[source][:, at : at + lanes]
        for number, place in enumerate(places):
            columns = pl.ds(pl.multiple_of(place * block, block), block)
            for first in range(0, width, 256):
                lane = slice(column + first, column + first + 256)
                here = right[:, right_at + first : right_at + first + 256]
                there = right_other[:, other_at + first : other_at + first + 256]
                total = dot(left[:, columns], here, TN) + dot(other[:, columns], there, TN)
                if number < 2:
                    sent[number * block : (number + 1) * block, lane] = total.astype(BF)
                elif number == 2:
                    far[:, lane] = total
                else:
                    near[:, lane] = total
        column += width


def finish_kernel(kind_first, *refs):
    out = refs[-1]
    block = out.shape[0]
    column = 0
    for near, beside, far in zip(refs[0:-1:3], refs[1:-1:3], refs[2:-1:3]):
        for at in range(0, near.shape[1], 256):
            lane = slice(at, at + 256)
            total = near[:, lane] + beside[block:, lane].astype(F32) + far[:, lane].astype(F32)
            kind, first = (kind_first * out.shape[2] + column + at) // out.shape[2] % 4, (column + at) % out.shape[2]
            out[:, kind, first : first + 256] = total
        column += near.shape[1]


def finish_last_kernel(kind_first, kept, *refs):
    finish_kernel(kind_first, *refs[:-1])


def fence_kernel(*refs):
    pass


def grad_after_kernel(products, count, passed, where, *refs):
    args, rest = refs[:count], refs[count + passed :]
    grad_kernel(products, count, where, *args, *rest[:3], rest[-1])


def rows_kernel(cloud, drop, keep, where, optical, radar, table, date_table, cotangent, *refs):
    own, other, upstream, dates_out, wide_table, places = refs
    here = where[0]
    dates, patches, _ = optical.shape
    pairs, half = dates // 2, patches // 2
    wide_table[...] = table[...].astype(F32)
    for patch in range(patches):
        places[patch : patch + 1, :] = wide_table[pl.ds(keep[0, patch], 1), :]
    for pair in range(pairs):
        found = []
        for number in range(2):
            date = pair * 2 + number
            at = here * dates + date
            seen = (1 - cloud[0, at]).astype(F32)
            kept = (1 - drop[0, at]).astype(F32)
            found.append(optical[date].astype(F32) * seen + radar[date].astype(F32) * kept + places[...])
        halves = [(rows[:half], rows[half:]) for rows in found]
        for out, swapped in ((own, 0), (other, 1)):
            picked = [jnp.where(here == swapped, first, second) for first, second in halves]
            for eight in range(0, half, 8):
                rows = jnp.concatenate([rows[eight : eight + 8] for rows in picked], axis=0)
                at = pair * half * 2 + eight * 2
                out[at : at + 16, :] = rows.astype(BF)
    block = 4 * pairs * 8
    for side in range(2):
        owner = here if side == 0 else 1 - here
        for pair in range(pairs):
            found = [cotangent[owner * dates + pair * 2 + number].astype(F32) for number in range(2)]
            for eight in range(half // 8):
                rows = jnp.concatenate([rows[eight * 8 : eight * 8 + 8] for rows in found], axis=0)
                at = eight * block + side * pairs * 16 + pair * 16
                upstream[at : at + 16, :] = rows.astype(BF)
    whole = date_table[...].astype(F32)
    flipped = jnp.concatenate([whole[dates:], whole[:dates]], axis=0)
    dates_out[...] = jnp.where(here == 0, whole, flipped)


class Plan:
    def __init__(self, blocks, moves, origins, weights, paired, locs, grads, sources=0, date_of=None, patch_of=None):
        self.date_of, self.patch_of = date_of, patch_of
        self.blocks, self.moves, self.origins = blocks, moves, origins
        self.arrays, self.table = len(weights.arrays), weights.table
        self.paired, self.locs, self.grads, self.sources = paired, locs, grads, sources


def call(body, outs, args, scratch=(), flops=0, kept=()):
    smem = pl.BlockSpec(memory_space=pltpu.SMEM)
    vmem = pl.BlockSpec(memory_space=pltpu.VMEM)
    specs = [smem if arg.dtype == jnp.int32 else vmem for arg in args]
    out_specs = [vmem] * len(outs)
    aliases = {}
    outs = list(outs)
    moved = sum(arg.size * arg.dtype.itemsize for arg in args)
    moved = moved + sum(out.size * out.dtype.itemsize for out in outs)
    for number in kept:
        specs[number] = pl.BlockSpec(memory_space=pl.ANY)
        out_specs.append(pl.BlockSpec(memory_space=pl.ANY))
        outs.append(jax.ShapeDtypeStruct(args[number].shape, args[number].dtype))
        aliases[number] = len(outs) - 1
    return pl.pallas_call(
        body,
        out_shape=outs,
        in_specs=specs,
        out_specs=out_specs,
        scratch_shapes=list(scratch),
        input_output_aliases=aliases,
        compiler_params=pltpu.CompilerParams(vmem_limit_bytes=VMEM_LIMIT),
        cost_estimate=pl.CostEstimate(flops=flops, bytes_accessed=moved, transcendentals=0),
    )(*args)


def fence(*arrays):
    anywhere = [pl.BlockSpec(memory_space=pl.ANY)] * len(arrays)
    return pl.pallas_call(
        fence_kernel,
        out_shape=[jax.ShapeDtypeStruct(array.shape, array.dtype) for array in arrays],
        in_specs=anywhere,
        out_specs=anywhere,
        input_output_aliases={number: number for number in range(len(arrays))},
    )(*arrays)


def swap(array, axis):
    return lax.ppermute(array, axis, [(0, 1), (1, 0)])


PAIRS = [(0, 1), (1, 0), (2, 3), (3, 2)]
APART = [(0, 2), (1, 3), (2, 0), (3, 1)]


def quarter_of(weights, number):
    rows = weights.shape[0]
    return by_kind(lax.dynamic_slice_in_dim(weights, number * (rows // 4), rows // 4, 0))


def by_kind(weights):
    return weights.transpose(1, 0, 2)


def whole_weights(weights):
    whole = lax.all_gather(weights.transpose(1, 0, 2), "date", axis=1, tiled=True)
    return Weights([whole], {kind: [(0, kind, 0)] for kind in range(4)})


def quarters():
    side, even = lax.axis_index("groups"), lax.axis_index("loc") % 2
    return side * 2 + even, (1 - side) * 2 + 1 - even


def gather_weights(weights, first, last):
    arrays = [by_kind(weights), first, swap(first, "groups"), lax.ppermute(first, "loc", PAIRS), last]
    return Weights(arrays, {kind: [(number, kind, number) for number in range(5)] for kind in range(4)})


def add_over_heads(partial, sizes):
    if sizes["mp"] == 2:
        return partial.astype(F32) + swap(partial, "mp").astype(F32)
    return lax.psum(partial.astype(F32), "mp")


def whole_grads(hidden, back_triple, upstream, mixed):
    width = mixed.shape[1]
    intake = dot(hidden, back_triple, TN)
    outlet = dot(upstream, mixed, TN)
    whole = jnp.concatenate([intake, outlet], axis=1).reshape(-1, 4, width)
    part = lax.psum_scatter(whole.astype(BF), ("loc", "date"), scatter_dimension=0, tiled=True)
    return part.astype(F32)


def summed(where, args, products, kept=()):
    rows, columns = args[products[0][0]].shape
    block, width = columns // 4, sum(product[-1] for product in products)
    return call(
        functools.partial(grad_after_kernel, products, len(args), len(kept)),
        (
            jax.ShapeDtypeStruct((2 * block, width), BF),
            jax.ShapeDtypeStruct((block, width), F32),
            jax.ShapeDtypeStruct((block, width), F32),
        ),
        (where, *args, *kept),
        scratch=(pltpu.VMEM((rows, columns), BF),),
        flops=4 * rows * columns * width,
        kept=tuple(range(1 + len(args), 1 + len(args) + len(kept))),
    )


def summed_over_loc(outs):
    sent, far, near = outs[:3]
    beside = lax.ppermute(sent, "loc", PAIRS)
    far = (far + beside[: far.shape[0]].astype(F32)).astype(BF)
    return near, beside, lax.ppermute(far, "loc", APART)


def finish(terms, width, kind_first, kept=None):
    out = jax.ShapeDtypeStruct((terms[0].shape[0], 4, width), F32)
    if kept is None:
        return call(functools.partial(finish_kernel, kind_first), (out,), terms)
    return call(functools.partial(finish_last_kernel, kind_first), (out,), (kept, *terms), kept=(0,))


def per_device(
    sizes,
    optical,
    radar,
    cloud,
    radar_drop,
    keep_index,
    place_table,
    date_table,
    spatial_gain,
    spatial_weights,
    temporal_gain,
    temporal_weights,
    cotangent,
):
    _, patches, dates_here, model = optical.shape
    patches_here, dates = cotangent.shape[1:3]
    width = spatial_weights.shape[2]
    rows = patches * dates_here
    here = lax.axis_index("date")
    first = here * dates_here
    paired = sizes["groups"] == 2 and sizes["loc"] == 4 and sizes["date"] == 2 and sizes["mp"] == 2
    paired = paired and dates_here % 2 == 0 and patches_here % 8 == 0 and model % 1024 == 0
    if paired:
        first_quarter, last_quarter = quarters()
        first_sent = quarter_of(spatial_weights, first_quarter)
    else:
        spatial, temporal = whole_weights(spatial_weights), whole_weights(temporal_weights)

    if paired:
        pairs, eights = dates_here // 2, patches_here // 8
        spatial_blocks, temporal_blocks = pairs, eights
        half_rows = eights * 16

        def temporal_whole(array):
            array = array.reshape(eights, 2, pairs, 2, 8, -1).transpose(1, 2, 3, 0, 4, 5)
            return jnp.where(here == 0, array, jnp.flip(array, 0)).reshape(dates, patches_here, -1)

        spatial_date, temporal_date, temporal_patch = (8, 2), (8, rows), (1, 8)
    else:
        spatial_blocks = 1 if rows <= 192 else dates_here
        temporal_blocks = patches_here // 8 if patches_here % 8 == 0 else 1

        def temporal_rows(array):
            array = array.reshape(dates, temporal_blocks, patches_here // temporal_blocks, -1)
            return array.transpose(1, 0, 2, 3).reshape(rows, -1)

        def temporal_whole(array):
            array = array.reshape(temporal_blocks, dates, patches_here // temporal_blocks, -1)
            return array.transpose(1, 0, 2, 3).reshape(dates, patches_here, -1)

        in_block = patches_here // temporal_blocks
        spatial_date, temporal_date, temporal_patch = (patches, rows), (in_block, rows), (1, in_block)
    spatial_size, temporal_size = rows // spatial_blocks, rows // temporal_blocks

    survive = (1 - cloud[0] * radar_drop[0]).astype(F32)
    side = lax.axis_index("groups") if paired else here
    where = jnp.stack([here, lax.axis_index("mp"), lax.axis_index("loc"), side]).astype(jnp.int32)
    optical_rows, radar_rows = optical[0].transpose(1, 0, 2), radar[0].transpose(1, 0, 2)
    cotangent_rows = cotangent[0].transpose(1, 0, 2)
    if paired:
        survive = jnp.where(here == 0, survive, jnp.roll(survive, dates_here))
    else:
        cloud_here = lax.dynamic_slice_in_dim(cloud, first, dates_here, 1)[0]
        drop_here = lax.dynamic_slice_in_dim(radar_drop, first, dates_here, 1)[0]
        places = jnp.take(place_table, keep_index[0], axis=0).astype(F32)[None]
        start = (
            optical_rows.astype(F32) * (1 - cloud_here).astype(F32)[:, None, None]
            + radar_rows.astype(F32) * (1 - drop_here).astype(F32)[:, None, None]
            + places
        ).astype(BF)
        start = start.reshape(rows, model)
        cotangent_rows = temporal_rows(cotangent_rows)
        date_rows = date_table.astype(F32)
    survive = jnp.repeat(survive, temporal_size // dates)[None]

    spatial_gain = spatial_gain[None]
    temporal_gain = temporal_gain[None]
    lanes = min(width, 256)

    def shape(*dims, dtype=BF):
        return jax.ShapeDtypeStruct(dims, dtype)

    def attend_dims(blocks):
        return (blocks * (width // lanes), lanes // HEAD_DIM * (rows // blocks), rows // blocks)

    layer_flops = 2 * rows * model * width * 4
    if paired:
        half = rows // 2
        own_start, other_start, cotangent_rows, date_rows = call(
            rows_kernel,
            (
                shape(half, model),
                shape(half, model),
                shape(rows, model),
                shape(dates, model, dtype=F32),
            ),
            (
                cloud,
                radar_drop,
                keep_index,
                where,
                optical_rows,
                radar_rows,
                place_table,
                date_table,
                cotangent_rows,
            ),
            scratch=(pltpu.VMEM(place_table.shape, F32), pltpu.VMEM((patches, model), F32)),
        )
        last_sent = quarter_of(spatial_weights, last_quarter)
        last_sent, own_start = fence(last_sent, own_start)
        origins = (own_start, other_start)
        spatial = gather_weights(spatial_weights, swap(first_sent, "date"), swap(last_sent, "date"))
        sent = [quarter_of(temporal_weights, number) for number in (first_quarter, last_quarter)]
        *sent, cotangent_rows = fence(*sent, cotangent_rows)
        temporal_first = swap(sent[0], "date")
        spatial_moves = [
            (side, pair * half_rows, (pair * 2 + side) * half_rows, half_rows)
            for side in range(2)
            for pair in range(pairs)
        ]
        temporal_moves = [
            (side, pair * half_rows + eight * 16, (eight * 2 + side) * pairs * 16 + pair * 16, 16)
            for side in range(2)
            for pair in range(pairs)
            for eight in range(eights)
        ]
        half_shapes = (shape(half, model), shape(half, model))
        own, quarter = shape(rows, model // 2), model // 4
        forward_grads = (own, own, shape(rows, 2 * quarter + width))
        temporal_grads = (
            own,
            shape(rows, model // 2 + 3 * width // 2),
            shape(rows, 3 * width // 2 + width),
        )
        back_shapes = (shape(rows, 3 * width // 2), shape(rows, 3 * width // 2))
        backward_grads = (own, shape(rows, model // 2 + 3 * width // 2))
    else:
        origins = (start,)
        spatial_moves = [(0, at * spatial_size, at * spatial_size, spatial_size) for at in range(spatial_blocks)]
        temporal_moves = [(0, at * temporal_size, at * temporal_size, temporal_size) for at in range(temporal_blocks)]
        half_shapes = (shape(rows, model),)
        forward_grads = temporal_grads = backward_grads = (shape(rows, model),)
        back_shapes = (shape(rows, 3 * width),)

    def plan_of(blocks, moves, weights, grads, sources=0, date_of=spatial_date, patch_of=None):
        return Plan(
            blocks, moves, len(origins), weights, paired, sizes["loc"], len(grads), sources, date_of, patch_of
        )

    plan = plan_of(spatial_blocks, spatial_moves, spatial, forward_grads)
    outs = call(
        functools.partial(spatial_forward_kernel, plan),
        (
            *half_shapes,
            *forward_grads,
            shape(rows, 3 * width),
            shape(*attend_dims(spatial_blocks), dtype=F32),
            shape(rows, width),
        ),
        (where, spatial_gain, cotangent_rows, *origins, *spatial.arrays),
        scratch=(
            pltpu.VMEM((rows, model), BF),
            pltpu.VMEM((rows, model), BF),
            pltpu.VMEM((rows, model), BF),
        ),
        flops=layer_flops,
    )
    partials, outs = outs[: len(origins)], outs[len(origins) :]
    forward, (triple, attend, mixed) = outs[: len(forward_grads)], outs[len(forward_grads) :]
    if paired:
        temporal_first, kept = fence(temporal_first, partials[1])
        partials = (partials[0], kept)
        there, early = call(
            between_kernel,
            (shape(half, model),),
            (origins[1], partials[1], swap(partials[1], "mp"), forward[2]),
            kept=(3,),
        )
        temporal = gather_weights(temporal_weights, temporal_first, swap(sent[1], "date"))
        early, there, *temporal.arrays[2:] = fence(early, swap(there, "date"), *temporal.arrays[2:])
        sources = (origins[0], partials[0], swap(partials[0], "mp"), there)
        early_other = swap(early, "date")
    else:
        spatial_out = (start.astype(F32) + add_over_heads(partials[0], sizes)).astype(BF)
        moved = lax.all_to_all(
            spatial_out.reshape(dates_here, patches, model),
            "date",
            split_axis=1,
            concat_axis=0,
            tiled=True,
        )
        sources = (temporal_rows(moved),)
    plan = plan_of(
        temporal_blocks,
        temporal_moves,
        temporal,
        temporal_grads,
        len(sources),
        temporal_date,
        temporal_patch,
    )
    outs = call(
        functools.partial(temporal_kernel, plan),
        (
            *temporal_grads,
            shape(rows, model),
            shape(rows, width),
            shape(rows, model),
            shape(rows, model),
            *(() if paired else back_shapes),
        ),
        (
            where,
            temporal_gain,
            survive,
            date_rows,
            cotangent_rows,
            *sources,
            *temporal.arrays,
        ),
        scratch=(
            pltpu.VMEM((rows, model), BF),
            pltpu.VMEM((rows, 3 * width), BF),
            pltpu.VMEM(attend_dims(temporal_blocks), F32),
            pltpu.VMEM((rows, width), BF),
            pltpu.VMEM((rows, 3 * width), BF),
        ),
        flops=2 * layer_flops,
    )
    middle, outs = outs[: len(temporal_grads)], outs[len(temporal_grads) :]
    (joined, temporal_mixed, temporal_partial, back_part), temporal_triples = outs[:4], outs[4:]
    if paired:
        back_part, early_other = fence(back_part, early_other)

    if sizes["mp"] == 2:
        others = swap(back_part, "mp")
    else:
        others = (lax.psum(back_part.astype(F32), "mp") - back_part.astype(F32)).astype(BF)
    *backs, last_sent = call(
        functools.partial(norm_back_kernel, temporal_moves, temporal_size),
        half_shapes,
        (temporal_gain, back_part, others, joined, cotangent_rows, middle[-1]),
        kept=(5,),
    )
    if paired:
        back_origins = (backs[0], swap(backs[1], "date"))
        early_there = swap(early_other[:, : 2 * quarter], "mp")
        middle_other = swap(middle[1], "date")
        part, columns = 3 * width // 2, model // 2
        *intake, kept = summed(
            where,
            (middle[0], middle_other, middle[1]),
            ((0, ((1, 0),), (2, columns), (1, columns), part),),
        )
    else:
        back = lax.all_to_all(
            temporal_whole(backs[0]), "date", split_axis=0, concat_axis=1, tiled=True
        )
        back_origins = (back.reshape(rows, model),)
        kept = temporal_triples[0]
    outlet = spatial.only((3,))
    plan = plan_of(spatial_blocks, spatial_moves, outlet, backward_grads)
    *outs, kept = call(
        functools.partial(spatial_backward_kernel, plan),
        (*backward_grads, *back_shapes),
        (where, triple, attend, kept, *back_origins, *outlet.arrays),
        scratch=(
            pltpu.VMEM((rows, model), BF),
            pltpu.VMEM((rows, width), BF),
            pltpu.VMEM((rows, 3 * width), BF),
        ),
        flops=layer_flops,
        kept=(3,),
    )
    backward, back_triples = outs[: len(backward_grads)], outs[len(backward_grads) :]
    encoded = (joined.astype(F32) + add_over_heads(temporal_partial, sizes)).astype(BF)
    encoded = temporal_whole(encoded).transpose(1, 0, 2)[None]
    if not paired:
        return (
            encoded,
            whole_grads(forward[0], back_triples[0], backward[0], mixed),
            whole_grads(middle[0], kept, cotangent_rows, temporal_mixed),
        )
    intake = [*summed_over_loc((*intake, kept))]
    last_other = swap(last_sent, "date")
    *sums, upstream_own, intake[1] = summed(
        where,
        (middle[0], middle_other, last_sent, last_other, forward[1], early_other, early_there),
        (
            (0, ((1, 0),), (2, 0), (3, 0), part),
            (4, ((5, quarter), (6, quarter)), (2, part), (3, part), width),
        ),
        kept=(backward[0], intake[1]),
    )
    outlet = [*summed_over_loc(sums)]
    half = model // 2
    backward_other = swap(backward[1], "date")
    *sums, outlet[0] = summed(
        where,
        (
            upstream_own,
            backward_other,
            mixed,
            early_other,
            forward[0],
            early_there,
            back_triples[0],
        ),
        (
            (0, ((1, 0),), (2, 0), (3, 2 * quarter), width),
            (4, ((3, 0), (5, 0)), (6, 0), (1, half), back_triples[0].shape[1]),
        ),
        kept=(outlet[0],),
    )
    spatial_terms = [*summed_over_loc(sums)]
    sums = summed(
        where,
        (forward[0], early_other, early_there, back_triples[1], swap(back_triples[1], "date")),
        ((0, ((1, 0), (2, 0)), (3, 0), (4, 0), back_triples[1].shape[1]),),
        kept=(spatial_terms[0],),
    )
    *sums, spatial_terms[0] = sums
    spatial_terms += summed_over_loc(sums)
    (temporal_grads,) = finish((*intake, *outlet), width, 0)
    spatial_grads, temporal_grads = finish(spatial_terms, width, 3, kept=temporal_grads)
    return (encoded, spatial_grads, temporal_grads)


def solution(mesh):
    in_specs = (
        P(("groups", "loc"), None, "date", None),
        P(("groups", "loc"), None, "date", None),
        P(("groups", "loc"), None),
        P(("groups", "loc"), None),
        P(("groups", "loc"), None),
        P(),
        P(),
        P(),
        P("date", None, "mp"),
        P(),
        P("date", None, "mp"),
        P(("groups", "loc"), "date", None, None),
    )
    out_specs = (
        P(("groups", "loc"), "date", None, None),
        P(("groups", "loc", "date"), None, "mp"),
        P(("groups", "loc", "date"), None, "mp"),
    )
    return jax.shard_map(
        functools.partial(per_device, dict(mesh.shape)),
        mesh=mesh,
        in_specs=in_specs,
        out_specs=out_specs,
        check_vma=False,
    )
```

```python
import functools

import jax
import jax.numpy as jnp
from jax import lax
from jax.experimental import pallas as pl
from jax.experimental.pallas import tpu as pltpu
from jax.sharding import PartitionSpec as P

HEAD_DIM = 64
EPSILON = 1e-05
CROSS = -1e30
BF = jnp.bfloat16
F32 = jnp.float32
NN = (((1,), (0,)), ((), ()))
NT = (((1,), (1,)), ((), ()))
TN = (((0,), (0,)), ((), ()))
VMEM_LIMIT = 56 * 1024 * 1024


def dot(left, right, dims):
    return lax.dot_general(left, right, dims, preferred_element_type=F32)


def statistics(rows):
    values = rows.astype(F32)
    centred = values - jnp.mean(values, -1, keepdims=True)
    inv_scale = lax.rsqrt(jnp.mean(centred * centred, -1, keepdims=True) + EPSILON)
    return centred * inv_scale, inv_scale


class Heads:
    def __init__(self, width):
        self.lanes = min(width, 256)
        self.count = self.lanes // HEAD_DIM
        owner = lax.broadcasted_iota(jnp.int32, (1, self.lanes), 1) // HEAD_DIM
        self.masks = [(owner == head).astype(F32) for head in range(self.count)]

    def stack(self, block):
        return jnp.concatenate([block * mask.astype(BF) for mask in self.masks], axis=0)

    def unstack(self, tall):
        rows = tall.shape[0] // self.count
        total = tall[0:rows] * self.masks[0]
        for head in range(1, self.count):
            total = total + tall[head * rows : (head + 1) * rows] * self.masks[head]
        return total


class Weights:
    def __init__(self, arrays, table):
        self.arrays, self.table = list(arrays), table

    def only(self, kinds):
        used = sorted({entry[0] for kind in kinds for entry in self.table[kind]})
        table = {
            kind: [(used.index(array), at, place) for array, at, place in self.table[kind]]
            for kind in kinds
        }
        return Weights([self.arrays[number] for number in used], table)


def first_row(number, rows, where):
    if number == 0:
        return where[0] * rows
    side, even = where[3], lax.rem(where[2], 2)
    side = side if number in (1, 3) else 1 - side
    even = even if number in (1, 2) else 1 - even
    return (1 - where[0]) * rows + (side * 2 + even) * (rows // 4)


def views(plan, refs, where, kind):
    found = []
    for array, at, place in plan.table[kind]:
        part = refs[array].at[at]
        if plan.paired:
            first = pl.multiple_of(first_row(place, refs[plan.table[kind][0][0]].shape[1], where), 128)
            found.append((part, pl.ds(first, part.shape[0])))
        else:
            found.append((part, slice(None)))
    return found


def rows_times(rows_ref, parts, out_ref, column):
    width = parts[0][0].shape[1]
    step = min(width, 256)
    for at in range(0, width, step):
        total = None
        for part, columns in parts:
            term = dot(rows_ref[:, columns], part[:, at : at + step], NN)
            total = term if total is None else total + term
        out_ref[:, column + at : column + at + step] = total.astype(out_ref.dtype)


def emit_own(rows_ref, out, at, date, loc_count):
    block = rows_ref.shape[1] // (2 * loc_count)
    for loc in range(loc_count):
        first = pl.multiple_of((loc * 2 + date) * block, block)
        out[:, at + loc * block : at + (loc + 1) * block] = rows_ref[:, pl.ds(first, block)]


def emit_half(rows_ref, out, at, date, core, loc_count):
    block = rows_ref.shape[1] // (2 * loc_count)
    for number in range(loc_count // 2):
        loc = core * (loc_count // 2) + number
        first = pl.multiple_of((loc * 2 + date) * block, block)
        out[:, at + number * block : at + (number + 1) * block] = rows_ref[:, pl.ds(first, block)]


def groups_of(size, spans, modulus, axis):
    shape = (size, 1) if axis == 0 else (1, size)
    return lax.rem(lax.broadcasted_iota(jnp.int32, shape, axis) // spans, modulus)


def spatial_bias(plan, size):
    query, key = (groups_of(size, *plan.date_of, axis) for axis in range(2))
    return jnp.where(query == key, 0.0, CROSS).astype(F32)


def temporal_bias(plan, size, survive):
    query, key = (groups_of(size, *plan.patch_of, axis) for axis in range(2))
    query_date, key_date = (groups_of(size, *plan.date_of, axis) for axis in range(2))
    allowed = (survive[...] == 1.0) | (query_date == key_date)
    return jnp.where(query == key, jnp.where(allowed, 0.0, -1000000000.0), CROSS).astype(F32)


def attention(triple_ref, bias, attend_ref, mixed_ref, blocks):
    width = triple_ref.shape[1] // 3
    heads = Heads(width)
    rows = triple_ref.shape[0] // blocks
    groups = width // heads.lanes
    bias = jnp.concatenate([bias] * heads.count, axis=0)
    for block in range(blocks):
        at = slice(block * rows, (block + 1) * rows)
        for group in range(groups):
            lane = group * heads.lanes
            queries = heads.stack(triple_ref[at, lane : lane + heads.lanes])
            keys = triple_ref[at, width + lane : width + lane + heads.lanes]
            values = triple_ref[at, 2 * width + lane : 2 * width + lane + heads.lanes]
            scores = dot(queries, keys, NT) * HEAD_DIM ** (-0.5) + bias
            raised = jnp.exp(scores - jnp.max(scores, -1, keepdims=True))
            attend = raised * (1.0 / jnp.sum(raised, -1, keepdims=True))
            attend_ref[block * groups + group] = attend
            mixed = heads.unstack(dot(attend.astype(BF), values, NN))
            mixed_ref[at, lane : lane + heads.lanes] = mixed.astype(BF)


def attention_back(triple_ref, attend_ref, back_mixed_ref, back_triple_ref, blocks):
    width = triple_ref.shape[1] // 3
    heads = Heads(width)
    rows = triple_ref.shape[0] // blocks
    groups = width // heads.lanes
    for block in range(blocks):
        at = slice(block * rows, (block + 1) * rows)
        for group in range(groups):
            lane = group * heads.lanes
            queries = heads.stack(triple_ref[at, lane : lane + heads.lanes])
            keys = triple_ref[at, width + lane : width + lane + heads.lanes]
            values = triple_ref[at, 2 * width + lane : 2 * width + lane + heads.lanes]
            back = heads.stack(back_mixed_ref[at, lane : lane + heads.lanes])
            attend = attend_ref[block * groups + group]
            back_attend = dot(back, values, NT)
            back_values = dot(attend.astype(BF), back, TN)
            inner = back_attend - jnp.sum(back_attend * attend, -1, keepdims=True)
            back_scores = (attend * inner * HEAD_DIM ** (-0.5)).astype(BF)
            back_queries = heads.unstack(dot(back_scores, keys, NN))
            back_keys = dot(back_scores, queries, TN)
            for number, term in enumerate((back_queries, back_keys, back_values)):
                first = number * width + lane
                back_triple_ref[at, first : first + heads.lanes] = term.astype(BF)


def normalize_into(rows_ref, gain_ref, hidden_ref, blocks):
    rows = rows_ref.shape[0] // blocks
    for block in range(blocks):
        at = slice(block * rows, (block + 1) * rows)
        normed, _ = statistics(rows_ref[at, :])
        hidden_ref[at, :] = (normed * gain_ref[...]).astype(BF)


def spatial_forward_kernel(plan, where, gain, cotangent, *refs):
    sources, refs = refs[: plan.origins], refs[plan.origins :]
    arrays, refs = refs[: plan.arrays], refs[plan.arrays :]
    partials, refs = refs[: plan.origins], refs[plan.origins :]
    grads, refs = refs[: plan.grads], refs[plan.grads :]
    triple, attend, mixed, start, hidden, whole = refs
    for source, at, to, size in plan.moves:
        start[to : to + size, :] = sources[source][at : at + size, :]
    normalize_into(start, gain, hidden, plan.blocks)
    width = mixed.shape[1]
    for kind in range(3):
        rows_times(hidden, views(plan, arrays, where, kind), triple, kind * width)
    bias = spatial_bias(plan, start.shape[0] // plan.blocks)
    attention(triple, bias, attend, mixed, plan.blocks)
    for part, features in views(plan, arrays, where, 3):
        whole[:, features] = dot(mixed[...], part[...], NT).astype(BF)
    for source, at, to, size in plan.moves:
        partials[source][at : at + size, :] = whole[to : to + size, :]
    if plan.paired:
        own_hidden, own_cotangent, sent = grads
        half = hidden.shape[1] // 4
        here, core = where[0], where[1]
        emit_own(hidden, own_hidden, 0, here, plan.locs)
        emit_own(cotangent, own_cotangent, 0, here, plan.locs)
        emit_half(hidden, sent, 0, 1 - here, core, plan.locs)
        emit_half(cotangent, sent, half, 1 - here, core, plan.locs)
        sent[:, 2 * half :] = mixed[...]
    else:
        grads[0][...] = hidden[...]


def between_kernel(start, here, there, kept, out, passed):
    total = here[...].astype(F32) + there[...].astype(F32)
    out[...] = (start[...].astype(F32) + total).astype(BF)


def temporal_kernel(plan, where, gain, survive, date_rows, cotangent, *refs):
    sources, refs = refs[: plan.sources], refs[plan.sources :]
    arrays, refs = refs[: plan.arrays], refs[plan.arrays :]
    grads, refs = refs[: plan.grads], refs[plan.grads :]
    joined, mixed, partial, back_part = refs[:4]
    back_triples, (hidden, triple, attend, back_mixed, back_triple) = refs[4:-5], refs[-5:]
    rows = joined.shape[0] // plan.blocks
    patches = rows // date_rows.shape[0]
    for source, at, to, size in plan.moves:
        if source == 0 and plan.sources > 1:
            total = sources[1][at : at + size, :].astype(F32) + sources[2][at : at + size, :].astype(F32)
            out = (sources[0][at : at + size, :].astype(F32) + total).astype(BF)
        else:
            out = sources[-1][at : at + size, :]
        out = out.astype(F32)
        dated = [
            out[at : at + patches] + date_rows[(to % rows + at) // patches : (to % rows + at) // patches + 1, :]
            for at in range(0, size, patches)
        ]
        joined[to : to + size, :] = jnp.concatenate(dated, axis=0).astype(BF)
    normalize_into(joined, gain, hidden, plan.blocks)
    width = mixed.shape[1]
    for kind in range(3):
        rows_times(hidden, views(plan, arrays, where, kind), triple, kind * width)
    outlet = views(plan, arrays, where, 3)
    rows_times(cotangent, outlet, back_mixed, 0)
    bias = temporal_bias(plan, joined.shape[0] // plan.blocks, survive)
    attention(triple, bias, attend, mixed, plan.blocks)
    for part, features in outlet:
        partial[:, features] = dot(mixed[...], part[...], NT).astype(BF)
    if plan.paired:
        own_hidden, sent, last = grads
        half = hidden.shape[1] // 2
        emit_own(hidden, own_hidden, 0, where[0], plan.locs)
        emit_own(hidden, sent, 0, 1 - where[0], plan.locs)
    else:
        grads[0][...] = hidden[...]
    attention_back(triple, attend, back_mixed, back_triple, plan.blocks)
    intakes = [views(plan, arrays, where, kind) for kind in range(3)]
    for entries in zip(*intakes):
        total = None
        for kind, (part, features) in enumerate(entries):
            term = dot(back_triple[:, kind * width : (kind + 1) * width], part[...], NT)
            total = term if total is None else total + term
        back_part[:, features] = total.astype(BF)
    split_columns(back_triple, back_triples)
    if plan.paired:
        split = sent.shape[1] - half
        sent[:, half:] = back_triple[:, :split]
        last[:, :split] = back_triple[:, split:]
        last[:, split:] = mixed[...]


def split_columns(whole, outs):
    at = 0
    for out in outs:
        out[...] = whole[:, at : at + out.shape[1]]
        at += out.shape[1]


def norm_back_kernel(moves, step, gain, here, there, joined, cotangent, kept, *outs):
    for at in range(0, joined.shape[0], step):
        span_here = slice(at, at + step)
        normed, inv_scale = statistics(joined[span_here, :])
        total = here[span_here, :].astype(F32) + there[span_here, :].astype(F32)
        scaled = total * gain[...]
        inner = (
            scaled
            - jnp.mean(scaled, -1, keepdims=True)
            - normed * jnp.mean(scaled * normed, -1, keepdims=True)
        )
        back = (cotangent[span_here, :].astype(F32) + inv_scale * inner).astype(BF)
        for target, to, first, size in moves:
            if at <= first < at + step:
                outs[target][to : to + size, :] = back[first - at : first - at + size]


def spatial_backward_kernel(plan, where, triple, attend, kept, *refs):
    sources, refs = refs[: plan.origins], refs[plan.origins :]
    arrays, refs = refs[: plan.arrays], refs[plan.arrays :]
    grads, refs = refs[: plan.grads], refs[plan.grads :]
    back_triples, (upstream, back_mixed, back_triple) = refs[:-4], refs[-3:]
    for source, at, to, size in plan.moves:
        upstream[to : to + size, :] = sources[source][at : at + size, :]
    if plan.paired:
        emit_own(upstream, grads[0], 0, where[0], plan.locs)
        emit_own(upstream, grads[1], 0, 1 - where[0], plan.locs)
    else:
        grads[0][...] = upstream[...]
    rows_times(upstream, views(plan, arrays, where, 3), back_mixed, 0)
    attention_back(triple, attend, back_mixed, back_triple, plan.blocks)
    split_columns(back_triple, back_triples)
    if plan.paired:
        half = upstream.shape[1] // 2
        grads[1][:, half:] = back_triple[:, : grads[1].shape[1] - half]


def grad_kernel(products, count, where, *refs):
    sent, far, near, other = refs[-4:]
    core, loc = where[1], where[2]
    block = near.shape[0]
    beside = loc + 1 - 2 * lax.rem(loc, 2)
    places = (lax.rem(beside + 2, 4), beside, lax.rem(loc + 2, 4), loc)
    column = 0
    for left, others, (right, right_at), (right_other, other_at), width in products:
        left, right, right_other = refs[left], refs[right], refs[right_other]
        lanes = other.shape[1] // len(others)
        for number, (source, at) in enumerate(others):
            to = 0
            if len(others) > 1:
                to = pl.multiple_of((core if number == 0 else 1 - core) * lanes, lanes)
            other[:, pl.ds(to, lanes)] = refs[source][:, at : at + lanes]
        for number, place in enumerate(places):
            columns = pl.ds(pl.multiple_of(place * block, block), block)
            for first in range(0, width, 256):
                lane = slice(column + first, column + first + 256)
                here = right[:, right_at + first : right_at + first + 256]
                there = right_other[:, other_at + first : other_at + first + 256]
                total = dot(left[:, columns], here, TN) + dot(other[:, columns], there, TN)
                if number < 2:
                    sent[number * block : (number + 1) * block, lane] = total.astype(BF)
                elif number == 2:
                    far[:, lane] = total
                else:
                    near[:, lane] = total
        column += width


def finish_kernel(kind_first, *refs):
    out = refs[-1]
    block = out.shape[0]
    column = 0
    for near, beside, far in zip(refs[0:-1:3], refs[1:-1:3], refs[2:-1:3]):
        for at in range(0, near.shape[1], 256):
            lane = slice(at, at + 256)
            total = near[:, lane] + beside[block:, lane].astype(F32) + far[:, lane].astype(F32)
            kind, first = (kind_first * out.shape[2] + column + at) // out.shape[2] % 4, (column + at) % out.shape[2]
            out[:, kind, first : first + 256] = total
        column += near.shape[1]


def finish_last_kernel(kind_first, kept, *refs):
    finish_kernel(kind_first, *refs[:-1])


def fence_kernel(*refs):
    pass


def grad_after_kernel(products, count, passed, where, *refs):
    args, rest = refs[:count], refs[count + passed :]
    grad_kernel(products, count, where, *args, *rest[:3], rest[-1])


def rows_kernel(cloud, drop, keep, where, optical, radar, table, date_table, cotangent, *refs):
    own, other, upstream, dates_out, wide_table, places = refs
    here = where[0]
    dates, patches, _ = optical.shape
    pairs, half = dates // 2, patches // 2
    wide_table[...] = table[...].astype(F32)
    for patch in range(patches):
        places[patch : patch + 1, :] = wide_table[pl.ds(keep[0, patch], 1), :]
    for pair in range(pairs):
        found = []
        for number in range(2):
            date = pair * 2 + number
            at = here * dates + date
            seen = (1 - cloud[0, at]).astype(F32)
            kept = (1 - drop[0, at]).astype(F32)
            found.append(optical[date].astype(F32) * seen + radar[date].astype(F32) * kept + places[...])
        halves = [(rows[:half], rows[half:]) for rows in found]
        for out, swapped in ((own, 0), (other, 1)):
            picked = [jnp.where(here == swapped, first, second) for first, second in halves]
            for eight in range(0, half, 8):
                rows = jnp.concatenate([rows[eight : eight + 8] for rows in picked], axis=0)
                at = pair * half * 2 + eight * 2
                out[at : at + 16, :] = rows.astype(BF)
    block = 4 * pairs * 8
    for side in range(2):
        owner = here if side == 0 else 1 - here
        for pair in range(pairs):
            found = [cotangent[owner * dates + pair * 2 + number].astype(F32) for number in range(2)]
            for eight in range(half // 8):
                rows = jnp.concatenate([rows[eight * 8 : eight * 8 + 8] for rows in found], axis=0)
                at = eight * block + side * pairs * 16 + pair * 16
                upstream[at : at + 16, :] = rows.astype(BF)
    whole = date_table[...].astype(F32)
    flipped = jnp.concatenate([whole[dates:], whole[:dates]], axis=0)
    dates_out[...] = jnp.where(here == 0, whole, flipped)


class Plan:
    def __init__(self, blocks, moves, origins, weights, paired, locs, grads, sources=0, date_of=None, patch_of=None):
        self.date_of, self.patch_of = date_of, patch_of
        self.blocks, self.moves, self.origins = blocks, moves, origins
        self.arrays, self.table = len(weights.arrays), weights.table
        self.paired, self.locs, self.grads, self.sources = paired, locs, grads, sources


def call(body, outs, args, scratch=(), flops=0, kept=()):
    smem = pl.BlockSpec(memory_space=pltpu.SMEM)
    vmem = pl.BlockSpec(memory_space=pltpu.VMEM)
    specs = [smem if arg.dtype == jnp.int32 else vmem for arg in args]
    out_specs = [vmem] * len(outs)
    aliases = {}
    outs = list(outs)
    moved = sum(arg.size * arg.dtype.itemsize for arg in args)
    moved = moved + sum(out.size * out.dtype.itemsize for out in outs)
    for number in kept:
        specs[number] = pl.BlockSpec(memory_space=pl.ANY)
        out_specs.append(pl.BlockSpec(memory_space=pl.ANY))
        outs.append(jax.ShapeDtypeStruct(args[number].shape, args[number].dtype))
        aliases[number] = len(outs) - 1
    return pl.pallas_call(
        body,
        out_shape=outs,
        in_specs=specs,
        out_specs=out_specs,
        scratch_shapes=list(scratch),
        input_output_aliases=aliases,
        compiler_params=pltpu.CompilerParams(vmem_limit_bytes=VMEM_LIMIT),
        cost_estimate=pl.CostEstimate(flops=flops, bytes_accessed=moved, transcendentals=0),
    )(*args)


def fence(*arrays):
    anywhere = [pl.BlockSpec(memory_space=pl.ANY)] * len(arrays)
    return pl.pallas_call(
        fence_kernel,
        out_shape=[jax.ShapeDtypeStruct(array.shape, array.dtype) for array in arrays],
        in_specs=anywhere,
        out_specs=anywhere,
        input_output_aliases={number: number for number in range(len(arrays))},
    )(*arrays)


def swap(array, axis):
    return lax.ppermute(array, axis, [(0, 1), (1, 0)])


PAIRS = [(0, 1), (1, 0), (2, 3), (3, 2)]
APART = [(0, 2), (1, 3), (2, 0), (3, 1)]


def quarter_of(weights, number):
    rows = weights.shape[0]
    return by_kind(lax.dynamic_slice_in_dim(weights, number * (rows // 4), rows // 4, 0))


def by_kind(weights):
    return weights.transpose(1, 0, 2)


def whole_weights(weights):
    whole = lax.all_gather(weights.transpose(1, 0, 2), "date", axis=1, tiled=True)
    return Weights([whole], {kind: [(0, kind, 0)] for kind in range(4)})


def quarters():
    side, even = lax.axis_index("groups"), lax.axis_index("loc") % 2
    return side * 2 + even, (1 - side) * 2 + 1 - even


def gather_weights(weights, first, last):
    arrays = [by_kind(weights), first, swap(first, "groups"), lax.ppermute(first, "loc", PAIRS), last]
    return Weights(arrays, {kind: [(number, kind, number) for number in range(5)] for kind in range(4)})


def add_over_heads(partial, sizes):
    if sizes["mp"] == 2:
        return partial.astype(F32) + swap(partial, "mp").astype(F32)
    return lax.psum(partial.astype(F32), "mp")


def whole_grads(hidden, back_triple, upstream, mixed):
    width = mixed.shape[1]
    intake = dot(hidden, back_triple, TN)
    outlet = dot(upstream, mixed, TN)
    whole = jnp.concatenate([intake, outlet], axis=1).reshape(-1, 4, width)
    part = lax.psum_scatter(whole.astype(BF), ("loc", "date"), scatter_dimension=0, tiled=True)
    return part.astype(F32)


def summed(where, args, products, kept=()):
    rows, columns = args[products[0][0]].shape
    block, width = columns // 4, sum(product[-1] for product in products)
    return call(
        functools.partial(grad_after_kernel, products, len(args), len(kept)),
        (
            jax.ShapeDtypeStruct((2 * block, width), BF),
            jax.ShapeDtypeStruct((block, width), F32),
            jax.ShapeDtypeStruct((block, width), F32),
        ),
        (where, *args, *kept),
        scratch=(pltpu.VMEM((rows, columns), BF),),
        flops=4 * rows * columns * width,
        kept=tuple(range(1 + len(args), 1 + len(args) + len(kept))),
    )


def summed_over_loc(outs):
    sent, far, near = outs[:3]
    beside = lax.ppermute(sent, "loc", PAIRS)
    far = (far + beside[: far.shape[0]].astype(F32)).astype(BF)
    return near, beside, lax.ppermute(far, "loc", APART)


def finish(terms, width, kind_first, kept=None):
    out = jax.ShapeDtypeStruct((terms[0].shape[0], 4, width), F32)
    if kept is None:
        return call(functools.partial(finish_kernel, kind_first), (out,), terms)
    return call(functools.partial(finish_last_kernel, kind_first), (out,), (kept, *terms), kept=(0,))


def per_device(
    sizes,
    optical,
    radar,
    cloud,
    radar_drop,
    keep_index,
    place_table,
    date_table,
    spatial_gain,
    spatial_weights,
    temporal_gain,
    temporal_weights,
    cotangent,
):
    _, patches, dates_here, model = optical.shape
    patches_here, dates = cotangent.shape[1:3]
    width = spatial_weights.shape[2]
    rows = patches * dates_here
    here = lax.axis_index("date")
    first = here * dates_here
    paired = sizes["groups"] == 2 and sizes["loc"] == 4 and sizes["date"] == 2 and sizes["mp"] == 2
    paired = paired and dates_here % 2 == 0 and patches_here % 8 == 0 and model % 1024 == 0
    if paired:
        first_quarter, last_quarter = quarters()
        first_sent = quarter_of(spatial_weights, first_quarter)
    else:
        spatial, temporal = whole_weights(spatial_weights), whole_weights(temporal_weights)

    if paired:
        pairs, eights = dates_here // 2, patches_here // 8
        spatial_blocks, temporal_blocks = pairs, eights
        half_rows = eights * 16

        def temporal_whole(array):
            array = array.reshape(eights, 2, pairs, 2, 8, -1).transpose(1, 2, 3, 0, 4, 5)
            return jnp.where(here == 0, array, jnp.flip(array, 0)).reshape(dates, patches_here, -1)

        spatial_date, temporal_date, temporal_patch = (8, 2), (8, rows), (1, 8)
    else:
        spatial_blocks = 1 if rows <= 192 else dates_here
        temporal_blocks = patches_here // 8 if patches_here % 8 == 0 else 1

        def temporal_rows(array):
            array = array.reshape(dates, temporal_blocks, patches_here // temporal_blocks, -1)
            return array.transpose(1, 0, 2, 3).reshape(rows, -1)

        def temporal_whole(array):
            array = array.reshape(temporal_blocks, dates, patches_here // temporal_blocks, -1)
            return array.transpose(1, 0, 2, 3).reshape(dates, patches_here, -1)

        in_block = patches_here // temporal_blocks
        spatial_date, temporal_date, temporal_patch = (patches, rows), (in_block, rows), (1, in_block)
    spatial_size, temporal_size = rows // spatial_blocks, rows // temporal_blocks

    survive = (1 - cloud[0] * radar_drop[0]).astype(F32)
    side = lax.axis_index("groups") if paired else here
    where = jnp.stack([here, lax.axis_index("mp"), lax.axis_index("loc"), side]).astype(jnp.int32)
    optical_rows, radar_rows = optical[0].transpose(1, 0, 2), radar[0].transpose(1, 0, 2)
    cotangent_rows = cotangent[0].transpose(1, 0, 2)
    if paired:
        survive = jnp.where(here == 0, survive, jnp.roll(survive, dates_here))
    else:
        cloud_here = lax.dynamic_slice_in_dim(cloud, first, dates_here, 1)[0]
        drop_here = lax.dynamic_slice_in_dim(radar_drop, first, dates_here, 1)[0]
        places = jnp.take(place_table, keep_index[0], axis=0).astype(F32)[None]
        start = (
            optical_rows.astype(F32) * (1 - cloud_here).astype(F32)[:, None, None]
            + radar_rows.astype(F32) * (1 - drop_here).astype(F32)[:, None, None]
            + places
        ).astype(BF)
        start = start.reshape(rows, model)
        cotangent_rows = temporal_rows(cotangent_rows)
        date_rows = date_table.astype(F32)
    survive = jnp.repeat(survive, temporal_size // dates)[None]

    spatial_gain = spatial_gain[None]
    temporal_gain = temporal_gain[None]
    lanes = min(width, 256)

    def shape(*dims, dtype=BF):
        return jax.ShapeDtypeStruct(dims, dtype)

    def attend_dims(blocks):
        return (blocks * (width // lanes), lanes // HEAD_DIM * (rows // blocks), rows // blocks)

    layer_flops = 2 * rows * model * width * 4
    if paired:
        half = rows // 2
        own_start, other_start, cotangent_rows, date_rows = call(
            rows_kernel,
            (
                shape(half, model),
                shape(half, model),
                shape(rows, model),
                shape(dates, model, dtype=F32),
            ),
            (
                cloud,
                radar_drop,
                keep_index,
                where,
                optical_rows,
                radar_rows,
                place_table,
                date_table,
                cotangent_rows,
            ),
            scratch=(pltpu.VMEM(place_table.shape, F32), pltpu.VMEM((patches, model), F32)),
        )
        last_sent = quarter_of(spatial_weights, last_quarter)
        last_sent, own_start = fence(last_sent, own_start)
        origins = (own_start, other_start)
        spatial = gather_weights(spatial_weights, swap(first_sent, "date"), swap(last_sent, "date"))
        sent = [quarter_of(temporal_weights, number) for number in (first_quarter, last_quarter)]
        *sent, cotangent_rows = fence(*sent, cotangent_rows)
        temporal_first = swap(sent[0], "date")
        spatial_moves = [
            (side, pair * half_rows, (pair * 2 + side) * half_rows, half_rows)
            for side in range(2)
            for pair in range(pairs)
        ]
        temporal_moves = [
            (side, pair * half_rows + eight * 16, (eight * 2 + side) * pairs * 16 + pair * 16, 16)
            for side in range(2)
            for pair in range(pairs)
            for eight in range(eights)
        ]
        half_shapes = (shape(half, model), shape(half, model))
        own, quarter = shape(rows, model // 2), model // 4
        forward_grads = (own, own, shape(rows, 2 * quarter + width))
        temporal_grads = (
            own,
            shape(rows, model // 2 + 3 * width // 2),
            shape(rows, 3 * width // 2 + width),
        )
        back_shapes = (shape(rows, 3 * width // 2), shape(rows, 3 * width // 2))
        backward_grads = (own, shape(rows, model // 2 + 3 * width // 2))
    else:
        origins = (start,)
        spatial_moves = [(0, at * spatial_size, at * spatial_size, spatial_size) for at in range(spatial_blocks)]
        temporal_moves = [(0, at * temporal_size, at * temporal_size, temporal_size) for at in range(temporal_blocks)]
        half_shapes = (shape(rows, model),)
        forward_grads = temporal_grads = backward_grads = (shape(rows, model),)
        back_shapes = (shape(rows, 3 * width),)

    def plan_of(blocks, moves, weights, grads, sources=0, date_of=spatial_date, patch_of=None):
        return Plan(
            blocks, moves, len(origins), weights, paired, sizes["loc"], len(grads), sources, date_of, patch_of
        )

    plan = plan_of(spatial_blocks, spatial_moves, spatial, forward_grads)
    outs = call(
        functools.partial(spatial_forward_kernel, plan),
        (
            *half_shapes,
            *forward_grads,
            shape(rows, 3 * width),
            shape(*attend_dims(spatial_blocks), dtype=F32),
            shape(rows, width),
        ),
        (where, spatial_gain, cotangent_rows, *origins, *spatial.arrays),
        scratch=(
            pltpu.VMEM((rows, model), BF),
            pltpu.VMEM((rows, model), BF),
            pltpu.VMEM((rows, model), BF),
        ),
        flops=layer_flops,
    )
    partials, outs = outs[: len(origins)], outs[len(origins) :]
    forward, (triple, attend, mixed) = outs[: len(forward_grads)], outs[len(forward_grads) :]
    if paired:
        temporal_first, kept = fence(temporal_first, partials[1])
        partials = (partials[0], kept)
        there, early = call(
            between_kernel,
            (shape(half, model),),
            (origins[1], partials[1], swap(partials[1], "mp"), forward[2]),
            kept=(3,),
        )
        temporal = gather_weights(temporal_weights, temporal_first, swap(sent[1], "date"))
        early, there, *temporal.arrays[2:] = fence(early, swap(there, "date"), *temporal.arrays[2:])
        sources = (origins[0], partials[0], swap(partials[0], "mp"), there)
        early_other = swap(early, "date")
    else:
        spatial_out = (start.astype(F32) + add_over_heads(partials[0], sizes)).astype(BF)
        moved = lax.all_to_all(
            spatial_out.reshape(dates_here, patches, model),
            "date",
            split_axis=1,
            concat_axis=0,
            tiled=True,
        )
        sources = (temporal_rows(moved),)
    plan = plan_of(
        temporal_blocks,
        temporal_moves,
        temporal,
        temporal_grads,
        len(sources),
        temporal_date,
        temporal_patch,
    )
    outs = call(
        functools.partial(temporal_kernel, plan),
        (
            *temporal_grads,
            shape(rows, model),
            shape(rows, width),
            shape(rows, model),
            shape(rows, model),
            *(() if paired else back_shapes),
        ),
        (
            where,
            temporal_gain,
            survive,
            date_rows,
            cotangent_rows,
            *sources,
            *temporal.arrays,
        ),
        scratch=(
            pltpu.VMEM((rows, model), BF),
            pltpu.VMEM((rows, 3 * width), BF),
            pltpu.VMEM(attend_dims(temporal_blocks), F32),
            pltpu.VMEM((rows, width), BF),
            pltpu.VMEM((rows, 3 * width), BF),
        ),
        flops=2 * layer_flops,
    )
    middle, outs = outs[: len(temporal_grads)], outs[len(temporal_grads) :]
    (joined, temporal_mixed, temporal_partial, back_part), temporal_triples = outs[:4], outs[4:]
    if paired:
        back_part, early_other = fence(back_part, early_other)

    if sizes["mp"] == 2:
        others = swap(back_part, "mp")
    else:
        others = (lax.psum(back_part.astype(F32), "mp") - back_part.astype(F32)).astype(BF)
    *backs, last_sent = call(
        functools.partial(norm_back_kernel, temporal_moves, temporal_size),
        half_shapes,
        (temporal_gain, back_part, others, joined, cotangent_rows, middle[-1]),
        kept=(5,),
    )
    if paired:
        back_origins = (backs[0], swap(backs[1], "date"))
        early_there = swap(early_other[:, : 2 * quarter], "mp")
        middle_other = swap(middle[1], "date")
        part, columns = 3 * width // 2, model // 2
        *intake, kept = summed(
            where,
            (middle[0], middle_other, middle[1]),
            ((0, ((1, 0),), (2, columns), (1, columns), part),),
        )
    else:
        back = lax.all_to_all(
            temporal_whole(backs[0]), "date", split_axis=0, concat_axis=1, tiled=True
        )
        back_origins = (back.reshape(rows, model),)
        kept = temporal_triples[0]
    outlet = spatial.only((3,))
    plan = plan_of(spatial_blocks, spatial_moves, outlet, backward_grads)
    *outs, kept = call(
        functools.partial(spatial_backward_kernel, plan),
        (*backward_grads, *back_shapes),
        (where, triple, attend, kept, *back_origins, *outlet.arrays),
        scratch=(
            pltpu.VMEM((rows, model), BF),
            pltpu.VMEM((rows, width), BF),
            pltpu.VMEM((rows, 3 * width), BF),
        ),
        flops=layer_flops,
        kept=(3,),
    )
    backward, back_triples = outs[: len(backward_grads)], outs[len(backward_grads) :]
    encoded = (joined.astype(F32) + add_over_heads(temporal_partial, sizes)).astype(BF)
    encoded = temporal_whole(encoded).transpose(1, 0, 2)[None]
    if not paired:
        return (
            encoded,
            whole_grads(forward[0], back_triples[0], backward[0], mixed),
            whole_grads(middle[0], kept, cotangent_rows, temporal_mixed),
        )
    intake = [*summed_over_loc((*intake, kept))]
    last_other = swap(last_sent, "date")
    *sums, upstream_own, intake[1] = summed(
        where,
        (middle[0], middle_other, last_sent, last_other, forward[1], early_other, early_there),
        (
            (0, ((1, 0),), (2, 0), (3, 0), part),
            (4, ((5, quarter), (6, quarter)), (2, part), (3, part), width),
        ),
        kept=(backward[0], intake[1]),
    )
    sums[0], intake[2] = fence(sums[0], intake[2])
    outlet = [*summed_over_loc(sums)]
    half = model // 2
    backward_other = swap(backward[1], "date")
    *sums, outlet[0] = summed(
        where,
        (
            upstream_own,
            backward_other,
            mixed,
            early_other,
            forward[0],
            early_there,
            back_triples[0],
        ),
        (
            (0, ((1, 0),), (2, 0), (3, 2 * quarter), width),
            (4, ((3, 0), (5, 0)), (6, 0), (1, half), back_triples[0].shape[1]),
        ),
        kept=(outlet[0],),
    )
    spatial_terms = [*summed_over_loc(sums)]
    sums = summed(
        where,
        (forward[0], early_other, early_there, back_triples[1], swap(back_triples[1], "date")),
        ((0, ((1, 0), (2, 0)), (3, 0), (4, 0), back_triples[1].shape[1]),),
        kept=(spatial_terms[0],),
    )
    *sums, spatial_terms[0] = sums
    spatial_terms += summed_over_loc(sums)
    (temporal_grads,) = finish((*intake, *outlet), width, 0)
    spatial_grads, temporal_grads = finish(spatial_terms, width, 3, kept=temporal_grads)
    return (encoded, spatial_grads, temporal_grads)


def solution(mesh):
    in_specs = (
        P(("groups", "loc"), None, "date", None),
        P(("groups", "loc"), None, "date", None),
        P(("groups", "loc"), None),
        P(("groups", "loc"), None),
        P(("groups", "loc"), None),
        P(),
        P(),
        P(),
        P("date", None, "mp"),
        P(),
        P("date", None, "mp"),
        P(("groups", "loc"), "date", None, None),
    )
    out_specs = (
        P(("groups", "loc"), "date", None, None),
        P(("groups", "loc", "date"), None, "mp"),
        P(("groups", "loc", "date"), None, "mp"),
    )
    return jax.shard_map(
        functools.partial(per_device, dict(mesh.shape)),
        mesh=mesh,
        in_specs=in_specs,
        out_specs=out_specs,
        check_vma=False,
    )
```

```python
import functools

import jax
import jax.numpy as jnp
from jax import lax
from jax.experimental import pallas as pl
from jax.experimental.pallas import tpu as pltpu
from jax.sharding import PartitionSpec as P

HEAD_DIM = 64
EPSILON = 1e-05
CROSS = -1e30
BF = jnp.bfloat16
F32 = jnp.float32
NN = (((1,), (0,)), ((), ()))
NT = (((1,), (1,)), ((), ()))
TN = (((0,), (0,)), ((), ()))
VMEM_LIMIT = 56 * 1024 * 1024


def dot(left, right, dims):
    return lax.dot_general(left, right, dims, preferred_element_type=F32)


def statistics(rows):
    values = rows.astype(F32)
    centred = values - jnp.mean(values, -1, keepdims=True)
    inv_scale = lax.rsqrt(jnp.mean(centred * centred, -1, keepdims=True) + EPSILON)
    return centred * inv_scale, inv_scale


class Heads:
    def __init__(self, width):
        self.lanes = min(width, 256)
        self.count = self.lanes // HEAD_DIM
        owner = lax.broadcasted_iota(jnp.int32, (1, self.lanes), 1) // HEAD_DIM
        self.masks = [(owner == head).astype(F32) for head in range(self.count)]

    def stack(self, block):
        return jnp.concatenate([block * mask.astype(BF) for mask in self.masks], axis=0)

    def unstack(self, tall):
        rows = tall.shape[0] // self.count
        total = tall[0:rows] * self.masks[0]
        for head in range(1, self.count):
            total = total + tall[head * rows : (head + 1) * rows] * self.masks[head]
        return total


class Weights:
    def __init__(self, arrays, table):
        self.arrays, self.table = list(arrays), table

    def only(self, kinds):
        used = sorted({entry[0] for kind in kinds for entry in self.table[kind]})
        table = {
            kind: [(used.index(array), at, place) for array, at, place in self.table[kind]]
            for kind in kinds
        }
        return Weights([self.arrays[number] for number in used], table)


def first_row(number, rows, where):
    if number == 0:
        return where[0] * rows
    side, even = where[3], lax.rem(where[2], 2)
    side = side if number in (1, 3) else 1 - side
    even = even if number in (1, 2) else 1 - even
    return (1 - where[0]) * rows + (side * 2 + even) * (rows // 4)


def views(plan, refs, where, kind):
    found = []
    for array, at, place in plan.table[kind]:
        part = refs[array].at[at]
        if plan.paired:
            first = pl.multiple_of(first_row(place, refs[plan.table[kind][0][0]].shape[1], where), 128)
            found.append((part, pl.ds(first, part.shape[0])))
        else:
            found.append((part, slice(None)))
    return found


def rows_times(rows_ref, parts, out_ref, column):
    width = parts[0][0].shape[1]
    step = min(width, 256)
    for at in range(0, width, step):
        total = None
        for part, columns in parts:
            term = dot(rows_ref[:, columns], part[:, at : at + step], NN)
            total = term if total is None else total + term
        out_ref[:, column + at : column + at + step] = total.astype(out_ref.dtype)


def emit_own(rows_ref, out, at, date, loc_count):
    block = rows_ref.shape[1] // (2 * loc_count)
    for loc in range(loc_count):
        first = pl.multiple_of((loc * 2 + date) * block, block)
        out[:, at + loc * block : at + (loc + 1) * block] = rows_ref[:, pl.ds(first, block)]


def emit_half(rows_ref, out, at, date, core, loc_count):
    block = rows_ref.shape[1] // (2 * loc_count)
    for number in range(loc_count // 2):
        loc = core * (loc_count // 2) + number
        first = pl.multiple_of((loc * 2 + date) * block, block)
        out[:, at + number * block : at + (number + 1) * block] = rows_ref[:, pl.ds(first, block)]


def groups_of(size, spans, modulus, axis):
    shape = (size, 1) if axis == 0 else (1, size)
    return lax.rem(lax.broadcasted_iota(jnp.int32, shape, axis) // spans, modulus)


def spatial_bias(plan, size):
    query, key = (groups_of(size, *plan.date_of, axis) for axis in range(2))
    return jnp.where(query == key, 0.0, CROSS).astype(F32)


def temporal_bias(plan, size, survive):
    query, key = (groups_of(size, *plan.patch_of, axis) for axis in range(2))
    query_date, key_date = (groups_of(size, *plan.date_of, axis) for axis in range(2))
    allowed = (survive[...] == 1.0) | (query_date == key_date)
    return jnp.where(query == key, jnp.where(allowed, 0.0, -1000000000.0), CROSS).astype(F32)


def attention(triple_ref, bias, attend_ref, mixed_ref, blocks):
    width = triple_ref.shape[1] // 3
    heads = Heads(width)
    rows = triple_ref.shape[0] // blocks
    groups = width // heads.lanes
    bias = jnp.concatenate([bias] * heads.count, axis=0)
    for block in range(blocks):
        at = slice(block * rows, (block + 1) * rows)
        for group in range(groups):
            lane = group * heads.lanes
            queries = heads.stack(triple_ref[at, lane : lane + heads.lanes])
            keys = triple_ref[at, width + lane : width + lane + heads.lanes]
            values = triple_ref[at, 2 * width + lane : 2 * width + lane + heads.lanes]
            scores = dot(queries, keys, NT) * HEAD_DIM ** (-0.5) + bias
            raised = jnp.exp(scores - jnp.max(scores, -1, keepdims=True))
            attend = raised * (1.0 / jnp.sum(raised, -1, keepdims=True))
            attend_ref[block * groups + group] = attend
            mixed = heads.unstack(dot(attend.astype(BF), values, NN))
            mixed_ref[at, lane : lane + heads.lanes] = mixed.astype(BF)


def attention_back(triple_ref, attend_ref, back_mixed_ref, back_triple_ref, blocks):
    width = triple_ref.shape[1] // 3
    heads = Heads(width)
    rows = triple_ref.shape[0] // blocks
    groups = width // heads.lanes
    for block in range(blocks):
        at = slice(block * rows, (block + 1) * rows)
        for group in range(groups):
            lane = group * heads.lanes
            queries = heads.stack(triple_ref[at, lane : lane + heads.lanes])
            keys = triple_ref[at, width + lane : width + lane + heads.lanes]
            values = triple_ref[at, 2 * width + lane : 2 * width + lane + heads.lanes]
            back = heads.stack(back_mixed_ref[at, lane : lane + heads.lanes])
            attend = attend_ref[block * groups + group]
            back_attend = dot(back, values, NT)
            back_values = dot(attend.astype(BF), back, TN)
            inner = back_attend - jnp.sum(back_attend * attend, -1, keepdims=True)
            back_scores = (attend * inner * HEAD_DIM ** (-0.5)).astype(BF)
            back_queries = heads.unstack(dot(back_scores, keys, NN))
            back_keys = dot(back_scores, queries, TN)
            for number, term in enumerate((back_queries, back_keys, back_values)):
                first = number * width + lane
                back_triple_ref[at, first : first + heads.lanes] = term.astype(BF)


def normalize_into(rows_ref, gain_ref, hidden_ref, blocks):
    rows = rows_ref.shape[0] // blocks
    for block in range(blocks):
        at = slice(block * rows, (block + 1) * rows)
        normed, _ = statistics(rows_ref[at, :])
        hidden_ref[at, :] = (normed * gain_ref[...]).astype(BF)


def spatial_forward_kernel(plan, where, gain, cotangent, *refs):
    sources, refs = refs[: plan.origins], refs[plan.origins :]
    arrays, refs = refs[: plan.arrays], refs[plan.arrays :]
    partials, refs = refs[: plan.origins], refs[plan.origins :]
    grads, refs = refs[: plan.grads], refs[plan.grads :]
    triple, attend, mixed, start, hidden, whole = refs
    for source, at, to, size in plan.moves:
        start[to : to + size, :] = sources[source][at : at + size, :]
    normalize_into(start, gain, hidden, plan.blocks)
    width = mixed.shape[1]
    for kind in range(3):
        rows_times(hidden, views(plan, arrays, where, kind), triple, kind * width)
    bias = spatial_bias(plan, start.shape[0] // plan.blocks)
    attention(triple, bias, attend, mixed, plan.blocks)
    for part, features in views(plan, arrays, where, 3):
        whole[:, features] = dot(mixed[...], part[...], NT).astype(BF)
    for source, at, to, size in plan.moves:
        partials[source][at : at + size, :] = whole[to : to + size, :]
    if plan.paired:
        own_hidden, own_cotangent, sent = grads
        half = hidden.shape[1] // 4
        here, core = where[0], where[1]
        emit_own(hidden, own_hidden, 0, here, plan.locs)
        emit_own(cotangent, own_cotangent, 0, here, plan.locs)
        emit_half(hidden, sent, 0, 1 - here, core, plan.locs)
        emit_half(cotangent, sent, half, 1 - here, core, plan.locs)
        sent[:, 2 * half :] = mixed[...]
    else:
        grads[0][...] = hidden[...]


def between_kernel(start, here, there, kept, out, passed):
    total = here[...].astype(F32) + there[...].astype(F32)
    out[...] = (start[...].astype(F32) + total).astype(BF)


def temporal_kernel(plan, where, gain, survive, date_rows, cotangent, *refs):
    sources, refs = refs[: plan.sources], refs[plan.sources :]
    arrays, refs = refs[: plan.arrays], refs[plan.arrays :]
    grads, refs = refs[: plan.grads], refs[plan.grads :]
    joined, mixed, partial, back_part = refs[:4]
    back_triples, (hidden, triple, attend, back_mixed, back_triple) = refs[4:-5], refs[-5:]
    rows = joined.shape[0] // plan.blocks
    patches = rows // date_rows.shape[0]
    for source, at, to, size in plan.moves:
        if source == 0 and plan.sources > 1:
            total = sources[1][at : at + size, :].astype(F32) + sources[2][at : at + size, :].astype(F32)
            out = (sources[0][at : at + size, :].astype(F32) + total).astype(BF)
        else:
            out = sources[-1][at : at + size, :]
        out = out.astype(F32)
        dated = [
            out[at : at + patches] + date_rows[(to % rows + at) // patches : (to % rows + at) // patches + 1, :]
            for at in range(0, size, patches)
        ]
        joined[to : to + size, :] = jnp.concatenate(dated, axis=0).astype(BF)
    normalize_into(joined, gain, hidden, plan.blocks)
    width = mixed.shape[1]
    for kind in range(3):
        rows_times(hidden, views(plan, arrays, where, kind), triple, kind * width)
    outlet = views(plan, arrays, where, 3)
    rows_times(cotangent, outlet, back_mixed, 0)
    bias = temporal_bias(plan, joined.shape[0] // plan.blocks, survive)
    attention(triple, bias, attend, mixed, plan.blocks)
    for part, features in outlet:
        partial[:, features] = dot(mixed[...], part[...], NT).astype(BF)
    if plan.paired:
        own_hidden, sent, last = grads
        half = hidden.shape[1] // 2
        emit_own(hidden, own_hidden, 0, where[0], plan.locs)
        emit_own(hidden, sent, 0, 1 - where[0], plan.locs)
    else:
        grads[0][...] = hidden[...]
    attention_back(triple, attend, back_mixed, back_triple, plan.blocks)
    intakes = [views(plan, arrays, where, kind) for kind in range(3)]
    for entries in zip(*intakes):
        total = None
        for kind, (part, features) in enumerate(entries):
            term = dot(back_triple[:, kind * width : (kind + 1) * width], part[...], NT)
            total = term if total is None else total + term
        back_part[:, features] = total.astype(BF)
    split_columns(back_triple, back_triples)
    if plan.paired:
        split = sent.shape[1] - half
        sent[:, half:] = back_triple[:, :split]
        last[:, :split] = back_triple[:, split:]
        last[:, split:] = mixed[...]


def split_columns(whole, outs):
    at = 0
    for out in outs:
        out[...] = whole[:, at : at + out.shape[1]]
        at += out.shape[1]


def norm_back_kernel(moves, step, gain, here, there, joined, cotangent, kept, *outs):
    for at in range(0, joined.shape[0], step):
        span_here = slice(at, at + step)
        normed, inv_scale = statistics(joined[span_here, :])
        total = here[span_here, :].astype(F32) + there[span_here, :].astype(F32)
        scaled = total * gain[...]
        inner = (
            scaled
            - jnp.mean(scaled, -1, keepdims=True)
            - normed * jnp.mean(scaled * normed, -1, keepdims=True)
        )
        back = (cotangent[span_here, :].astype(F32) + inv_scale * inner).astype(BF)
        for target, to, first, size in moves:
            if at <= first < at + step:
                outs[target][to : to + size, :] = back[first - at : first - at + size]


def spatial_backward_kernel(plan, where, triple, attend, kept, *refs):
    sources, refs = refs[: plan.origins], refs[plan.origins :]
    arrays, refs = refs[: plan.arrays], refs[plan.arrays :]
    grads, refs = refs[: plan.grads], refs[plan.grads :]
    back_triples, (upstream, back_mixed, back_triple) = refs[:-4], refs[-3:]
    for source, at, to, size in plan.moves:
        upstream[to : to + size, :] = sources[source][at : at + size, :]
    if plan.paired:
        emit_own(upstream, grads[0], 0, where[0], plan.locs)
        emit_own(upstream, grads[1], 0, 1 - where[0], plan.locs)
    else:
        grads[0][...] = upstream[...]
    rows_times(upstream, views(plan, arrays, where, 3), back_mixed, 0)
    attention_back(triple, attend, back_mixed, back_triple, plan.blocks)
    split_columns(back_triple, back_triples)
    if plan.paired:
        half = upstream.shape[1] // 2
        grads[1][:, half:] = back_triple[:, : grads[1].shape[1] - half]


def grad_kernel(products, count, where, *refs):
    sent, far, near, other = refs[-4:]
    core, loc = where[1], where[2]
    block = near.shape[0]
    beside = loc + 1 - 2 * lax.rem(loc, 2)
    places = (lax.rem(beside + 2, 4), beside, lax.rem(loc + 2, 4), loc)
    column = 0
    for left, others, (right, right_at), (right_other, other_at), width in products:
        left, right, right_other = refs[left], refs[right], refs[right_other]
        lanes = other.shape[1] // len(others)
        for number, (source, at) in enumerate(others):
            to = 0
            if len(others) > 1:
                to = pl.multiple_of((core if number == 0 else 1 - core) * lanes, lanes)
            other[:, pl.ds(to, lanes)] = refs[source][:, at : at + lanes]
        for number, place in enumerate(places):
            columns = pl.ds(pl.multiple_of(place * block, block), block)
            for first in range(0, width, 256):
                lane = slice(column + first, column + first + 256)
                here = right[:, right_at + first : right_at + first + 256]
                there = right_other[:, other_at + first : other_at + first + 256]
                total = dot(left[:, columns], here, TN) + dot(other[:, columns], there, TN)
                if number < 2:
                    sent[number * block : (number + 1) * block, lane] = total.astype(BF)
                elif number == 2:
                    far[:, lane] = total
                else:
                    near[:, lane] = total
        column += width


def finish_kernel(kind_first, *refs):
    out = refs[-1]
    block = out.shape[0]
    column = 0
    for near, beside, far in zip(refs[0:-1:3], refs[1:-1:3], refs[2:-1:3]):
        for at in range(0, near.shape[1], 256):
            lane = slice(at, at + 256)
            total = near[:, lane] + beside[block:, lane].astype(F32) + far[:, lane].astype(F32)
            kind, first = (kind_first * out.shape[2] + column + at) // out.shape[2] % 4, (column + at) % out.shape[2]
            out[:, kind, first : first + 256] = total
        column += near.shape[1]


def finish_last_kernel(kind_first, kept, *refs):
    finish_kernel(kind_first, *refs[:-1])


def fence_kernel(*refs):
    pass


def grad_after_kernel(products, count, passed, where, *refs):
    args, rest = refs[:count], refs[count + passed :]
    grad_kernel(products, count, where, *args, *rest[:3], rest[-1])


def rows_kernel(cloud, drop, keep, where, optical, radar, table, date_table, cotangent, *refs):
    own, other, upstream, dates_out, wide_table, places = refs
    here = where[0]
    dates, patches, _ = optical.shape
    pairs, half = dates // 2, patches // 2
    wide_table[...] = table[...].astype(F32)
    for patch in range(patches):
        places[patch : patch + 1, :] = wide_table[pl.ds(keep[0, patch], 1), :]
    for pair in range(pairs):
        found = []
        for number in range(2):
            date = pair * 2 + number
            at = here * dates + date
            seen = (1 - cloud[0, at]).astype(F32)
            kept = (1 - drop[0, at]).astype(F32)
            found.append(optical[date].astype(F32) * seen + radar[date].astype(F32) * kept + places[...])
        halves = [(rows[:half], rows[half:]) for rows in found]
        for out, swapped in ((own, 0), (other, 1)):
            picked = [jnp.where(here == swapped, first, second) for first, second in halves]
            for eight in range(0, half, 8):
                rows = jnp.concatenate([rows[eight : eight + 8] for rows in picked], axis=0)
                at = pair * half * 2 + eight * 2
                out[at : at + 16, :] = rows.astype(BF)
    block = 4 * pairs * 8
    for side in range(2):
        owner = here if side == 0 else 1 - here
        for pair in range(pairs):
            found = [cotangent[owner * dates + pair * 2 + number].astype(F32) for number in range(2)]
            for eight in range(half // 8):
                rows = jnp.concatenate([rows[eight * 8 : eight * 8 + 8] for rows in found], axis=0)
                at = eight * block + side * pairs * 16 + pair * 16
                upstream[at : at + 16, :] = rows.astype(BF)
    whole = date_table[...].astype(F32)
    flipped = jnp.concatenate([whole[dates:], whole[:dates]], axis=0)
    dates_out[...] = jnp.where(here == 0, whole, flipped)


class Plan:
    def __init__(self, blocks, moves, origins, weights, paired, locs, grads, sources=0, date_of=None, patch_of=None):
        self.date_of, self.patch_of = date_of, patch_of
        self.blocks, self.moves, self.origins = blocks, moves, origins
        self.arrays, self.table = len(weights.arrays), weights.table
        self.paired, self.locs, self.grads, self.sources = paired, locs, grads, sources


def call(body, outs, args, scratch=(), flops=0, kept=()):
    smem = pl.BlockSpec(memory_space=pltpu.SMEM)
    vmem = pl.BlockSpec(memory_space=pltpu.VMEM)
    specs = [smem if arg.dtype == jnp.int32 else vmem for arg in args]
    out_specs = [vmem] * len(outs)
    aliases = {}
    outs = list(outs)
    moved = sum(arg.size * arg.dtype.itemsize for arg in args)
    moved = moved + sum(out.size * out.dtype.itemsize for out in outs)
    for number in kept:
        specs[number] = pl.BlockSpec(memory_space=pl.ANY)
        out_specs.append(pl.BlockSpec(memory_space=pl.ANY))
        outs.append(jax.ShapeDtypeStruct(args[number].shape, args[number].dtype))
        aliases[number] = len(outs) - 1
    return pl.pallas_call(
        body,
        out_shape=outs,
        in_specs=specs,
        out_specs=out_specs,
        scratch_shapes=list(scratch),
        input_output_aliases=aliases,
        compiler_params=pltpu.CompilerParams(vmem_limit_bytes=VMEM_LIMIT),
        cost_estimate=pl.CostEstimate(flops=flops, bytes_accessed=moved, transcendentals=0),
    )(*args)


def fence(*arrays):
    anywhere = [pl.BlockSpec(memory_space=pl.ANY)] * len(arrays)
    return pl.pallas_call(
        fence_kernel,
        out_shape=[jax.ShapeDtypeStruct(array.shape, array.dtype) for array in arrays],
        in_specs=anywhere,
        out_specs=anywhere,
        input_output_aliases={number: number for number in range(len(arrays))},
    )(*arrays)


def swap(array, axis):
    return lax.ppermute(array, axis, [(0, 1), (1, 0)])


PAIRS = [(0, 1), (1, 0), (2, 3), (3, 2)]
APART = [(0, 2), (1, 3), (2, 0), (3, 1)]


def quarter_of(weights, number):
    rows = weights.shape[0]
    return by_kind(lax.dynamic_slice_in_dim(weights, number * (rows // 4), rows // 4, 0))


def by_kind(weights):
    return weights.transpose(1, 0, 2)


def whole_weights(weights):
    whole = lax.all_gather(weights.transpose(1, 0, 2), "date", axis=1, tiled=True)
    return Weights([whole], {kind: [(0, kind, 0)] for kind in range(4)})


def quarters():
    side, even = lax.axis_index("groups"), lax.axis_index("loc") % 2
    return side * 2 + even, (1 - side) * 2 + 1 - even


def gather_weights(weights, first, last):
    arrays = [by_kind(weights), first, swap(first, "groups"), lax.ppermute(first, "loc", PAIRS), last]
    return Weights(arrays, {kind: [(number, kind, number) for number in range(5)] for kind in range(4)})


def add_over_heads(partial, sizes):
    if sizes["mp"] == 2:
        return partial.astype(F32) + swap(partial, "mp").astype(F32)
    return lax.psum(partial.astype(F32), "mp")


def whole_grads(hidden, back_triple, upstream, mixed):
    width = mixed.shape[1]
    intake = dot(hidden, back_triple, TN)
    outlet = dot(upstream, mixed, TN)
    whole = jnp.concatenate([intake, outlet], axis=1).reshape(-1, 4, width)
    part = lax.psum_scatter(whole.astype(BF), ("loc", "date"), scatter_dimension=0, tiled=True)
    return part.astype(F32)


def summed(where, args, products, kept=()):
    rows, columns = args[products[0][0]].shape
    block, width = columns // 4, sum(product[-1] for product in products)
    return call(
        functools.partial(grad_after_kernel, products, len(args), len(kept)),
        (
            jax.ShapeDtypeStruct((2 * block, width), BF),
            jax.ShapeDtypeStruct((block, width), F32),
            jax.ShapeDtypeStruct((block, width), F32),
        ),
        (where, *args, *kept),
        scratch=(pltpu.VMEM((rows, columns), BF),),
        flops=4 * rows * columns * width,
        kept=tuple(range(1 + len(args), 1 + len(args) + len(kept))),
    )


def summed_over_loc(outs):
    sent, far, near = outs[:3]
    beside = lax.ppermute(sent, "loc", PAIRS)
    far = (far + beside[: far.shape[0]].astype(F32)).astype(BF)
    return near, beside, lax.ppermute(far, "loc", APART)


def finish(terms, width, kind_first, kept=None):
    out = jax.ShapeDtypeStruct((terms[0].shape[0], 4, width), F32)
    if kept is None:
        return call(functools.partial(finish_kernel, kind_first), (out,), terms)
    return call(functools.partial(finish_last_kernel, kind_first), (out,), (kept, *terms), kept=(0,))


def per_device(
    sizes,
    optical,
    radar,
    cloud,
    radar_drop,
    keep_index,
    place_table,
    date_table,
    spatial_gain,
    spatial_weights,
    temporal_gain,
    temporal_weights,
    cotangent,
):
    _, patches, dates_here, model = optical.shape
    patches_here, dates = cotangent.shape[1:3]
    width = spatial_weights.shape[2]
    rows = patches * dates_here
    here = lax.axis_index("date")
    first = here * dates_here
    paired = sizes["groups"] == 2 and sizes["loc"] == 4 and sizes["date"] == 2 and sizes["mp"] == 2
    paired = paired and dates_here % 2 == 0 and patches_here % 8 == 0 and model % 1024 == 0
    if paired:
        first_quarter, last_quarter = quarters()
        first_sent = quarter_of(spatial_weights, first_quarter)
    else:
        spatial, temporal = whole_weights(spatial_weights), whole_weights(temporal_weights)

    if paired:
        pairs, eights = dates_here // 2, patches_here // 8
        spatial_blocks, temporal_blocks = pairs, eights
        half_rows = eights * 16

        def temporal_whole(array):
            array = array.reshape(eights, 2, pairs, 2, 8, -1).transpose(1, 2, 3, 0, 4, 5)
            return jnp.where(here == 0, array, jnp.flip(array, 0)).reshape(dates, patches_here, -1)

        spatial_date, temporal_date, temporal_patch = (8, 2), (8, rows), (1, 8)
    else:
        spatial_blocks = 1 if rows <= 192 else dates_here
        temporal_blocks = patches_here // 8 if patches_here % 8 == 0 else 1

        def temporal_rows(array):
            array = array.reshape(dates, temporal_blocks, patches_here // temporal_blocks, -1)
            return array.transpose(1, 0, 2, 3).reshape(rows, -1)

        def temporal_whole(array):
            array = array.reshape(temporal_blocks, dates, patches_here // temporal_blocks, -1)
            return array.transpose(1, 0, 2, 3).reshape(dates, patches_here, -1)

        in_block = patches_here // temporal_blocks
        spatial_date, temporal_date, temporal_patch = (patches, rows), (in_block, rows), (1, in_block)
    spatial_size, temporal_size = rows // spatial_blocks, rows // temporal_blocks

    survive = (1 - cloud[0] * radar_drop[0]).astype(F32)
    side = lax.axis_index("groups") if paired else here
    where = jnp.stack([here, lax.axis_index("mp"), lax.axis_index("loc"), side]).astype(jnp.int32)
    optical_rows, radar_rows = optical[0].transpose(1, 0, 2), radar[0].transpose(1, 0, 2)
    cotangent_rows = cotangent[0].transpose(1, 0, 2)
    if paired:
        survive = jnp.where(here == 0, survive, jnp.roll(survive, dates_here))
    else:
        cloud_here = lax.dynamic_slice_in_dim(cloud, first, dates_here, 1)[0]
        drop_here = lax.dynamic_slice_in_dim(radar_drop, first, dates_here, 1)[0]
        places = jnp.take(place_table, keep_index[0], axis=0).astype(F32)[None]
        start = (
            optical_rows.astype(F32) * (1 - cloud_here).astype(F32)[:, None, None]
            + radar_rows.astype(F32) * (1 - drop_here).astype(F32)[:, None, None]
            + places
        ).astype(BF)
        start = start.reshape(rows, model)
        cotangent_rows = temporal_rows(cotangent_rows)
        date_rows = date_table.astype(F32)
    survive = jnp.repeat(survive, temporal_size // dates)[None]

    spatial_gain = spatial_gain[None]
    temporal_gain = temporal_gain[None]
    lanes = min(width, 256)

    def shape(*dims, dtype=BF):
        return jax.ShapeDtypeStruct(dims, dtype)

    def attend_dims(blocks):
        return (blocks * (width // lanes), lanes // HEAD_DIM * (rows // blocks), rows // blocks)

    layer_flops = 2 * rows * model * width * 4
    if paired:
        half = rows // 2
        own_start, other_start, cotangent_rows, date_rows = call(
            rows_kernel,
            (
                shape(half, model),
                shape(half, model),
                shape(rows, model),
                shape(dates, model, dtype=F32),
            ),
            (
                cloud,
                radar_drop,
                keep_index,
                where,
                optical_rows,
                radar_rows,
                place_table,
                date_table,
                cotangent_rows,
            ),
            scratch=(pltpu.VMEM(place_table.shape, F32), pltpu.VMEM((patches, model), F32)),
        )
        last_sent = quarter_of(spatial_weights, last_quarter)
        last_sent, own_start = fence(last_sent, own_start)
        origins = (own_start, other_start)
        spatial = gather_weights(spatial_weights, swap(first_sent, "date"), swap(last_sent, "date"))
        sent = [quarter_of(temporal_weights, number) for number in (first_quarter, last_quarter)]
        *sent, cotangent_rows = fence(*sent, cotangent_rows)
        temporal_first = swap(sent[0], "date")
        spatial_moves = [
            (side, pair * half_rows, (pair * 2 + side) * half_rows, half_rows)
            for side in range(2)
            for pair in range(pairs)
        ]
        temporal_moves = [
            (side, pair * half_rows + eight * 16, (eight * 2 + side) * pairs * 16 + pair * 16, 16)
            for side in range(2)
            for pair in range(pairs)
            for eight in range(eights)
        ]
        half_shapes = (shape(half, model), shape(half, model))
        own, quarter = shape(rows, model // 2), model // 4
        forward_grads = (own, own, shape(rows, 2 * quarter + width))
        temporal_grads = (
            own,
            shape(rows, model // 2 + 3 * width // 2),
            shape(rows, 3 * width // 2 + width),
        )
        back_shapes = (shape(rows, 2 * width), shape(rows, width))
        backward_grads = (own, shape(rows, model // 2 + 2 * width))
    else:
        origins = (start,)
        spatial_moves = [(0, at * spatial_size, at * spatial_size, spatial_size) for at in range(spatial_blocks)]
        temporal_moves = [(0, at * temporal_size, at * temporal_size, temporal_size) for at in range(temporal_blocks)]
        half_shapes = (shape(rows, model),)
        forward_grads = temporal_grads = backward_grads = (shape(rows, model),)
        back_shapes = (shape(rows, 3 * width),)

    def plan_of(blocks, moves, weights, grads, sources=0, date_of=spatial_date, patch_of=None):
        return Plan(
            blocks, moves, len(origins), weights, paired, sizes["loc"], len(grads), sources, date_of, patch_of
        )

    plan = plan_of(spatial_blocks, spatial_moves, spatial, forward_grads)
    outs = call(
        functools.partial(spatial_forward_kernel, plan),
        (
            *half_shapes,
            *forward_grads,
            shape(rows, 3 * width),
            shape(*attend_dims(spatial_blocks), dtype=F32),
            shape(rows, width),
        ),
        (where, spatial_gain, cotangent_rows, *origins, *spatial.arrays),
        scratch=(
            pltpu.VMEM((rows, model), BF),
            pltpu.VMEM((rows, model), BF),
            pltpu.VMEM((rows, model), BF),
        ),
        flops=layer_flops,
    )
    partials, outs = outs[: len(origins)], outs[len(origins) :]
    forward, (triple, attend, mixed) = outs[: len(forward_grads)], outs[len(forward_grads) :]
    if paired:
        temporal_first, kept = fence(temporal_first, partials[1])
        partials = (partials[0], kept)
        there, early = call(
            between_kernel,
            (shape(half, model),),
            (origins[1], partials[1], swap(partials[1], "mp"), forward[2]),
            kept=(3,),
        )
        temporal = gather_weights(temporal_weights, temporal_first, swap(sent[1], "date"))
        early, there, *temporal.arrays[2:] = fence(early, swap(there, "date"), *temporal.arrays[2:])
        sources = (origins[0], partials[0], swap(partials[0], "mp"), there)
        early_other = swap(early, "date")
    else:
        spatial_out = (start.astype(F32) + add_over_heads(partials[0], sizes)).astype(BF)
        moved = lax.all_to_all(
            spatial_out.reshape(dates_here, patches, model),
            "date",
            split_axis=1,
            concat_axis=0,
            tiled=True,
        )
        sources = (temporal_rows(moved),)
    plan = plan_of(
        temporal_blocks,
        temporal_moves,
        temporal,
        temporal_grads,
        len(sources),
        temporal_date,
        temporal_patch,
    )
    outs = call(
        functools.partial(temporal_kernel, plan),
        (
            *temporal_grads,
            shape(rows, model),
            shape(rows, width),
            shape(rows, model),
            shape(rows, model),
            *(() if paired else back_shapes),
        ),
        (
            where,
            temporal_gain,
            survive,
            date_rows,
            cotangent_rows,
            *sources,
            *temporal.arrays,
        ),
        scratch=(
            pltpu.VMEM((rows, model), BF),
            pltpu.VMEM((rows, 3 * width), BF),
            pltpu.VMEM(attend_dims(temporal_blocks), F32),
            pltpu.VMEM((rows, width), BF),
            pltpu.VMEM((rows, 3 * width), BF),
        ),
        flops=2 * layer_flops,
    )
    middle, outs = outs[: len(temporal_grads)], outs[len(temporal_grads) :]
    (joined, temporal_mixed, temporal_partial, back_part), temporal_triples = outs[:4], outs[4:]
    if paired:
        back_part, early_other = fence(back_part, early_other)

    if sizes["mp"] == 2:
        others = swap(back_part, "mp")
    else:
        others = (lax.psum(back_part.astype(F32), "mp") - back_part.astype(F32)).astype(BF)
    *backs, last_sent = call(
        functools.partial(norm_back_kernel, temporal_moves, temporal_size),
        half_shapes,
        (temporal_gain, back_part, others, joined, cotangent_rows, middle[-1]),
        kept=(5,),
    )
    if paired:
        back_origins = (backs[0], swap(backs[1], "date"))
        early_there = swap(early_other[:, : 2 * quarter], "mp")
        middle_other = swap(middle[1], "date")
        part, columns = 3 * width // 2, model // 2
        *intake, kept = summed(
            where,
            (middle[0], middle_other, middle[1]),
            ((0, ((1, 0),), (2, columns), (1, columns), part),),
        )
    else:
        back = lax.all_to_all(
            temporal_whole(backs[0]), "date", split_axis=0, concat_axis=1, tiled=True
        )
        back_origins = (back.reshape(rows, model),)
        kept = temporal_triples[0]
    outlet = spatial.only((3,))
    plan = plan_of(spatial_blocks, spatial_moves, outlet, backward_grads)
    *outs, kept = call(
        functools.partial(spatial_backward_kernel, plan),
        (*backward_grads, *back_shapes),
        (where, triple, attend, kept, *back_origins, *outlet.arrays),
        scratch=(
            pltpu.VMEM((rows, model), BF),
            pltpu.VMEM((rows, width), BF),
            pltpu.VMEM((rows, 3 * width), BF),
        ),
        flops=layer_flops,
        kept=(3,),
    )
    backward, back_triples = outs[: len(backward_grads)], outs[len(backward_grads) :]
    encoded = (joined.astype(F32) + add_over_heads(temporal_partial, sizes)).astype(BF)
    encoded = temporal_whole(encoded).transpose(1, 0, 2)[None]
    if not paired:
        return (
            encoded,
            whole_grads(forward[0], back_triples[0], backward[0], mixed),
            whole_grads(middle[0], kept, cotangent_rows, temporal_mixed),
        )
    intake = [*summed_over_loc((*intake, kept))]
    last_other = swap(last_sent, "date")
    *sums, upstream_own, intake[1] = summed(
        where,
        (middle[0], middle_other, last_sent, last_other, forward[1], early_other, early_there),
        (
            (0, ((1, 0),), (2, 0), (3, 0), part),
            (4, ((5, quarter), (6, quarter)), (2, part), (3, part), width),
        ),
        kept=(backward[0], intake[1]),
    )
    sums[0], intake[2] = fence(sums[0], intake[2])
    outlet = [*summed_over_loc(sums)]
    half = model // 2
    backward_other = swap(backward[1], "date")
    *sums, outlet[0] = summed(
        where,
        (
            upstream_own,
            backward_other,
            mixed,
            early_other,
            forward[0],
            early_there,
            back_triples[0],
        ),
        (
            (0, ((1, 0),), (2, 0), (3, 2 * quarter), width),
            (4, ((3, 0), (5, 0)), (6, 0), (1, half), back_triples[0].shape[1]),
        ),
        kept=(outlet[0],),
    )
    spatial_terms = [*summed_over_loc(sums)]
    sums = summed(
        where,
        (forward[0], early_other, early_there, back_triples[1], swap(back_triples[1], "date")),
        ((0, ((1, 0), (2, 0)), (3, 0), (4, 0), back_triples[1].shape[1]),),
        kept=(spatial_terms[0],),
    )
    *sums, spatial_terms[0] = sums
    spatial_terms += summed_over_loc(sums)
    (temporal_grads,) = finish((*intake, *outlet), width, 0)
    spatial_grads, temporal_grads = finish(spatial_terms, width, 3, kept=temporal_grads)
    return (encoded, spatial_grads, temporal_grads)


def solution(mesh):
    in_specs = (
        P(("groups", "loc"), None, "date", None),
        P(("groups", "loc"), None, "date", None),
        P(("groups", "loc"), None),
        P(("groups", "loc"), None),
        P(("groups", "loc"), None),
        P(),
        P(),
        P(),
        P("date", None, "mp"),
        P(),
        P("date", None, "mp"),
        P(("groups", "loc"), "date", None, None),
    )
    out_specs = (
        P(("groups", "loc"), "date", None, None),
        P(("groups", "loc", "date"), None, "mp"),
        P(("groups", "loc", "date"), None, "mp"),
    )
    return jax.shard_map(
        functools.partial(per_device, dict(mesh.shape)),
        mesh=mesh,
        in_specs=in_specs,
        out_specs=out_specs,
        check_vma=False,
    )
```

```python
import functools

import jax
import jax.numpy as jnp
from jax import lax
from jax.experimental import pallas as pl
from jax.experimental.pallas import tpu as pltpu
from jax.sharding import PartitionSpec as P

HEAD_DIM = 64
EPSILON = 1e-05
CROSS = -1e30
BF = jnp.bfloat16
F32 = jnp.float32
NN = (((1,), (0,)), ((), ()))
NT = (((1,), (1,)), ((), ()))
TN = (((0,), (0,)), ((), ()))
VMEM_LIMIT = 56 * 1024 * 1024


def dot(left, right, dims):
    return lax.dot_general(left, right, dims, preferred_element_type=F32)


def statistics(rows):
    values = rows.astype(F32)
    centred = values - jnp.mean(values, -1, keepdims=True)
    inv_scale = lax.rsqrt(jnp.mean(centred * centred, -1, keepdims=True) + EPSILON)
    return centred * inv_scale, inv_scale


class Heads:
    def __init__(self, width):
        self.lanes = min(width, 256)
        self.count = self.lanes // HEAD_DIM
        owner = lax.broadcasted_iota(jnp.int32, (1, self.lanes), 1) // HEAD_DIM
        self.masks = [(owner == head).astype(F32) for head in range(self.count)]

    def stack(self, block):
        return jnp.concatenate([block * mask.astype(BF) for mask in self.masks], axis=0)

    def unstack(self, tall):
        rows = tall.shape[0] // self.count
        total = tall[0:rows] * self.masks[0]
        for head in range(1, self.count):
            total = total + tall[head * rows : (head + 1) * rows] * self.masks[head]
        return total


class Weights:
    def __init__(self, arrays, table):
        self.arrays, self.table = list(arrays), table

    def only(self, kinds):
        used = sorted({entry[0] for kind in kinds for entry in self.table[kind]})
        table = {
            kind: [(used.index(array), at, place) for array, at, place in self.table[kind]]
            for kind in kinds
        }
        return Weights([self.arrays[number] for number in used], table)


def first_row(number, rows, where):
    if number == 0:
        return where[0] * rows
    side, even = where[3], lax.rem(where[2], 2)
    side = side if number in (1, 3) else 1 - side
    even = even if number in (1, 2) else 1 - even
    return (1 - where[0]) * rows + (side * 2 + even) * (rows // 4)


def views(plan, refs, where, kind):
    found = []
    for array, at, place in plan.table[kind]:
        part = refs[array].at[at]
        if plan.paired:
            first = pl.multiple_of(first_row(place, refs[plan.table[kind][0][0]].shape[1], where), 128)
            found.append((part, pl.ds(first, part.shape[0])))
        else:
            found.append((part, slice(None)))
    return found


def rows_times(rows_ref, parts, out_ref, column):
    width = parts[0][0].shape[1]
    step = min(width, 256)
    for at in range(0, width, step):
        total = None
        for part, columns in parts:
            term = dot(rows_ref[:, columns], part[:, at : at + step], NN)
            total = term if total is None else total + term
        out_ref[:, column + at : column + at + step] = total.astype(out_ref.dtype)


def emit_own(rows_ref, out, at, date, loc_count):
    block = rows_ref.shape[1] // (2 * loc_count)
    for loc in range(loc_count):
        first = pl.multiple_of((loc * 2 + date) * block, block)
        out[:, at + loc * block : at + (loc + 1) * block] = rows_ref[:, pl.ds(first, block)]


def emit_half(rows_ref, out, at, date, core, loc_count):
    block = rows_ref.shape[1] // (2 * loc_count)
    for number in range(loc_count // 2):
        loc = core * (loc_count // 2) + number
        first = pl.multiple_of((loc * 2 + date) * block, block)
        out[:, at + number * block : at + (number + 1) * block] = rows_ref[:, pl.ds(first, block)]


def groups_of(size, spans, modulus, axis):
    shape = (size, 1) if axis == 0 else (1, size)
    return lax.rem(lax.broadcasted_iota(jnp.int32, shape, axis) // spans, modulus)


def spatial_bias(plan, size):
    query, key = (groups_of(size, *plan.date_of, axis) for axis in range(2))
    return jnp.where(query == key, 0.0, CROSS).astype(F32)


def temporal_bias(plan, size, survive):
    query, key = (groups_of(size, *plan.patch_of, axis) for axis in range(2))
    query_date, key_date = (groups_of(size, *plan.date_of, axis) for axis in range(2))
    allowed = (survive[...] == 1.0) | (query_date == key_date)
    return jnp.where(query == key, jnp.where(allowed, 0.0, -1000000000.0), CROSS).astype(F32)


def attention(triple_ref, bias, attend_ref, mixed_ref, blocks):
    width = triple_ref.shape[1] // 3
    heads = Heads(width)
    rows = triple_ref.shape[0] // blocks
    groups = width // heads.lanes
    bias = jnp.concatenate([bias] * heads.count, axis=0)
    for block in range(blocks):
        at = slice(block * rows, (block + 1) * rows)
        for group in range(groups):
            lane = group * heads.lanes
            queries = heads.stack(triple_ref[at, lane : lane + heads.lanes])
            keys = triple_ref[at, width + lane : width + lane + heads.lanes]
            values = triple_ref[at, 2 * width + lane : 2 * width + lane + heads.lanes]
            scores = dot(queries, keys, NT) * HEAD_DIM ** (-0.5) + bias
            raised = jnp.exp(scores - jnp.max(scores, -1, keepdims=True))
            attend = raised * (1.0 / jnp.sum(raised, -1, keepdims=True))
            attend_ref[block * groups + group] = attend
            mixed = heads.unstack(dot(attend.astype(BF), values, NN))
            mixed_ref[at, lane : lane + heads.lanes] = mixed.astype(BF)


def attention_back(triple_ref, attend_ref, back_mixed_ref, back_triple_ref, blocks):
    width = triple_ref.shape[1] // 3
    heads = Heads(width)
    rows = triple_ref.shape[0] // blocks
    groups = width // heads.lanes
    for block in range(blocks):
        at = slice(block * rows, (block + 1) * rows)
        for group in range(groups):
            lane = group * heads.lanes
            queries = heads.stack(triple_ref[at, lane : lane + heads.lanes])
            keys = triple_ref[at, width + lane : width + lane + heads.lanes]
            values = triple_ref[at, 2 * width + lane : 2 * width + lane + heads.lanes]
            back = heads.stack(back_mixed_ref[at, lane : lane + heads.lanes])
            attend = attend_ref[block * groups + group]
            back_attend = dot(back, values, NT)
            back_values = dot(attend.astype(BF), back, TN)
            inner = back_attend - jnp.sum(back_attend * attend, -1, keepdims=True)
            back_scores = (attend * inner * HEAD_DIM ** (-0.5)).astype(BF)
            back_queries = heads.unstack(dot(back_scores, keys, NN))
            back_keys = dot(back_scores, queries, TN)
            for number, term in enumerate((back_queries, back_keys, back_values)):
                first = number * width + lane
                back_triple_ref[at, first : first + heads.lanes] = term.astype(BF)


def normalize_into(rows_ref, gain_ref, hidden_ref, blocks):
    rows = rows_ref.shape[0] // blocks
    for block in range(blocks):
        at = slice(block * rows, (block + 1) * rows)
        normed, _ = statistics(rows_ref[at, :])
        hidden_ref[at, :] = (normed * gain_ref[...]).astype(BF)


def spatial_forward_kernel(plan, where, gain, cotangent, *refs):
    sources, refs = refs[: plan.origins], refs[plan.origins :]
    arrays, refs = refs[: plan.arrays], refs[plan.arrays :]
    partials, refs = refs[: plan.origins], refs[plan.origins :]
    grads, refs = refs[: plan.grads], refs[plan.grads :]
    triple, attend, mixed, start, hidden, whole = refs
    for source, at, to, size in plan.moves:
        start[to : to + size, :] = sources[source][at : at + size, :]
    normalize_into(start, gain, hidden, plan.blocks)
    width = mixed.shape[1]
    for kind in range(3):
        rows_times(hidden, views(plan, arrays, where, kind), triple, kind * width)
    bias = spatial_bias(plan, start.shape[0] // plan.blocks)
    attention(triple, bias, attend, mixed, plan.blocks)
    for part, features in views(plan, arrays, where, 3):
        whole[:, features] = dot(mixed[...], part[...], NT).astype(BF)
    for source, at, to, size in plan.moves:
        partials[source][at : at + size, :] = whole[to : to + size, :]
    if plan.paired:
        own_hidden, own_cotangent, sent = grads
        half = hidden.shape[1] // 4
        here, core = where[0], where[1]
        emit_own(hidden, own_hidden, 0, here, plan.locs)
        emit_own(cotangent, own_cotangent, 0, here, plan.locs)
        emit_half(hidden, sent, 0, 1 - here, core, plan.locs)
        emit_half(cotangent, sent, half, 1 - here, core, plan.locs)
        sent[:, 2 * half :] = mixed[...]
    else:
        grads[0][...] = hidden[...]


def between_kernel(start, here, there, kept, out, passed):
    total = here[...].astype(F32) + there[...].astype(F32)
    out[...] = (start[...].astype(F32) + total).astype(BF)


def temporal_kernel(plan, where, gain, survive, date_rows, cotangent, *refs):
    sources, refs = refs[: plan.sources], refs[plan.sources :]
    arrays, refs = refs[: plan.arrays], refs[plan.arrays :]
    grads, refs = refs[: plan.grads], refs[plan.grads :]
    joined, mixed, partial, back_part = refs[:4]
    back_triples, (hidden, triple, attend, back_mixed, back_triple) = refs[4:-5], refs[-5:]
    rows = joined.shape[0] // plan.blocks
    patches = rows // date_rows.shape[0]
    for source, at, to, size in plan.moves:
        if source == 0 and plan.sources > 1:
            total = sources[1][at : at + size, :].astype(F32) + sources[2][at : at + size, :].astype(F32)
            out = (sources[0][at : at + size, :].astype(F32) + total).astype(BF)
        else:
            out = sources[-1][at : at + size, :]
        out = out.astype(F32)
        dated = [
            out[at : at + patches] + date_rows[(to % rows + at) // patches : (to % rows + at) // patches + 1, :]
            for at in range(0, size, patches)
        ]
        joined[to : to + size, :] = jnp.concatenate(dated, axis=0).astype(BF)
    normalize_into(joined, gain, hidden, plan.blocks)
    width = mixed.shape[1]
    for kind in range(3):
        rows_times(hidden, views(plan, arrays, where, kind), triple, kind * width)
    outlet = views(plan, arrays, where, 3)
    rows_times(cotangent, outlet, back_mixed, 0)
    bias = temporal_bias(plan, joined.shape[0] // plan.blocks, survive)
    attention(triple, bias, attend, mixed, plan.blocks)
    for part, features in outlet:
        partial[:, features] = dot(mixed[...], part[...], NT).astype(BF)
    if plan.paired:
        own_hidden, sent, last = grads
        half = hidden.shape[1] // 2
        emit_own(hidden, own_hidden, 0, where[0], plan.locs)
        emit_own(hidden, sent, 0, 1 - where[0], plan.locs)
    else:
        grads[0][...] = hidden[...]
    attention_back(triple, attend, back_mixed, back_triple, plan.blocks)
    intakes = [views(plan, arrays, where, kind) for kind in range(3)]
    for entries in zip(*intakes):
        total = None
        for kind, (part, features) in enumerate(entries):
            term = dot(back_triple[:, kind * width : (kind + 1) * width], part[...], NT)
            total = term if total is None else total + term
        back_part[:, features] = total.astype(BF)
    split_columns(back_triple, back_triples)
    if plan.paired:
        split = sent.shape[1] - half
        sent[:, half:] = back_triple[:, :split]
        last[:, :split] = back_triple[:, split:]
        last[:, split:] = mixed[...]


def split_columns(whole, outs):
    at = 0
    for out in outs:
        out[...] = whole[:, at : at + out.shape[1]]
        at += out.shape[1]


def norm_back_kernel(moves, step, gain, here, there, joined, cotangent, kept, *outs):
    for at in range(0, joined.shape[0], step):
        span_here = slice(at, at + step)
        normed, inv_scale = statistics(joined[span_here, :])
        total = here[span_here, :].astype(F32) + there[span_here, :].astype(F32)
        scaled = total * gain[...]
        inner = (
            scaled
            - jnp.mean(scaled, -1, keepdims=True)
            - normed * jnp.mean(scaled * normed, -1, keepdims=True)
        )
        back = (cotangent[span_here, :].astype(F32) + inv_scale * inner).astype(BF)
        for target, to, first, size in moves:
            if at <= first < at + step:
                outs[target][to : to + size, :] = back[first - at : first - at + size]


def spatial_backward_kernel(plan, where, triple, attend, kept, *refs):
    sources, refs = refs[: plan.origins], refs[plan.origins :]
    arrays, refs = refs[: plan.arrays], refs[plan.arrays :]
    grads, refs = refs[: plan.grads], refs[plan.grads :]
    back_triples, (upstream, back_mixed, back_triple) = refs[:-4], refs[-3:]
    for source, at, to, size in plan.moves:
        upstream[to : to + size, :] = sources[source][at : at + size, :]
    if plan.paired:
        emit_own(upstream, grads[0], 0, where[0], plan.locs)
        emit_own(upstream, grads[1], 0, 1 - where[0], plan.locs)
    else:
        grads[0][...] = upstream[...]
    rows_times(upstream, views(plan, arrays, where, 3), back_mixed, 0)
    attention_back(triple, attend, back_mixed, back_triple, plan.blocks)
    split_columns(back_triple, back_triples)
    if plan.paired:
        half = upstream.shape[1] // 2
        grads[1][:, half:] = back_triple[:, : grads[1].shape[1] - half]


def grad_kernel(products, count, where, *refs):
    sent, far, near, other = refs[-4:]
    core, loc = where[1], where[2]
    block = near.shape[0]
    beside = loc + 1 - 2 * lax.rem(loc, 2)
    places = (lax.rem(beside + 2, 4), beside, lax.rem(loc + 2, 4), loc)
    column = 0
    for left, others, (right, right_at), (right_other, other_at), width in products:
        left, right, right_other = refs[left], refs[right], refs[right_other]
        lanes = other.shape[1] // len(others)
        for number, (source, at) in enumerate(others):
            to = 0
            if len(others) > 1:
                to = pl.multiple_of((core if number == 0 else 1 - core) * lanes, lanes)
            other[:, pl.ds(to, lanes)] = refs[source][:, at : at + lanes]
        for number, place in enumerate(places):
            columns = pl.ds(pl.multiple_of(place * block, block), block)
            for first in range(0, width, 256):
                lane = slice(column + first, column + first + 256)
                here = right[:, right_at + first : right_at + first + 256]
                there = right_other[:, other_at + first : other_at + first + 256]
                total = dot(left[:, columns], here, TN) + dot(other[:, columns], there, TN)
                if number < 2:
                    sent[number * block : (number + 1) * block, lane] = total.astype(BF)
                elif number == 2:
                    far[:, lane] = total
                else:
                    near[:, lane] = total
        column += width


def finish_kernel(kind_first, *refs):
    out = refs[-1]
    block = out.shape[0]
    column = 0
    for near, beside, far in zip(refs[0:-1:3], refs[1:-1:3], refs[2:-1:3]):
        for at in range(0, near.shape[1], 256):
            lane = slice(at, at + 256)
            total = near[:, lane] + beside[block:, lane].astype(F32) + far[:, lane].astype(F32)
            kind, first = (kind_first * out.shape[2] + column + at) // out.shape[2] % 4, (column + at) % out.shape[2]
            out[:, kind, first : first + 256] = total
        column += near.shape[1]


def finish_last_kernel(kind_first, kept, *refs):
    finish_kernel(kind_first, *refs[:-1])


def fence_kernel(*refs):
    pass


def grad_after_kernel(products, count, passed, where, *refs):
    args, rest = refs[:count], refs[count + passed :]
    grad_kernel(products, count, where, *args, *rest[:3], rest[-1])


def rows_kernel(cloud, drop, keep, where, optical, radar, table, date_table, cotangent, *refs):
    own, other, upstream, dates_out, wide_table, places = refs
    here = where[0]
    dates, patches, _ = optical.shape
    pairs, half = dates // 2, patches // 2
    wide_table[...] = table[...].astype(F32)
    for patch in range(patches):
        places[patch : patch + 1, :] = wide_table[pl.ds(keep[0, patch], 1), :]
    for pair in range(pairs):
        found = []
        for number in range(2):
            date = pair * 2 + number
            at = here * dates + date
            seen = (1 - cloud[0, at]).astype(F32)
            kept = (1 - drop[0, at]).astype(F32)
            found.append(optical[date].astype(F32) * seen + radar[date].astype(F32) * kept + places[...])
        halves = [(rows[:half], rows[half:]) for rows in found]
        for out, swapped in ((own, 0), (other, 1)):
            picked = [jnp.where(here == swapped, first, second) for first, second in halves]
            for eight in range(0, half, 8):
                rows = jnp.concatenate([rows[eight : eight + 8] for rows in picked], axis=0)
                at = pair * half * 2 + eight * 2
                out[at : at + 16, :] = rows.astype(BF)
    block = 4 * pairs * 8
    for side in range(2):
        owner = here if side == 0 else 1 - here
        for pair in range(pairs):
            found = [cotangent[owner * dates + pair * 2 + number].astype(F32) for number in range(2)]
            for eight in range(half // 8):
                rows = jnp.concatenate([rows[eight * 8 : eight * 8 + 8] for rows in found], axis=0)
                at = eight * block + side * pairs * 16 + pair * 16
                upstream[at : at + 16, :] = rows.astype(BF)
    whole = date_table[...].astype(F32)
    flipped = jnp.concatenate([whole[dates:], whole[:dates]], axis=0)
    dates_out[...] = jnp.where(here == 0, whole, flipped)


class Plan:
    def __init__(self, blocks, moves, origins, weights, paired, locs, grads, sources=0, date_of=None, patch_of=None):
        self.date_of, self.patch_of = date_of, patch_of
        self.blocks, self.moves, self.origins = blocks, moves, origins
        self.arrays, self.table = len(weights.arrays), weights.table
        self.paired, self.locs, self.grads, self.sources = paired, locs, grads, sources


def call(body, outs, args, scratch=(), flops=0, kept=()):
    smem = pl.BlockSpec(memory_space=pltpu.SMEM)
    vmem = pl.BlockSpec(memory_space=pltpu.VMEM)
    specs = [smem if arg.dtype == jnp.int32 else vmem for arg in args]
    out_specs = [vmem] * len(outs)
    aliases = {}
    outs = list(outs)
    moved = sum(arg.size * arg.dtype.itemsize for arg in args)
    moved = moved + sum(out.size * out.dtype.itemsize for out in outs)
    for number in kept:
        specs[number] = pl.BlockSpec(memory_space=pl.ANY)
        out_specs.append(pl.BlockSpec(memory_space=pl.ANY))
        outs.append(jax.ShapeDtypeStruct(args[number].shape, args[number].dtype))
        aliases[number] = len(outs) - 1
    return pl.pallas_call(
        body,
        out_shape=outs,
        in_specs=specs,
        out_specs=out_specs,
        scratch_shapes=list(scratch),
        input_output_aliases=aliases,
        compiler_params=pltpu.CompilerParams(vmem_limit_bytes=VMEM_LIMIT),
        cost_estimate=pl.CostEstimate(flops=flops, bytes_accessed=moved, transcendentals=0),
    )(*args)


def fence(*arrays):
    anywhere = [pl.BlockSpec(memory_space=pl.ANY)] * len(arrays)
    return pl.pallas_call(
        fence_kernel,
        out_shape=[jax.ShapeDtypeStruct(array.shape, array.dtype) for array in arrays],
        in_specs=anywhere,
        out_specs=anywhere,
        input_output_aliases={number: number for number in range(len(arrays))},
    )(*arrays)


def swap(array, axis):
    return lax.ppermute(array, axis, [(0, 1), (1, 0)])


PAIRS = [(0, 1), (1, 0), (2, 3), (3, 2)]
APART = [(0, 2), (1, 3), (2, 0), (3, 1)]


def quarter_of(weights, number):
    rows = weights.shape[0]
    return by_kind(lax.dynamic_slice_in_dim(weights, number * (rows // 4), rows // 4, 0))


def by_kind(weights):
    return weights.transpose(1, 0, 2)


def whole_weights(weights):
    whole = lax.all_gather(weights.transpose(1, 0, 2), "date", axis=1, tiled=True)
    return Weights([whole], {kind: [(0, kind, 0)] for kind in range(4)})


def quarters():
    side, even = lax.axis_index("groups"), lax.axis_index("loc") % 2
    return side * 2 + even, (1 - side) * 2 + 1 - even


def gather_weights(weights, first, last):
    arrays = [by_kind(weights), first, swap(first, "groups"), lax.ppermute(first, "loc", PAIRS), last]
    return Weights(arrays, {kind: [(number, kind, number) for number in range(5)] for kind in range(4)})


def add_over_heads(partial, sizes):
    if sizes["mp"] == 2:
        return partial.astype(F32) + swap(partial, "mp").astype(F32)
    return lax.psum(partial.astype(F32), "mp")


def whole_grads(hidden, back_triple, upstream, mixed):
    width = mixed.shape[1]
    intake = dot(hidden, back_triple, TN)
    outlet = dot(upstream, mixed, TN)
    whole = jnp.concatenate([intake, outlet], axis=1).reshape(-1, 4, width)
    part = lax.psum_scatter(whole.astype(BF), ("loc", "date"), scatter_dimension=0, tiled=True)
    return part.astype(F32)


def summed(where, args, products, kept=()):
    rows, columns = args[products[0][0]].shape
    block, width = columns // 4, sum(product[-1] for product in products)
    return call(
        functools.partial(grad_after_kernel, products, len(args), len(kept)),
        (
            jax.ShapeDtypeStruct((2 * block, width), BF),
            jax.ShapeDtypeStruct((block, width), F32),
            jax.ShapeDtypeStruct((block, width), F32),
        ),
        (where, *args, *kept),
        scratch=(pltpu.VMEM((rows, columns), BF),),
        flops=4 * rows * columns * width,
        kept=tuple(range(1 + len(args), 1 + len(args) + len(kept))),
    )


def summed_over_loc(outs):
    sent, far, near = outs[:3]
    beside = lax.ppermute(sent, "loc", PAIRS)
    far = (far + beside[: far.shape[0]].astype(F32)).astype(BF)
    return near, beside, lax.ppermute(far, "loc", APART)


def finish(terms, width, kind_first, kept=None):
    out = jax.ShapeDtypeStruct((terms[0].shape[0], 4, width), F32)
    if kept is None:
        return call(functools.partial(finish_kernel, kind_first), (out,), terms)
    return call(functools.partial(finish_last_kernel, kind_first), (out,), (kept, *terms), kept=(0,))


def per_device(
    sizes,
    optical,
    radar,
    cloud,
    radar_drop,
    keep_index,
    place_table,
    date_table,
    spatial_gain,
    spatial_weights,
    temporal_gain,
    temporal_weights,
    cotangent,
):
    _, patches, dates_here, model = optical.shape
    patches_here, dates = cotangent.shape[1:3]
    width = spatial_weights.shape[2]
    rows = patches * dates_here
    here = lax.axis_index("date")
    first = here * dates_here
    paired = sizes["groups"] == 2 and sizes["loc"] == 4 and sizes["date"] == 2 and sizes["mp"] == 2
    paired = paired and dates_here % 2 == 0 and patches_here % 8 == 0 and model % 1024 == 0
    if paired:
        first_quarter, last_quarter = quarters()
        first_sent = quarter_of(spatial_weights, first_quarter)
    else:
        spatial, temporal = whole_weights(spatial_weights), whole_weights(temporal_weights)

    if paired:
        pairs, eights = dates_here // 2, patches_here // 8
        spatial_blocks, temporal_blocks = pairs, eights
        half_rows = eights * 16

        def temporal_whole(array):
            array = array.reshape(eights, 2, pairs, 2, 8, -1).transpose(1, 2, 3, 0, 4, 5)
            return jnp.where(here == 0, array, jnp.flip(array, 0)).reshape(dates, patches_here, -1)

        spatial_date, temporal_date, temporal_patch = (8, 2), (8, rows), (1, 8)
    else:
        spatial_blocks = 1 if rows <= 192 else dates_here
        temporal_blocks = patches_here // 8 if patches_here % 8 == 0 else 1

        def temporal_rows(array):
            array = array.reshape(dates, temporal_blocks, patches_here // temporal_blocks, -1)
            return array.transpose(1, 0, 2, 3).reshape(rows, -1)

        def temporal_whole(array):
            array = array.reshape(temporal_blocks, dates, patches_here // temporal_blocks, -1)
            return array.transpose(1, 0, 2, 3).reshape(dates, patches_here, -1)

        in_block = patches_here // temporal_blocks
        spatial_date, temporal_date, temporal_patch = (patches, rows), (in_block, rows), (1, in_block)
    spatial_size, temporal_size = rows // spatial_blocks, rows // temporal_blocks

    survive = (1 - cloud[0] * radar_drop[0]).astype(F32)
    side = lax.axis_index("groups") if paired else here
    where = jnp.stack([here, lax.axis_index("mp"), lax.axis_index("loc"), side]).astype(jnp.int32)
    optical_rows, radar_rows = optical[0].transpose(1, 0, 2), radar[0].transpose(1, 0, 2)
    cotangent_rows = cotangent[0].transpose(1, 0, 2)
    if paired:
        survive = jnp.where(here == 0, survive, jnp.roll(survive, dates_here))
    else:
        cloud_here = lax.dynamic_slice_in_dim(cloud, first, dates_here, 1)[0]
        drop_here = lax.dynamic_slice_in_dim(radar_drop, first, dates_here, 1)[0]
        places = jnp.take(place_table, keep_index[0], axis=0).astype(F32)[None]
        start = (
            optical_rows.astype(F32) * (1 - cloud_here).astype(F32)[:, None, None]
            + radar_rows.astype(F32) * (1 - drop_here).astype(F32)[:, None, None]
            + places
        ).astype(BF)
        start = start.reshape(rows, model)
        cotangent_rows = temporal_rows(cotangent_rows)
        date_rows = date_table.astype(F32)
    survive = jnp.repeat(survive, temporal_size // dates)[None]

    spatial_gain = spatial_gain[None]
    temporal_gain = temporal_gain[None]
    lanes = min(width, 256)

    def shape(*dims, dtype=BF):
        return jax.ShapeDtypeStruct(dims, dtype)

    def attend_dims(blocks):
        return (blocks * (width // lanes), lanes // HEAD_DIM * (rows // blocks), rows // blocks)

    layer_flops = 2 * rows * model * width * 4
    if paired:
        half = rows // 2
        own_start, other_start, cotangent_rows, date_rows = call(
            rows_kernel,
            (
                shape(half, model),
                shape(half, model),
                shape(rows, model),
                shape(dates, model, dtype=F32),
            ),
            (
                cloud,
                radar_drop,
                keep_index,
                where,
                optical_rows,
                radar_rows,
                place_table,
                date_table,
                cotangent_rows,
            ),
            scratch=(pltpu.VMEM(place_table.shape, F32), pltpu.VMEM((patches, model), F32)),
        )
        last_sent = quarter_of(spatial_weights, last_quarter)
        last_sent, own_start = fence(last_sent, own_start)
        origins = (own_start, other_start)
        spatial = gather_weights(spatial_weights, swap(first_sent, "date"), swap(last_sent, "date"))
        sent = [quarter_of(temporal_weights, number) for number in (first_quarter, last_quarter)]
        *sent, cotangent_rows = fence(*sent, cotangent_rows)
        temporal_first = swap(sent[0], "date")
        spatial_moves = [
            (side, pair * half_rows, (pair * 2 + side) * half_rows, half_rows)
            for side in range(2)
            for pair in range(pairs)
        ]
        temporal_moves = [
            (side, pair * half_rows + eight * 16, (eight * 2 + side) * pairs * 16 + pair * 16, 16)
            for side in range(2)
            for pair in range(pairs)
            for eight in range(eights)
        ]
        half_shapes = (shape(half, model), shape(half, model))
        own, quarter = shape(rows, model // 2), model // 4
        forward_grads = (own, own, shape(rows, 2 * quarter + width))
        temporal_grads = (
            own,
            shape(rows, model // 2 + 3 * width // 2),
            shape(rows, 3 * width // 2 + width),
        )
        back_shapes = (shape(rows, width), shape(rows, 2 * width))
        backward_grads = (own, shape(rows, model // 2 + width))
    else:
        origins = (start,)
        spatial_moves = [(0, at * spatial_size, at * spatial_size, spatial_size) for at in range(spatial_blocks)]
        temporal_moves = [(0, at * temporal_size, at * temporal_size, temporal_size) for at in range(temporal_blocks)]
        half_shapes = (shape(rows, model),)
        forward_grads = temporal_grads = backward_grads = (shape(rows, model),)
        back_shapes = (shape(rows, 3 * width),)

    def plan_of(blocks, moves, weights, grads, sources=0, date_of=spatial_date, patch_of=None):
        return Plan(
            blocks, moves, len(origins), weights, paired, sizes["loc"], len(grads), sources, date_of, patch_of
        )

    plan = plan_of(spatial_blocks, spatial_moves, spatial, forward_grads)
    outs = call(
        functools.partial(spatial_forward_kernel, plan),
        (
            *half_shapes,
            *forward_grads,
            shape(rows, 3 * width),
            shape(*attend_dims(spatial_blocks), dtype=F32),
            shape(rows, width),
        ),
        (where, spatial_gain, cotangent_rows, *origins, *spatial.arrays),
        scratch=(
            pltpu.VMEM((rows, model), BF),
            pltpu.VMEM((rows, model), BF),
            pltpu.VMEM((rows, model), BF),
        ),
        flops=layer_flops,
    )
    partials, outs = outs[: len(origins)], outs[len(origins) :]
    forward, (triple, attend, mixed) = outs[: len(forward_grads)], outs[len(forward_grads) :]
    if paired:
        temporal_first, kept = fence(temporal_first, partials[1])
        partials = (partials[0], kept)
        there, early = call(
            between_kernel,
            (shape(half, model),),
            (origins[1], partials[1], swap(partials[1], "mp"), forward[2]),
            kept=(3,),
        )
        temporal = gather_weights(temporal_weights, temporal_first, swap(sent[1], "date"))
        early, there, *temporal.arrays[2:] = fence(early, swap(there, "date"), *temporal.arrays[2:])
        sources = (origins[0], partials[0], swap(partials[0], "mp"), there)
        early_other = swap(early, "date")
    else:
        spatial_out = (start.astype(F32) + add_over_heads(partials[0], sizes)).astype(BF)
        moved = lax.all_to_all(
            spatial_out.reshape(dates_here, patches, model),
            "date",
            split_axis=1,
            concat_axis=0,
            tiled=True,
        )
        sources = (temporal_rows(moved),)
    plan = plan_of(
        temporal_blocks,
        temporal_moves,
        temporal,
        temporal_grads,
        len(sources),
        temporal_date,
        temporal_patch,
    )
    outs = call(
        functools.partial(temporal_kernel, plan),
        (
            *temporal_grads,
            shape(rows, model),
            shape(rows, width),
            shape(rows, model),
            shape(rows, model),
            *(() if paired else back_shapes),
        ),
        (
            where,
            temporal_gain,
            survive,
            date_rows,
            cotangent_rows,
            *sources,
            *temporal.arrays,
        ),
        scratch=(
            pltpu.VMEM((rows, model), BF),
            pltpu.VMEM((rows, 3 * width), BF),
            pltpu.VMEM(attend_dims(temporal_blocks), F32),
            pltpu.VMEM((rows, width), BF),
            pltpu.VMEM((rows, 3 * width), BF),
        ),
        flops=2 * layer_flops,
    )
    middle, outs = outs[: len(temporal_grads)], outs[len(temporal_grads) :]
    (joined, temporal_mixed, temporal_partial, back_part), temporal_triples = outs[:4], outs[4:]
    if paired:
        back_part, early_other = fence(back_part, early_other)

    if sizes["mp"] == 2:
        others = swap(back_part, "mp")
    else:
        others = (lax.psum(back_part.astype(F32), "mp") - back_part.astype(F32)).astype(BF)
    *backs, last_sent = call(
        functools.partial(norm_back_kernel, temporal_moves, temporal_size),
        half_shapes,
        (temporal_gain, back_part, others, joined, cotangent_rows, middle[-1]),
        kept=(5,),
    )
    if paired:
        back_origins = (backs[0], swap(backs[1], "date"))
        early_there = swap(early_other[:, : 2 * quarter], "mp")
        middle_other = swap(middle[1], "date")
        part, columns = 3 * width // 2, model // 2
        *intake, kept = summed(
            where,
            (middle[0], middle_other, middle[1]),
            ((0, ((1, 0),), (2, columns), (1, columns), part),),
        )
    else:
        back = lax.all_to_all(
            temporal_whole(backs[0]), "date", split_axis=0, concat_axis=1, tiled=True
        )
        back_origins = (back.reshape(rows, model),)
        kept = temporal_triples[0]
    outlet = spatial.only((3,))
    plan = plan_of(spatial_blocks, spatial_moves, outlet, backward_grads)
    *outs, kept = call(
        functools.partial(spatial_backward_kernel, plan),
        (*backward_grads, *back_shapes),
        (where, triple, attend, kept, *back_origins, *outlet.arrays),
        scratch=(
            pltpu.VMEM((rows, model), BF),
            pltpu.VMEM((rows, width), BF),
            pltpu.VMEM((rows, 3 * width), BF),
        ),
        flops=layer_flops,
        kept=(3,),
    )
    backward, back_triples = outs[: len(backward_grads)], outs[len(backward_grads) :]
    encoded = (joined.astype(F32) + add_over_heads(temporal_partial, sizes)).astype(BF)
    encoded = temporal_whole(encoded).transpose(1, 0, 2)[None]
    if not paired:
        return (
            encoded,
            whole_grads(forward[0], back_triples[0], backward[0], mixed),
            whole_grads(middle[0], kept, cotangent_rows, temporal_mixed),
        )
    intake = [*summed_over_loc((*intake, kept))]
    last_other = swap(last_sent, "date")
    *sums, upstream_own, intake[1] = summed(
        where,
        (middle[0], middle_other, last_sent, last_other, forward[1], early_other, early_there),
        (
            (0, ((1, 0),), (2, 0), (3, 0), part),
            (4, ((5, quarter), (6, quarter)), (2, part), (3, part), width),
        ),
        kept=(backward[0], intake[1]),
    )
    sums[0], intake[2] = fence(sums[0], intake[2])
    outlet = [*summed_over_loc(sums)]
    half = model // 2
    backward_other = swap(backward[1], "date")
    *sums, outlet[0] = summed(
        where,
        (
            upstream_own,
            backward_other,
            mixed,
            early_other,
            forward[0],
            early_there,
            back_triples[0],
        ),
        (
            (0, ((1, 0),), (2, 0), (3, 2 * quarter), width),
            (4, ((3, 0), (5, 0)), (6, 0), (1, half), back_triples[0].shape[1]),
        ),
        kept=(outlet[0],),
    )
    spatial_terms = [*summed_over_loc(sums)]
    sums = summed(
        where,
        (forward[0], early_other, early_there, back_triples[1], swap(back_triples[1], "date")),
        ((0, ((1, 0), (2, 0)), (3, 0), (4, 0), back_triples[1].shape[1]),),
        kept=(spatial_terms[0],),
    )
    *sums, spatial_terms[0] = sums
    spatial_terms += summed_over_loc(sums)
    (temporal_grads,) = finish((*intake, *outlet), width, 0)
    spatial_grads, temporal_grads = finish(spatial_terms, width, 3, kept=temporal_grads)
    return (encoded, spatial_grads, temporal_grads)


def solution(mesh):
    in_specs = (
        P(("groups", "loc"), None, "date", None),
        P(("groups", "loc"), None, "date", None),
        P(("groups", "loc"), None),
        P(("groups", "loc"), None),
        P(("groups", "loc"), None),
        P(),
        P(),
        P(),
        P("date", None, "mp"),
        P(),
        P("date", None, "mp"),
        P(("groups", "loc"), "date", None, None),
    )
    out_specs = (
        P(("groups", "loc"), "date", None, None),
        P(("groups", "loc", "date"), None, "mp"),
        P(("groups", "loc", "date"), None, "mp"),
    )
    return jax.shard_map(
        functools.partial(per_device, dict(mesh.shape)),
        mesh=mesh,
        in_specs=in_specs,
        out_specs=out_specs,
        check_vma=False,
    )
```

```python
import functools

import jax
import jax.numpy as jnp
from jax import lax
from jax.experimental import pallas as pl
from jax.experimental.pallas import tpu as pltpu
from jax.sharding import PartitionSpec as P

HEAD_DIM = 64
EPSILON = 1e-05
CROSS = -1e30
BF = jnp.bfloat16
F32 = jnp.float32
NN = (((1,), (0,)), ((), ()))
NT = (((1,), (1,)), ((), ()))
TN = (((0,), (0,)), ((), ()))
VMEM_LIMIT = 56 * 1024 * 1024


def dot(left, right, dims):
    return lax.dot_general(left, right, dims, preferred_element_type=F32)


def statistics(rows):
    values = rows.astype(F32)
    centred = values - jnp.mean(values, -1, keepdims=True)
    inv_scale = lax.rsqrt(jnp.mean(centred * centred, -1, keepdims=True) + EPSILON)
    return centred * inv_scale, inv_scale


class Heads:
    def __init__(self, width):
        self.lanes = min(width, 256)
        self.count = self.lanes // HEAD_DIM
        owner = lax.broadcasted_iota(jnp.int32, (1, self.lanes), 1) // HEAD_DIM
        self.masks = [(owner == head).astype(F32) for head in range(self.count)]

    def stack(self, block):
        return jnp.concatenate([block * mask.astype(BF) for mask in self.masks], axis=0)

    def unstack(self, tall):
        rows = tall.shape[0] // self.count
        total = tall[0:rows] * self.masks[0]
        for head in range(1, self.count):
            total = total + tall[head * rows : (head + 1) * rows] * self.masks[head]
        return total


class Weights:
    def __init__(self, arrays, table):
        self.arrays, self.table = list(arrays), table

    def only(self, kinds):
        used = sorted({entry[0] for kind in kinds for entry in self.table[kind]})
        table = {
            kind: [(used.index(array), at, place) for array, at, place in self.table[kind]]
            for kind in kinds
        }
        return Weights([self.arrays[number] for number in used], table)


def first_row(number, rows, where):
    if number == 0:
        return where[0] * rows
    side, even = where[3], lax.rem(where[2], 2)
    side = side if number in (1, 3) else 1 - side
    even = even if number in (1, 2) else 1 - even
    return (1 - where[0]) * rows + (side * 2 + even) * (rows // 4)


def views(plan, refs, where, kind):
    found = []
    for array, at, place in plan.table[kind]:
        part = refs[array].at[at]
        if plan.paired:
            first = pl.multiple_of(first_row(place, refs[plan.table[kind][0][0]].shape[1], where), 128)
            found.append((part, pl.ds(first, part.shape[0])))
        else:
            found.append((part, slice(None)))
    return found


def joint(parts):
    small = [entry for entry in parts if entry[0].shape[0] < 256]
    pairs = [small[at : at + 2] for at in range(0, len(small), 2)]
    return [[entry] for entry in parts if entry[0].shape[0] >= 256] + pairs


def rows_times(rows_ref, parts, out_ref, column):
    width = parts[0][0].shape[1]
    step = min(width, 256)
    for at in range(0, width, step):
        total = None
        for group in joint(parts):
            left = [rows_ref[:, columns] for _, columns in group]
            right = [part[:, at : at + step] for part, _ in group]
            if len(group) > 1:
                left, right = [jnp.concatenate(left, axis=1)], [jnp.concatenate(right, axis=0)]
            term = dot(left[0], right[0], NN)
            total = term if total is None else total + term
        out_ref[:, column + at : column + at + step] = total.astype(out_ref.dtype)


def emit_own(rows_ref, out, at, date, loc_count):
    block = rows_ref.shape[1] // (2 * loc_count)
    for loc in range(loc_count):
        first = pl.multiple_of((loc * 2 + date) * block, block)
        out[:, at + loc * block : at + (loc + 1) * block] = rows_ref[:, pl.ds(first, block)]


def emit_half(rows_ref, out, at, date, core, loc_count):
    block = rows_ref.shape[1] // (2 * loc_count)
    for number in range(loc_count // 2):
        loc = core * (loc_count // 2) + number
        first = pl.multiple_of((loc * 2 + date) * block, block)
        out[:, at + number * block : at + (number + 1) * block] = rows_ref[:, pl.ds(first, block)]


def groups_of(size, spans, modulus, axis):
    shape = (size, 1) if axis == 0 else (1, size)
    return lax.rem(lax.broadcasted_iota(jnp.int32, shape, axis) // spans, modulus)


def spatial_bias(plan, size):
    query, key = (groups_of(size, *plan.date_of, axis) for axis in range(2))
    return jnp.where(query == key, 0.0, CROSS).astype(F32)


def temporal_bias(plan, size, survive):
    query, key = (groups_of(size, *plan.patch_of, axis) for axis in range(2))
    query_date, key_date = (groups_of(size, *plan.date_of, axis) for axis in range(2))
    allowed = (survive[...] == 1.0) | (query_date == key_date)
    return jnp.where(query == key, jnp.where(allowed, 0.0, -1000000000.0), CROSS).astype(F32)


def attention(triple_ref, bias, attend_ref, mixed_ref, blocks):
    width = triple_ref.shape[1] // 3
    heads = Heads(width)
    rows = triple_ref.shape[0] // blocks
    groups = width // heads.lanes
    bias = jnp.concatenate([bias] * heads.count, axis=0)
    for block in range(blocks):
        at = slice(block * rows, (block + 1) * rows)
        for group in range(groups):
            lane = group * heads.lanes
            queries = heads.stack(triple_ref[at, lane : lane + heads.lanes])
            keys = triple_ref[at, width + lane : width + lane + heads.lanes]
            values = triple_ref[at, 2 * width + lane : 2 * width + lane + heads.lanes]
            scores = dot(queries, keys, NT) * HEAD_DIM ** (-0.5) + bias
            raised = jnp.exp(scores - jnp.max(scores, -1, keepdims=True))
            attend = raised * (1.0 / jnp.sum(raised, -1, keepdims=True))
            attend_ref[block * groups + group] = attend
            mixed = heads.unstack(dot(attend.astype(BF), values, NN))
            mixed_ref[at, lane : lane + heads.lanes] = mixed.astype(BF)


def attention_back(triple_ref, attend_ref, back_mixed_ref, back_triple_ref, blocks):
    width = triple_ref.shape[1] // 3
    heads = Heads(width)
    rows = triple_ref.shape[0] // blocks
    groups = width // heads.lanes
    for block in range(blocks):
        at = slice(block * rows, (block + 1) * rows)
        for group in range(groups):
            lane = group * heads.lanes
            queries = heads.stack(triple_ref[at, lane : lane + heads.lanes])
            keys = triple_ref[at, width + lane : width + lane + heads.lanes]
            values = triple_ref[at, 2 * width + lane : 2 * width + lane + heads.lanes]
            back = heads.stack(back_mixed_ref[at, lane : lane + heads.lanes])
            attend = attend_ref[block * groups + group]
            back_attend = dot(back, values, NT)
            back_values = dot(attend.astype(BF), back, TN)
            inner = back_attend - jnp.sum(back_attend * attend, -1, keepdims=True)
            back_scores = (attend * inner * HEAD_DIM ** (-0.5)).astype(BF)
            back_queries = heads.unstack(dot(back_scores, keys, NN))
            back_keys = dot(back_scores, queries, TN)
            for number, term in enumerate((back_queries, back_keys, back_values)):
                first = number * width + lane
                back_triple_ref[at, first : first + heads.lanes] = term.astype(BF)


def normalize_into(rows_ref, gain_ref, hidden_ref, blocks):
    rows = rows_ref.shape[0] // blocks
    for block in range(blocks):
        at = slice(block * rows, (block + 1) * rows)
        normed, _ = statistics(rows_ref[at, :])
        hidden_ref[at, :] = (normed * gain_ref[...]).astype(BF)


def spatial_forward_kernel(plan, where, gain, cotangent, *refs):
    sources, refs = refs[: plan.origins], refs[plan.origins :]
    arrays, refs = refs[: plan.arrays], refs[plan.arrays :]
    partials, refs = refs[: plan.origins], refs[plan.origins :]
    grads, refs = refs[: plan.grads], refs[plan.grads :]
    triple, attend, mixed, start, hidden, whole = refs
    for source, at, to, size in plan.moves:
        start[to : to + size, :] = sources[source][at : at + size, :]
    normalize_into(start, gain, hidden, plan.blocks)
    width = mixed.shape[1]
    for kind in range(3):
        rows_times(hidden, views(plan, arrays, where, kind), triple, kind * width)
    bias = spatial_bias(plan, start.shape[0] // plan.blocks)
    attention(triple, bias, attend, mixed, plan.blocks)
    for part, features in views(plan, arrays, where, 3):
        whole[:, features] = dot(mixed[...], part[...], NT).astype(BF)
    for source, at, to, size in plan.moves:
        partials[source][at : at + size, :] = whole[to : to + size, :]
    if plan.paired:
        own_hidden, own_cotangent, sent = grads
        half = hidden.shape[1] // 4
        here, core = where[0], where[1]
        emit_own(hidden, own_hidden, 0, here, plan.locs)
        emit_own(cotangent, own_cotangent, 0, here, plan.locs)
        emit_half(hidden, sent, 0, 1 - here, core, plan.locs)
        emit_half(cotangent, sent, half, 1 - here, core, plan.locs)
        sent[:, 2 * half :] = mixed[...]
    else:
        grads[0][...] = hidden[...]


def between_kernel(start, here, there, kept, out, passed):
    total = here[...].astype(F32) + there[...].astype(F32)
    out[...] = (start[...].astype(F32) + total).astype(BF)


def temporal_kernel(plan, where, gain, survive, date_rows, cotangent, *refs):
    sources, refs = refs[: plan.sources], refs[plan.sources :]
    arrays, refs = refs[: plan.arrays], refs[plan.arrays :]
    grads, refs = refs[: plan.grads], refs[plan.grads :]
    joined, mixed, partial, back_part = refs[:4]
    back_triples, (hidden, triple, attend, back_mixed, back_triple) = refs[4:-5], refs[-5:]
    rows = joined.shape[0] // plan.blocks
    patches = rows // date_rows.shape[0]
    for source, at, to, size in plan.moves:
        if source == 0 and plan.sources > 1:
            total = sources[1][at : at + size, :].astype(F32) + sources[2][at : at + size, :].astype(F32)
            out = (sources[0][at : at + size, :].astype(F32) + total).astype(BF)
        else:
            out = sources[-1][at : at + size, :]
        out = out.astype(F32)
        dated = [
            out[at : at + patches] + date_rows[(to % rows + at) // patches : (to % rows + at) // patches + 1, :]
            for at in range(0, size, patches)
        ]
        joined[to : to + size, :] = jnp.concatenate(dated, axis=0).astype(BF)
    normalize_into(joined, gain, hidden, plan.blocks)
    width = mixed.shape[1]
    for kind in range(3):
        rows_times(hidden, views(plan, arrays, where, kind), triple, kind * width)
    outlet = views(plan, arrays, where, 3)
    rows_times(cotangent, outlet, back_mixed, 0)
    bias = temporal_bias(plan, joined.shape[0] // plan.blocks, survive)
    attention(triple, bias, attend, mixed, plan.blocks)
    for part, features in outlet:
        partial[:, features] = dot(mixed[...], part[...], NT).astype(BF)
    if plan.paired:
        own_hidden, sent, last = grads
        half = hidden.shape[1] // 2
        emit_own(hidden, own_hidden, 0, where[0], plan.locs)
        emit_own(hidden, sent, 0, 1 - where[0], plan.locs)
    else:
        grads[0][...] = hidden[...]
    attention_back(triple, attend, back_mixed, back_triple, plan.blocks)
    intakes = [views(plan, arrays, where, kind) for kind in range(3)]
    for entries in zip(*intakes):
        total = None
        for kind, (part, features) in enumerate(entries):
            term = dot(back_triple[:, kind * width : (kind + 1) * width], part[...], NT)
            total = term if total is None else total + term
        back_part[:, features] = total.astype(BF)
    split_columns(back_triple, back_triples)
    if plan.paired:
        split = sent.shape[1] - half
        sent[:, half:] = back_triple[:, :split]
        last[:, :split] = back_triple[:, split:]
        last[:, split:] = mixed[...]


def split_columns(whole, outs):
    at = 0
    for out in outs:
        out[...] = whole[:, at : at + out.shape[1]]
        at += out.shape[1]


def norm_back_kernel(moves, step, gain, here, there, joined, cotangent, kept, *outs):
    for at in range(0, joined.shape[0], step):
        span_here = slice(at, at + step)
        normed, inv_scale = statistics(joined[span_here, :])
        total = here[span_here, :].astype(F32) + there[span_here, :].astype(F32)
        scaled = total * gain[...]
        inner = (
            scaled
            - jnp.mean(scaled, -1, keepdims=True)
            - normed * jnp.mean(scaled * normed, -1, keepdims=True)
        )
        back = (cotangent[span_here, :].astype(F32) + inv_scale * inner).astype(BF)
        for target, to, first, size in moves:
            if at <= first < at + step:
                outs[target][to : to + size, :] = back[first - at : first - at + size]


def spatial_backward_kernel(plan, where, triple, attend, kept, *refs):
    sources, refs = refs[: plan.origins], refs[plan.origins :]
    arrays, refs = refs[: plan.arrays], refs[plan.arrays :]
    grads, refs = refs[: plan.grads], refs[plan.grads :]
    back_triples, (upstream, back_mixed, back_triple) = refs[:-4], refs[-3:]
    for source, at, to, size in plan.moves:
        upstream[to : to + size, :] = sources[source][at : at + size, :]
    if plan.paired:
        emit_own(upstream, grads[0], 0, where[0], plan.locs)
        emit_own(upstream, grads[1], 0, 1 - where[0], plan.locs)
    else:
        grads[0][...] = upstream[...]
    rows_times(upstream, views(plan, arrays, where, 3), back_mixed, 0)
    attention_back(triple, attend, back_mixed, back_triple, plan.blocks)
    split_columns(back_triple, back_triples)
    if plan.paired:
        half = upstream.shape[1] // 2
        grads[1][:, half:] = back_triple[:, : grads[1].shape[1] - half]


def grad_kernel(products, count, where, *refs):
    sent, far, near, other = refs[-4:]
    core, loc = where[1], where[2]
    block = near.shape[0]
    beside = loc + 1 - 2 * lax.rem(loc, 2)
    places = (lax.rem(beside + 2, 4), beside, lax.rem(loc + 2, 4), loc)
    column = 0
    for left, others, (right, right_at), (right_other, other_at), width in products:
        left, right, right_other = refs[left], refs[right], refs[right_other]
        lanes = other.shape[1] // len(others)
        for number, (source, at) in enumerate(others):
            to = 0
            if len(others) > 1:
                to = pl.multiple_of((core if number == 0 else 1 - core) * lanes, lanes)
            other[:, pl.ds(to, lanes)] = refs[source][:, at : at + lanes]
        for number, place in enumerate(places):
            columns = pl.ds(pl.multiple_of(place * block, block), block)
            for first in range(0, width, 256):
                lane = slice(column + first, column + first + 256)
                here = right[:, right_at + first : right_at + first + 256]
                there = right_other[:, other_at + first : other_at + first + 256]
                total = dot(left[:, columns], here, TN) + dot(other[:, columns], there, TN)
                if number < 2:
                    sent[number * block : (number + 1) * block, lane] = total.astype(BF)
                elif number == 2:
                    far[:, lane] = total
                else:
                    near[:, lane] = total
        column += width


def finish_kernel(kind_first, *refs):
    out = refs[-1]
    block = out.shape[0]
    column = 0
    for near, beside, far in zip(refs[0:-1:3], refs[1:-1:3], refs[2:-1:3]):
        for at in range(0, near.shape[1], 256):
            lane = slice(at, at + 256)
            total = near[:, lane] + beside[block:, lane].astype(F32) + far[:, lane].astype(F32)
            kind, first = (kind_first * out.shape[2] + column + at) // out.shape[2] % 4, (column + at) % out.shape[2]
            out[:, kind, first : first + 256] = total
        column += near.shape[1]


def finish_last_kernel(kind_first, kept, *refs):
    finish_kernel(kind_first, *refs[:-1])


def fence_kernel(*refs):
    pass


def grad_after_kernel(products, count, passed, where, *refs):
    args, rest = refs[:count], refs[count + passed :]
    grad_kernel(products, count, where, *args, *rest[:3], rest[-1])


def rows_kernel(cloud, drop, keep, where, optical, radar, table, date_table, cotangent, *refs):
    own, other, upstream, dates_out, wide_table, places = refs
    here = where[0]
    dates, patches, _ = optical.shape
    pairs, half = dates // 2, patches // 2
    wide_table[...] = table[...].astype(F32)
    for patch in range(patches):
        places[patch : patch + 1, :] = wide_table[pl.ds(keep[0, patch], 1), :]
    for pair in range(pairs):
        found = []
        for number in range(2):
            date = pair * 2 + number
            at = here * dates + date
            seen = (1 - cloud[0, at]).astype(F32)
            kept = (1 - drop[0, at]).astype(F32)
            found.append(optical[date].astype(F32) * seen + radar[date].astype(F32) * kept + places[...])
        halves = [(rows[:half], rows[half:]) for rows in found]
        for out, swapped in ((own, 0), (other, 1)):
            picked = [jnp.where(here == swapped, first, second) for first, second in halves]
            for eight in range(0, half, 8):
                rows = jnp.concatenate([rows[eight : eight + 8] for rows in picked], axis=0)
                at = pair * half * 2 + eight * 2
                out[at : at + 16, :] = rows.astype(BF)
    block = 4 * pairs * 8
    for side in range(2):
        owner = here if side == 0 else 1 - here
        for pair in range(pairs):
            found = [cotangent[owner * dates + pair * 2 + number].astype(F32) for number in range(2)]
            for eight in range(half // 8):
                rows = jnp.concatenate([rows[eight * 8 : eight * 8 + 8] for rows in found], axis=0)
                at = eight * block + side * pairs * 16 + pair * 16
                upstream[at : at + 16, :] = rows.astype(BF)
    whole = date_table[...].astype(F32)
    flipped = jnp.concatenate([whole[dates:], whole[:dates]], axis=0)
    dates_out[...] = jnp.where(here == 0, whole, flipped)


class Plan:
    def __init__(self, blocks, moves, origins, weights, paired, locs, grads, sources=0, date_of=None, patch_of=None):
        self.date_of, self.patch_of = date_of, patch_of
        self.blocks, self.moves, self.origins = blocks, moves, origins
        self.arrays, self.table = len(weights.arrays), weights.table
        self.paired, self.locs, self.grads, self.sources = paired, locs, grads, sources


def call(body, outs, args, scratch=(), flops=0, kept=()):
    smem = pl.BlockSpec(memory_space=pltpu.SMEM)
    vmem = pl.BlockSpec(memory_space=pltpu.VMEM)
    specs = [smem if arg.dtype == jnp.int32 else vmem for arg in args]
    out_specs = [vmem] * len(outs)
    aliases = {}
    outs = list(outs)
    moved = sum(arg.size * arg.dtype.itemsize for arg in args)
    moved = moved + sum(out.size * out.dtype.itemsize for out in outs)
    for number in kept:
        specs[number] = pl.BlockSpec(memory_space=pl.ANY)
        out_specs.append(pl.BlockSpec(memory_space=pl.ANY))
        outs.append(jax.ShapeDtypeStruct(args[number].shape, args[number].dtype))
        aliases[number] = len(outs) - 1
    return pl.pallas_call(
        body,
        out_shape=outs,
        in_specs=specs,
        out_specs=out_specs,
        scratch_shapes=list(scratch),
        input_output_aliases=aliases,
        compiler_params=pltpu.CompilerParams(vmem_limit_bytes=VMEM_LIMIT),
        cost_estimate=pl.CostEstimate(flops=flops, bytes_accessed=moved, transcendentals=0),
    )(*args)


def fence(*arrays):
    anywhere = [pl.BlockSpec(memory_space=pl.ANY)] * len(arrays)
    return pl.pallas_call(
        fence_kernel,
        out_shape=[jax.ShapeDtypeStruct(array.shape, array.dtype) for array in arrays],
        in_specs=anywhere,
        out_specs=anywhere,
        input_output_aliases={number: number for number in range(len(arrays))},
    )(*arrays)


def swap(array, axis):
    return lax.ppermute(array, axis, [(0, 1), (1, 0)])


PAIRS = [(0, 1), (1, 0), (2, 3), (3, 2)]
APART = [(0, 2), (1, 3), (2, 0), (3, 1)]


def quarter_of(weights, number):
    rows = weights.shape[0]
    return by_kind(lax.dynamic_slice_in_dim(weights, number * (rows // 4), rows // 4, 0))


def by_kind(weights):
    return weights.transpose(1, 0, 2)


def whole_weights(weights):
    whole = lax.all_gather(weights.transpose(1, 0, 2), "date", axis=1, tiled=True)
    return Weights([whole], {kind: [(0, kind, 0)] for kind in range(4)})


def quarters():
    side, even = lax.axis_index("groups"), lax.axis_index("loc") % 2
    return side * 2 + even, (1 - side) * 2 + 1 - even


def gather_weights(weights, first, last):
    arrays = [by_kind(weights), first, swap(first, "groups"), lax.ppermute(first, "loc", PAIRS), last]
    return Weights(arrays, {kind: [(number, kind, number) for number in range(5)] for kind in range(4)})


def add_over_heads(partial, sizes):
    if sizes["mp"] == 2:
        return partial.astype(F32) + swap(partial, "mp").astype(F32)
    return lax.psum(partial.astype(F32), "mp")


def whole_grads(hidden, back_triple, upstream, mixed):
    width = mixed.shape[1]
    intake = dot(hidden, back_triple, TN)
    outlet = dot(upstream, mixed, TN)
    whole = jnp.concatenate([intake, outlet], axis=1).reshape(-1, 4, width)
    part = lax.psum_scatter(whole.astype(BF), ("loc", "date"), scatter_dimension=0, tiled=True)
    return part.astype(F32)


def summed(where, args, products, kept=()):
    rows, columns = args[products[0][0]].shape
    block, width = columns // 4, sum(product[-1] for product in products)
    return call(
        functools.partial(grad_after_kernel, products, len(args), len(kept)),
        (
            jax.ShapeDtypeStruct((2 * block, width), BF),
            jax.ShapeDtypeStruct((block, width), F32),
            jax.ShapeDtypeStruct((block, width), F32),
        ),
        (where, *args, *kept),
        scratch=(pltpu.VMEM((rows, columns), BF),),
        flops=4 * rows * columns * width,
        kept=tuple(range(1 + len(args), 1 + len(args) + len(kept))),
    )


def summed_over_loc(outs):
    sent, far, near = outs[:3]
    beside = lax.ppermute(sent, "loc", PAIRS)
    far = (far + beside[: far.shape[0]].astype(F32)).astype(BF)
    return near, beside, lax.ppermute(far, "loc", APART)


def finish(terms, width, kind_first, kept=None):
    out = jax.ShapeDtypeStruct((terms[0].shape[0], 4, width), F32)
    if kept is None:
        return call(functools.partial(finish_kernel, kind_first), (out,), terms)
    return call(functools.partial(finish_last_kernel, kind_first), (out,), (kept, *terms), kept=(0,))


def per_device(
    sizes,
    optical,
    radar,
    cloud,
    radar_drop,
    keep_index,
    place_table,
    date_table,
    spatial_gain,
    spatial_weights,
    temporal_gain,
    temporal_weights,
    cotangent,
):
    _, patches, dates_here, model = optical.shape
    patches_here, dates = cotangent.shape[1:3]
    width = spatial_weights.shape[2]
    rows = patches * dates_here
    here = lax.axis_index("date")
    first = here * dates_here
    paired = sizes["groups"] == 2 and sizes["loc"] == 4 and sizes["date"] == 2 and sizes["mp"] == 2
    paired = paired and dates_here % 2 == 0 and patches_here % 8 == 0 and model % 1024 == 0
    if paired:
        first_quarter, last_quarter = quarters()
        first_sent = quarter_of(spatial_weights, first_quarter)
    else:
        spatial, temporal = whole_weights(spatial_weights), whole_weights(temporal_weights)

    if paired:
        pairs, eights = dates_here // 2, patches_here // 8
        spatial_blocks, temporal_blocks = pairs, eights
        half_rows = eights * 16

        def temporal_whole(array):
            array = array.reshape(eights, 2, pairs, 2, 8, -1).transpose(1, 2, 3, 0, 4, 5)
            return jnp.where(here == 0, array, jnp.flip(array, 0)).reshape(dates, patches_here, -1)

        spatial_date, temporal_date, temporal_patch = (8, 2), (8, rows), (1, 8)
    else:
        spatial_blocks = 1 if rows <= 192 else dates_here
        temporal_blocks = patches_here // 8 if patches_here % 8 == 0 else 1

        def temporal_rows(array):
            array = array.reshape(dates, temporal_blocks, patches_here // temporal_blocks, -1)
            return array.transpose(1, 0, 2, 3).reshape(rows, -1)

        def temporal_whole(array):
            array = array.reshape(temporal_blocks, dates, patches_here // temporal_blocks, -1)
            return array.transpose(1, 0, 2, 3).reshape(dates, patches_here, -1)

        in_block = patches_here // temporal_blocks
        spatial_date, temporal_date, temporal_patch = (patches, rows), (in_block, rows), (1, in_block)
    spatial_size, temporal_size = rows // spatial_blocks, rows // temporal_blocks

    survive = (1 - cloud[0] * radar_drop[0]).astype(F32)
    side = lax.axis_index("groups") if paired else here
    where = jnp.stack([here, lax.axis_index("mp"), lax.axis_index("loc"), side]).astype(jnp.int32)
    optical_rows, radar_rows = optical[0].transpose(1, 0, 2), radar[0].transpose(1, 0, 2)
    cotangent_rows = cotangent[0].transpose(1, 0, 2)
    if paired:
        survive = jnp.where(here == 0, survive, jnp.roll(survive, dates_here))
    else:
        cloud_here = lax.dynamic_slice_in_dim(cloud, first, dates_here, 1)[0]
        drop_here = lax.dynamic_slice_in_dim(radar_drop, first, dates_here, 1)[0]
        places = jnp.take(place_table, keep_index[0], axis=0).astype(F32)[None]
        start = (
            optical_rows.astype(F32) * (1 - cloud_here).astype(F32)[:, None, None]
            + radar_rows.astype(F32) * (1 - drop_here).astype(F32)[:, None, None]
            + places
        ).astype(BF)
        start = start.reshape(rows, model)
        cotangent_rows = temporal_rows(cotangent_rows)
        date_rows = date_table.astype(F32)
    survive = jnp.repeat(survive, temporal_size // dates)[None]

    spatial_gain = spatial_gain[None]
    temporal_gain = temporal_gain[None]
    lanes = min(width, 256)

    def shape(*dims, dtype=BF):
        return jax.ShapeDtypeStruct(dims, dtype)

    def attend_dims(blocks):
        return (blocks * (width // lanes), lanes // HEAD_DIM * (rows // blocks), rows // blocks)

    layer_flops = 2 * rows * model * width * 4
    if paired:
        half = rows // 2
        own_start, other_start, cotangent_rows, date_rows = call(
            rows_kernel,
            (
                shape(half, model),
                shape(half, model),
                shape(rows, model),
                shape(dates, model, dtype=F32),
            ),
            (
                cloud,
                radar_drop,
                keep_index,
                where,
                optical_rows,
                radar_rows,
                place_table,
                date_table,
                cotangent_rows,
            ),
            scratch=(pltpu.VMEM(place_table.shape, F32), pltpu.VMEM((patches, model), F32)),
        )
        last_sent = quarter_of(spatial_weights, last_quarter)
        last_sent, own_start = fence(last_sent, own_start)
        origins = (own_start, other_start)
        spatial = gather_weights(spatial_weights, swap(first_sent, "date"), swap(last_sent, "date"))
        sent = [quarter_of(temporal_weights, number) for number in (first_quarter, last_quarter)]
        *sent, cotangent_rows = fence(*sent, cotangent_rows)
        temporal_first = swap(sent[0], "date")
        spatial_moves = [
            (side, pair * half_rows, (pair * 2 + side) * half_rows, half_rows)
            for side in range(2)
            for pair in range(pairs)
        ]
        temporal_moves = [
            (side, pair * half_rows + eight * 16, (eight * 2 + side) * pairs * 16 + pair * 16, 16)
            for side in range(2)
            for pair in range(pairs)
            for eight in range(eights)
        ]
        half_shapes = (shape(half, model), shape(half, model))
        own, quarter = shape(rows, model // 2), model // 4
        forward_grads = (own, own, shape(rows, 2 * quarter + width))
        temporal_grads = (
            own,
            shape(rows, model // 2 + 3 * width // 2),
            shape(rows, 3 * width // 2 + width),
        )
        back_shapes = (shape(rows, 3 * width // 2), shape(rows, 3 * width // 2))
        backward_grads = (own, shape(rows, model // 2 + 3 * width // 2))
    else:
        origins = (start,)
        spatial_moves = [(0, at * spatial_size, at * spatial_size, spatial_size) for at in range(spatial_blocks)]
        temporal_moves = [(0, at * temporal_size, at * temporal_size, temporal_size) for at in range(temporal_blocks)]
        half_shapes = (shape(rows, model),)
        forward_grads = temporal_grads = backward_grads = (shape(rows, model),)
        back_shapes = (shape(rows, 3 * width),)

    def plan_of(blocks, moves, weights, grads, sources=0, date_of=spatial_date, patch_of=None):
        return Plan(
            blocks, moves, len(origins), weights, paired, sizes["loc"], len(grads), sources, date_of, patch_of
        )

    plan = plan_of(spatial_blocks, spatial_moves, spatial, forward_grads)
    outs = call(
        functools.partial(spatial_forward_kernel, plan),
        (
            *half_shapes,
            *forward_grads,
            shape(rows, 3 * width),
            shape(*attend_dims(spatial_blocks), dtype=F32),
            shape(rows, width),
        ),
        (where, spatial_gain, cotangent_rows, *origins, *spatial.arrays),
        scratch=(
            pltpu.VMEM((rows, model), BF),
            pltpu.VMEM((rows, model), BF),
            pltpu.VMEM((rows, model), BF),
        ),
        flops=layer_flops,
    )
    partials, outs = outs[: len(origins)], outs[len(origins) :]
    forward, (triple, attend, mixed) = outs[: len(forward_grads)], outs[len(forward_grads) :]
    if paired:
        temporal_first, kept = fence(temporal_first, partials[1])
        partials = (partials[0], kept)
        there, early = call(
            between_kernel,
            (shape(half, model),),
            (origins[1], partials[1], swap(partials[1], "mp"), forward[2]),
            kept=(3,),
        )
        temporal = gather_weights(temporal_weights, temporal_first, swap(sent[1], "date"))
        early, there, *temporal.arrays[2:] = fence(early, swap(there, "date"), *temporal.arrays[2:])
        sources = (origins[0], partials[0], swap(partials[0], "mp"), there)
        early_other = swap(early, "date")
    else:
        spatial_out = (start.astype(F32) + add_over_heads(partials[0], sizes)).astype(BF)
        moved = lax.all_to_all(
            spatial_out.reshape(dates_here, patches, model),
            "date",
            split_axis=1,
            concat_axis=0,
            tiled=True,
        )
        sources = (temporal_rows(moved),)
    plan = plan_of(
        temporal_blocks,
        temporal_moves,
        temporal,
        temporal_grads,
        len(sources),
        temporal_date,
        temporal_patch,
    )
    outs = call(
        functools.partial(temporal_kernel, plan),
        (
            *temporal_grads,
            shape(rows, model),
            shape(rows, width),
            shape(rows, model),
            shape(rows, model),
            *(() if paired else back_shapes),
        ),
        (
            where,
            temporal_gain,
            survive,
            date_rows,
            cotangent_rows,
            *sources,
            *temporal.arrays,
        ),
        scratch=(
            pltpu.VMEM((rows, model), BF),
            pltpu.VMEM((rows, 3 * width), BF),
            pltpu.VMEM(attend_dims(temporal_blocks), F32),
            pltpu.VMEM((rows, width), BF),
            pltpu.VMEM((rows, 3 * width), BF),
        ),
        flops=2 * layer_flops,
    )
    middle, outs = outs[: len(temporal_grads)], outs[len(temporal_grads) :]
    (joined, temporal_mixed, temporal_partial, back_part), temporal_triples = outs[:4], outs[4:]
    if paired:
        back_part, early_other = fence(back_part, early_other)

    if sizes["mp"] == 2:
        others = swap(back_part, "mp")
    else:
        others = (lax.psum(back_part.astype(F32), "mp") - back_part.astype(F32)).astype(BF)
    *backs, last_sent = call(
        functools.partial(norm_back_kernel, temporal_moves, temporal_size),
        half_shapes,
        (temporal_gain, back_part, others, joined, cotangent_rows, middle[-1]),
        kept=(5,),
    )
    if paired:
        back_origins = (backs[0], swap(backs[1], "date"))
        early_there = swap(early_other[:, : 2 * quarter], "mp")
        middle_other = swap(middle[1], "date")
        part, columns = 3 * width // 2, model // 2
        *intake, kept = summed(
            where,
            (middle[0], middle_other, middle[1]),
            ((0, ((1, 0),), (2, columns), (1, columns), part),),
        )
    else:
        back = lax.all_to_all(
            temporal_whole(backs[0]), "date", split_axis=0, concat_axis=1, tiled=True
        )
        back_origins = (back.reshape(rows, model),)
        kept = temporal_triples[0]
    outlet = spatial.only((3,))
    plan = plan_of(spatial_blocks, spatial_moves, outlet, backward_grads)
    *outs, kept = call(
        functools.partial(spatial_backward_kernel, plan),
        (*backward_grads, *back_shapes),
        (where, triple, attend, kept, *back_origins, *outlet.arrays),
        scratch=(
            pltpu.VMEM((rows, model), BF),
            pltpu.VMEM((rows, width), BF),
            pltpu.VMEM((rows, 3 * width), BF),
        ),
        flops=layer_flops,
        kept=(3,),
    )
    backward, back_triples = outs[: len(backward_grads)], outs[len(backward_grads) :]
    encoded = (joined.astype(F32) + add_over_heads(temporal_partial, sizes)).astype(BF)
    encoded = temporal_whole(encoded).transpose(1, 0, 2)[None]
    if not paired:
        return (
            encoded,
            whole_grads(forward[0], back_triples[0], backward[0], mixed),
            whole_grads(middle[0], kept, cotangent_rows, temporal_mixed),
        )
    intake = [*summed_over_loc((*intake, kept))]
    last_other = swap(last_sent, "date")
    *sums, upstream_own, intake[1] = summed(
        where,
        (middle[0], middle_other, last_sent, last_other, forward[1], early_other, early_there),
        (
            (0, ((1, 0),), (2, 0), (3, 0), part),
            (4, ((5, quarter), (6, quarter)), (2, part), (3, part), width),
        ),
        kept=(backward[0], intake[1]),
    )
    sums[0], intake[2] = fence(sums[0], intake[2])
    outlet = [*summed_over_loc(sums)]
    half = model // 2
    backward_other = swap(backward[1], "date")
    *sums, outlet[0] = summed(
        where,
        (
            upstream_own,
            backward_other,
            mixed,
            early_other,
            forward[0],
            early_there,
            back_triples[0],
        ),
        (
            (0, ((1, 0),), (2, 0), (3, 2 * quarter), width),
            (4, ((3, 0), (5, 0)), (6, 0), (1, half), back_triples[0].shape[1]),
        ),
        kept=(outlet[0],),
    )
    spatial_terms = [*summed_over_loc(sums)]
    sums = summed(
        where,
        (forward[0], early_other, early_there, back_triples[1], swap(back_triples[1], "date")),
        ((0, ((1, 0), (2, 0)), (3, 0), (4, 0), back_triples[1].shape[1]),),
        kept=(spatial_terms[0],),
    )
    *sums, spatial_terms[0] = sums
    spatial_terms += summed_over_loc(sums)
    (temporal_grads,) = finish((*intake, *outlet), width, 0)
    spatial_grads, temporal_grads = finish(spatial_terms, width, 3, kept=temporal_grads)
    return (encoded, spatial_grads, temporal_grads)


def solution(mesh):
    in_specs = (
        P(("groups", "loc"), None, "date", None),
        P(("groups", "loc"), None, "date", None),
        P(("groups", "loc"), None),
        P(("groups", "loc"), None),
        P(("groups", "loc"), None),
        P(),
        P(),
        P(),
        P("date", None, "mp"),
        P(),
        P("date", None, "mp"),
        P(("groups", "loc"), "date", None, None),
    )
    out_specs = (
        P(("groups", "loc"), "date", None, None),
        P(("groups", "loc", "date"), None, "mp"),
        P(("groups", "loc", "date"), None, "mp"),
    )
    return jax.shard_map(
        functools.partial(per_device, dict(mesh.shape)),
        mesh=mesh,
        in_specs=in_specs,
        out_specs=out_specs,
        check_vma=False,
    )
```
